32 devices in a mesh: dp: 4 (over x, core), fsdp: 8 (over z, y).
Axes of the slice: x: 2, y: 2, z: 4, core: 2. Of those that a mesh axis runs over, the one named last changes fastest.
Arguments:
- tokens: bfloat16 [12288, 2048], P(('dp', 'fsdp')), may hold values from -6 to 6
- cotangent: bfloat16 [12288, 2048], P(('dp', 'fsdp')), may hold values from -6 to 6
- lengths: int32 [32, 4], P(('dp', 'fsdp')), may hold values from 1 to 288, 384 in all within a row
- routing: int32 [32, 8], P(('dp', 'fsdp')), may hold values from 0 to 7, each once within a row
- in_weight: float32 [2048, 2304], P(('dp', 'fsdp')), may hold values from -0.125 to 0.125
- in_first: float32 [2048, 2304], P(('dp', 'fsdp')), may hold values from -640 to 640
- in_second: float32 [2048, 2304], P(('dp', 'fsdp')), may hold values from 12288 to 49152
- out_weight: float32 [2048, 2048], P(('dp', 'fsdp')), may hold values from -1 to 1
- out_first: float32 [2048, 2048], P(('dp', 'fsdp')), may hold values from -160 to 160
- out_second: float32 [2048, 2048], P(('dp', 'fsdp')), may hold values from 614 to 2457
- up_weight: float32 [2048, 8192], P(('dp', 'fsdp')), may hold values from -0.125 to 0.125
- up_first: float32 [2048, 8192], P(('dp', 'fsdp')), may hold values from -224 to 224
- up_second: float32 [2048, 8192], P(('dp', 'fsdp')), may hold values from 1228 to 4915
- down_weight: float32 [8192, 2048], P(('dp', 'fsdp')), may hold values from -0.0625 to 0.0625
- down_first: float32 [8192, 2048], P(('dp', 'fsdp')), may hold values from -320 to 320
- down_second: float32 [8192, 2048], P(('dp', 'fsdp')), may hold values from 3072 to 12288
- vectors: float32 [2048, 11], P(('dp', 'fsdp')), may hold values from -0.8 to 1.4
- vector_first: float32 [2048, 11], P(('dp', 'fsdp')), may hold values from -640 to 640
- vector_second: float32 [2048, 11], P(('dp', 'fsdp')), may hold values from 12288 to 49152
Outputs:
- result: bfloat16 [12288, 2048], P(('dp', 'fsdp'))
- token_grad: bfloat16 [12288, 2048], P(('dp', 'fsdp'))
- in_new: float32 [2048, 2304], P(('dp', 'fsdp'))
- in_first_new: float32 [2048, 2304], P(('dp', 'fsdp'))
- in_second_new: float32 [2048, 2304], P(('dp', 'fsdp'))
- out_new: float32 [2048, 2048], P(('dp', 'fsdp'))
- out_first_new: float32 [2048, 2048], P(('dp', 'fsdp'))
- out_second_new: float32 [2048, 2048], P(('dp', 'fsdp'))
- up_new: float32 [2048, 8192], P(('dp', 'fsdp'))
- up_first_new: float32 [2048, 8192], P(('dp', 'fsdp'))
- up_second_new: float32 [2048, 8192], P(('dp', 'fsdp'))
- down_new: float32 [8192, 2048], P(('dp', 'fsdp'))
- down_first_new: float32 [8192, 2048], P(('dp', 'fsdp'))
- down_second_new: float32 [8192, 2048], P(('dp', 'fsdp'))
- vectors_new: float32 [2048, 11], P(('dp', 'fsdp'))
- vector_first_new: float32 [2048, 11], P(('dp', 'fsdp'))
- vector_second_new: float32 [2048, 11], P(('dp', 'fsdp'))
The draws below stay inside these ranges and needn't reach their ends.
Inputs may be any that keep to these rules, and one draw needn't show every extreme that they name: `lengths`: each row sums to 384, and its largest entry is 288. `routing`: each row is a permutation of 0 to 7.
All inputs are finite; a program needn't handle non-finite values.
Results may differ from the reference program's by a relative error of at most 0.013.
Values may be sent and summed in bfloat16 or wider, within the bound.
A program may use at most 576 MiB of HBM per device.

```python
import math
import jax
import jax.numpy as jnp
import numpy as np
from jax import lax

D = 2048
FF = 8192
HD = 128
TOK_DEV = 384
SEQ_DEV = 4
STEP = 5
LEN_MOST = 288
TOKENS = 12288
NVEC = 11
N_DP = 4
N_FSDP = 8


def draw_vectors(key, part):
    key = jax.random.fold_in(key, 11)
    noise = jnp.clip(jax.random.normal(key, (D, NVEC), jnp.float32), -4.0, 4.0)
    column = jnp.arange(NVEC, dtype=jnp.int32)[None, :]
    gains = (column == 0) | (column == 4)
    return jnp.where(gains, 1.0 + 0.1 * noise, 0.2 * noise)


def levels(key, dims, split, low, largest):
    def one(dim, blocks):
        heights = jax.random.uniform(jax.random.fold_in(jax.random.fold_in(key, 6), dim), (blocks,), jnp.float32, low / len(split), largest / len(split))
        return jnp.repeat(jnp.exp(heights), dims[dim] // blocks).reshape((-1,) + (1,) * (len(dims) - dim - 1))

    level = one(*split[0])
    for cut in split[1:]:
        level = level * one(*cut)
    return level


def length_profile(number_of, total, bound, slope):
    weights = [(1 << 20) // math.isqrt(grade ** slope) + 1 for grade in range(2, number_of + 1)]
    rest, counts = total - bound - (number_of - 1), [1] * (number_of - 1)
    while rest > 0:
        candidates = [i for i in range(number_of - 1) if counts[i] < bound]
        pool, remaining = sum([weights[i] for i in candidates]), rest
        for i in candidates:
            extra = min(bound - counts[i], max(1, remaining * weights[i] // pool), rest)
            counts[i] = counts[i] + extra
            rest = rest - extra
    return np.array([bound] + counts)


def ragged(rng, number_of, total, bound, lean):
    if number_of == 2:
        one = jax.random.randint(rng, (), max(1, total - bound), min(bound, total - 1) + 1)
        return jnp.stack([one, total - one])
    tallies = jnp.asarray(length_profile(number_of, total, bound, lean), jnp.int32)
    pairs = (number_of - 1) // 2
    donor, taker = tallies[1:1 + 2 * pairs:2], tallies[2:2 + 2 * pairs:2]
    slack = jnp.minimum(donor - 1, bound - taker)
    passed = jax.random.randint(jax.random.fold_in(rng, 1), (pairs,), 0, 1 << 20) % (slack + 1)
    tallies = tallies.at[1:1 + 2 * pairs:2].set(donor - passed).at[2:2 + 2 * pairs:2].set(taker + passed)
    return tallies[jax.random.permutation(jax.random.fold_in(rng, 2), number_of)]


def scatter_about(key, shape, spread, bound, pieces=(), kind=jnp.bfloat16):
    values = spread * jax.random.normal(key, shape, jnp.float32)
    if pieces:
        values = values * levels(key, shape, pieces, -0.22, 0.18)
    return jnp.clip(values, -bound, bound).astype(kind)


def setup_inputs(seed: int = 0) -> dict:
    key_of = jax.random.split(jax.random.key(seed), 20)
    tokens = scatter_about(key_of[0], (TOKENS, D), 1.0, 6.0, ((0, 32),))
    cotangent = scatter_about(key_of[1], (TOKENS, D), 1.0, 6.0, ((0, 32),))
    lengths = jax.vmap(lambda own: ragged(own, SEQ_DEV, TOK_DEV, LEN_MOST, 2))(jax.random.split(key_of[2], (N_DP * N_FSDP))).reshape((N_DP * N_FSDP, SEQ_DEV)).astype(jnp.int32)
    routing = jax.vmap(lambda own: jax.random.permutation(own, N_FSDP))(jax.random.split(key_of[3], (N_DP * N_FSDP))).reshape((N_DP * N_FSDP, N_FSDP)).astype(jnp.int32)
    in_weight = scatter_about(key_of[4], (D, D + 2 * HD), D ** -0.5, 0.125, ((0, 32),), jnp.float32)
    in_first = scatter_about(key_of[5], (D, D + 2 * HD), (TOKENS ** 0.5), 640.0, ((0, 32),), jnp.float32)
    in_second = jnp.clip(jnp.exp(math.log(49152.0) - 1.3862944 * jax.random.uniform(key_of[6], (D, D + 2 * HD), jnp.float32) ** levels(key_of[6], (D, D + 2 * HD), ((0, 32),), -0.2, 0.2)), 12288.0, 49152.0)
    out_weight = scatter_about(key_of[7], (D, D), (D * 8 // TOK_DEV) ** -0.5, 1.0, ((0, 32),), jnp.float32)
    out_first = scatter_about(key_of[8], (D, D), ((TOKENS // 20) ** 0.5), 160.0, ((0, 32),), jnp.float32)
    out_second = jnp.clip(jnp.exp(math.log(2457.0) - 1.38670144 * jax.random.uniform(key_of[9], (D, D), jnp.float32) ** levels(key_of[9], (D, D), ((0, 32),), -0.2, 0.2)), 614.0, 2457.0)
    up_weight = scatter_about(key_of[10], (D, FF), D ** -0.5, 0.125, ((0, 32),), jnp.float32)
    up_first = scatter_about(key_of[11], (D, FF), ((TOKENS // 10) ** 0.5), 224.0, ((0, 32),), jnp.float32)
    up_second = jnp.clip(jnp.exp(math.log(4915.0) - 1.386905 * jax.random.uniform(key_of[12], (D, FF), jnp.float32) ** levels(key_of[12], (D, FF), ((0, 32),), -0.2, 0.2)), 1228.0, 4915.0)
    down_weight = scatter_about(key_of[13], (FF, D), FF ** -0.5, 0.0625, ((0, 32),), jnp.float32)
    down_first = scatter_about(key_of[14], (FF, D), ((TOKENS // 4) ** 0.5), 320.0, ((0, 32),), jnp.float32)
    down_second = jnp.clip(jnp.exp(math.log(12288.0) - 1.3862944 * jax.random.uniform(key_of[15], (FF, D), jnp.float32) ** levels(key_of[15], (FF, D), ((0, 32),), -0.2, 0.2)), 3072.0, 12288.0)
    vectors = draw_vectors(jax.random.fold_in(key_of[19], 71), 0)
    vector_first = scatter_about(key_of[17], (D, NVEC), (TOKENS ** 0.5), 640.0, ((0, 32),), jnp.float32)
    vector_second = jnp.clip(jnp.exp(math.log(49152.0) - 1.3862944 * jax.random.uniform(key_of[18], (D, NVEC), jnp.float32) ** levels(key_of[18], (D, NVEC), ((0, 32),), -0.2, 0.2)), 12288.0, 49152.0)
    return {"tokens": tokens, "cotangent": cotangent, "lengths": lengths, "routing": routing, "in_weight": in_weight, "in_first": in_first, "in_second": in_second, "out_weight": out_weight, "out_first": out_first, "out_second": out_second, "up_weight": up_weight, "up_first": up_first, "up_second": up_second, "down_weight": down_weight, "down_first": down_first, "down_second": down_second, "vectors": vectors, "vector_first": vector_first, "vector_second": vector_second}


eps_norm = 1e-05
beta_one = 0.5
beta_two = 0.5
adam_eps = 1e-08
decay_rate = 0.1
highest = lax.Precision.HIGHEST

@jax.custom_vjp
def low(v):
    return lax.optimization_barrier(v.astype(jnp.bfloat16)).astype(jnp.float32)

@jax.custom_vjp
def low_back(v):
    return v

def low_keep(v):
    return (low(v), None)

def low_pass(kept, grad):
    return (grad,)

def back_keep(v):
    return (v, None)

def back_low(kept, grad):
    return (low(grad),)
low.defvjp(low_keep, low_pass)
low_back.defvjp(back_keep, back_low)

def layer_norm(values, gain, shift):
    centered = values - lax.optimization_barrier(jnp.mean(values, axis=-1, keepdims=True))
    scaled = centered * lax.rsqrt(lax.optimization_barrier(jnp.mean(centered * centered, axis=-1, keepdims=True)) + eps_norm)
    return scaled * gain + shift

def gelu_tanh(values):
    return 0.5 * values * (1.0 + jnp.tanh(0.7978845608028654 * (values + 0.044715 * values * values * values)))

def segment_mask(sizes, count):
    ends = jnp.cumsum(sizes)
    places = jnp.arange(count, dtype=jnp.int32)
    labels = lax.optimization_barrier(jnp.sum((places[:, None] >= ends[None, :]).astype(jnp.int32), axis=1))
    return (labels[:, None] == labels[None, :]) & (places[None, :] <= places[:, None])

def forward(inputs, w_query, w_branch, w_hidden, w_output, table, allowed):
    count = inputs.shape[0]
    heads = D // HD
    norm_one = low(layer_norm(inputs, table[:, 0], table[:, 1]))
    mixed = jnp.dot(norm_one, w_query, precision=highest)
    query = low(low_back(mixed[:, :D] + table[:, 2]))
    keys = low(low_back(mixed[:, D:D + HD]))
    values = low(low_back(mixed[:, D + HD:]))
    scale = 1.0 / math.sqrt(HD)
    scores = scale * jnp.einsum('thd,sd->hts', query.reshape(count, heads, HD), keys, precision=highest)
    scores = low_back(jnp.where(allowed[None], scores, -1e+30))
    top = lax.optimization_barrier(jnp.max(scores, axis=-1, keepdims=True))
    expo = jnp.exp(scores - top)
    probs = low(expo / lax.optimization_barrier(jnp.sum(expo, axis=-1, keepdims=True)))
    attended = jnp.einsum('hts,sd->thd', probs, values, precision=highest).reshape(count, D)
    attended = low(low_back(attended))
    branch = low_back(jnp.dot(attended, w_branch, precision=highest) + table[:, 3])
    middle = inputs + branch
    norm_two = low(layer_norm(middle, table[:, 4], table[:, 5]))
    hidden_bias = table[:, 7:].T.reshape(FF)
    hidden = low_back(jnp.dot(norm_two, w_hidden, precision=highest) + hidden_bias)
    active = low(gelu_tanh(hidden))
    output = low_back(jnp.dot(active, w_output, precision=highest) + table[:, 6])
    return middle + output

def adam_update(weight, first, second, grad, rate, decay):
    first_new = beta_one * first + (1.0 - beta_one) * grad
    second_new = beta_two * second + (1.0 - beta_two) * grad * grad
    fix_one = 1.0 - beta_one ** STEP
    fix_two = 1.0 - beta_two ** STEP
    step_size = first_new / fix_one / (jnp.sqrt(second_new / fix_two) + adam_eps)
    weight_new = weight - rate * (step_size + decay * weight)
    return (weight_new, first_new, second_new)

def reference(tokens, cotangent, lengths, routing, in_weight, in_first, in_second, out_weight, out_first, out_second, up_weight, up_first, up_second, down_weight, down_first, down_second, vectors, vector_first, vector_second):
    devices = N_DP * N_FSDP
    piece = TOK_DEV // N_FSDP
    slots = jnp.arange(N_FSDP, dtype=jnp.int32)
    inverse = lax.optimization_barrier(jnp.sum(jnp.where(routing[:, :, None] == slots[None, None, :], slots[None, :, None], 0), axis=1)).astype(jnp.int32)
    compute = jnp.arange(devices, dtype=jnp.int32)
    group = compute // N_FSDP
    member = compute % N_FSDP
    sources = group[:, None] * N_FSDP + slots[None, :]
    chosen = inverse[sources, member[:, None]]
    rows = (sources * TOK_DEV + chosen * piece)[:, :, None] + jnp.arange(piece, dtype=jnp.int32)[None, None, :]
    rows = rows.reshape(devices, TOK_DEV).astype(jnp.int32)
    params = tuple((item.astype(jnp.bfloat16).astype(jnp.float32) for item in (in_weight, out_weight, up_weight, down_weight, vectors)))
    tokens_full = tokens.astype(jnp.float32)
    cot_full = cotangent.astype(jnp.float32)

    def batch_step(totals, item):
        index, sizes = item
        inputs = tokens_full[index]
        grad_y = cot_full[index]
        allowed = segment_mask(sizes, TOK_DEV)

        def local(inputs, w_query, w_branch, w_hidden, w_output, table):
            return forward(inputs, w_query, w_branch, w_hidden, w_output, table, allowed)
        output, pull = jax.vjp(local, inputs, *params)
        grads = pull(grad_y)
        totals = tuple((total + grad for total, grad in zip(totals, grads[1:])))
        return (totals, (output.astype(jnp.bfloat16), grads[0].astype(jnp.bfloat16)))
    zeros = tuple((jnp.zeros_like(item) for item in params))
    totals, (outputs, backs) = lax.scan(batch_step, zeros, (rows, lengths))
    flat = rows.reshape(-1)
    result = jnp.zeros((TOKENS, D), jnp.bfloat16).at[flat].set(outputs.reshape(-1, D))
    token_grad = jnp.zeros((TOKENS, D), jnp.bfloat16).at[flat].set(backs.reshape(-1, D))
    grad_in, grad_out, grad_up, grad_down, grad_vec = totals
    in_new = adam_update(in_weight, in_first, in_second, grad_in, 1.0 / math.sqrt(D), decay_rate)
    out_new = adam_update(out_weight, out_first, out_second, grad_out, 1.0 / math.sqrt(D * 8 // TOK_DEV), decay_rate)
    up_new = adam_update(up_weight, up_first, up_second, grad_up, 1.0 / math.sqrt(D), decay_rate)
    down_new = adam_update(down_weight, down_first, down_second, grad_down, 1.0 / math.sqrt(FF), decay_rate)
    vec_new = adam_update(vectors, vector_first, vector_second, grad_vec, 0.1, 0.0)
    return (result, token_grad, in_new[0], in_new[1], in_new[2], out_new[0], out_new[1], out_new[2], up_new[0], up_new[1], up_new[2], down_new[0], down_new[1], down_new[2], vec_new[0], vec_new[1], vec_new[2])
```

```python
import math

import jax
import jax.numpy as jnp
from jax import lax
from jax.sharding import PartitionSpec as P

D = 2048
FF = 8192
HD = 128
TOK_DEV = 384
STEP = 5
NVEC = 11


eps_norm = 1e-05
beta_one = 0.5
beta_two = 0.5
adam_eps = 1e-08
decay_rate = 0.1


def layer_norm(values, gain, shift):
    centered = values - jnp.mean(values, axis=-1, keepdims=True)
    scaled = centered * lax.rsqrt(jnp.mean(centered * centered, axis=-1, keepdims=True) + eps_norm)
    return scaled * gain + shift


def gelu_tanh(values):
    return (
        0.5
        * values
        * (1.0 + jnp.tanh(0.7978845608028654 * (values + 0.044715 * values * values * values)))
    )


def segment_mask(sizes, count):
    ends = jnp.cumsum(sizes)
    places = jnp.arange(count, dtype=jnp.int32)
    labels = jnp.sum((places[:, None] >= ends[None, :]).astype(jnp.int32), axis=1)
    return (labels[:, None] == labels[None, :]) & (places[None, :] <= places[:, None])


def adam_update(weight, first, second, grad, rate, decay):
    grad = grad.astype(jnp.float32)
    first_new = beta_one * first + (1.0 - beta_one) * grad
    second_new = beta_two * second + (1.0 - beta_two) * grad * grad
    fix_one = 1.0 - beta_one**STEP
    fix_two = 1.0 - beta_two**STEP
    step_size = first_new / fix_one / (jnp.sqrt(second_new / fix_two) + adam_eps)
    weight_new = weight - rate * (step_size + decay * weight)
    return (weight_new, first_new, second_new)


def contract_rows(left, right):
    return lax.dot_general(
        left, right, (((0,), (0,)), ((), ())), preferred_element_type=jnp.float32
    )


def contract_cols(left, right):
    return lax.dot_general(
        left, right, (((1,), (1,)), ((), ())), preferred_element_type=jnp.float32
    )


def shards(
    tokens,
    cotangent,
    lengths,
    routing,
    in_weight,
    in_first,
    in_second,
    out_weight,
    out_first,
    out_second,
    up_weight,
    up_first,
    up_second,
    down_weight,
    down_first,
    down_second,
    vectors,
    vector_first,
    vector_second,
):
    bf = jnp.bfloat16
    heads = D // HD
    count = tokens.shape[0]
    parts = lax.axis_size("fsdp")
    groups = lax.axis_size("dp")
    both = ("dp", "fsdp")
    piece = count // parts
    width_in = D + 2 * HD
    slots = jnp.arange(parts, dtype=jnp.int32)
    order = routing[0]
    inverse = jnp.sum(jnp.where(order[:, None] == slots[None, :], slots[:, None], 0), axis=0)

    def deal(array):
        return jnp.take(array.reshape(parts, piece, D), inverse, axis=0).reshape(count, D)

    def undeal(array):
        return jnp.take(array.reshape(parts, piece, D), order, axis=0).reshape(count, D)

    rows = in_weight.shape[0]
    small = jnp.concatenate(
        [
            in_weight.astype(bf),
            out_weight.astype(bf),
            jnp.pad(vectors.astype(bf), ((0, 0), (0, 128 - NVEC))),
        ],
        axis=1,
    )
    whole_small = lax.all_gather(small, both, axis=0, tiled=True)
    whole_in = whole_small[:, :width_in]
    whole_out = whole_small[:, width_in : width_in + D]
    inputs_here = lax.all_to_all(deal(tokens), "fsdp", split_axis=0, concat_axis=0, tiled=True)
    grad_here = lax.all_to_all(deal(cotangent), "fsdp", split_axis=0, concat_axis=0, tiled=True)
    up_block = lax.all_to_all(up_weight.astype(bf), both, split_axis=1, concat_axis=0, tiled=True)
    part_up = lax.all_gather(up_block.T, "fsdp", axis=0, tiled=True)
    part_down = lax.all_gather(down_weight.astype(bf), "fsdp", axis=0, tiled=True)

    table = whole_small[:, width_in + D : width_in + D + NVEC].astype(jnp.float32)
    gain_one = table[:, 0]
    shift_one = table[:, 1]
    query_bias = table[:, 2]
    branch_bias = table[:, 3]
    gain_two = table[:, 4]
    shift_two = table[:, 5]
    output_bias = table[:, 6]
    hidden_bias = table[:, 7:].T.reshape(FF)
    ff_here = FF // groups
    ff_start = lax.axis_index("dp") * ff_here
    hidden_bias_here = lax.dynamic_slice(hidden_bias, (ff_start,), (ff_here,))
    allowed = segment_mask(lengths[0], count)
    scale = 1.0 / math.sqrt(HD)
    inputs = inputs_here.astype(jnp.float32)
    norm_one_b = layer_norm(inputs, gain_one, shift_one).astype(bf)
    mixed = jnp.dot(norm_one_b, whole_in, preferred_element_type=jnp.float32)
    query_b = (mixed[:, :D] + query_bias).astype(bf)
    keys_b = mixed[:, D : D + HD].astype(bf)
    values_b = mixed[:, D + HD :].astype(bf)
    query_heads = query_b.reshape(count, heads, HD)

    def score_table():
        raw = (
            jnp.einsum("thd,sd->hts", query_heads, keys_b, preferred_element_type=jnp.float32)
            * scale
        )
        return jnp.where(allowed[None], raw, -1e30)

    scores = score_table()
    top = jnp.max(scores, axis=-1, keepdims=True)
    expo = jnp.exp(scores - top)
    total = jnp.sum(expo, axis=-1, keepdims=True)
    logsum = top + jnp.log(total)
    probs_b = (expo / total).astype(bf)
    attended_b = (
        jnp.einsum("hts,sd->thd", probs_b, values_b, preferred_element_type=jnp.float32)
        .reshape(count, D)
        .astype(bf)
    )
    middle = inputs + (
        jnp.dot(attended_b, whole_out, preferred_element_type=jnp.float32) + branch_bias
    )
    norm_two_b = layer_norm(middle, gain_two, shift_two).astype(bf)

    norm_all = lax.all_gather(norm_two_b, "dp", axis=0, tiled=True)
    grad_all = lax.all_gather(grad_here, "dp", axis=0, tiled=True)
    hidden = contract_cols(norm_all, part_up) + hidden_bias_here
    grad_active = contract_cols(grad_all, part_down)
    gelu_value, gelu_pull = jax.vjp(gelu_tanh, hidden)
    active_b = gelu_value.astype(bf)
    grad_hidden_f = gelu_pull(grad_active)[0]
    grad_hidden_b = grad_hidden_f.astype(bf)
    grad_norm_two = lax.psum_scatter(
        jnp.dot(grad_hidden_b, part_up, preferred_element_type=jnp.float32).astype(bf),
        "dp",
        scatter_dimension=0,
        tiled=True,
    ).astype(jnp.float32)
    up_grad_block = lax.psum_scatter(
        contract_rows(grad_hidden_b, norm_all).astype(bf),
        "fsdp",
        scatter_dimension=0,
        tiled=True,
    )
    down_grad = lax.psum_scatter(
        contract_rows(active_b, grad_all).astype(bf), "fsdp", scatter_dimension=0, tiled=True
    )
    branch_two = lax.psum_scatter(
        jnp.dot(active_b, part_down, preferred_element_type=jnp.float32).astype(bf),
        "dp",
        scatter_dimension=0,
        tiled=True,
    ).astype(jnp.float32)
    result = middle + (branch_two + output_bias)

    grad_y = grad_here.astype(jnp.float32)
    norm_value_two, pull_two = jax.vjp(layer_norm, middle, gain_two, shift_two)
    grad_middle_norm, grad_gain_two, grad_shift_two = pull_two(grad_norm_two)
    grad_middle = grad_y + grad_middle_norm
    grad_branch_b = grad_middle.astype(bf)
    grad_attended_b = contract_cols(grad_branch_b, whole_out).astype(bf)
    grad_heads = grad_attended_b.reshape(count, heads, HD)
    probs = jnp.exp(score_table() - logsum)
    probs_again_b = probs.astype(bf)
    grad_probs = jnp.einsum("thd,sd->hts", grad_heads, values_b, preferred_element_type=jnp.float32)
    grad_values_b = jnp.einsum(
        "hts,thd->sd", probs_again_b, grad_heads, preferred_element_type=jnp.float32
    ).astype(bf)
    weighted = jnp.sum(probs * grad_probs, axis=-1, keepdims=True)
    grad_scores_b = (probs * (grad_probs - weighted)).astype(bf)
    grad_query_b = (
        (
            jnp.einsum("hts,sd->thd", grad_scores_b, keys_b, preferred_element_type=jnp.float32)
            * scale
        )
        .reshape(count, D)
        .astype(bf)
    )
    grad_keys_b = (
        jnp.einsum("hts,thd->sd", grad_scores_b, query_heads, preferred_element_type=jnp.float32)
        * scale
    ).astype(bf)
    grad_mixed_b = jnp.concatenate([grad_query_b, grad_keys_b, grad_values_b], axis=1)
    grad_norm_one = contract_cols(grad_mixed_b, whole_in)
    norm_value_one, pull_one = jax.vjp(layer_norm, inputs, gain_one, shift_one)
    grad_inputs_norm, grad_gain_one, grad_shift_one = pull_one(grad_norm_one)
    grad_inputs = grad_middle + grad_inputs_norm
    back_result = lax.all_to_all(
        result.astype(bf), "fsdp", split_axis=0, concat_axis=0, tiled=True
    )
    back_grad = lax.all_to_all(
        grad_inputs.astype(bf), "fsdp", split_axis=0, concat_axis=0, tiled=True
    )
    hidden_sums = jnp.sum(grad_hidden_b.astype(jnp.float32), axis=0)
    hidden_whole = lax.dynamic_update_slice(
        jnp.zeros((FF,), jnp.float32), hidden_sums, (ff_start,)
    )
    vector_grad = jnp.concatenate(
        [
            jnp.stack(
                [
                    grad_gain_one,
                    grad_shift_one,
                    jnp.sum(grad_query_b.astype(jnp.float32), axis=0),
                    jnp.sum(grad_branch_b.astype(jnp.float32), axis=0),
                    grad_gain_two,
                    grad_shift_two,
                    jnp.sum(grad_y, axis=0),
                ],
                axis=0,
            ),
            hidden_whole.reshape(FF // D, D),
        ],
        axis=0,
    )
    owners = groups * parts
    vector_grad = vector_grad.reshape(NVEC, owners, rows).transpose(1, 0, 2)
    vector_grad = jnp.pad(vector_grad, ((0, 0), (0, 16 - NVEC), (0, 128 - rows)))
    vector_sum = lax.psum_scatter(
        vector_grad.reshape(owners * 16, 128), both, scatter_dimension=0, tiled=True
    )
    small_grad = lax.psum_scatter(
        jnp.concatenate(
            [
                contract_rows(norm_one_b, grad_mixed_b).astype(bf),
                contract_rows(attended_b, grad_branch_b).astype(bf),
            ],
            axis=1,
        ),
        both,
        scatter_dimension=0,
        tiled=True,
    )
    grad_up = lax.all_to_all(up_grad_block.T, both, split_axis=0, concat_axis=1, tiled=True)
    grad_in = small_grad[:, :width_in]
    grad_out = small_grad[:, width_in : width_in + D]
    grad_vec = vector_sum[:NVEC, :rows].T
    in_new = adam_update(in_weight, in_first, in_second, grad_in, 1.0 / math.sqrt(D), decay_rate)
    out_new = adam_update(
        out_weight, out_first, out_second, grad_out, 1.0 / math.sqrt(D * 8 // TOK_DEV), decay_rate
    )
    up_new = adam_update(up_weight, up_first, up_second, grad_up, 1.0 / math.sqrt(D), decay_rate)
    down_new = adam_update(
        down_weight, down_first, down_second, down_grad, 1.0 / math.sqrt(FF), decay_rate
    )
    vec_new = adam_update(vectors, vector_first, vector_second, grad_vec, 0.1, 0.0)
    return (undeal(back_result), undeal(back_grad)) + in_new + out_new + up_new + down_new + vec_new


def solution(mesh):
    spec = P(("dp", "fsdp"), None)
    return jax.shard_map(
        shards,
        mesh=mesh,
        in_specs=(spec,) * 19,
        out_specs=(spec,) * 17,
        check_vma=False,
    )
```

```python
import functools
import math

import jax
import jax.numpy as jnp
from jax import lax
from jax.experimental import pallas as pl
from jax.experimental.pallas import tpu as pltpu
from jax.sharding import PartitionSpec as P

D = 2048
FF = 8192
HD = 128
TOK_DEV = 384
STEP = 5
NVEC = 11


eps_norm = 1e-05
beta_one = 0.5
beta_two = 0.5
adam_eps = 1e-08
decay_rate = 0.1


def layer_norm(values, gain, shift):
    centered = values - jnp.mean(values, axis=-1, keepdims=True)
    scaled = centered * lax.rsqrt(jnp.mean(centered * centered, axis=-1, keepdims=True) + eps_norm)
    return scaled * gain + shift


def gelu_tanh(values):
    return (
        0.5
        * values
        * (1.0 + jnp.tanh(0.7978845608028654 * (values + 0.044715 * values * values * values)))
    )


def segment_mask(sizes, count):
    ends = jnp.cumsum(sizes)
    places = jnp.arange(count, dtype=jnp.int32)
    labels = jnp.sum((places[:, None] >= ends[None, :]).astype(jnp.int32), axis=1)
    return (labels[:, None] == labels[None, :]) & (places[None, :] <= places[:, None])


def adam_update(weight, first, second, grad, rate, decay):
    grad = grad.astype(jnp.float32)
    first_new = beta_one * first + (1.0 - beta_one) * grad
    second_new = beta_two * second + (1.0 - beta_two) * grad * grad
    fix_one = 1.0 - beta_one**STEP
    fix_two = 1.0 - beta_two**STEP
    step_size = first_new / fix_one / (jnp.sqrt(second_new / fix_two) + adam_eps)
    weight_new = weight - rate * (step_size + decay * weight)
    return (weight_new, first_new, second_new)


def contract_rows(left, right):
    return lax.dot_general(
        left, right, (((0,), (0,)), ((), ())), preferred_element_type=jnp.float32
    )


def contract_cols(left, right):
    return lax.dot_general(
        left, right, (((1,), (1,)), ((), ())), preferred_element_type=jnp.float32
    )


MESH = pl.DeviceIdType.MESH
F32 = jnp.float32
BF = jnp.bfloat16


def wrap(value, count):
    return lax.rem(value + 2 * count, count)


def ring_place(index, parts):
    if parts != 8:
        return index
    z, y = lax.div(index, 2), lax.rem(index, 2)
    return z + y * (7 - 2 * z)


def ring_index(place, parts):
    place = wrap(place, parts)
    if parts != 8:
        return place
    back = lax.div(place, 4)
    return (1 - back) * 2 * place + back * (15 - 2 * place)


def remote(src, dst, send, recv, dp, fs):
    return pltpu.make_async_remote_copy(
        src_ref=src, dst_ref=dst, send_sem=send, recv_sem=recv, device_id=(dp, fs), device_id_type=MESH
    )


def greet(targets):
    barrier = pltpu.get_barrier_semaphore()
    for dp, fs in targets:
        pl.semaphore_signal(barrier, inc=1, device_id=(dp, fs), device_id_type=MESH)
    pl.semaphore_wait(barrier, len(targets))


def greet_all(me, parts, owners):
    barrier = pltpu.get_barrier_semaphore()

    def one(i, carry):
        peer = wrap(me + i, owners)
        pl.semaphore_signal(
            barrier, inc=1, device_id=(lax.div(peer, parts), lax.rem(peer, parts)), device_id_type=MESH
        )
        return carry

    lax.fori_loop(1, owners, one, 0)
    pl.semaphore_wait(barrier, owners - 1)


def loop(low, high, body):
    def one(i, carry):
        body(i)
        return carry

    lax.fori_loop(low, high, one, 0)


def deal_copy(parts, dp, f, src, dst, send, recv, d, came=False):
    to = wrap(f + d, parts)
    place = wrap(f - d, parts) if came else f
    return remote(src.at[to], dst.at[place], send.at[d], recv.at[d], dp, to)


def owner_copy(me, parts, owners, src, dst, send, recv, d, came=False):
    to = wrap(me + d, owners)
    place = wrap(me - d, owners) if came else me
    return remote(
        src.at[to], dst.at[place], send.at[d], recv.at[d], lax.div(to, parts), lax.rem(to, parts)
    )


def spread_kernel(
    parts, groups,
    xd, gd, inb, ovb, upb,
    xo, eall, win, wov, upo,
    local, xs, xr, gs, gr, us, ur, rs, rr, ns, nr, ss, sr, ens, enr, ess, esr,
):
    dp, f = lax.axis_index("dp"), lax.axis_index("fsdp")
    owners, rows_x = groups * parts, groups // 2
    x, core = lax.div(dp, 2), lax.rem(dp, 2)
    sib = x * 2 + 1 - core
    me = dp * parts + f
    p = ring_place(f, parts)
    nxt, prv = ring_index(p + 1, parts), ring_index(p - 1, parts)
    whole = (win, wov)
    mine = [
        pltpu.make_async_copy(inb, win.at[me], local.at[0]),
        pltpu.make_async_copy(ovb, wov.at[me], local.at[1]),
        pltpu.make_async_copy(xd.at[f], xo.at[f], local.at[2]),
        pltpu.make_async_copy(gd.at[f], eall.at[dp, f], local.at[3]),
        pltpu.make_async_copy(upb.at[me], upo.at[me], local.at[4]),
    ]
    for copy in mine:
        copy.start()
    greet_all(me, parts, owners)
    for copy in mine:
        copy.wait()

    def x_copies(d, came=False):
        return deal_copy(parts, dp, f, xd, xo, xs, xr, d, came)

    def g_copies(d, came=False):
        return deal_copy(parts, dp, f, gd, eall.at[dp], gs, gr, d, came)

    def u_copies(d, came=False):
        return owner_copy(me, parts, owners, upb, upo, us, ur, d, came)

    def origin(h, s):
        return ring_index(p - s if h == 0 else p + s, parts)

    def ring_send(h, s):
        ref = whole[h].at[dp * parts + origin(h, s)]
        return remote(ref, ref, rs.at[h, s], rr.at[h, s], dp, nxt if h == 0 else prv)

    def ring_recv(h, s):
        ref = whole[h].at[dp * parts + origin(h, s)]
        return remote(ref, ref, rs.at[h, s - 1], rr.at[h, s - 1], dp, nxt if h == 0 else prv)

    def x_send(h, s, dx):
        ref = whole[h].at[dp * parts + origin(h, s)]
        to = wrap(x + dx, rows_x) * 2 + core
        return remote(ref, ref, ns.at[h, s, dx], nr.at[h, s, dx], to, f)

    def x_recv(h, s, dx):
        came = wrap(x - dx, rows_x) * 2 + core
        ref = whole[h].at[came * parts + origin(h, s)]
        return remote(ref, ref, ns.at[h, s, dx], nr.at[h, s, dx], came, f)

    def sib_send(h, s, dx):
        came = wrap(x - dx, rows_x) * 2 + core
        ref = whole[h].at[came * parts + origin(h, s)]
        return remote(ref, ref, ss.at[h, s, dx], sr.at[h, s, dx], sib, f)

    def sib_recv(h, s, dx):
        came = wrap(x - dx, rows_x) * 2 + 1 - core
        ref = whole[h].at[came * parts + origin(h, s)]
        return remote(ref, ref, ss.at[h, s, dx], sr.at[h, s, dx], sib, f)

    def e_x_send(d, dx):
        ref = eall.at[dp, wrap(f - d, parts)]
        to = wrap(x + dx, rows_x) * 2 + core
        return remote(ref, ref, ens.at[d, dx], enr.at[d, dx], to, f)

    def e_x_recv(d, dx):
        came = wrap(x - dx, rows_x) * 2 + core
        ref = eall.at[came, wrap(f - d, parts)]
        return remote(ref, ref, ens.at[d, dx], enr.at[d, dx], came, f)

    def e_sib_send(d, dx):
        came = wrap(x - dx, rows_x) * 2 + core
        ref = eall.at[came, wrap(f - d, parts)]
        return remote(ref, ref, ess.at[d, dx], esr.at[d, dx], sib, f)

    def e_sib_recv(d, dx):
        came = wrap(x - dx, rows_x) * 2 + 1 - core
        ref = eall.at[came, wrap(f - d, parts)]
        return remote(ref, ref, ess.at[d, dx], esr.at[d, dx], sib, f)

    loop(1, parts, lambda d: x_copies(d).start())

    def ring_step(s):
        for h in range(2):
            @pl.when(s > 0)
            def _():
                ring_recv(h, s).wait_recv()

            @pl.when(s < parts - 1)
            def _():
                ring_send(h, s).start()

            for dx in range(1, rows_x):
                x_send(h, s, dx).start()
            sib_send(h, s, 0).start()

    ring_step(jnp.int32(0))
    loop(1, parts, lambda d: g_copies(d).start())
    loop(1, owners, lambda d: u_copies(d).start())
    loop(1, parts, ring_step)

    def e_step(d):
        @pl.when(d > 0)
        def _():
            g_copies(d, True).wait_recv()

        for dx in range(1, rows_x):
            e_x_send(d, dx).start()
        e_sib_send(d, 0).start()

    loop(0, parts, e_step)

    def relay(s):
        for h in range(2):
            for dx in range(1, rows_x):
                x_recv(h, s, dx).wait_recv()
                sib_send(h, s, dx).start()

    loop(0, parts, relay)

    def e_relay(d):
        for dx in range(1, rows_x):
            e_x_recv(d, dx).wait_recv()
            e_sib_send(d, dx).start()

    loop(0, parts, e_relay)

    def finish(s):
        for h in range(2):
            @pl.when(s < parts - 1)
            def _():
                ring_send(h, s).wait_send()

            for dx in range(1, rows_x):
                x_send(h, s, dx).wait_send()
            for dx in range(rows_x):
                sib_recv(h, s, dx).wait_recv()
                sib_send(h, s, dx).wait_send()
        for dx in range(1, rows_x):
            e_x_send(s, dx).wait_send()
        for dx in range(rows_x):
            e_sib_recv(s, dx).wait_recv()
            e_sib_send(s, dx).wait_send()

        @pl.when(s > 0)
        def _():
            x_copies(s, True).wait_recv()
            x_copies(s).wait_send()
            g_copies(s).wait_send()

    loop(0, parts, finish)

    def u_finish(d):
        u_copies(d, True).wait_recv()
        u_copies(d).wait_send()

    loop(1, owners, u_finish)


def spread(parts, groups, xd, gd, inb, ovb, upb):
    owners, rows_x = groups * parts, groups // 2
    dma = pltpu.SemaphoreType.DMA
    return pl.pallas_call(
        functools.partial(spread_kernel, parts, groups),
        out_shape=(
            jax.ShapeDtypeStruct(xd.shape, BF),
            jax.ShapeDtypeStruct((groups,) + gd.shape, BF),
            jax.ShapeDtypeStruct((owners,) + inb.shape, BF),
            jax.ShapeDtypeStruct((owners,) + ovb.shape, BF),
            jax.ShapeDtypeStruct(upb.shape, BF),
        ),
        in_specs=[pl.BlockSpec(memory_space=pl.ANY)] * 5,
        out_specs=(pl.BlockSpec(memory_space=pl.ANY),) * 5,
        scratch_shapes=[
            dma((5,)),
            dma((parts,)), dma((parts,)), dma((parts,)), dma((parts,)),
            dma((owners,)), dma((owners,)),
            dma((2, parts)), dma((2, parts)),
            dma((2, parts, rows_x)), dma((2, parts, rows_x)),
            dma((2, parts, rows_x)), dma((2, parts, rows_x)),
            dma((parts, rows_x)), dma((parts, rows_x)),
            dma((parts, rows_x)), dma((parts, rows_x)),
        ],
        compiler_params=pltpu.CompilerParams(collective_id=0, has_side_effects=True),
    )(xd, gd, inb, ovb, upb)


def group_gather_kernel(groups, chunks, src, out, local, ns, nr, ss, sr):
    dp, f = lax.axis_index("dp"), lax.axis_index("fsdp")
    rows_x = groups // 2
    x, core = lax.div(dp, 2), lax.rem(dp, 2)
    sib = x * 2 + 1 - core
    size = src.shape[0] // chunks
    mine = pltpu.make_async_copy(src, out.at[dp], local)
    mine.start()
    greet([(sib, f)] + [(wrap(x + dx, rows_x) * 2 + core, f) for dx in range(1, rows_x)])

    def part(ref, k):
        return ref.at[pl.ds(k * size, size)]

    def x_send(k, dx):
        to = wrap(x + dx, rows_x) * 2 + core
        return remote(part(src, k), part(out.at[dp], k), ns.at[k, dx], nr.at[k, dx], to, f)

    def x_recv(k, dx):
        came = wrap(x - dx, rows_x) * 2 + core
        ref = part(out.at[came], k)
        return remote(ref, ref, ns.at[k, dx], nr.at[k, dx], came, f)

    def sib_send(k, dx):
        came = wrap(x - dx, rows_x) * 2 + core
        ref = part(out.at[came], k)
        return remote(part(src, k) if dx == 0 else ref, ref, ss.at[k, dx], sr.at[k, dx], sib, f)

    def sib_recv(k, dx):
        came = wrap(x - dx, rows_x) * 2 + 1 - core
        ref = part(out.at[came], k)
        return remote(ref, ref, ss.at[k, dx], sr.at[k, dx], sib, f)

    for k in range(chunks):
        for dx in range(1, rows_x):
            x_send(k, dx).start()
    for k in range(chunks):
        sib_send(k, 0).start()
    for k in range(chunks):
        for dx in range(1, rows_x):
            x_recv(k, dx).wait_recv()
            sib_send(k, dx).start()
    mine.wait()
    for k in range(chunks):
        for dx in range(rows_x):
            sib_recv(k, dx).wait_recv()
            sib_send(k, dx).wait_send()
        for dx in range(1, rows_x):
            x_send(k, dx).wait_send()


def group_gather(groups, src):
    chunks, rows_x = 4, groups // 2
    dma = pltpu.SemaphoreType.DMA
    return pl.pallas_call(
        functools.partial(group_gather_kernel, groups, chunks),
        out_shape=jax.ShapeDtypeStruct((groups,) + src.shape, BF),
        in_specs=[pl.BlockSpec(memory_space=pl.ANY)],
        out_specs=pl.BlockSpec(memory_space=pl.ANY),
        scratch_shapes=[dma(())] + [dma((chunks, rows_x))] * 4,
        compiler_params=pltpu.CompilerParams(collective_id=1, has_side_effects=True),
    )(src)


def group_sum_kernel(groups, chunks, src, out, loc, sibr, xb, xrb, ls, ns, nr, ss, sr):
    dp, f = lax.axis_index("dp"), lax.axis_index("fsdp")
    rows_x = groups // 2
    x, core = lax.div(dp, 2), lax.rem(dp, 2)
    sib = x * 2 + 1 - core
    size = out.shape[0] // chunks
    greet([(sib, f)] + [(wrap(x + dx, rows_x) * 2 + core, f) for dx in range(1, rows_x)])

    def sib_copy(k):
        piece = src.at[:, 1 - core, pl.ds(k * size, size)]
        return remote(piece, sibr.at[k], ss.at[k], sr.at[k], sib, f)

    def own_copy(k):
        return pltpu.make_async_copy(src.at[:, core, pl.ds(k * size, size)], loc.at[k], ls.at[k])

    def x_copy(k, dx):
        to = wrap(x + dx, rows_x) * 2 + core
        return remote(xb.at[k, dx - 1], xrb.at[k, dx - 1], ns.at[k, dx], nr.at[k, dx], to, f)

    for k in range(chunks):
        sib_copy(k).start()
        own_copy(k).start()
    for k in range(chunks):
        sib_copy(k).wait_recv()
        own_copy(k).wait()
        for dx in range(1, rows_x):
            to = wrap(x + dx, rows_x)
            xb[k, dx - 1] = (sibr[k, to].astype(F32) + loc[k, to].astype(F32)).astype(BF)
            x_copy(k, dx).start()
    for k in range(chunks):
        total = sibr[k, x].astype(F32) + loc[k, x].astype(F32)
        for dx in range(1, rows_x):
            x_copy(k, dx).wait_recv()
            total = total + xrb[k, dx - 1].astype(F32)
        out[pl.ds(k * size, size), :] = total
    for k in range(chunks):
        sib_copy(k).wait_send()
        for dx in range(1, rows_x):
            x_copy(k, dx).wait_send()


def group_sum(groups, src):
    chunks, rows_x = 4, groups // 2
    count, width = src.shape[2:]
    size = count // chunks
    dma = pltpu.SemaphoreType.DMA
    return pl.pallas_call(
        functools.partial(group_sum_kernel, groups, chunks),
        out_shape=jax.ShapeDtypeStruct((count, width), F32),
        in_specs=[pl.BlockSpec(memory_space=pl.ANY)],
        out_specs=pl.BlockSpec(memory_space=pltpu.VMEM),
        scratch_shapes=[
            pltpu.VMEM((chunks, rows_x, size, width), BF),
            pltpu.VMEM((chunks, rows_x, size, width), BF),
            pltpu.VMEM((chunks, rows_x - 1, size, width), BF),
            pltpu.VMEM((chunks, rows_x - 1, size, width), BF),
            dma((chunks,)),
            dma((chunks, rows_x)), dma((chunks, rows_x)),
            dma((chunks,)), dma((chunks,)),
        ],
        compiler_params=pltpu.CompilerParams(
            collective_id=2, has_side_effects=True, vmem_limit_bytes=48 * 2**20
        ),
    )(src)


def ffn_grad_kernel(
    parts, groups, act, dhid, nrm, grd, down, up, acc, got, gone, rs, rr
):
    dp, f = lax.axis_index("dp"), lax.axis_index("fsdp")
    p = ring_place(f, parts)
    nxt, prv = ring_index(p + 1, parts), ring_index(p - 1, parts)
    block, width = down.shape
    half = width // 2
    greet([(dp, nxt), (dp, prv)])
    pairs = ((act, grd, down), (dhid, nrm, up))

    def copy(h, m, s):
        return remote(
            gone.at[h, m, lax.rem(s, 2)], got.at[h, m, s], rs.at[h, m, s], rr.at[h, m, s],
            dp, nxt if h == 0 else prv,
        )

    def step(s):
        for m in range(2):
            left, right, out = pairs[m]
            for h in range(2):
                c = ring_index(p - 1 - s if h == 0 else p + 1 + s, parts)
                if len(left.shape) == 2:
                    piece = left[:, pl.ds(pl.multiple_of(c * block, block), block)]
                else:
                    piece = left[c]
                acc[...] = lax.dot_general(
                    piece, right[:, h * half : (h + 1) * half],
                    (((0,), (0,)), ((), ())), preferred_element_type=F32,
                )

                @pl.when(s > 0)
                def _():
                    copy(h, m, s - 1).wait_recv()
                    acc[...] += got[h, m, s - 1].astype(F32)

                @pl.when((s >= 2) & (s < parts - 1))
                def _():
                    copy(h, m, s - 2).wait_send()

                @pl.when(s < parts - 1)
                def _():
                    gone[h, m, lax.rem(s, 2)] = acc[...].astype(BF)
                    copy(h, m, s).start()

                @pl.when(s == parts - 1)
                def _():
                    out[:, h * half : (h + 1) * half] = acc[...]

    loop(0, parts, step)
    for m in range(2):
        for h in range(2):
            for s in range(max(parts - 3, 0), parts - 1):
                copy(h, m, s).wait_send()


def ffn_grad(parts, groups, act, dhid, nrm, grd):
    width = nrm.shape[1]
    block = FF // (groups * parts)
    if block % 128:
        act = act.reshape(act.shape[0], parts, block).transpose(1, 0, 2)
        dhid = dhid.reshape(dhid.shape[0], parts, block).transpose(1, 0, 2)
    dma = pltpu.SemaphoreType.DMA
    vmem = pl.BlockSpec(memory_space=pltpu.VMEM)
    return pl.pallas_call(
        functools.partial(ffn_grad_kernel, parts, groups),
        out_shape=(jax.ShapeDtypeStruct((block, width), F32),) * 2,
        in_specs=[vmem] * 4,
        out_specs=(vmem,) * 2,
        scratch_shapes=[
            pltpu.VMEM((block, width // 2), F32),
            pltpu.VMEM((2, 2, parts - 1, block, width // 2), BF),
            pltpu.VMEM((2, 2, 2, block, width // 2), BF),
            dma((2, 2, parts)), dma((2, 2, parts)),
        ],
        compiler_params=pltpu.CompilerParams(
            collective_id=3, has_side_effects=True, vmem_limit_bytes=60 * 2**20
        ),
    )(act, dhid, nrm, grd)


def finish_kernel(
    parts, groups,
    grads, res, gx, upg, vec,
    total, res_out, gx_out, upg_out, vec_out,
    loc, sibr, xb, xrb, got, gone,
    local, ls, ss, sr, ns, nr, rs, rr, as_, ar, bs, br, us, ur, vs, vr,
):
    dp, f = lax.axis_index("dp"), lax.axis_index("fsdp")
    owners, rows_x = groups * parts, groups // 2
    x, core = lax.div(dp, 2), lax.rem(dp, 2)
    sib = x * 2 + 1 - core
    me = dp * parts + f
    p = ring_place(f, parts)
    nxt, prv = ring_index(p + 1, parts), ring_index(p - 1, parts)
    half = grads.shape[4] // 2
    mine = [
        pltpu.make_async_copy(res.at[f], res_out.at[f], local.at[0]),
        pltpu.make_async_copy(gx.at[f], gx_out.at[f], local.at[1]),
        pltpu.make_async_copy(upg.at[me], upg_out.at[me], local.at[2]),
        pltpu.make_async_copy(vec.at[me], vec_out.at[me], local.at[3]),
    ]
    for copy in mine:
        copy.start()
    greet_all(me, parts, owners)

    def chunk(h, s):
        return ring_index(p - 1 - s if h == 0 else p + 1 + s, parts)

    def sib_copy(h, s):
        piece = grads.at[:, 1 - core, chunk(h, s), :, pl.ds(h * half, half)]
        return remote(piece, sibr.at[h, s], ss.at[h, s], sr.at[h, s], sib, f)

    def own_copy(h, s):
        piece = grads.at[:, core, chunk(h, s), :, pl.ds(h * half, half)]
        return pltpu.make_async_copy(piece, loc.at[h, s], ls.at[h, s])

    def x_copy(h, s, dx):
        to = wrap(x + dx, rows_x) * 2 + core
        return remote(
            xb.at[h, s, dx - 1], xrb.at[h, s, dx - 1], ns.at[h, s, dx], nr.at[h, s, dx], to, f
        )

    def ring_copy(h, s):
        return remote(
            gone.at[h, s], got.at[h, s], rs.at[h, s], rr.at[h, s], dp, nxt if h == 0 else prv
        )

    def res_copies(d, came=False):
        return deal_copy(parts, dp, f, res, res_out, as_, ar, d, came)

    def gx_copies(d, came=False):
        return deal_copy(parts, dp, f, gx, gx_out, bs, br, d, came)

    def upg_copies(d, came=False):
        return owner_copy(me, parts, owners, upg, upg_out, us, ur, d, came)

    def vec_copies(d, came=False):
        return owner_copy(me, parts, owners, vec, vec_out, vs, vr, d, came)

    def begin(s):
        for h in range(2):
            sib_copy(h, s).start()
            own_copy(h, s).start()

    loop(0, parts, begin)

    def others(d):
        upg_copies(d).start()
        vec_copies(d).start()

    def returns(d):
        res_copies(d).start()
        gx_copies(d).start()

    loop(1, parts, returns)
    loop(1, owners, others)

    def pair(s):
        for h in range(2):
            sib_copy(h, s).wait_recv()
            own_copy(h, s).wait()
            for dx in range(1, rows_x):
                to = wrap(x + dx, rows_x)
                xb[h, s, dx - 1] = (sibr[h, s, to].astype(F32) + loc[h, s, to].astype(F32)).astype(BF)
                x_copy(h, s, dx).start()

    loop(0, parts, pair)

    def step(s):
        for h in range(2):
            for dx in range(1, rows_x):
                x_copy(h, s, dx).wait_recv()

            def value():
                here = sibr[h, s, x].astype(F32) + loc[h, s, x].astype(F32)
                for dx in range(1, rows_x):
                    here = here + xrb[h, s, dx - 1].astype(F32)
                return here

            @pl.when(s == 0)
            def _():
                gone[h, s] = value().astype(BF)
                ring_copy(h, s).start()

            @pl.when((s > 0) & (s < parts - 1))
            def _():
                ring_copy(h, s - 1).wait_recv()
                gone[h, s] = (value() + got[h, s - 1].astype(F32)).astype(BF)
                ring_copy(h, s).start()

            @pl.when(s == parts - 1)
            def _():
                ring_copy(h, s - 1).wait_recv()
                total[:, h * half : (h + 1) * half] = value() + got[h, s - 1].astype(F32)

    loop(0, parts, step)

    def finish(s):
        for h in range(2):
            sib_copy(h, s).wait_send()
            for dx in range(1, rows_x):
                x_copy(h, s, dx).wait_send()

            @pl.when(s < parts - 1)
            def _():
                ring_copy(h, s).wait_send()

        @pl.when(s > 0)
        def _():
            for copies in (res_copies, gx_copies):
                copies(s, True).wait_recv()
                copies(s).wait_send()

    loop(0, parts, finish)

    def owner_finish(d):
        for copies in (upg_copies, vec_copies):
            copies(d, True).wait_recv()
            copies(d).wait_send()

    loop(1, owners, owner_finish)
    for copy in mine:
        copy.wait()


def finish_sums(parts, groups, grads, res, gx, upg, vec):
    owners, rows_x = groups * parts, groups // 2
    rows, width = grads.shape[3:]
    half = width // 2
    dma = pltpu.SemaphoreType.DMA
    hbm = pl.BlockSpec(memory_space=pl.ANY)
    return pl.pallas_call(
        functools.partial(finish_kernel, parts, groups),
        out_shape=(
            jax.ShapeDtypeStruct((rows, width), F32),
            jax.ShapeDtypeStruct(res.shape, BF),
            jax.ShapeDtypeStruct(gx.shape, BF),
            jax.ShapeDtypeStruct(upg.shape, BF),
            jax.ShapeDtypeStruct(vec.shape, F32),
        ),
        in_specs=[hbm] * 5,
        out_specs=(pl.BlockSpec(memory_space=pltpu.VMEM),) + (hbm,) * 4,
        scratch_shapes=[
            pltpu.VMEM((2, parts, rows_x, rows, half), BF),
            pltpu.VMEM((2, parts, rows_x, rows, half), BF),
            pltpu.VMEM((2, parts, rows_x - 1, rows, half), BF),
            pltpu.VMEM((2, parts, rows_x - 1, rows, half), BF),
            pltpu.VMEM((2, parts, rows, half), BF),
            pltpu.VMEM((2, parts, rows, half), BF),
            dma((4,)),
            dma((2, parts)), dma((2, parts)), dma((2, parts)),
            dma((2, parts, rows_x)), dma((2, parts, rows_x)),
            dma((2, parts)), dma((2, parts)),
            dma((parts,)), dma((parts,)), dma((parts,)), dma((parts,)),
            dma((owners,)), dma((owners,)), dma((owners,)), dma((owners,)),
        ],
        compiler_params=pltpu.CompilerParams(
            collective_id=4, has_side_effects=True, vmem_limit_bytes=60 * 2**20
        ),
    )(grads, res, gx, upg, vec)


def shards(
    tokens,
    cotangent,
    lengths,
    routing,
    in_weight,
    in_first,
    in_second,
    out_weight,
    out_first,
    out_second,
    up_weight,
    up_first,
    up_second,
    down_weight,
    down_first,
    down_second,
    vectors,
    vector_first,
    vector_second,
):
    bf = jnp.bfloat16
    heads = D // HD
    count = tokens.shape[0]
    parts = lax.axis_size("fsdp")
    groups = lax.axis_size("dp")
    both = ("dp", "fsdp")
    piece = count // parts
    width_in = D + 2 * HD
    slots = jnp.arange(parts, dtype=jnp.int32)
    order = routing[0]
    inverse = jnp.sum(jnp.where(order[:, None] == slots[None, :], slots[:, None], 0), axis=0)

    def deal(array):
        return jnp.take(array.reshape(parts, piece, D), inverse, axis=0)

    def undeal(array):
        return jnp.take(array, order, axis=0).reshape(count, D)

    rows = in_weight.shape[0]
    owners = groups * parts
    out_vec = jnp.concatenate(
        [out_weight.astype(bf), jnp.pad(vectors.astype(bf), ((0, 0), (0, 128 - NVEC)))], axis=1
    )
    up_pieces = up_weight.astype(bf).reshape(rows, owners, FF // owners).transpose(1, 0, 2)
    x_dealt, grad_dealt, whole_in, whole_out, up_block = spread(
        parts,
        groups,
        deal(tokens),
        deal(cotangent),
        in_weight.astype(bf),
        out_vec,
        up_pieces,
    )
    inputs_here = x_dealt.reshape(count, D)
    grad_all = grad_dealt.reshape(groups * count, D)
    grad_here = lax.dynamic_index_in_dim(
        grad_dealt, lax.axis_index("dp"), 0, keepdims=False
    ).reshape(count, D)
    whole_in = whole_in.reshape(D, width_in)
    whole_out = whole_out.reshape(D, D + 128)
    part_up = lax.all_gather(up_block.reshape(D, FF // owners).T, "fsdp", axis=0, tiled=True)
    part_down = lax.all_gather(down_weight.astype(bf), "fsdp", axis=0, tiled=True)

    table = whole_out[:, D : D + NVEC].astype(jnp.float32)
    whole_out = whole_out[:, :D]
    gain_one = table[:, 0]
    shift_one = table[:, 1]
    query_bias = table[:, 2]
    branch_bias = table[:, 3]
    gain_two = table[:, 4]
    shift_two = table[:, 5]
    output_bias = table[:, 6]
    hidden_bias = table[:, 7:].T.reshape(FF)
    ff_here = FF // groups
    ff_start = lax.axis_index("dp") * ff_here
    hidden_bias_here = lax.dynamic_slice(hidden_bias, (ff_start,), (ff_here,))
    allowed = segment_mask(lengths[0], count)
    scale = 1.0 / math.sqrt(HD)
    inputs = inputs_here.astype(jnp.float32)
    norm_one_b = layer_norm(inputs, gain_one, shift_one).astype(bf)
    mixed = jnp.dot(norm_one_b, whole_in, preferred_element_type=jnp.float32)
    query_b = (mixed[:, :D] + query_bias).astype(bf)
    keys_b = mixed[:, D : D + HD].astype(bf)
    values_b = mixed[:, D + HD :].astype(bf)
    query_heads = query_b.reshape(count, heads, HD)

    def score_table():
        raw = (
            jnp.einsum("thd,sd->hts", query_heads, keys_b, preferred_element_type=jnp.float32)
            * scale
        )
        return jnp.where(allowed[None], raw, -1e30)

    scores = score_table()
    top = jnp.max(scores, axis=-1, keepdims=True)
    expo = jnp.exp(scores - top)
    total = jnp.sum(expo, axis=-1, keepdims=True)
    logsum = top + jnp.log(total)
    probs_b = (expo / total).astype(bf)
    attended_b = (
        jnp.einsum("hts,sd->thd", probs_b, values_b, preferred_element_type=jnp.float32)
        .reshape(count, D)
        .astype(bf)
    )
    middle = inputs + (
        jnp.dot(attended_b, whole_out, preferred_element_type=jnp.float32) + branch_bias
    )
    norm_two_b = layer_norm(middle, gain_two, shift_two).astype(bf)

    norm_all = group_gather(groups, norm_two_b).reshape(groups * count, D)
    hidden = contract_cols(norm_all, part_up) + hidden_bias_here
    grad_active = contract_cols(grad_all, part_down)
    gelu_value, gelu_pull = jax.vjp(gelu_tanh, hidden)
    active_b = gelu_value.astype(bf)
    grad_hidden_f = gelu_pull(grad_active)[0]
    grad_hidden_b = grad_hidden_f.astype(bf)
    grad_norm_two = group_sum(
        groups,
        jnp.dot(grad_hidden_b, part_up, preferred_element_type=jnp.float32)
        .astype(bf)
        .reshape(groups // 2, 2, count, D),
    )
    down_grad, up_grad_block = ffn_grad(
        parts, groups, active_b, grad_hidden_b, norm_all, grad_all
    )
    branch_two = lax.psum_scatter(
        jnp.dot(active_b, part_down, preferred_element_type=jnp.float32).astype(bf),
        "dp",
        scatter_dimension=0,
        tiled=True,
    ).astype(jnp.float32)
    result = middle + (branch_two + output_bias)

    grad_y = grad_here.astype(jnp.float32)
    norm_value_two, pull_two = jax.vjp(layer_norm, middle, gain_two, shift_two)
    grad_middle_norm, grad_gain_two, grad_shift_two = pull_two(grad_norm_two)
    grad_middle = grad_y + grad_middle_norm
    grad_branch_b = grad_middle.astype(bf)
    grad_attended_b = contract_cols(grad_branch_b, whole_out).astype(bf)
    grad_heads = grad_attended_b.reshape(count, heads, HD)
    probs = jnp.exp(score_table() - logsum)
    probs_again_b = probs.astype(bf)
    grad_probs = jnp.einsum("thd,sd->hts", grad_heads, values_b, preferred_element_type=jnp.float32)
    grad_values_b = jnp.einsum(
        "hts,thd->sd", probs_again_b, grad_heads, preferred_element_type=jnp.float32
    ).astype(bf)
    weighted = jnp.sum(probs * grad_probs, axis=-1, keepdims=True)
    grad_scores_b = (probs * (grad_probs - weighted)).astype(bf)
    grad_query_b = (
        (
            jnp.einsum("hts,sd->thd", grad_scores_b, keys_b, preferred_element_type=jnp.float32)
            * scale
        )
        .reshape(count, D)
        .astype(bf)
    )
    grad_keys_b = (
        jnp.einsum("hts,thd->sd", grad_scores_b, query_heads, preferred_element_type=jnp.float32)
        * scale
    ).astype(bf)
    grad_mixed_b = jnp.concatenate([grad_query_b, grad_keys_b, grad_values_b], axis=1)
    grad_norm_one = contract_cols(grad_mixed_b, whole_in)
    norm_value_one, pull_one = jax.vjp(layer_norm, inputs, gain_one, shift_one)
    grad_inputs_norm, grad_gain_one, grad_shift_one = pull_one(grad_norm_one)
    grad_inputs = grad_middle + grad_inputs_norm
    hidden_sums = jnp.sum(grad_hidden_b.astype(jnp.float32), axis=0)
    hidden_whole = lax.dynamic_update_slice(
        jnp.zeros((FF,), jnp.float32), hidden_sums, (ff_start,)
    )
    vector_grad = jnp.concatenate(
        [
            jnp.stack(
                [
                    grad_gain_one,
                    grad_shift_one,
                    jnp.sum(grad_query_b.astype(jnp.float32), axis=0),
                    jnp.sum(grad_branch_b.astype(jnp.float32), axis=0),
                    grad_gain_two,
                    grad_shift_two,
                    jnp.sum(grad_y, axis=0),
                ],
                axis=0,
            ),
            hidden_whole.reshape(FF // D, D),
        ],
        axis=0,
    )
    vector_grad = vector_grad.reshape(NVEC, owners, rows).transpose(1, 0, 2)
    vector_grad = jnp.pad(vector_grad, ((0, 0), (0, 16 - NVEC), (0, 128 - rows)))
    small_part = jnp.concatenate(
        [
            contract_rows(norm_one_b, grad_mixed_b).astype(bf),
            contract_rows(attended_b, grad_branch_b).astype(bf),
        ],
        axis=1,
    )
    small_grad, back_result, back_grad, grad_up, vector_sum = finish_sums(
        parts,
        groups,
        small_part.reshape(groups // 2, 2, parts, rows, width_in + D),
        result.astype(bf).reshape(parts, piece, D),
        grad_inputs.astype(bf).reshape(parts, piece, D),
        up_grad_block.T.astype(bf).reshape(owners, rows, FF // owners),
        vector_grad,
    )
    grad_up = grad_up.transpose(1, 0, 2).reshape(rows, FF)
    vector_sum = jnp.sum(vector_sum, axis=0)
    grad_in = small_grad[:, :width_in]
    grad_out = small_grad[:, width_in : width_in + D]
    grad_vec = vector_sum[:NVEC, :rows].T
    in_new = adam_update(in_weight, in_first, in_second, grad_in, 1.0 / math.sqrt(D), decay_rate)
    out_new = adam_update(
        out_weight, out_first, out_second, grad_out, 1.0 / math.sqrt(D * 8 // TOK_DEV), decay_rate
    )
    up_new = adam_update(up_weight, up_first, up_second, grad_up, 1.0 / math.sqrt(D), decay_rate)
    down_new = adam_update(
        down_weight, down_first, down_second, down_grad, 1.0 / math.sqrt(FF), decay_rate
    )
    vec_new = adam_update(vectors, vector_first, vector_second, grad_vec, 0.1, 0.0)
    return (undeal(back_result), undeal(back_grad)) + in_new + out_new + up_new + down_new + vec_new


def solution(mesh):
    spec = P(("dp", "fsdp"), None)
    return jax.shard_map(
        shards,
        mesh=mesh,
        in_specs=(spec,) * 19,
        out_specs=(spec,) * 17,
        check_vma=False,
    )
```

```python
import functools
import math

import jax
import jax.numpy as jnp
from jax import lax
from jax.experimental import pallas as pl
from jax.experimental.pallas import tpu as pltpu
from jax.sharding import PartitionSpec as P

D = 2048
FF = 8192
HD = 128
TOK_DEV = 384
STEP = 5
NVEC = 11


eps_norm = 1e-05
beta_one = 0.5
beta_two = 0.5
adam_eps = 1e-08
decay_rate = 0.1


def layer_norm(values, gain, shift):
    centered = values - jnp.mean(values, axis=-1, keepdims=True)
    scaled = centered * lax.rsqrt(jnp.mean(centered * centered, axis=-1, keepdims=True) + eps_norm)
    return scaled * gain + shift


def gelu_tanh(values):
    return (
        0.5
        * values
        * (1.0 + jnp.tanh(0.7978845608028654 * (values + 0.044715 * values * values * values)))
    )


def segment_mask(sizes, count):
    ends = jnp.cumsum(sizes)
    places = jnp.arange(count, dtype=jnp.int32)
    labels = jnp.sum((places[:, None] >= ends[None, :]).astype(jnp.int32), axis=1)
    return (labels[:, None] == labels[None, :]) & (places[None, :] <= places[:, None])


def adam_update(weight, first, second, grad, rate, decay):
    grad = grad.astype(jnp.float32)
    first_new = beta_one * first + (1.0 - beta_one) * grad
    second_new = beta_two * second + (1.0 - beta_two) * grad * grad
    fix_one = 1.0 - beta_one**STEP
    fix_two = 1.0 - beta_two**STEP
    step_size = first_new / fix_one / (jnp.sqrt(second_new / fix_two) + adam_eps)
    weight_new = weight - rate * (step_size + decay * weight)
    return (weight_new, first_new, second_new)


def contract_rows(left, right):
    return lax.dot_general(
        left, right, (((0,), (0,)), ((), ())), preferred_element_type=jnp.float32
    )


def contract_cols(left, right):
    return lax.dot_general(
        left, right, (((1,), (1,)), ((), ())), preferred_element_type=jnp.float32
    )


MESH = pl.DeviceIdType.MESH
F32 = jnp.float32
BF = jnp.bfloat16


def wrap(value, count):
    return lax.rem(value + 2 * count, count)


def ring_place(index, parts):
    if parts != 8:
        return index
    z, y = lax.div(index, 2), lax.rem(index, 2)
    return z + y * (7 - 2 * z)


def ring_index(place, parts):
    place = wrap(place, parts)
    if parts != 8:
        return place
    back = lax.div(place, 4)
    return (1 - back) * 2 * place + back * (15 - 2 * place)


def remote(src, dst, send, recv, dp, fs):
    return pltpu.make_async_remote_copy(
        src_ref=src, dst_ref=dst, send_sem=send, recv_sem=recv, device_id=(dp, fs), device_id_type=MESH
    )


def lasting(micros):
    return pl.CostEstimate(
        flops=int(micros * 1.1e9), bytes_accessed=int(micros * 3.3e6), transcendentals=0
    )


def greet(targets):
    barrier = pltpu.get_barrier_semaphore()
    for dp, fs in targets:
        pl.semaphore_signal(barrier, inc=1, device_id=(dp, fs), device_id_type=MESH)
    pl.semaphore_wait(barrier, len(targets))


def greet_all(me, parts, owners):
    barrier = pltpu.get_barrier_semaphore()

    def one(i, carry):
        peer = wrap(me + i, owners)
        pl.semaphore_signal(
            barrier, inc=1, device_id=(lax.div(peer, parts), lax.rem(peer, parts)), device_id_type=MESH
        )
        return carry

    lax.fori_loop(1, owners, one, 0)
    pl.semaphore_wait(barrier, owners - 1)


def loop(low, high, body):
    def one(i, carry):
        body(i)
        return carry

    lax.fori_loop(low, high, one, 0)


def deal_copy(parts, dp, f, src, dst, send, recv, d, came=False):
    to = wrap(f + d, parts)
    place = wrap(f - d, parts) if came else f
    return remote(src.at[to], dst.at[place], send.at[d], recv.at[d], dp, to)


def owner_copy(me, parts, owners, src, dst, send, recv, d, came=False):
    to = wrap(me + d, owners)
    place = wrap(me - d, owners) if came else me
    return remote(
        src.at[to], dst.at[place], send.at[d], recv.at[d], lax.div(to, parts), lax.rem(to, parts)
    )


def spread_kernel(
    parts, groups,
    xd, gd, inb, ovb, upb,
    xo, eall, win, wov, upo,
    local, xs, xr, gs, gr, us, ur, rs, rr, ns, nr, ss, sr, ens, enr, ess, esr,
):
    dp, f = lax.axis_index("dp"), lax.axis_index("fsdp")
    owners, rows_x = groups * parts, groups // 2
    x, core = lax.div(dp, 2), lax.rem(dp, 2)
    sib = x * 2 + 1 - core
    me = dp * parts + f
    p = ring_place(f, parts)
    nxt, prv = ring_index(p + 1, parts), ring_index(p - 1, parts)
    whole = (win, wov)
    mine = [
        pltpu.make_async_copy(inb, win.at[me], local.at[0]),
        pltpu.make_async_copy(ovb, wov.at[me], local.at[1]),
        pltpu.make_async_copy(xd.at[f], xo.at[f], local.at[2]),
        pltpu.make_async_copy(gd.at[f], eall.at[dp, f], local.at[3]),
        pltpu.make_async_copy(upb.at[me], upo.at[me], local.at[4]),
    ]
    for copy in mine:
        copy.start()
    greet_all(me, parts, owners)
    for copy in mine:
        copy.wait()

    def x_copies(d, came=False):
        return deal_copy(parts, dp, f, xd, xo, xs, xr, d, came)

    def g_copies(d, came=False):
        return deal_copy(parts, dp, f, gd, eall.at[dp], gs, gr, d, came)

    def u_copies(d, came=False):
        return owner_copy(me, parts, owners, upb, upo, us, ur, d, came)

    def origin(h, s):
        return ring_index(p - s if h == 0 else p + s, parts)

    def ring_send(h, s):
        ref = whole[h].at[dp * parts + origin(h, s)]
        return remote(ref, ref, rs.at[h, s], rr.at[h, s], dp, nxt if h == 0 else prv)

    def ring_recv(h, s):
        ref = whole[h].at[dp * parts + origin(h, s)]
        return remote(ref, ref, rs.at[h, s - 1], rr.at[h, s - 1], dp, nxt if h == 0 else prv)

    def x_send(h, s, dx):
        ref = whole[h].at[dp * parts + origin(h, s)]
        to = wrap(x + dx, rows_x) * 2 + core
        return remote(ref, ref, ns.at[h, s, dx], nr.at[h, s, dx], to, f)

    def x_recv(h, s, dx):
        came = wrap(x - dx, rows_x) * 2 + core
        ref = whole[h].at[came * parts + origin(h, s)]
        return remote(ref, ref, ns.at[h, s, dx], nr.at[h, s, dx], came, f)

    def sib_send(h, s, dx):
        came = wrap(x - dx, rows_x) * 2 + core
        ref = whole[h].at[came * parts + origin(h, s)]
        return remote(ref, ref, ss.at[h, s, dx], sr.at[h, s, dx], sib, f)

    def sib_recv(h, s, dx):
        came = wrap(x - dx, rows_x) * 2 + 1 - core
        ref = whole[h].at[came * parts + origin(h, s)]
        return remote(ref, ref, ss.at[h, s, dx], sr.at[h, s, dx], sib, f)

    def e_x_send(d, dx):
        ref = eall.at[dp, wrap(f - d, parts)]
        to = wrap(x + dx, rows_x) * 2 + core
        return remote(ref, ref, ens.at[d, dx], enr.at[d, dx], to, f)

    def e_x_recv(d, dx):
        came = wrap(x - dx, rows_x) * 2 + core
        ref = eall.at[came, wrap(f - d, parts)]
        return remote(ref, ref, ens.at[d, dx], enr.at[d, dx], came, f)

    def e_sib_send(d, dx):
        came = wrap(x - dx, rows_x) * 2 + core
        ref = eall.at[came, wrap(f - d, parts)]
        return remote(ref, ref, ess.at[d, dx], esr.at[d, dx], sib, f)

    def e_sib_recv(d, dx):
        came = wrap(x - dx, rows_x) * 2 + 1 - core
        ref = eall.at[came, wrap(f - d, parts)]
        return remote(ref, ref, ess.at[d, dx], esr.at[d, dx], sib, f)

    def ring_step(s):
        for h in range(2):
            @pl.when(s > 0)
            def _():
                ring_recv(h, s).wait_recv()

            @pl.when(s < parts - 1)
            def _():
                ring_send(h, s).start()

            for dx in range(1, rows_x):
                x_send(h, s, dx).start()
            sib_send(h, s, 0).start()

    def e_step(d):
        @pl.when(d > 0)
        def _():
            g_copies(d, True).wait_recv()

        for dx in range(1, rows_x):
            e_x_send(d, dx).start()
        e_sib_send(d, 0).start()

    def relay(s):
        for h in range(2):
            for dx in range(1, rows_x):
                x_recv(h, s, dx).wait_recv()
                sib_send(h, s, dx).start()

    def e_relay(d):
        for dx in range(1, rows_x):
            e_x_recv(d, dx).wait_recv()
            e_sib_send(d, dx).start()

    each = -(-(owners - 1) // parts)

    def main(s):
        @pl.when(s < parts)
        def _():
            ring_step(s)

        @pl.when(s < parts - 1)
        def _():
            x_copies(s + 1).start()
            g_copies(s + 1).start()

        for j in range(each):
            d = s * each + 1 + j

            @pl.when(d < owners)
            def _():
                u_copies(d).start()

        @pl.when((s >= 1) & (s <= parts))
        def _():
            e_step(s - 1)

        @pl.when((s >= 2) & (s < parts + 2))
        def _():
            relay(s - 2)

        @pl.when(s >= 3)
        def _():
            e_relay(s - 3)

    loop(0, parts + 3, main)

    def finish(s):
        for h in range(2):
            @pl.when(s < parts - 1)
            def _():
                ring_send(h, s).wait_send()

            for dx in range(1, rows_x):
                x_send(h, s, dx).wait_send()
            for dx in range(rows_x):
                sib_recv(h, s, dx).wait_recv()
                sib_send(h, s, dx).wait_send()
        for dx in range(1, rows_x):
            e_x_send(s, dx).wait_send()
        for dx in range(rows_x):
            e_sib_recv(s, dx).wait_recv()
            e_sib_send(s, dx).wait_send()

        @pl.when(s > 0)
        def _():
            x_copies(s, True).wait_recv()
            x_copies(s).wait_send()
            g_copies(s).wait_send()

    loop(0, parts, finish)

    def u_finish(d):
        u_copies(d, True).wait_recv()
        u_copies(d).wait_send()

    loop(1, owners, u_finish)


def spread(parts, groups, xd, gd, inb, ovb, upb):
    owners, rows_x = groups * parts, groups // 2
    dma = pltpu.SemaphoreType.DMA
    return pl.pallas_call(
        functools.partial(spread_kernel, parts, groups),
        out_shape=(
            jax.ShapeDtypeStruct(xd.shape, BF),
            jax.ShapeDtypeStruct((groups,) + gd.shape, BF),
            jax.ShapeDtypeStruct((owners,) + inb.shape, BF),
            jax.ShapeDtypeStruct((owners,) + ovb.shape, BF),
            jax.ShapeDtypeStruct(upb.shape, BF),
        ),
        in_specs=[pl.BlockSpec(memory_space=pl.ANY)] * 5,
        out_specs=(pl.BlockSpec(memory_space=pl.ANY),) * 5,
        scratch_shapes=[
            dma((5,)),
            dma((parts,)), dma((parts,)), dma((parts,)), dma((parts,)),
            dma((owners,)), dma((owners,)),
            dma((2, parts)), dma((2, parts)),
            dma((2, parts, rows_x)), dma((2, parts, rows_x)),
            dma((2, parts, rows_x)), dma((2, parts, rows_x)),
            dma((parts, rows_x)), dma((parts, rows_x)),
            dma((parts, rows_x)), dma((parts, rows_x)),
        ],
        compiler_params=pltpu.CompilerParams(collective_id=0, has_side_effects=True),
        cost_estimate=lasting(200),
    )(xd, gd, inb, ovb, upb)


def group_gather_kernel(groups, chunks, src, out, local, ns, nr, ss, sr):
    dp, f = lax.axis_index("dp"), lax.axis_index("fsdp")
    rows_x = groups // 2
    x, core = lax.div(dp, 2), lax.rem(dp, 2)
    sib = x * 2 + 1 - core
    size = src.shape[0] // chunks
    mine = pltpu.make_async_copy(src, out.at[dp], local)
    mine.start()
    greet([(sib, f)] + [(wrap(x + dx, rows_x) * 2 + core, f) for dx in range(1, rows_x)])

    def part(ref, k):
        return ref.at[pl.ds(k * size, size)]

    def x_send(k, dx):
        to = wrap(x + dx, rows_x) * 2 + core
        return remote(part(src, k), part(out.at[dp], k), ns.at[k, dx], nr.at[k, dx], to, f)

    def x_recv(k, dx):
        came = wrap(x - dx, rows_x) * 2 + core
        ref = part(out.at[came], k)
        return remote(ref, ref, ns.at[k, dx], nr.at[k, dx], came, f)

    def sib_send(k, dx):
        came = wrap(x - dx, rows_x) * 2 + core
        ref = part(out.at[came], k)
        return remote(part(src, k) if dx == 0 else ref, ref, ss.at[k, dx], sr.at[k, dx], sib, f)

    def sib_recv(k, dx):
        came = wrap(x - dx, rows_x) * 2 + 1 - core
        ref = part(out.at[came], k)
        return remote(ref, ref, ss.at[k, dx], sr.at[k, dx], sib, f)

    for k in range(chunks):
        for dx in range(1, rows_x):
            x_send(k, dx).start()
    for k in range(chunks):
        sib_send(k, 0).start()
    for k in range(chunks):
        for dx in range(1, rows_x):
            x_recv(k, dx).wait_recv()
            sib_send(k, dx).start()
    mine.wait()
    for k in range(chunks):
        for dx in range(rows_x):
            sib_recv(k, dx).wait_recv()
            sib_send(k, dx).wait_send()
        for dx in range(1, rows_x):
            x_send(k, dx).wait_send()


def group_gather(groups, src):
    chunks, rows_x = 4, groups // 2
    dma = pltpu.SemaphoreType.DMA
    return pl.pallas_call(
        functools.partial(group_gather_kernel, groups, chunks),
        out_shape=jax.ShapeDtypeStruct((groups,) + src.shape, BF),
        in_specs=[pl.BlockSpec(memory_space=pl.ANY)],
        out_specs=pl.BlockSpec(memory_space=pl.ANY),
        scratch_shapes=[dma(())] + [dma((chunks, rows_x))] * 4,
        compiler_params=pltpu.CompilerParams(collective_id=1, has_side_effects=True),
        cost_estimate=lasting(45),
    )(src)


def group_sum_kernel(groups, chunks, src, out, loc, sibr, xb, xrb, ls, ns, nr, ss, sr):
    dp, f = lax.axis_index("dp"), lax.axis_index("fsdp")
    rows_x = groups // 2
    x, core = lax.div(dp, 2), lax.rem(dp, 2)
    sib = x * 2 + 1 - core
    size = out.shape[0] // chunks
    greet([(sib, f)] + [(wrap(x + dx, rows_x) * 2 + core, f) for dx in range(1, rows_x)])

    def sib_copy(k):
        piece = src.at[:, 1 - core, pl.ds(k * size, size)]
        return remote(piece, sibr.at[k], ss.at[k], sr.at[k], sib, f)

    def own_copy(k):
        return pltpu.make_async_copy(src.at[:, core, pl.ds(k * size, size)], loc.at[k], ls.at[k])

    def x_copy(k, dx):
        to = wrap(x + dx, rows_x) * 2 + core
        return remote(xb.at[k, dx - 1], xrb.at[k, dx - 1], ns.at[k, dx], nr.at[k, dx], to, f)

    for k in range(chunks):
        sib_copy(k).start()
        own_copy(k).start()
    for k in range(chunks):
        sib_copy(k).wait_recv()
        own_copy(k).wait()
        for dx in range(1, rows_x):
            to = wrap(x + dx, rows_x)
            xb[k, dx - 1] = (sibr[k, to].astype(F32) + loc[k, to].astype(F32)).astype(BF)
            x_copy(k, dx).start()
    for k in range(chunks):
        total = sibr[k, x].astype(F32) + loc[k, x].astype(F32)
        for dx in range(1, rows_x):
            x_copy(k, dx).wait_recv()
            total = total + xrb[k, dx - 1].astype(F32)
        out[pl.ds(k * size, size), :] = total
    for k in range(chunks):
        sib_copy(k).wait_send()
        for dx in range(1, rows_x):
            x_copy(k, dx).wait_send()


def group_sum(groups, src):
    chunks, rows_x = 4, groups // 2
    count, width = src.shape[2:]
    size = count // chunks
    dma = pltpu.SemaphoreType.DMA
    return pl.pallas_call(
        functools.partial(group_sum_kernel, groups, chunks),
        out_shape=jax.ShapeDtypeStruct((count, width), F32),
        in_specs=[pl.BlockSpec(memory_space=pl.ANY)],
        out_specs=pl.BlockSpec(memory_space=pltpu.VMEM),
        scratch_shapes=[
            pltpu.VMEM((chunks, rows_x, size, width), BF),
            pltpu.VMEM((chunks, rows_x, size, width), BF),
            pltpu.VMEM((chunks, rows_x - 1, size, width), BF),
            pltpu.VMEM((chunks, rows_x - 1, size, width), BF),
            dma((chunks,)),
            dma((chunks, rows_x)), dma((chunks, rows_x)),
            dma((chunks,)), dma((chunks,)),
        ],
        compiler_params=pltpu.CompilerParams(
            collective_id=2, has_side_effects=True, vmem_limit_bytes=48 * 2**20
        ),
        cost_estimate=lasting(40),
    )(src)


def row_sum_kernel(parts, groups, left, right, out, acc, got, gone, rs, rr):
    dp, f = lax.axis_index("dp"), lax.axis_index("fsdp")
    p = ring_place(f, parts)
    nxt, prv = ring_index(p + 1, parts), ring_index(p - 1, parts)
    block, width = out.shape
    streams = acc.shape[0]
    cut = width // streams
    greet([(dp, nxt), (dp, prv)])

    def copy(h, s):
        return remote(
            gone.at[h, lax.rem(s, 2)], got.at[h, s], rs.at[h, s], rr.at[h, s],
            dp, nxt if h % 2 == 0 else prv,
        )

    def step(s):
        for h in range(streams):
            c = ring_index(p - 1 - s if h % 2 == 0 else p + 1 + s, parts)
            if len(left.shape) == 2:
                piece = left[:, pl.ds(pl.multiple_of(c * block, block), block)]
            else:
                piece = left[c]
            columns = slice(h * cut, (h + 1) * cut)
            acc[h] = lax.dot_general(
                piece, right[:, columns], (((0,), (0,)), ((), ())), preferred_element_type=F32
            )

            @pl.when(s > 0)
            def _():
                copy(h, s - 1).wait_recv()
                acc[h] += got[h, s - 1].astype(F32)

            @pl.when((s >= 2) & (s < parts - 1))
            def _():
                copy(h, s - 2).wait_send()

            @pl.when(s < parts - 1)
            def _():
                gone[h, lax.rem(s, 2)] = acc[h].astype(BF)
                copy(h, s).start()

            @pl.when(s == parts - 1)
            def _():
                out[:, columns] = acc[h]

    loop(0, parts, step)
    for h in range(streams):
        for s in range(max(parts - 3, 0), parts - 1):
            copy(h, s).wait_send()


def row_sum(parts, groups, left, right):
    width = right.shape[1]
    block = FF // (groups * parts)
    streams = 4
    if block % 128:
        left = left.reshape(left.shape[0], parts, block).transpose(1, 0, 2)
    dma = pltpu.SemaphoreType.DMA
    vmem = pl.BlockSpec(memory_space=pltpu.VMEM)
    return pl.pallas_call(
        functools.partial(row_sum_kernel, parts, groups),
        out_shape=jax.ShapeDtypeStruct((block, width), F32),
        in_specs=[vmem] * 2,
        out_specs=vmem,
        scratch_shapes=[
            pltpu.VMEM((streams, block, width // streams), F32),
            pltpu.VMEM((streams, parts - 1, block, width // streams), BF),
            pltpu.VMEM((streams, 2, block, width // streams), BF),
            dma((streams, parts)), dma((streams, parts)),
        ],
        compiler_params=pltpu.CompilerParams(
            collective_id=3, has_side_effects=True, vmem_limit_bytes=56 * 2**20
        ),
        cost_estimate=lasting(95),
    )(left, right)


def finish_kernel(
    parts, groups,
    grads, res, gx, upg, vec,
    total, res_out, gx_out, upg_out, vec_out,
    loc, sibr, xb, xrb, got, gone,
    local, ls, ss, sr, ns, nr, rs, rr, as_, ar, bs, br, us, ur, vs, vr,
):
    dp, f = lax.axis_index("dp"), lax.axis_index("fsdp")
    owners, rows_x = groups * parts, groups // 2
    x, core = lax.div(dp, 2), lax.rem(dp, 2)
    sib = x * 2 + 1 - core
    me = dp * parts + f
    p = ring_place(f, parts)
    nxt, prv = ring_index(p + 1, parts), ring_index(p - 1, parts)
    half = grads.shape[4] // 2
    mine = [
        pltpu.make_async_copy(res.at[f], res_out.at[f], local.at[0]),
        pltpu.make_async_copy(gx.at[f], gx_out.at[f], local.at[1]),
        pltpu.make_async_copy(upg.at[me], upg_out.at[me], local.at[2]),
        pltpu.make_async_copy(vec.at[me], vec_out.at[me], local.at[3]),
    ]
    for copy in mine:
        copy.start()
    greet_all(me, parts, owners)

    def chunk(h, s):
        return ring_index(p - 1 - s if h == 0 else p + 1 + s, parts)

    def sib_copy(h, s):
        piece = grads.at[:, 1 - core, chunk(h, s), :, pl.ds(h * half, half)]
        return remote(piece, sibr.at[h, s], ss.at[h, s], sr.at[h, s], sib, f)

    def own_copy(h, s):
        piece = grads.at[:, core, chunk(h, s), :, pl.ds(h * half, half)]
        return pltpu.make_async_copy(piece, loc.at[h, s], ls.at[h, s])

    def x_copy(h, s, dx):
        to = wrap(x + dx, rows_x) * 2 + core
        return remote(
            xb.at[h, s, dx - 1], xrb.at[h, s, dx - 1], ns.at[h, s, dx], nr.at[h, s, dx], to, f
        )

    def ring_copy(h, s):
        return remote(
            gone.at[h, s], got.at[h, s], rs.at[h, s], rr.at[h, s], dp, nxt if h == 0 else prv
        )

    def res_copies(d, came=False):
        return deal_copy(parts, dp, f, res, res_out, as_, ar, d, came)

    def gx_copies(d, came=False):
        return deal_copy(parts, dp, f, gx, gx_out, bs, br, d, came)

    def upg_copies(d, came=False):
        return owner_copy(me, parts, owners, upg, upg_out, us, ur, d, came)

    def vec_copies(d, came=False):
        return owner_copy(me, parts, owners, vec, vec_out, vs, vr, d, came)

    def begin(s):
        for h in range(2):
            sib_copy(h, s).start()
            own_copy(h, s).start()

    def pair(s):
        for h in range(2):
            sib_copy(h, s).wait_recv()
            own_copy(h, s).wait()
            for dx in range(1, rows_x):
                to = wrap(x + dx, rows_x)
                xb[h, s, dx - 1] = (sibr[h, s, to].astype(F32) + loc[h, s, to].astype(F32)).astype(BF)
                x_copy(h, s, dx).start()

    def step(s):
        for h in range(2):
            for dx in range(1, rows_x):
                x_copy(h, s, dx).wait_recv()

            def value():
                here = sibr[h, s, x].astype(F32) + loc[h, s, x].astype(F32)
                for dx in range(1, rows_x):
                    here = here + xrb[h, s, dx - 1].astype(F32)
                return here

            @pl.when(s == 0)
            def _():
                gone[h, s] = value().astype(BF)
                ring_copy(h, s).start()

            @pl.when((s > 0) & (s < parts - 1))
            def _():
                ring_copy(h, s - 1).wait_recv()
                gone[h, s] = (value() + got[h, s - 1].astype(F32)).astype(BF)
                ring_copy(h, s).start()

            @pl.when(s == parts - 1)
            def _():
                ring_copy(h, s - 1).wait_recv()
                total[:, h * half : (h + 1) * half] = value() + got[h, s - 1].astype(F32)

    each = -(-(owners - 1) // parts)
    ahead, near = min(4, parts), min(2, parts)
    for s in range(ahead):
        begin(s)
    for s in range(near):
        pair(s)

    def main(s):
        @pl.when(s < parts - ahead)
        def _():
            begin(s + ahead)

        @pl.when(s < parts - near)
        def _():
            pair(s + near)

        step(s)

        @pl.when(s < parts - 1)
        def _():
            res_copies(s + 1).start()
            gx_copies(s + 1).start()

        for j in range(each):
            d = s * each + 1 + j

            @pl.when(d < owners)
            def _():
                upg_copies(d).start()
                vec_copies(d).start()

    loop(0, parts, main)

    def finish(s):
        for h in range(2):
            sib_copy(h, s).wait_send()
            for dx in range(1, rows_x):
                x_copy(h, s, dx).wait_send()

            @pl.when(s < parts - 1)
            def _():
                ring_copy(h, s).wait_send()

        @pl.when(s > 0)
        def _():
            for copies in (res_copies, gx_copies):
                copies(s, True).wait_recv()
                copies(s).wait_send()

    loop(0, parts, finish)

    def owner_finish(d):
        for copies in (upg_copies, vec_copies):
            copies(d, True).wait_recv()
            copies(d).wait_send()

    loop(1, owners, owner_finish)
    for copy in mine:
        copy.wait()


def finish_sums(parts, groups, grads, res, gx, upg, vec):
    owners, rows_x = groups * parts, groups // 2
    rows, width = grads.shape[3:]
    half = width // 2
    dma = pltpu.SemaphoreType.DMA
    hbm = pl.BlockSpec(memory_space=pl.ANY)
    return pl.pallas_call(
        functools.partial(finish_kernel, parts, groups),
        out_shape=(
            jax.ShapeDtypeStruct((rows, width), F32),
            jax.ShapeDtypeStruct(res.shape, BF),
            jax.ShapeDtypeStruct(gx.shape, BF),
            jax.ShapeDtypeStruct(upg.shape, BF),
            jax.ShapeDtypeStruct(vec.shape, F32),
        ),
        in_specs=[hbm] * 5,
        out_specs=(pl.BlockSpec(memory_space=pltpu.VMEM),) + (hbm,) * 4,
        scratch_shapes=[
            pltpu.VMEM((2, parts, rows_x, rows, half), BF),
            pltpu.VMEM((2, parts, rows_x, rows, half), BF),
            pltpu.VMEM((2, parts, rows_x - 1, rows, half), BF),
            pltpu.VMEM((2, parts, rows_x - 1, rows, half), BF),
            pltpu.VMEM((2, parts, rows, half), BF),
            pltpu.VMEM((2, parts, rows, half), BF),
            dma((4,)),
            dma((2, parts)), dma((2, parts)), dma((2, parts)),
            dma((2, parts, rows_x)), dma((2, parts, rows_x)),
            dma((2, parts)), dma((2, parts)),
            dma((parts,)), dma((parts,)), dma((parts,)), dma((parts,)),
            dma((owners,)), dma((owners,)), dma((owners,)), dma((owners,)),
        ],
        compiler_params=pltpu.CompilerParams(
            collective_id=4, has_side_effects=True, vmem_limit_bytes=60 * 2**20
        ),
        cost_estimate=lasting(140),
    )(grads, res, gx, upg, vec)


def shards(
    tokens,
    cotangent,
    lengths,
    routing,
    in_weight,
    in_first,
    in_second,
    out_weight,
    out_first,
    out_second,
    up_weight,
    up_first,
    up_second,
    down_weight,
    down_first,
    down_second,
    vectors,
    vector_first,
    vector_second,
):
    bf = jnp.bfloat16
    heads = D // HD
    count = tokens.shape[0]
    parts = lax.axis_size("fsdp")
    groups = lax.axis_size("dp")
    both = ("dp", "fsdp")
    piece = count // parts
    width_in = D + 2 * HD
    slots = jnp.arange(parts, dtype=jnp.int32)
    order = routing[0]
    inverse = jnp.sum(jnp.where(order[:, None] == slots[None, :], slots[:, None], 0), axis=0)

    def deal(array):
        return jnp.take(array.reshape(parts, piece, D), inverse, axis=0)

    def undeal(array):
        return jnp.take(array, order, axis=0).reshape(count, D)

    rows = in_weight.shape[0]
    owners = groups * parts
    out_vec = jnp.concatenate(
        [out_weight.astype(bf), jnp.pad(vectors.astype(bf), ((0, 0), (0, 128 - NVEC)))], axis=1
    )
    up_pieces = up_weight.astype(bf).reshape(rows, owners, FF // owners).transpose(1, 0, 2)
    x_dealt, grad_dealt, whole_in, whole_out, up_block = spread(
        parts,
        groups,
        deal(tokens),
        deal(cotangent),
        in_weight.astype(bf),
        out_vec,
        up_pieces,
    )
    inputs_here = x_dealt.reshape(count, D)
    grad_all = grad_dealt.reshape(groups * count, D)
    grad_here = lax.dynamic_index_in_dim(
        grad_dealt, lax.axis_index("dp"), 0, keepdims=False
    ).reshape(count, D)
    whole_in = whole_in.reshape(D, width_in)
    whole_out = whole_out.reshape(D, D + 128)
    part_down = lax.all_gather(down_weight.astype(bf), "fsdp", axis=0, tiled=True)
    up_block, part_down = lax.optimization_barrier((up_block, part_down))
    part_up = lax.all_gather(up_block.reshape(D, FF // owners).T, "fsdp", axis=0, tiled=True)

    table = whole_out[:, D : D + NVEC].astype(jnp.float32)
    whole_out = whole_out[:, :D]
    gain_one = table[:, 0]
    shift_one = table[:, 1]
    query_bias = table[:, 2]
    branch_bias = table[:, 3]
    gain_two = table[:, 4]
    shift_two = table[:, 5]
    output_bias = table[:, 6]
    hidden_bias = table[:, 7:].T.reshape(FF)
    ff_here = FF // groups
    ff_start = lax.axis_index("dp") * ff_here
    hidden_bias_here = lax.dynamic_slice(hidden_bias, (ff_start,), (ff_here,))
    allowed = segment_mask(lengths[0], count)
    scale = 1.0 / math.sqrt(HD)
    inputs = inputs_here.astype(jnp.float32)
    norm_one_b = layer_norm(inputs, gain_one, shift_one).astype(bf)
    mixed = jnp.dot(norm_one_b, whole_in, preferred_element_type=jnp.float32)
    query_b = (mixed[:, :D] + query_bias).astype(bf)
    keys_b = mixed[:, D : D + HD].astype(bf)
    values_b = mixed[:, D + HD :].astype(bf)
    query_heads = query_b.reshape(count, heads, HD)

    def score_table():
        raw = (
            jnp.einsum("thd,sd->hts", query_heads, keys_b, preferred_element_type=jnp.float32)
            * scale
        )
        return jnp.where(allowed[None], raw, -1e30)

    scores = score_table()
    top = jnp.max(scores, axis=-1, keepdims=True)
    expo = jnp.exp(scores - top)
    total = jnp.sum(expo, axis=-1, keepdims=True)
    logsum = top + jnp.log(total)
    probs_b = (expo / total).astype(bf)
    attended_b = (
        jnp.einsum("hts,sd->thd", probs_b, values_b, preferred_element_type=jnp.float32)
        .reshape(count, D)
        .astype(bf)
    )
    middle = inputs + (
        jnp.dot(attended_b, whole_out, preferred_element_type=jnp.float32) + branch_bias
    )
    norm_two_b = layer_norm(middle, gain_two, shift_two).astype(bf)

    norm_all = group_gather(groups, norm_two_b).reshape(groups * count, D)
    hidden = contract_cols(norm_all, part_up) + hidden_bias_here
    grad_active = contract_cols(grad_all, part_down)
    gelu_value, gelu_pull = jax.vjp(gelu_tanh, hidden)
    active_b = gelu_value.astype(bf)
    grad_hidden_f = gelu_pull(grad_active)[0]
    grad_hidden_b = grad_hidden_f.astype(bf)
    grad_norm_two = group_sum(
        groups,
        jnp.dot(grad_hidden_b, part_up, preferred_element_type=jnp.float32)
        .astype(bf)
        .reshape(groups // 2, 2, count, D),
    )
    up_grad_block = row_sum(parts, groups, grad_hidden_b, norm_all)
    down_grad = lax.psum_scatter(
        contract_rows(active_b, grad_all).astype(bf), "fsdp", scatter_dimension=0, tiled=True
    )
    branch_two = lax.psum_scatter(
        jnp.dot(active_b, part_down, preferred_element_type=jnp.float32).astype(bf),
        "dp",
        scatter_dimension=0,
        tiled=True,
    ).astype(jnp.float32)
    result = middle + (branch_two + output_bias)

    grad_y = grad_here.astype(jnp.float32)
    norm_value_two, pull_two = jax.vjp(layer_norm, middle, gain_two, shift_two)
    grad_middle_norm, grad_gain_two, grad_shift_two = pull_two(grad_norm_two)
    grad_middle = grad_y + grad_middle_norm
    grad_branch_b = grad_middle.astype(bf)
    grad_attended_b = contract_cols(grad_branch_b, whole_out).astype(bf)
    grad_heads = grad_attended_b.reshape(count, heads, HD)
    probs = jnp.exp(score_table() - logsum)
    probs_again_b = probs.astype(bf)
    grad_probs = jnp.einsum("thd,sd->hts", grad_heads, values_b, preferred_element_type=jnp.float32)
    grad_values_b = jnp.einsum(
        "hts,thd->sd", probs_again_b, grad_heads, preferred_element_type=jnp.float32
    ).astype(bf)
    weighted = jnp.sum(probs * grad_probs, axis=-1, keepdims=True)
    grad_scores_b = (probs * (grad_probs - weighted)).astype(bf)
    grad_query_b = (
        (
            jnp.einsum("hts,sd->thd", grad_scores_b, keys_b, preferred_element_type=jnp.float32)
            * scale
        )
        .reshape(count, D)
        .astype(bf)
    )
    grad_keys_b = (
        jnp.einsum("hts,thd->sd", grad_scores_b, query_heads, preferred_element_type=jnp.float32)
        * scale
    ).astype(bf)
    grad_mixed_b = jnp.concatenate([grad_query_b, grad_keys_b, grad_values_b], axis=1)
    grad_norm_one = contract_cols(grad_mixed_b, whole_in)
    norm_value_one, pull_one = jax.vjp(layer_norm, inputs, gain_one, shift_one)
    grad_inputs_norm, grad_gain_one, grad_shift_one = pull_one(grad_norm_one)
    grad_inputs = grad_middle + grad_inputs_norm
    hidden_sums = jnp.sum(grad_hidden_b.astype(jnp.float32), axis=0)
    hidden_whole = lax.dynamic_update_slice(
        jnp.zeros((FF,), jnp.float32), hidden_sums, (ff_start,)
    )
    vector_grad = jnp.concatenate(
        [
            jnp.stack(
                [
                    grad_gain_one,
                    grad_shift_one,
                    jnp.sum(grad_query_b.astype(jnp.float32), axis=0),
                    jnp.sum(grad_branch_b.astype(jnp.float32), axis=0),
                    grad_gain_two,
                    grad_shift_two,
                    jnp.sum(grad_y, axis=0),
                ],
                axis=0,
            ),
            hidden_whole.reshape(FF // D, D),
        ],
        axis=0,
    )
    vector_grad = vector_grad.reshape(NVEC, owners, rows).transpose(1, 0, 2)
    vector_grad = jnp.pad(vector_grad, ((0, 0), (0, 16 - NVEC), (0, 128 - rows)))
    small_part = jnp.concatenate(
        [
            contract_rows(norm_one_b, grad_mixed_b).astype(bf),
            contract_rows(attended_b, grad_branch_b).astype(bf),
        ],
        axis=1,
    )
    small_grad, back_result, back_grad, grad_up, vector_sum = finish_sums(
        parts,
        groups,
        small_part.reshape(groups // 2, 2, parts, rows, width_in + D),
        result.astype(bf).reshape(parts, piece, D),
        grad_inputs.astype(bf).reshape(parts, piece, D),
        up_grad_block.T.astype(bf).reshape(owners, rows, FF // owners),
        vector_grad,
    )
    grad_up = grad_up.transpose(1, 0, 2).reshape(rows, FF)
    vector_sum = jnp.sum(vector_sum, axis=0)
    grad_in = small_grad[:, :width_in]
    grad_out = small_grad[:, width_in : width_in + D]
    grad_vec = vector_sum[:NVEC, :rows].T
    in_new = adam_update(in_weight, in_first, in_second, grad_in, 1.0 / math.sqrt(D), decay_rate)
    out_new = adam_update(
        out_weight, out_first, out_second, grad_out, 1.0 / math.sqrt(D * 8 // TOK_DEV), decay_rate
    )
    up_new = adam_update(up_weight, up_first, up_second, grad_up, 1.0 / math.sqrt(D), decay_rate)
    down_new = adam_update(
        down_weight, down_first, down_second, down_grad, 1.0 / math.sqrt(FF), decay_rate
    )
    vec_new = adam_update(vectors, vector_first, vector_second, grad_vec, 0.1, 0.0)
    return (undeal(back_result), undeal(back_grad)) + in_new + out_new + up_new + down_new + vec_new


def solution(mesh):
    spec = P(("dp", "fsdp"), None)
    return jax.shard_map(
        shards,
        mesh=mesh,
        in_specs=(spec,) * 19,
        out_specs=(spec,) * 17,
        check_vma=False,
    )
```

```python
import functools
import math

import jax
import jax.numpy as jnp
from jax import lax
from jax.experimental import pallas as pl
from jax.experimental.pallas import tpu as pltpu
from jax.sharding import PartitionSpec as P

D = 2048
FF = 8192
HD = 128
TOK_DEV = 384
STEP = 5
NVEC = 11


eps_norm = 1e-05
beta_one = 0.5
beta_two = 0.5
adam_eps = 1e-08
decay_rate = 0.1


def layer_norm(values, gain, shift):
    centered = values - jnp.mean(values, axis=-1, keepdims=True)
    scaled = centered * lax.rsqrt(jnp.mean(centered * centered, axis=-1, keepdims=True) + eps_norm)
    return scaled * gain + shift


def gelu_tanh(values):
    return (
        0.5
        * values
        * (1.0 + jnp.tanh(0.7978845608028654 * (values + 0.044715 * values * values * values)))
    )


def segment_mask(sizes, count):
    ends = jnp.cumsum(sizes)
    places = jnp.arange(count, dtype=jnp.int32)
    labels = jnp.sum((places[:, None] >= ends[None, :]).astype(jnp.int32), axis=1)
    return (labels[:, None] == labels[None, :]) & (places[None, :] <= places[:, None])


def adam_update(weight, first, second, grad, rate, decay):
    grad = grad.astype(jnp.float32)
    first_new = beta_one * first + (1.0 - beta_one) * grad
    second_new = beta_two * second + (1.0 - beta_two) * grad * grad
    fix_one = 1.0 - beta_one**STEP
    fix_two = 1.0 - beta_two**STEP
    step_size = first_new / fix_one / (jnp.sqrt(second_new / fix_two) + adam_eps)
    weight_new = weight - rate * (step_size + decay * weight)
    return (weight_new, first_new, second_new)


def contract_rows(left, right):
    return lax.dot_general(
        left, right, (((0,), (0,)), ((), ())), preferred_element_type=jnp.float32
    )


def contract_cols(left, right):
    return lax.dot_general(
        left, right, (((1,), (1,)), ((), ())), preferred_element_type=jnp.float32
    )


MESH = pl.DeviceIdType.MESH
F32 = jnp.float32
BF = jnp.bfloat16


def wrap(value, count):
    return lax.rem(value + 2 * count, count)


def ring_place(index, parts):
    if parts != 8:
        return index
    z, y = lax.div(index, 2), lax.rem(index, 2)
    return z + y * (7 - 2 * z)


def ring_index(place, parts):
    place = wrap(place, parts)
    if parts != 8:
        return place
    back = lax.div(place, 4)
    return (1 - back) * 2 * place + back * (15 - 2 * place)


def remote(src, dst, send, recv, dp, fs):
    return pltpu.make_async_remote_copy(
        src_ref=src, dst_ref=dst, send_sem=send, recv_sem=recv, device_id=(dp, fs), device_id_type=MESH
    )


def lasting(micros):
    return pl.CostEstimate(
        flops=int(micros * 1.1e9), bytes_accessed=int(micros * 3.3e6), transcendentals=0
    )


def greet(targets):
    barrier = pltpu.get_barrier_semaphore()
    for dp, fs in targets:
        pl.semaphore_signal(barrier, inc=1, device_id=(dp, fs), device_id_type=MESH)
    pl.semaphore_wait(barrier, len(targets))


def greet_all(me, parts, owners):
    barrier = pltpu.get_barrier_semaphore()

    def one(i, carry):
        peer = wrap(me + i, owners)
        pl.semaphore_signal(
            barrier, inc=1, device_id=(lax.div(peer, parts), lax.rem(peer, parts)), device_id_type=MESH
        )
        return carry

    lax.fori_loop(1, owners, one, 0)
    pl.semaphore_wait(barrier, owners - 1)


def loop(low, high, body):
    def one(i, carry):
        body(i)
        return carry

    lax.fori_loop(low, high, one, 0)


def deal_copy(parts, dp, f, src, dst, send, recv, d, came=False):
    to = wrap(f + d, parts)
    place = wrap(f - d, parts) if came else f
    return remote(src.at[to], dst.at[place], send.at[d], recv.at[d], dp, to)


def owner_copy(me, parts, owners, src, dst, send, recv, d, came=False):
    to = wrap(me + d, owners)
    place = wrap(me - d, owners) if came else me
    return remote(
        src.at[to], dst.at[place], send.at[d], recv.at[d], lax.div(to, parts), lax.rem(to, parts)
    )


def spread_kernel(
    parts, groups,
    xd, gd, inb, ovb, upb,
    xo, eall, win, wov, upo,
    local, xs, xr, gs, gr, us, ur, rs, rr, ns, nr, ss, sr, ens, enr, ess, esr,
):
    dp, f = lax.axis_index("dp"), lax.axis_index("fsdp")
    owners, rows_x = groups * parts, groups // 2
    x, core = lax.div(dp, 2), lax.rem(dp, 2)
    sib = x * 2 + 1 - core
    me = dp * parts + f
    p = ring_place(f, parts)
    nxt, prv = ring_index(p + 1, parts), ring_index(p - 1, parts)
    whole = (win, wov)
    mine = [
        pltpu.make_async_copy(inb, win.at[me], local.at[0]),
        pltpu.make_async_copy(ovb, wov.at[me], local.at[1]),
        pltpu.make_async_copy(xd.at[f], xo.at[f], local.at[2]),
        pltpu.make_async_copy(gd.at[f], eall.at[dp, f], local.at[3]),
        pltpu.make_async_copy(upb.at[me], upo.at[me], local.at[4]),
    ]
    for copy in mine:
        copy.start()
    greet_all(me, parts, owners)
    for copy in mine:
        copy.wait()

    def x_copies(d, came=False):
        return deal_copy(parts, dp, f, xd, xo, xs, xr, d, came)

    def g_copies(d, came=False):
        return deal_copy(parts, dp, f, gd, eall.at[dp], gs, gr, d, came)

    def u_copies(d, came=False):
        return owner_copy(me, parts, owners, upb, upo, us, ur, d, came)

    def origin(h, s):
        return ring_index(p - s if h == 0 else p + s, parts)

    def ring_send(h, s):
        ref = whole[h].at[dp * parts + origin(h, s)]
        return remote(ref, ref, rs.at[h, s], rr.at[h, s], dp, nxt if h == 0 else prv)

    def ring_recv(h, s):
        ref = whole[h].at[dp * parts + origin(h, s)]
        return remote(ref, ref, rs.at[h, s - 1], rr.at[h, s - 1], dp, nxt if h == 0 else prv)

    def x_send(h, s, dx):
        ref = whole[h].at[dp * parts + origin(h, s)]
        to = wrap(x + dx, rows_x) * 2 + core
        return remote(ref, ref, ns.at[h, s, dx], nr.at[h, s, dx], to, f)

    def x_recv(h, s, dx):
        came = wrap(x - dx, rows_x) * 2 + core
        ref = whole[h].at[came * parts + origin(h, s)]
        return remote(ref, ref, ns.at[h, s, dx], nr.at[h, s, dx], came, f)

    def sib_send(h, s, dx):
        came = wrap(x - dx, rows_x) * 2 + core
        ref = whole[h].at[came * parts + origin(h, s)]
        return remote(ref, ref, ss.at[h, s, dx], sr.at[h, s, dx], sib, f)

    def sib_recv(h, s, dx):
        came = wrap(x - dx, rows_x) * 2 + 1 - core
        ref = whole[h].at[came * parts + origin(h, s)]
        return remote(ref, ref, ss.at[h, s, dx], sr.at[h, s, dx], sib, f)

    def e_x_send(d, dx):
        ref = eall.at[dp, wrap(f - d, parts)]
        to = wrap(x + dx, rows_x) * 2 + core
        return remote(ref, ref, ens.at[d, dx], enr.at[d, dx], to, f)

    def e_x_recv(d, dx):
        came = wrap(x - dx, rows_x) * 2 + core
        ref = eall.at[came, wrap(f - d, parts)]
        return remote(ref, ref, ens.at[d, dx], enr.at[d, dx], came, f)

    def e_sib_send(d, dx):
        came = wrap(x - dx, rows_x) * 2 + core
        ref = eall.at[came, wrap(f - d, parts)]
        return remote(ref, ref, ess.at[d, dx], esr.at[d, dx], sib, f)

    def e_sib_recv(d, dx):
        came = wrap(x - dx, rows_x) * 2 + 1 - core
        ref = eall.at[came, wrap(f - d, parts)]
        return remote(ref, ref, ess.at[d, dx], esr.at[d, dx], sib, f)

    def ring_step(s):
        for h in range(2):
            @pl.when(s > 0)
            def _():
                ring_recv(h, s).wait_recv()

            @pl.when(s < parts - 1)
            def _():
                ring_send(h, s).start()

            for dx in range(1, rows_x):
                x_send(h, s, dx).start()
            sib_send(h, s, 0).start()

    def e_step(d):
        @pl.when(d > 0)
        def _():
            g_copies(d, True).wait_recv()

        for dx in range(1, rows_x):
            e_x_send(d, dx).start()
        e_sib_send(d, 0).start()

    def relay(s):
        for h in range(2):
            for dx in range(1, rows_x):
                x_recv(h, s, dx).wait_recv()
                sib_send(h, s, dx).start()

    def e_relay(d):
        for dx in range(1, rows_x):
            e_x_recv(d, dx).wait_recv()
            e_sib_send(d, dx).start()

    each = -(-(owners - 1) // parts)

    def main(s):
        @pl.when(s < parts)
        def _():
            ring_step(s)

        @pl.when(s < parts - 1)
        def _():
            x_copies(s + 1).start()
            g_copies(s + 1).start()

        for j in range(each):
            d = s * each + 1 + j

            @pl.when(d < owners)
            def _():
                u_copies(d).start()

        @pl.when((s >= 1) & (s <= parts))
        def _():
            e_step(s - 1)

        @pl.when((s >= 2) & (s < parts + 2))
        def _():
            relay(s - 2)

        @pl.when(s >= 3)
        def _():
            e_relay(s - 3)

    loop(0, parts + 3, main)

    def finish(s):
        for h in range(2):
            @pl.when(s < parts - 1)
            def _():
                ring_send(h, s).wait_send()

            for dx in range(1, rows_x):
                x_send(h, s, dx).wait_send()
            for dx in range(rows_x):
                sib_recv(h, s, dx).wait_recv()
                sib_send(h, s, dx).wait_send()
        for dx in range(1, rows_x):
            e_x_send(s, dx).wait_send()
        for dx in range(rows_x):
            e_sib_recv(s, dx).wait_recv()
            e_sib_send(s, dx).wait_send()

        @pl.when(s > 0)
        def _():
            x_copies(s, True).wait_recv()
            x_copies(s).wait_send()
            g_copies(s).wait_send()

    loop(0, parts, finish)

    def u_finish(d):
        u_copies(d, True).wait_recv()
        u_copies(d).wait_send()

    loop(1, owners, u_finish)


def spread(parts, groups, xd, gd, inb, ovb, upb):
    owners, rows_x = groups * parts, groups // 2
    dma = pltpu.SemaphoreType.DMA
    return pl.pallas_call(
        functools.partial(spread_kernel, parts, groups),
        out_shape=(
            jax.ShapeDtypeStruct(xd.shape, BF),
            jax.ShapeDtypeStruct((groups,) + gd.shape, BF),
            jax.ShapeDtypeStruct((owners,) + inb.shape, BF),
            jax.ShapeDtypeStruct((owners,) + ovb.shape, BF),
            jax.ShapeDtypeStruct(upb.shape, BF),
        ),
        in_specs=[pl.BlockSpec(memory_space=pl.ANY)] * 5,
        out_specs=(pl.BlockSpec(memory_space=pl.ANY),) * 5,
        scratch_shapes=[
            dma((5,)),
            dma((parts,)), dma((parts,)), dma((parts,)), dma((parts,)),
            dma((owners,)), dma((owners,)),
            dma((2, parts)), dma((2, parts)),
            dma((2, parts, rows_x)), dma((2, parts, rows_x)),
            dma((2, parts, rows_x)), dma((2, parts, rows_x)),
            dma((parts, rows_x)), dma((parts, rows_x)),
            dma((parts, rows_x)), dma((parts, rows_x)),
        ],
        compiler_params=pltpu.CompilerParams(collective_id=0, has_side_effects=True),
        cost_estimate=lasting(200),
    )(xd, gd, inb, ovb, upb)


def ffn_kernel(
    groups, chunks,
    src, eall, w1, w2, b1,
    hall, act, dhid, ypart, dsum, hsum,
    hb, eb, ab, db, yb, pown, psib, sibr, xb, xrb,
    local, ns, nr, ss, sr, hs, es, as_, ds, ys, gss, gsr, gns, gnr,
):
    dp, f = lax.axis_index("dp"), lax.axis_index("fsdp")
    rows_x = groups // 2
    x, core = lax.div(dp, 2), lax.rem(dp, 2)
    sib = x * 2 + 1 - core
    count, width = src.shape
    units = w1.shape[0]
    size = count // chunks
    tile = min(256, units)
    mine = pltpu.make_async_copy(src, hall.at[dp], local)
    mine.start()
    greet([(sib, f)] + [(wrap(x + dx, rows_x) * 2 + core, f) for dx in range(1, rows_x)])

    def part(ref, k):
        return ref.at[pl.ds(k * size, size)]

    def x_send(k, dx):
        to = wrap(x + dx, rows_x) * 2 + core
        return remote(part(src, k), part(hall.at[dp], k), ns.at[k, dx], nr.at[k, dx], to, f)

    def x_recv(k, dx):
        came = wrap(x - dx, rows_x) * 2 + core
        ref = part(hall.at[came], k)
        return remote(ref, ref, ns.at[k, dx], nr.at[k, dx], came, f)

    def own_send(k):
        return remote(part(src, k), part(hall.at[dp], k), ss.at[k, 0], sr.at[k, 0], sib, f)

    def sib_send(k, dx):
        came = wrap(x - dx, rows_x) * 2 + core
        ref = part(hall.at[came], k)
        return remote(ref, ref, ss.at[k, dx], sr.at[k, dx], sib, f)

    def sib_recv(k, dx):
        came = wrap(x - dx, rows_x) * 2 + 1 - core
        ref = part(hall.at[came], k)
        return remote(ref, ref, ss.at[k, dx], sr.at[k, dx], sib, f)

    def sum_sib(dx, k):
        return remote(
            part(psib.at[dx], k), part(sibr.at[dx], k), gss.at[dx, k], gsr.at[dx, k], sib, f
        )

    def sum_x(dx, k):
        to = wrap(x + dx, rows_x) * 2 + core
        return remote(
            part(xb.at[dx - 1], k), part(xrb.at[dx - 1], k), gns.at[dx, k], gnr.at[dx, k], to, f
        )

    def a_copy(i):
        return pltpu.make_async_copy(ab.at[i], act.at[group_of(i)], as_.at[i])

    def d_copy(i):
        return pltpu.make_async_copy(db.at[lax.rem(i, 2)], dhid.at[group_of(i)], ds.at[i])

    def group_of(i):
        dx, c = lax.div(i, 2), lax.rem(i, 2)
        far = jnp.minimum(dx, 1)
        same = (1 - far) * (1 - c) + far * c
        other_core = same * core + (1 - same) * (1 - core)
        return wrap(x + dx, rows_x) * 2 + other_core

    for k in range(chunks):
        for dx in range(1, rows_x):
            x_send(k, dx).start()
    for k in range(chunks):
        own_send(k).start()
    mine.wait()

    def e_load(i):
        return pltpu.make_async_copy(eall.at[group_of(i)], eb, es)

    hsum[...] = jnp.zeros_like(hsum)

    def one(i):
        dx, c = lax.div(i, 2), lax.rem(i, 2)
        g = group_of(i)
        slot = lax.rem(i, 2)
        came = wrap(rows_x - dx, rows_x)
        e_load(i).start()

        @pl.when((dx > 0) & (c == 0))
        def _():
            for k in range(chunks):
                x_recv(k, came).wait_recv()
                sib_send(k, came).start()
            for k in range(chunks):
                sib_recv(k, came).wait_recv()

        @pl.when((dx == 0) & (c == 1))
        def _():
            for k in range(chunks):
                sib_recv(k, 0).wait_recv()

        load = pltpu.make_async_copy(hall.at[g], hb, hs)
        load.start()

        @pl.when(i >= 2)
        def _():
            d_copy(i - 2).wait()

        load.wait()
        e_load(i).wait()

        def hidden(t):
            columns = pl.ds(pl.multiple_of(t * tile, tile), tile)
            u = lax.dot_general(
                hb[...], w1[columns, :], (((1,), (1,)), ((), ())), preferred_element_type=F32
            ) + b1[:, columns]
            da = lax.dot_general(
                eb[...], w2[columns, :], (((1,), (1,)), ((), ())), preferred_element_type=F32
            )
            square = u * u
            th = jnp.tanh(0.7978845608028654 * (u + 0.044715 * square * u))
            half_sum = 0.5 * (1.0 + th)
            slope = half_sum + 0.5 * u * (1.0 - th * th) * (
                0.7978845608028654 * (1.0 + 3.0 * 0.044715 * square)
            )
            ab[i, :, columns] = (u * half_sum).astype(BF)
            du = (slope * da).astype(BF)
            db[slot, :, columns] = du
            hsum[:, columns] += jnp.sum(du.astype(F32), axis=0, keepdims=True)

        loop(0, units // tile, hidden)
        a_copy(i).start()
        d_copy(i).start()

        same_core = ((dx == 0) & (c == 0)) | ((dx > 0) & (c == 1))

        def rows(k):
            begin = pl.multiple_of(k * size, size)
            dh = jnp.dot(
                db[slot, pl.ds(begin, size), :], w1[...], preferred_element_type=F32
            )

            @pl.when(i == 0)
            def _():
                pown[pl.ds(begin, size), :] = dh

            @pl.when(jnp.logical_not(same_core))
            def _():
                psib[dx, pl.ds(begin, size), :] = dh.astype(BF)
                sum_sib(dx, k).start()

            @pl.when(same_core & (dx > 0))
            def _():
                sum_sib(dx, k).wait_recv()
                xb[dx - 1, pl.ds(begin, size), :] = (
                    dh + sibr[dx, pl.ds(begin, size), :].astype(F32)
                ).astype(BF)
                sum_x(dx, k).start()

        loop(0, chunks, rows)

    loop(0, groups, one)

    def y_copy(i):
        return pltpu.make_async_copy(yb.at[lax.rem(i, 2)], ypart.at[group_of(i)], ys.at[i])

    def y_one(i):
        @pl.when(i >= 2)
        def _():
            y_copy(i - 2).wait()

        def rows(k):
            begin = pl.multiple_of(k * size, size)
            yb[lax.rem(i, 2), pl.ds(begin, size), :] = jnp.dot(
                ab[i, pl.ds(begin, size), :], w2[...], preferred_element_type=F32
            ).astype(BF)

        loop(0, chunks, rows)
        y_copy(i).start()

    loop(0, groups, y_one)

    def collect(k):
        at = pl.ds(pl.multiple_of(k * size, size), size)
        sum_sib(0, k).wait_recv()
        total = pown[at, :] + sibr[0, at, :].astype(F32)
        for dx in range(1, rows_x):
            sum_x(rows_x - dx, k).wait_recv()
            total = total + xrb[rows_x - dx - 1, at, :].astype(F32)
        dsum[at, :] = total

    loop(0, chunks, collect)

    def last(k):
        for dx in range(rows_x):
            sum_sib(dx, k).wait_send()
        for dx in range(1, rows_x):
            sum_x(dx, k).wait_send()
            x_send(k, dx).wait_send()
            sib_send(k, dx).wait_send()
        own_send(k).wait_send()

    loop(0, chunks, last)

    def drain(i):
        a_copy(i).wait()

        @pl.when(i >= groups - 2)
        def _():
            d_copy(i).wait()
            y_copy(i).wait()

    loop(0, groups, drain)


def ffn(groups, src, eall, w1, w2, b1):
    chunks, rows_x = 4, groups // 2
    count, width = src.shape
    units = w1.shape[0]
    dma = pltpu.SemaphoreType.DMA
    hbm = pl.BlockSpec(memory_space=pl.ANY)
    vmem = pl.BlockSpec(memory_space=pltpu.VMEM)
    return pl.pallas_call(
        functools.partial(ffn_kernel, groups, chunks),
        out_shape=(
            jax.ShapeDtypeStruct((groups, count, width), BF),
            jax.ShapeDtypeStruct((groups, count, units), BF),
            jax.ShapeDtypeStruct((groups, count, units), BF),
            jax.ShapeDtypeStruct((groups, count, width), BF),
            jax.ShapeDtypeStruct((count, width), F32),
            jax.ShapeDtypeStruct((1, units), F32),
        ),
        in_specs=[hbm, hbm, vmem, vmem, vmem],
        out_specs=(hbm,) * 4 + (vmem,) * 2,
        scratch_shapes=[
            pltpu.VMEM((count, width), BF),
            pltpu.VMEM((count, width), BF),
            pltpu.VMEM((groups, count, units), BF),
            pltpu.VMEM((2, count, units), BF),
            pltpu.VMEM((2, count, width), BF),
            pltpu.VMEM((count, width), F32),
            pltpu.VMEM((rows_x, count, width), BF),
            pltpu.VMEM((rows_x, count, width), BF),
            pltpu.VMEM((rows_x - 1, count, width), BF),
            pltpu.VMEM((rows_x - 1, count, width), BF),
            dma(()),
            dma((chunks, rows_x)), dma((chunks, rows_x)),
            dma((chunks, rows_x)), dma((chunks, rows_x)),
            dma(()), dma(()),
            dma((groups,)), dma((groups,)), dma((groups,)),
            dma((rows_x, chunks)), dma((rows_x, chunks)),
            dma((rows_x, chunks)), dma((rows_x, chunks)),
        ],
        compiler_params=pltpu.CompilerParams(
            collective_id=1, has_side_effects=True, vmem_limit_bytes=60 * 2**20
        ),
        cost_estimate=lasting(95),
    )(src, eall, w1, w2, b1)


def row_sum_kernel(parts, groups, left, right, out, acc, got, gone, rs, rr):
    dp, f = lax.axis_index("dp"), lax.axis_index("fsdp")
    p = ring_place(f, parts)
    nxt, prv = ring_index(p + 1, parts), ring_index(p - 1, parts)
    block, width = out.shape
    streams = acc.shape[0]
    cut = width // streams
    greet([(dp, nxt), (dp, prv)])

    def copy(h, s):
        return remote(
            gone.at[h, lax.rem(s, 2)], got.at[h, s], rs.at[h, s], rr.at[h, s],
            dp, nxt if h % 2 == 0 else prv,
        )

    def step(s):
        for h in range(streams):
            c = ring_index(p - 1 - s if h % 2 == 0 else p + 1 + s, parts)
            if len(left.shape) == 2:
                piece = left[:, pl.ds(pl.multiple_of(c * block, block), block)]
            else:
                piece = left[c]
            columns = slice(h * cut, (h + 1) * cut)
            acc[h] = lax.dot_general(
                piece, right[:, columns], (((0,), (0,)), ((), ())), preferred_element_type=F32
            )

            @pl.when(s > 0)
            def _():
                copy(h, s - 1).wait_recv()
                acc[h] += got[h, s - 1].astype(F32)

            @pl.when((s >= 2) & (s < parts - 1))
            def _():
                copy(h, s - 2).wait_send()

            @pl.when(s < parts - 1)
            def _():
                gone[h, lax.rem(s, 2)] = acc[h].astype(BF)
                copy(h, s).start()

            @pl.when(s == parts - 1)
            def _():
                out[:, columns] = acc[h]

    loop(0, parts, step)
    for h in range(streams):
        for s in range(max(parts - 3, 0), parts - 1):
            copy(h, s).wait_send()


def row_sum(parts, groups, left, right):
    width = right.shape[1]
    block = FF // (groups * parts)
    streams = 4
    if block % 128:
        left = left.reshape(left.shape[0], parts, block).transpose(1, 0, 2)
    dma = pltpu.SemaphoreType.DMA
    vmem = pl.BlockSpec(memory_space=pltpu.VMEM)
    return pl.pallas_call(
        functools.partial(row_sum_kernel, parts, groups),
        out_shape=jax.ShapeDtypeStruct((block, width), F32),
        in_specs=[vmem] * 2,
        out_specs=vmem,
        scratch_shapes=[
            pltpu.VMEM((streams, block, width // streams), F32),
            pltpu.VMEM((streams, parts - 1, block, width // streams), BF),
            pltpu.VMEM((streams, 2, block, width // streams), BF),
            dma((streams, parts)), dma((streams, parts)),
        ],
        compiler_params=pltpu.CompilerParams(
            collective_id=3, has_side_effects=True, vmem_limit_bytes=56 * 2**20
        ),
        cost_estimate=lasting(95),
    )(left, right)


def finish_kernel(
    parts, groups,
    grads, res, gx, upg, vec,
    total, res_out, gx_out, upg_out, vec_out,
    loc, sibr, xb, xrb, got, gone,
    local, ls, ss, sr, ns, nr, rs, rr, as_, ar, bs, br, us, ur, vs, vr,
):
    dp, f = lax.axis_index("dp"), lax.axis_index("fsdp")
    owners, rows_x = groups * parts, groups // 2
    x, core = lax.div(dp, 2), lax.rem(dp, 2)
    sib = x * 2 + 1 - core
    me = dp * parts + f
    p = ring_place(f, parts)
    nxt, prv = ring_index(p + 1, parts), ring_index(p - 1, parts)
    half = grads.shape[4] // 2
    mine = [
        pltpu.make_async_copy(res.at[f], res_out.at[f], local.at[0]),
        pltpu.make_async_copy(gx.at[f], gx_out.at[f], local.at[1]),
        pltpu.make_async_copy(upg.at[me], upg_out.at[me], local.at[2]),
        pltpu.make_async_copy(vec.at[me], vec_out.at[me], local.at[3]),
    ]
    for copy in mine:
        copy.start()
    greet_all(me, parts, owners)

    def chunk(h, s):
        return ring_index(p - 1 - s if h == 0 else p + 1 + s, parts)

    def sib_copy(h, s):
        piece = grads.at[:, 1 - core, chunk(h, s), :, pl.ds(h * half, half)]
        return remote(piece, sibr.at[h, s], ss.at[h, s], sr.at[h, s], sib, f)

    def own_copy(h, s):
        piece = grads.at[:, core, chunk(h, s), :, pl.ds(h * half, half)]
        return pltpu.make_async_copy(piece, loc.at[h, s], ls.at[h, s])

    def x_copy(h, s, dx):
        to = wrap(x + dx, rows_x) * 2 + core
        return remote(
            xb.at[h, s, dx - 1], xrb.at[h, s, dx - 1], ns.at[h, s, dx], nr.at[h, s, dx], to, f
        )

    def ring_copy(h, s):
        return remote(
            gone.at[h, s], got.at[h, s], rs.at[h, s], rr.at[h, s], dp, nxt if h == 0 else prv
        )

    def res_copies(d, came=False):
        return deal_copy(parts, dp, f, res, res_out, as_, ar, d, came)

    def gx_copies(d, came=False):
        return deal_copy(parts, dp, f, gx, gx_out, bs, br, d, came)

    def upg_copies(d, came=False):
        return owner_copy(me, parts, owners, upg, upg_out, us, ur, d, came)

    def vec_copies(d, came=False):
        return owner_copy(me, parts, owners, vec, vec_out, vs, vr, d, came)

    def begin(s):
        for h in range(2):
            sib_copy(h, s).start()
            own_copy(h, s).start()

    def pair(s):
        for h in range(2):
            sib_copy(h, s).wait_recv()
            own_copy(h, s).wait()
            for dx in range(1, rows_x):
                to = wrap(x + dx, rows_x)
                xb[h, s, dx - 1] = (sibr[h, s, to].astype(F32) + loc[h, s, to].astype(F32)).astype(BF)
                x_copy(h, s, dx).start()

    def step(s):
        for h in range(2):
            for dx in range(1, rows_x):
                x_copy(h, s, dx).wait_recv()

            def value():
                here = sibr[h, s, x].astype(F32) + loc[h, s, x].astype(F32)
                for dx in range(1, rows_x):
                    here = here + xrb[h, s, dx - 1].astype(F32)
                return here

            @pl.when(s == 0)
            def _():
                gone[h, s] = value().astype(BF)
                ring_copy(h, s).start()

            @pl.when((s > 0) & (s < parts - 1))
            def _():
                ring_copy(h, s - 1).wait_recv()
                gone[h, s] = (value() + got[h, s - 1].astype(F32)).astype(BF)
                ring_copy(h, s).start()

            @pl.when(s == parts - 1)
            def _():
                ring_copy(h, s - 1).wait_recv()
                total[:, h * half : (h + 1) * half] = value() + got[h, s - 1].astype(F32)

    each = -(-(owners - 1) // parts)
    ahead, near = min(4, parts), min(2, parts)
    for s in range(ahead):
        begin(s)
    for s in range(near):
        pair(s)

    def main(s):
        @pl.when(s < parts - ahead)
        def _():
            begin(s + ahead)

        @pl.when(s < parts - near)
        def _():
            pair(s + near)

        step(s)

        @pl.when(s < parts - 1)
        def _():
            res_copies(s + 1).start()
            gx_copies(s + 1).start()

        for j in range(each):
            d = s * each + 1 + j

            @pl.when(d < owners)
            def _():
                upg_copies(d).start()
                vec_copies(d).start()

    loop(0, parts, main)

    def finish(s):
        for h in range(2):
            sib_copy(h, s).wait_send()
            for dx in range(1, rows_x):
                x_copy(h, s, dx).wait_send()

            @pl.when(s < parts - 1)
            def _():
                ring_copy(h, s).wait_send()

        @pl.when(s > 0)
        def _():
            for copies in (res_copies, gx_copies):
                copies(s, True).wait_recv()
                copies(s).wait_send()

    loop(0, parts, finish)

    def owner_finish(d):
        for copies in (upg_copies, vec_copies):
            copies(d, True).wait_recv()
            copies(d).wait_send()

    loop(1, owners, owner_finish)
    for copy in mine:
        copy.wait()


def finish_sums(parts, groups, grads, res, gx, upg, vec):
    owners, rows_x = groups * parts, groups // 2
    rows, width = grads.shape[3:]
    half = width // 2
    dma = pltpu.SemaphoreType.DMA
    hbm = pl.BlockSpec(memory_space=pl.ANY)
    return pl.pallas_call(
        functools.partial(finish_kernel, parts, groups),
        out_shape=(
            jax.ShapeDtypeStruct((rows, width), F32),
            jax.ShapeDtypeStruct(res.shape, BF),
            jax.ShapeDtypeStruct(gx.shape, BF),
            jax.ShapeDtypeStruct(upg.shape, BF),
            jax.ShapeDtypeStruct(vec.shape, F32),
        ),
        in_specs=[hbm] * 5,
        out_specs=(pl.BlockSpec(memory_space=pltpu.VMEM),) + (hbm,) * 4,
        scratch_shapes=[
            pltpu.VMEM((2, parts, rows_x, rows, half), BF),
            pltpu.VMEM((2, parts, rows_x, rows, half), BF),
            pltpu.VMEM((2, parts, rows_x - 1, rows, half), BF),
            pltpu.VMEM((2, parts, rows_x - 1, rows, half), BF),
            pltpu.VMEM((2, parts, rows, half), BF),
            pltpu.VMEM((2, parts, rows, half), BF),
            dma((4,)),
            dma((2, parts)), dma((2, parts)), dma((2, parts)),
            dma((2, parts, rows_x)), dma((2, parts, rows_x)),
            dma((2, parts)), dma((2, parts)),
            dma((parts,)), dma((parts,)), dma((parts,)), dma((parts,)),
            dma((owners,)), dma((owners,)), dma((owners,)), dma((owners,)),
        ],
        compiler_params=pltpu.CompilerParams(
            collective_id=4, has_side_effects=True, vmem_limit_bytes=60 * 2**20
        ),
        cost_estimate=lasting(140),
    )(grads, res, gx, upg, vec)


def shards(
    tokens,
    cotangent,
    lengths,
    routing,
    in_weight,
    in_first,
    in_second,
    out_weight,
    out_first,
    out_second,
    up_weight,
    up_first,
    up_second,
    down_weight,
    down_first,
    down_second,
    vectors,
    vector_first,
    vector_second,
):
    bf = jnp.bfloat16
    heads = D // HD
    count = tokens.shape[0]
    parts = lax.axis_size("fsdp")
    groups = lax.axis_size("dp")
    both = ("dp", "fsdp")
    piece = count // parts
    width_in = D + 2 * HD
    slots = jnp.arange(parts, dtype=jnp.int32)
    order = routing[0]
    inverse = jnp.sum(jnp.where(order[:, None] == slots[None, :], slots[:, None], 0), axis=0)

    def deal(array):
        return jnp.take(array.reshape(parts, piece, D), inverse, axis=0)

    def undeal(array):
        return jnp.take(array, order, axis=0).reshape(count, D)

    rows = in_weight.shape[0]
    owners = groups * parts
    out_vec = jnp.concatenate(
        [out_weight.astype(bf), jnp.pad(vectors.astype(bf), ((0, 0), (0, 128 - NVEC)))], axis=1
    )
    up_pieces = up_weight.astype(bf).reshape(rows, owners, FF // owners).transpose(1, 0, 2)
    x_dealt, grad_dealt, whole_in, whole_out, up_block = spread(
        parts,
        groups,
        deal(tokens),
        deal(cotangent),
        in_weight.astype(bf),
        out_vec,
        up_pieces,
    )
    inputs_here = x_dealt.reshape(count, D)
    grad_all = grad_dealt.reshape(groups * count, D)
    grad_here = lax.dynamic_index_in_dim(
        grad_dealt, lax.axis_index("dp"), 0, keepdims=False
    ).reshape(count, D)
    whole_in = whole_in.reshape(D, width_in)
    whole_out = whole_out.reshape(D, D + 128)
    part_down = lax.all_gather(down_weight.astype(bf), "fsdp", axis=0, tiled=True)
    up_block, part_down = lax.optimization_barrier((up_block, part_down))
    part_up = lax.all_gather(up_block.reshape(D, FF // owners).T, "fsdp", axis=0, tiled=True)

    table = whole_out[:, D : D + NVEC].astype(jnp.float32)
    whole_out = whole_out[:, :D]
    gain_one = table[:, 0]
    shift_one = table[:, 1]
    query_bias = table[:, 2]
    branch_bias = table[:, 3]
    gain_two = table[:, 4]
    shift_two = table[:, 5]
    output_bias = table[:, 6]
    hidden_bias = table[:, 7:].T.reshape(FF)
    ff_here = FF // groups
    ff_start = lax.axis_index("dp") * ff_here
    hidden_bias_here = lax.dynamic_slice(hidden_bias, (ff_start,), (ff_here,))
    allowed = segment_mask(lengths[0], count)
    scale = 1.0 / math.sqrt(HD)
    inputs = inputs_here.astype(jnp.float32)
    norm_one_b = layer_norm(inputs, gain_one, shift_one).astype(bf)
    mixed = jnp.dot(norm_one_b, whole_in, preferred_element_type=jnp.float32)
    query_b = (mixed[:, :D] + query_bias).astype(bf)
    keys_b = mixed[:, D : D + HD].astype(bf)
    values_b = mixed[:, D + HD :].astype(bf)
    query_heads = query_b.reshape(count, heads, HD)

    def score_table():
        raw = (
            jnp.einsum("thd,sd->hts", query_heads, keys_b, preferred_element_type=jnp.float32)
            * scale
        )
        return jnp.where(allowed[None], raw, -1e30)

    scores = score_table()
    top = jnp.max(scores, axis=-1, keepdims=True)
    expo = jnp.exp(scores - top)
    total = jnp.sum(expo, axis=-1, keepdims=True)
    logsum = top + jnp.log(total)
    probs_b = (expo / total).astype(bf)
    attended_b = (
        jnp.einsum("hts,sd->thd", probs_b, values_b, preferred_element_type=jnp.float32)
        .reshape(count, D)
        .astype(bf)
    )
    middle = inputs + (
        jnp.dot(attended_b, whole_out, preferred_element_type=jnp.float32) + branch_bias
    )
    norm_two_b = layer_norm(middle, gain_two, shift_two).astype(bf)

    norm_all, active_b, grad_hidden_b, branch_parts, grad_norm_two, hidden_sums = ffn(
        groups,
        norm_two_b,
        grad_dealt.reshape(groups, count, D),
        part_up,
        part_down,
        hidden_bias_here.reshape(1, ff_here),
    )
    norm_all = norm_all.reshape(groups * count, D)
    active_b = active_b.reshape(groups * count, ff_here)
    grad_hidden_b = grad_hidden_b.reshape(groups * count, ff_here)
    down_grad = lax.psum_scatter(
        contract_rows(active_b, grad_all).astype(bf), "fsdp", scatter_dimension=0, tiled=True
    )
    up_grad_block = row_sum(parts, groups, grad_hidden_b, norm_all)
    branch_two = lax.psum_scatter(
        branch_parts.reshape(groups * count, D), "dp", scatter_dimension=0, tiled=True
    ).astype(jnp.float32)
    result = middle + (branch_two + output_bias)

    grad_y = grad_here.astype(jnp.float32)
    norm_value_two, pull_two = jax.vjp(layer_norm, middle, gain_two, shift_two)
    grad_middle_norm, grad_gain_two, grad_shift_two = pull_two(grad_norm_two)
    grad_middle = grad_y + grad_middle_norm
    grad_branch_b = grad_middle.astype(bf)
    grad_attended_b = contract_cols(grad_branch_b, whole_out).astype(bf)
    grad_heads = grad_attended_b.reshape(count, heads, HD)
    probs = jnp.exp(score_table() - logsum)
    probs_again_b = probs.astype(bf)
    grad_probs = jnp.einsum("thd,sd->hts", grad_heads, values_b, preferred_element_type=jnp.float32)
    grad_values_b = jnp.einsum(
        "hts,thd->sd", probs_again_b, grad_heads, preferred_element_type=jnp.float32
    ).astype(bf)
    weighted = jnp.sum(probs * grad_probs, axis=-1, keepdims=True)
    grad_scores_b = (probs * (grad_probs - weighted)).astype(bf)
    grad_query_b = (
        (
            jnp.einsum("hts,sd->thd", grad_scores_b, keys_b, preferred_element_type=jnp.float32)
            * scale
        )
        .reshape(count, D)
        .astype(bf)
    )
    grad_keys_b = (
        jnp.einsum("hts,thd->sd", grad_scores_b, query_heads, preferred_element_type=jnp.float32)
        * scale
    ).astype(bf)
    grad_mixed_b = jnp.concatenate([grad_query_b, grad_keys_b, grad_values_b], axis=1)
    grad_norm_one = contract_cols(grad_mixed_b, whole_in)
    norm_value_one, pull_one = jax.vjp(layer_norm, inputs, gain_one, shift_one)
    grad_inputs_norm, grad_gain_one, grad_shift_one = pull_one(grad_norm_one)
    grad_inputs = grad_middle + grad_inputs_norm
    hidden_whole = lax.dynamic_update_slice(
        jnp.zeros((FF,), jnp.float32), hidden_sums[0], (ff_start,)
    )
    vector_grad = jnp.concatenate(
        [
            jnp.stack(
                [
                    grad_gain_one,
                    grad_shift_one,
                    jnp.sum(grad_query_b.astype(jnp.float32), axis=0),
                    jnp.sum(grad_branch_b.astype(jnp.float32), axis=0),
                    grad_gain_two,
                    grad_shift_two,
                    jnp.sum(grad_y, axis=0),
                ],
                axis=0,
            ),
            hidden_whole.reshape(FF // D, D),
        ],
        axis=0,
    )
    vector_grad = vector_grad.reshape(NVEC, owners, rows).transpose(1, 0, 2)
    vector_grad = jnp.pad(vector_grad, ((0, 0), (0, 16 - NVEC), (0, 128 - rows)))
    small_part = jnp.concatenate(
        [
            contract_rows(norm_one_b, grad_mixed_b).astype(bf),
            contract_rows(attended_b, grad_branch_b).astype(bf),
        ],
        axis=1,
    )
    small_grad, back_result, back_grad, grad_up, vector_sum = finish_sums(
        parts,
        groups,
        small_part.reshape(groups // 2, 2, parts, rows, width_in + D),
        result.astype(bf).reshape(parts, piece, D),
        grad_inputs.astype(bf).reshape(parts, piece, D),
        up_grad_block.T.astype(bf).reshape(owners, rows, FF // owners),
        vector_grad,
    )
    grad_up = grad_up.transpose(1, 0, 2).reshape(rows, FF)
    vector_sum = jnp.sum(vector_sum, axis=0)
    grad_in = small_grad[:, :width_in]
    grad_out = small_grad[:, width_in : width_in + D]
    grad_vec = vector_sum[:NVEC, :rows].T
    in_new = adam_update(in_weight, in_first, in_second, grad_in, 1.0 / math.sqrt(D), decay_rate)
    out_new = adam_update(
        out_weight, out_first, out_second, grad_out, 1.0 / math.sqrt(D * 8 // TOK_DEV), decay_rate
    )
    up_new = adam_update(up_weight, up_first, up_second, grad_up, 1.0 / math.sqrt(D), decay_rate)
    down_new = adam_update(
        down_weight, down_first, down_second, down_grad, 1.0 / math.sqrt(FF), decay_rate
    )
    vec_new = adam_update(vectors, vector_first, vector_second, grad_vec, 0.1, 0.0)
    return (undeal(back_result), undeal(back_grad)) + in_new + out_new + up_new + down_new + vec_new


def solution(mesh):
    spec = P(("dp", "fsdp"), None)
    return jax.shard_map(
        shards,
        mesh=mesh,
        in_specs=(spec,) * 19,
        out_specs=(spec,) * 17,
        check_vma=False,
    )
```

```python
import functools
import math

import jax
import jax.numpy as jnp
from jax import lax
from jax.experimental import pallas as pl
from jax.experimental.pallas import tpu as pltpu
from jax.sharding import PartitionSpec as P

D = 2048
FF = 8192
HD = 128
TOK_DEV = 384
STEP = 5
NVEC = 11


eps_norm = 1e-05
beta_one = 0.5
beta_two = 0.5
adam_eps = 1e-08
decay_rate = 0.1


def layer_norm(values, gain, shift):
    centered = values - jnp.mean(values, axis=-1, keepdims=True)
    scaled = centered * lax.rsqrt(jnp.mean(centered * centered, axis=-1, keepdims=True) + eps_norm)
    return scaled * gain + shift


def gelu_tanh(values):
    return (
        0.5
        * values
        * (1.0 + jnp.tanh(0.7978845608028654 * (values + 0.044715 * values * values * values)))
    )


def segment_mask(sizes, count):
    ends = jnp.cumsum(sizes)
    places = jnp.arange(count, dtype=jnp.int32)
    labels = jnp.sum((places[:, None] >= ends[None, :]).astype(jnp.int32), axis=1)
    return (labels[:, None] == labels[None, :]) & (places[None, :] <= places[:, None])


def adam_update(weight, first, second, grad, rate, decay):
    grad = grad.astype(jnp.float32)
    first_new = beta_one * first + (1.0 - beta_one) * grad
    second_new = beta_two * second + (1.0 - beta_two) * grad * grad
    fix_one = 1.0 - beta_one**STEP
    fix_two = 1.0 - beta_two**STEP
    step_size = first_new / fix_one / (jnp.sqrt(second_new / fix_two) + adam_eps)
    weight_new = weight - rate * (step_size + decay * weight)
    return (weight_new, first_new, second_new)


def contract_rows(left, right):
    return lax.dot_general(
        left, right, (((0,), (0,)), ((), ())), preferred_element_type=jnp.float32
    )


def contract_cols(left, right):
    return lax.dot_general(
        left, right, (((1,), (1,)), ((), ())), preferred_element_type=jnp.float32
    )


MESH = pl.DeviceIdType.MESH
F32 = jnp.float32
BF = jnp.bfloat16


def wrap(value, count):
    return lax.rem(value + 2 * count, count)


def ring_place(index, parts):
    if parts != 8:
        return index
    z, y = lax.div(index, 2), lax.rem(index, 2)
    return z + y * (7 - 2 * z)


def ring_index(place, parts):
    place = wrap(place, parts)
    if parts != 8:
        return place
    back = lax.div(place, 4)
    return (1 - back) * 2 * place + back * (15 - 2 * place)


def remote(src, dst, send, recv, dp, fs):
    return pltpu.make_async_remote_copy(
        src_ref=src, dst_ref=dst, send_sem=send, recv_sem=recv, device_id=(dp, fs), device_id_type=MESH
    )


def lasting(micros):
    return pl.CostEstimate(
        flops=int(micros * 1.1e9), bytes_accessed=int(micros * 3.3e6), transcendentals=0
    )


def greet(targets):
    barrier = pltpu.get_barrier_semaphore()
    for dp, fs in targets:
        pl.semaphore_signal(barrier, inc=1, device_id=(dp, fs), device_id_type=MESH)
    pl.semaphore_wait(barrier, len(targets))


def greet_all(me, parts, owners):
    barrier = pltpu.get_barrier_semaphore()

    def one(i, carry):
        peer = wrap(me + i, owners)
        pl.semaphore_signal(
            barrier, inc=1, device_id=(lax.div(peer, parts), lax.rem(peer, parts)), device_id_type=MESH
        )
        return carry

    lax.fori_loop(1, owners, one, 0)
    pl.semaphore_wait(barrier, owners - 1)


def loop(low, high, body):
    def one(i, carry):
        body(i)
        return carry

    lax.fori_loop(low, high, one, 0)


def deal_copy(parts, dp, f, src, dst, send, recv, d, came=False):
    to = wrap(f + d, parts)
    place = wrap(f - d, parts) if came else f
    return remote(src.at[to], dst.at[place], send.at[d], recv.at[d], dp, to)


def owner_copy(me, parts, owners, src, dst, send, recv, d, came=False):
    to = wrap(me + d, owners)
    place = wrap(me - d, owners) if came else me
    return remote(
        src.at[to], dst.at[place], send.at[d], recv.at[d], lax.div(to, parts), lax.rem(to, parts)
    )


def spread_kernel(
    parts, groups,
    xd, gd, inb, ovb,
    xo, eall, win, wov,
    local, xs, xr, gs, gr, rs, rr, ns, nr, ss, sr, ens, enr, ess, esr,
):
    dp, f = lax.axis_index("dp"), lax.axis_index("fsdp")
    owners, rows_x = groups * parts, groups // 2
    x, core = lax.div(dp, 2), lax.rem(dp, 2)
    sib = x * 2 + 1 - core
    me = dp * parts + f
    p = ring_place(f, parts)
    nxt, prv = ring_index(p + 1, parts), ring_index(p - 1, parts)
    whole = (win, wov)
    mine = [
        pltpu.make_async_copy(inb, win.at[me], local.at[0]),
        pltpu.make_async_copy(ovb, wov.at[me], local.at[1]),
        pltpu.make_async_copy(xd.at[f], xo.at[f], local.at[2]),
        pltpu.make_async_copy(gd.at[f], eall.at[dp, f], local.at[3]),
    ]
    for copy in mine:
        copy.start()
    greet(
        [(dp, wrap(f + d, parts)) for d in range(1, parts)]
        + [(sib, f)]
        + [(wrap(x + dx, rows_x) * 2 + core, f) for dx in range(1, rows_x)]
    )
    for copy in mine:
        copy.wait()

    def x_copies(d, came=False):
        return deal_copy(parts, dp, f, xd, xo, xs, xr, d, came)

    def g_copies(d, came=False):
        return deal_copy(parts, dp, f, gd, eall.at[dp], gs, gr, d, came)

    def origin(h, s):
        return ring_index(p - s if h == 0 else p + s, parts)

    def ring_send(h, s):
        ref = whole[h].at[dp * parts + origin(h, s)]
        return remote(ref, ref, rs.at[h, s], rr.at[h, s], dp, nxt if h == 0 else prv)

    def ring_recv(h, s):
        ref = whole[h].at[dp * parts + origin(h, s)]
        return remote(ref, ref, rs.at[h, s - 1], rr.at[h, s - 1], dp, nxt if h == 0 else prv)

    def x_send(h, s, dx):
        ref = whole[h].at[dp * parts + origin(h, s)]
        to = wrap(x + dx, rows_x) * 2 + core
        return remote(ref, ref, ns.at[h, s, dx], nr.at[h, s, dx], to, f)

    def x_recv(h, s, dx):
        came = wrap(x - dx, rows_x) * 2 + core
        ref = whole[h].at[came * parts + origin(h, s)]
        return remote(ref, ref, ns.at[h, s, dx], nr.at[h, s, dx], came, f)

    def sib_send(h, s, dx):
        came = wrap(x - dx, rows_x) * 2 + core
        ref = whole[h].at[came * parts + origin(h, s)]
        return remote(ref, ref, ss.at[h, s, dx], sr.at[h, s, dx], sib, f)

    def sib_recv(h, s, dx):
        came = wrap(x - dx, rows_x) * 2 + 1 - core
        ref = whole[h].at[came * parts + origin(h, s)]
        return remote(ref, ref, ss.at[h, s, dx], sr.at[h, s, dx], sib, f)

    def e_x_send(d, dx):
        ref = eall.at[dp, wrap(f - d, parts)]
        to = wrap(x + dx, rows_x) * 2 + core
        return remote(ref, ref, ens.at[d, dx], enr.at[d, dx], to, f)

    def e_x_recv(d, dx):
        came = wrap(x - dx, rows_x) * 2 + core
        ref = eall.at[came, wrap(f - d, parts)]
        return remote(ref, ref, ens.at[d, dx], enr.at[d, dx], came, f)

    def e_sib_send(d, dx):
        came = wrap(x - dx, rows_x) * 2 + core
        ref = eall.at[came, wrap(f - d, parts)]
        return remote(ref, ref, ess.at[d, dx], esr.at[d, dx], sib, f)

    def e_sib_recv(d, dx):
        came = wrap(x - dx, rows_x) * 2 + 1 - core
        ref = eall.at[came, wrap(f - d, parts)]
        return remote(ref, ref, ess.at[d, dx], esr.at[d, dx], sib, f)

    def ring_step(s):
        for h in range(2):
            @pl.when(s > 0)
            def _():
                ring_recv(h, s).wait_recv()

            @pl.when(s < parts - 1)
            def _():
                ring_send(h, s).start()

            for dx in range(1, rows_x):
                x_send(h, s, dx).start()
            sib_send(h, s, 0).start()

    def e_step(d):
        @pl.when(d > 0)
        def _():
            g_copies(d, True).wait_recv()

        for dx in range(1, rows_x):
            e_x_send(d, dx).start()
        e_sib_send(d, 0).start()

    def relay(s):
        for h in range(2):
            for dx in range(1, rows_x):
                x_recv(h, s, dx).wait_recv()
                sib_send(h, s, dx).start()

    def e_relay(d):
        for dx in range(1, rows_x):
            e_x_recv(d, dx).wait_recv()
            e_sib_send(d, dx).start()

    def main(s):
        @pl.when(s < parts)
        def _():
            ring_step(s)

        @pl.when(s < parts - 1)
        def _():
            x_copies(s + 1).start()
            g_copies(s + 1).start()

        @pl.when((s >= 1) & (s <= parts))
        def _():
            e_step(s - 1)

        @pl.when((s >= 2) & (s < parts + 2))
        def _():
            relay(s - 2)

        @pl.when(s >= 3)
        def _():
            e_relay(s - 3)

    loop(0, parts + 3, main)

    def finish(s):
        for h in range(2):
            @pl.when(s < parts - 1)
            def _():
                ring_send(h, s).wait_send()

            for dx in range(1, rows_x):
                x_send(h, s, dx).wait_send()
            for dx in range(rows_x):
                sib_recv(h, s, dx).wait_recv()
                sib_send(h, s, dx).wait_send()
        for dx in range(1, rows_x):
            e_x_send(s, dx).wait_send()
        for dx in range(rows_x):
            e_sib_recv(s, dx).wait_recv()
            e_sib_send(s, dx).wait_send()

        @pl.when(s > 0)
        def _():
            x_copies(s, True).wait_recv()
            x_copies(s).wait_send()
            g_copies(s).wait_send()

    loop(0, parts, finish)


def exchange_kernel(parts, groups, src, dst, local, us, ur):
    dp, f = lax.axis_index("dp"), lax.axis_index("fsdp")
    owners = groups * parts
    me = dp * parts + f
    mine = pltpu.make_async_copy(src.at[me], dst.at[me], local)
    mine.start()
    greet_all(me, parts, owners)
    loop(1, owners, lambda d: owner_copy(me, parts, owners, src, dst, us, ur, d).start())
    mine.wait()

    def finish(d):
        owner_copy(me, parts, owners, src, dst, us, ur, d, True).wait_recv()
        owner_copy(me, parts, owners, src, dst, us, ur, d).wait_send()

    loop(1, owners, finish)


def exchange(parts, groups, src):
    owners = groups * parts
    dma = pltpu.SemaphoreType.DMA
    return pl.pallas_call(
        functools.partial(exchange_kernel, parts, groups),
        out_shape=jax.ShapeDtypeStruct(src.shape, BF),
        in_specs=[pl.BlockSpec(memory_space=pl.ANY)],
        out_specs=pl.BlockSpec(memory_space=pl.ANY),
        scratch_shapes=[dma(()), dma((owners,)), dma((owners,))],
        compiler_params=pltpu.CompilerParams(collective_id=5, has_side_effects=True),
        cost_estimate=lasting(25),
    )(src)


def spread(parts, groups, xd, gd, inb, ovb):
    owners, rows_x = groups * parts, groups // 2
    dma = pltpu.SemaphoreType.DMA
    return pl.pallas_call(
        functools.partial(spread_kernel, parts, groups),
        out_shape=(
            jax.ShapeDtypeStruct(xd.shape, BF),
            jax.ShapeDtypeStruct((groups,) + gd.shape, BF),
            jax.ShapeDtypeStruct((owners,) + inb.shape, BF),
            jax.ShapeDtypeStruct((owners,) + ovb.shape, BF),
        ),
        in_specs=[pl.BlockSpec(memory_space=pl.ANY)] * 4,
        out_specs=(pl.BlockSpec(memory_space=pl.ANY),) * 4,
        scratch_shapes=[
            dma((4,)),
            dma((parts,)), dma((parts,)), dma((parts,)), dma((parts,)),
            dma((2, parts)), dma((2, parts)),
            dma((2, parts, rows_x)), dma((2, parts, rows_x)),
            dma((2, parts, rows_x)), dma((2, parts, rows_x)),
            dma((parts, rows_x)), dma((parts, rows_x)),
            dma((parts, rows_x)), dma((parts, rows_x)),
        ],
        compiler_params=pltpu.CompilerParams(collective_id=0, has_side_effects=True),
        cost_estimate=lasting(200),
    )(xd, gd, inb, ovb)


def ffn_kernel(
    groups, chunks,
    src, eall, w1, w2, b1,
    hall, act, dhid, ypart, dsum, hsum,
    hb, eb, ab, db, yb, pown, psib, sibr, xb, xrb,
    local, ns, nr, ss, sr, hs, es, as_, ds, ys, gss, gsr, gns, gnr,
):
    dp, f = lax.axis_index("dp"), lax.axis_index("fsdp")
    rows_x = groups // 2
    x, core = lax.div(dp, 2), lax.rem(dp, 2)
    sib = x * 2 + 1 - core
    count, width = src.shape
    units = w1.shape[0]
    size, cut = count // chunks, width // chunks
    tile = min(256, units)
    mine = pltpu.make_async_copy(src, hall.at[dp], local)
    mine.start()
    greet([(sib, f)] + [(wrap(x + dx, rows_x) * 2 + core, f) for dx in range(1, rows_x)])

    def part(ref, k):
        return ref.at[pl.ds(k * size, size)]

    def x_send(k, dx):
        to = wrap(x + dx, rows_x) * 2 + core
        return remote(part(src, k), part(hall.at[dp], k), ns.at[k, dx], nr.at[k, dx], to, f)

    def x_recv(k, dx):
        came = wrap(x - dx, rows_x) * 2 + core
        ref = part(hall.at[came], k)
        return remote(ref, ref, ns.at[k, dx], nr.at[k, dx], came, f)

    def own_send(k):
        return remote(part(src, k), part(hall.at[dp], k), ss.at[k, 0], sr.at[k, 0], sib, f)

    def sib_send(k, dx):
        came = wrap(x - dx, rows_x) * 2 + core
        ref = part(hall.at[came], k)
        return remote(ref, ref, ss.at[k, dx], sr.at[k, dx], sib, f)

    def sib_recv(k, dx):
        came = wrap(x - dx, rows_x) * 2 + 1 - core
        ref = part(hall.at[came], k)
        return remote(ref, ref, ss.at[k, dx], sr.at[k, dx], sib, f)

    def cols(k):
        return pl.ds(pl.multiple_of(k * cut, cut), cut)

    def sum_sib(dx, k):
        return remote(
            psib.at[dx, :, cols(k)], sibr.at[dx, :, cols(k)], gss.at[dx, k], gsr.at[dx, k], sib, f
        )

    def sum_x(dx, k):
        to = wrap(x + dx, rows_x) * 2 + core
        return remote(
            xb.at[dx - 1, :, cols(k)], xrb.at[dx - 1, :, cols(k)],
            gns.at[dx, k], gnr.at[dx, k], to, f,
        )

    def group_of(dx, c):
        return wrap(x + dx, rows_x) * 2 + (core if c == 0 else 1 - core)

    def side(c):
        return slice(c * count, (c + 1) * count)

    def a_copy(dx, c):
        return pltpu.make_async_copy(ab.at[dx, side(c)], act.at[group_of(dx, c)], as_.at[dx, c])

    def d_copy(dx, c):
        return pltpu.make_async_copy(db.at[side(c)], dhid.at[group_of(dx, c)], ds.at[dx, c])

    def h_load(dx, c):
        return pltpu.make_async_copy(hall.at[group_of(dx, c)], hb.at[side(c)], hs.at[c])

    def e_load(dx, c):
        return pltpu.make_async_copy(eall.at[group_of(dx, c)], eb.at[side(c)], es.at[c])

    for k in range(chunks):
        for dx in range(1, rows_x):
            x_send(k, dx).start()
    for k in range(chunks):
        own_send(k).start()
    mine.wait()

    hsum[...] = jnp.zeros_like(hsum)

    def one(dx):
        came = wrap(rows_x - dx, rows_x)
        for c in range(2):
            e_load(dx, c).start()

        @pl.when(dx > 0)
        def _():
            for k in range(chunks):
                x_recv(k, came).wait_recv()
                sib_send(k, came).start()

        h_load(dx, 0).start()
        for k in range(chunks):
            sib_recv(k, came).wait_recv()
        h_load(dx, 1).start()

        @pl.when(dx > 0)
        def _():
            for c in range(2):
                d_copy(dx - 1, c).wait()

        for c in range(2):
            e_load(dx, c).wait()
            h_load(dx, c).wait()

        def hidden(t):
            columns = pl.ds(pl.multiple_of(t * tile, tile), tile)
            u = lax.dot_general(
                hb[...], w1[columns, :], (((1,), (1,)), ((), ())), preferred_element_type=F32
            ) + b1[:, columns]
            da = lax.dot_general(
                eb[...], w2[columns, :], (((1,), (1,)), ((), ())), preferred_element_type=F32
            )
            square = u * u
            th = jnp.tanh(0.7978845608028654 * (u + 0.044715 * square * u))
            half_sum = 0.5 * (1.0 + th)
            slope = half_sum + 0.5 * u * (1.0 - th * th) * (
                0.7978845608028654 * (1.0 + 3.0 * 0.044715 * square)
            )
            ab[dx, :, columns] = (u * half_sum).astype(BF)
            du = (slope * da).astype(BF)
            db[:, columns] = du
            hsum[:, columns] += jnp.sum(du.astype(F32), axis=0, keepdims=True)

        loop(0, units // tile, hidden)
        for c in range(2):
            a_copy(dx, c).start()
            d_copy(dx, c).start()

        def other_side(k):
            psib[dx, :, cols(k)] = jnp.dot(
                db[side(1), :], w1[:, cols(k)], preferred_element_type=F32
            ).astype(BF)
            sum_sib(dx, k).start()

        loop(0, chunks, other_side)

        def own_side(k):
            dh = jnp.dot(db[side(0), :], w1[:, cols(k)], preferred_element_type=F32)

            @pl.when(dx == 0)
            def _():
                pown[:, cols(k)] = dh

            @pl.when(dx > 0)
            def _():
                sum_sib(dx, k).wait_recv()
                xb[dx - 1, :, cols(k)] = (dh + sibr[dx, :, cols(k)].astype(F32)).astype(BF)
                sum_x(dx, k).start()

        loop(0, chunks, own_side)

    loop(0, rows_x, one)

    def y_copy(dx, c):
        return pltpu.make_async_copy(yb.at[c], ypart.at[group_of(dx, c)], ys.at[dx, c])

    def y_one(dx):
        for c in range(2):
            @pl.when(dx > 0)
            def _():
                y_copy(dx - 1, c).wait()

            def block(k):
                yb[c, :, cols(k)] = jnp.dot(
                    ab[dx, side(c), :], w2[:, cols(k)], preferred_element_type=F32
                ).astype(BF)

            loop(0, chunks, block)
            y_copy(dx, c).start()

    loop(0, rows_x, y_one)

    def collect(k):
        sum_sib(0, k).wait_recv()
        total = pown[:, cols(k)] + sibr[0, :, cols(k)].astype(F32)
        for dx in range(1, rows_x):
            sum_x(dx, k).wait_recv()
            total = total + xrb[dx - 1, :, cols(k)].astype(F32)
        dsum[:, cols(k)] = total

    loop(0, chunks, collect)

    def last(k):
        for dx in range(rows_x):
            sum_sib(dx, k).wait_send()
        for dx in range(1, rows_x):
            sum_x(dx, k).wait_send()
            x_send(k, dx).wait_send()
            sib_send(k, dx).wait_send()
        own_send(k).wait_send()

    loop(0, chunks, last)

    def drain(dx):
        for c in range(2):
            a_copy(dx, c).wait()

    loop(0, rows_x, drain)
    for c in range(2):
        d_copy(rows_x - 1, c).wait()
        y_copy(rows_x - 1, c).wait()


def ffn(groups, src, eall, w1, w2, b1):
    chunks, rows_x = 4, groups // 2
    count, width = src.shape
    units = w1.shape[0]
    dma = pltpu.SemaphoreType.DMA
    hbm = pl.BlockSpec(memory_space=pl.ANY)
    vmem = pl.BlockSpec(memory_space=pltpu.VMEM)
    return pl.pallas_call(
        functools.partial(ffn_kernel, groups, chunks),
        out_shape=(
            jax.ShapeDtypeStruct((groups, count, width), BF),
            jax.ShapeDtypeStruct((groups, count, units), BF),
            jax.ShapeDtypeStruct((groups, count, units), BF),
            jax.ShapeDtypeStruct((groups, count, width), BF),
            jax.ShapeDtypeStruct((count, width), F32),
            jax.ShapeDtypeStruct((1, units), F32),
        ),
        in_specs=[hbm, hbm, vmem, vmem, vmem],
        out_specs=(hbm,) * 4 + (vmem,) * 2,
        scratch_shapes=[
            pltpu.VMEM((2 * count, width), BF),
            pltpu.VMEM((2 * count, width), BF),
            pltpu.VMEM((rows_x, 2 * count, units), BF),
            pltpu.VMEM((2 * count, units), BF),
            pltpu.VMEM((2, count, width), BF),
            pltpu.VMEM((count, width), F32),
            pltpu.VMEM((rows_x, count, width), BF),
            pltpu.VMEM((rows_x, count, width), BF),
            pltpu.VMEM((rows_x - 1, count, width), BF),
            pltpu.VMEM((rows_x - 1, count, width), BF),
            dma(()),
            dma((chunks, rows_x)), dma((chunks, rows_x)),
            dma((chunks, rows_x)), dma((chunks, rows_x)),
            dma((2,)), dma((2,)),
            dma((rows_x, 2)), dma((rows_x, 2)), dma((rows_x, 2)),
            dma((rows_x, chunks)), dma((rows_x, chunks)),
            dma((rows_x, chunks)), dma((rows_x, chunks)),
        ],
        compiler_params=pltpu.CompilerParams(
            collective_id=1, has_side_effects=True, vmem_limit_bytes=60 * 2**20
        ),
        cost_estimate=lasting(95),
    )(src, eall, w1, w2, b1)


def row_sum_kernel(parts, groups, left, right, out, acc, got, gone, rs, rr):
    dp, f = lax.axis_index("dp"), lax.axis_index("fsdp")
    p = ring_place(f, parts)
    nxt, prv = ring_index(p + 1, parts), ring_index(p - 1, parts)
    block, width = out.shape
    streams = acc.shape[0]
    cut = width // streams
    greet([(dp, nxt), (dp, prv)])

    def copy(h, s):
        return remote(
            gone.at[h, lax.rem(s, 2)], got.at[h, s], rs.at[h, s], rr.at[h, s],
            dp, nxt if h % 2 == 0 else prv,
        )

    def step(s):
        for h in range(streams):
            c = ring_index(p - 1 - s if h % 2 == 0 else p + 1 + s, parts)
            if len(left.shape) == 2:
                piece = left[:, pl.ds(pl.multiple_of(c * block, block), block)]
            else:
                piece = left[c]
            columns = slice(h * cut, (h + 1) * cut)
            acc[h] = lax.dot_general(
                piece, right[:, columns], (((0,), (0,)), ((), ())), preferred_element_type=F32
            )

            @pl.when(s > 0)
            def _():
                copy(h, s - 1).wait_recv()
                acc[h] += got[h, s - 1].astype(F32)

            @pl.when((s >= 2) & (s < parts - 1))
            def _():
                copy(h, s - 2).wait_send()

            @pl.when(s < parts - 1)
            def _():
                gone[h, lax.rem(s, 2)] = acc[h].astype(BF)
                copy(h, s).start()

            @pl.when(s == parts - 1)
            def _():
                out[:, columns] = acc[h]

    loop(0, parts, step)
    for h in range(streams):
        for s in range(max(parts - 3, 0), parts - 1):
            copy(h, s).wait_send()


def row_sum(parts, groups, left, right):
    width = right.shape[1]
    block = FF // (groups * parts)
    streams = 4
    if block % 128:
        left = left.reshape(left.shape[0], parts, block).transpose(1, 0, 2)
    dma = pltpu.SemaphoreType.DMA
    vmem = pl.BlockSpec(memory_space=pltpu.VMEM)
    return pl.pallas_call(
        functools.partial(row_sum_kernel, parts, groups),
        out_shape=jax.ShapeDtypeStruct((block, width), F32),
        in_specs=[vmem] * 2,
        out_specs=vmem,
        scratch_shapes=[
            pltpu.VMEM((streams, block, width // streams), F32),
            pltpu.VMEM((streams, parts - 1, block, width // streams), BF),
            pltpu.VMEM((streams, 2, block, width // streams), BF),
            dma((streams, parts)), dma((streams, parts)),
        ],
        compiler_params=pltpu.CompilerParams(
            collective_id=3, has_side_effects=True, vmem_limit_bytes=56 * 2**20
        ),
        cost_estimate=lasting(95),
    )(left, right)


def finish_kernel(
    parts, groups,
    grads, res, gx, upg, vec,
    total, res_out, gx_out, upg_out, vec_out,
    loc, sibr, xb, xrb, got, gone,
    local, ls, ss, sr, ns, nr, rs, rr, as_, ar, bs, br, us, ur, vs, vr,
):
    dp, f = lax.axis_index("dp"), lax.axis_index("fsdp")
    owners, rows_x = groups * parts, groups // 2
    x, core = lax.div(dp, 2), lax.rem(dp, 2)
    sib = x * 2 + 1 - core
    me = dp * parts + f
    p = ring_place(f, parts)
    nxt, prv = ring_index(p + 1, parts), ring_index(p - 1, parts)
    half = grads.shape[4] // 2
    mine = [
        pltpu.make_async_copy(res.at[f], res_out.at[f], local.at[0]),
        pltpu.make_async_copy(gx.at[f], gx_out.at[f], local.at[1]),
        pltpu.make_async_copy(upg.at[me], upg_out.at[me], local.at[2]),
        pltpu.make_async_copy(vec.at[me], vec_out.at[me], local.at[3]),
    ]
    for copy in mine:
        copy.start()
    greet_all(me, parts, owners)

    def chunk(h, s):
        return ring_index(p - 1 - s if h == 0 else p + 1 + s, parts)

    def sib_copy(h, s):
        piece = grads.at[:, 1 - core, chunk(h, s), :, pl.ds(h * half, half)]
        return remote(piece, sibr.at[h, s], ss.at[h, s], sr.at[h, s], sib, f)

    def own_copy(h, s):
        piece = grads.at[:, core, chunk(h, s), :, pl.ds(h * half, half)]
        return pltpu.make_async_copy(piece, loc.at[h, s], ls.at[h, s])

    def x_copy(h, s, dx):
        to = wrap(x + dx, rows_x) * 2 + core
        return remote(
            xb.at[h, s, dx - 1], xrb.at[h, s, dx - 1], ns.at[h, s, dx], nr.at[h, s, dx], to, f
        )

    def ring_copy(h, s):
        return remote(
            gone.at[h, s], got.at[h, s], rs.at[h, s], rr.at[h, s], dp, nxt if h == 0 else prv
        )

    def res_copies(d, came=False):
        return deal_copy(parts, dp, f, res, res_out, as_, ar, d, came)

    def gx_copies(d, came=False):
        return deal_copy(parts, dp, f, gx, gx_out, bs, br, d, came)

    def upg_copies(d, came=False):
        return owner_copy(me, parts, owners, upg, upg_out, us, ur, d, came)

    def vec_copies(d, came=False):
        return owner_copy(me, parts, owners, vec, vec_out, vs, vr, d, came)

    def begin(s):
        for h in range(2):
            sib_copy(h, s).start()
            own_copy(h, s).start()

    def pair(s):
        for h in range(2):
            sib_copy(h, s).wait_recv()
            own_copy(h, s).wait()
            for dx in range(1, rows_x):
                to = wrap(x + dx, rows_x)
                xb[h, s, dx - 1] = (sibr[h, s, to].astype(F32) + loc[h, s, to].astype(F32)).astype(BF)
                x_copy(h, s, dx).start()

    def step(s):
        for h in range(2):
            for dx in range(1, rows_x):
                x_copy(h, s, dx).wait_recv()

            def value():
                here = sibr[h, s, x].astype(F32) + loc[h, s, x].astype(F32)
                for dx in range(1, rows_x):
                    here = here + xrb[h, s, dx - 1].astype(F32)
                return here

            @pl.when(s == 0)
            def _():
                gone[h, s] = value().astype(BF)
                ring_copy(h, s).start()

            @pl.when((s > 0) & (s < parts - 1))
            def _():
                ring_copy(h, s - 1).wait_recv()
                gone[h, s] = (value() + got[h, s - 1].astype(F32)).astype(BF)
                ring_copy(h, s).start()

            @pl.when(s == parts - 1)
            def _():
                ring_copy(h, s - 1).wait_recv()
                total[:, h * half : (h + 1) * half] = value() + got[h, s - 1].astype(F32)

    each = -(-(owners - 1) // parts)
    ahead, near = min(4, parts), min(2, parts)
    for s in range(ahead):
        begin(s)
    for s in range(near):
        pair(s)

    def main(s):
        @pl.when(s < parts - ahead)
        def _():
            begin(s + ahead)

        @pl.when(s < parts - near)
        def _():
            pair(s + near)

        step(s)

        @pl.when(s < parts - 1)
        def _():
            res_copies(s + 1).start()
            gx_copies(s + 1).start()

        for j in range(each):
            d = s * each + 1 + j

            @pl.when(d < owners)
            def _():
                upg_copies(d).start()
                vec_copies(d).start()

    loop(0, parts, main)

    def finish(s):
        for h in range(2):
            sib_copy(h, s).wait_send()
            for dx in range(1, rows_x):
                x_copy(h, s, dx).wait_send()

            @pl.when(s < parts - 1)
            def _():
                ring_copy(h, s).wait_send()

        @pl.when(s > 0)
        def _():
            for copies in (res_copies, gx_copies):
                copies(s, True).wait_recv()
                copies(s).wait_send()

    loop(0, parts, finish)

    def owner_finish(d):
        for copies in (upg_copies, vec_copies):
            copies(d, True).wait_recv()
            copies(d).wait_send()

    loop(1, owners, owner_finish)
    for copy in mine:
        copy.wait()


def finish_sums(parts, groups, grads, res, gx, upg, vec):
    owners, rows_x = groups * parts, groups // 2
    rows, width = grads.shape[3:]
    half = width // 2
    dma = pltpu.SemaphoreType.DMA
    hbm = pl.BlockSpec(memory_space=pl.ANY)
    return pl.pallas_call(
        functools.partial(finish_kernel, parts, groups),
        out_shape=(
            jax.ShapeDtypeStruct((rows, width), F32),
            jax.ShapeDtypeStruct(res.shape, BF),
            jax.ShapeDtypeStruct(gx.shape, BF),
            jax.ShapeDtypeStruct(upg.shape, BF),
            jax.ShapeDtypeStruct(vec.shape, F32),
        ),
        in_specs=[hbm] * 5,
        out_specs=(pl.BlockSpec(memory_space=pltpu.VMEM),) + (hbm,) * 4,
        scratch_shapes=[
            pltpu.VMEM((2, parts, rows_x, rows, half), BF),
            pltpu.VMEM((2, parts, rows_x, rows, half), BF),
            pltpu.VMEM((2, parts, rows_x - 1, rows, half), BF),
            pltpu.VMEM((2, parts, rows_x - 1, rows, half), BF),
            pltpu.VMEM((2, parts, rows, half), BF),
            pltpu.VMEM((2, parts, rows, half), BF),
            dma((4,)),
            dma((2, parts)), dma((2, parts)), dma((2, parts)),
            dma((2, parts, rows_x)), dma((2, parts, rows_x)),
            dma((2, parts)), dma((2, parts)),
            dma((parts,)), dma((parts,)), dma((parts,)), dma((parts,)),
            dma((owners,)), dma((owners,)), dma((owners,)), dma((owners,)),
        ],
        compiler_params=pltpu.CompilerParams(
            collective_id=4, has_side_effects=True, vmem_limit_bytes=60 * 2**20
        ),
        cost_estimate=lasting(140),
    )(grads, res, gx, upg, vec)


def shards(
    tokens,
    cotangent,
    lengths,
    routing,
    in_weight,
    in_first,
    in_second,
    out_weight,
    out_first,
    out_second,
    up_weight,
    up_first,
    up_second,
    down_weight,
    down_first,
    down_second,
    vectors,
    vector_first,
    vector_second,
):
    bf = jnp.bfloat16
    heads = D // HD
    count = tokens.shape[0]
    parts = lax.axis_size("fsdp")
    groups = lax.axis_size("dp")
    both = ("dp", "fsdp")
    piece = count // parts
    width_in = D + 2 * HD
    slots = jnp.arange(parts, dtype=jnp.int32)
    order = routing[0]
    inverse = jnp.sum(jnp.where(order[:, None] == slots[None, :], slots[:, None], 0), axis=0)

    def deal(array):
        return jnp.take(array.reshape(parts, piece, D), inverse, axis=0)

    def undeal(array):
        return jnp.take(array, order, axis=0).reshape(count, D)

    rows = in_weight.shape[0]
    owners = groups * parts
    out_vec = jnp.concatenate(
        [out_weight.astype(bf), jnp.pad(vectors.astype(bf), ((0, 0), (0, 128 - NVEC)))], axis=1
    )
    up_pieces = up_weight.astype(bf).reshape(rows, owners, FF // owners).transpose(1, 0, 2)
    up_block, dealt, dealt_grad, out_vec = lax.optimization_barrier(
        (exchange(parts, groups, up_pieces), deal(tokens), deal(cotangent), out_vec)
    )
    x_dealt, grad_dealt, whole_in, whole_out = spread(
        parts, groups, dealt, dealt_grad, in_weight.astype(bf), out_vec
    )
    inputs_here = x_dealt.reshape(count, D)
    grad_all = grad_dealt.reshape(groups * count, D)
    grad_here = lax.dynamic_index_in_dim(
        grad_dealt, lax.axis_index("dp"), 0, keepdims=False
    ).reshape(count, D)
    whole_in = whole_in.reshape(D, width_in)
    whole_out = whole_out.reshape(D, D + 128)
    part_down = lax.all_gather(down_weight.astype(bf), "fsdp", axis=0, tiled=True)
    part_up = lax.all_gather(up_block.reshape(D, FF // owners).T, "fsdp", axis=0, tiled=True)

    table = whole_out[:, D : D + NVEC].astype(jnp.float32)
    whole_out = whole_out[:, :D]
    gain_one = table[:, 0]
    shift_one = table[:, 1]
    query_bias = table[:, 2]
    branch_bias = table[:, 3]
    gain_two = table[:, 4]
    shift_two = table[:, 5]
    output_bias = table[:, 6]
    hidden_bias = table[:, 7:].T.reshape(FF)
    ff_here = FF // groups
    ff_start = lax.axis_index("dp") * ff_here
    hidden_bias_here = lax.dynamic_slice(hidden_bias, (ff_start,), (ff_here,))
    allowed = segment_mask(lengths[0], count)
    scale = 1.0 / math.sqrt(HD)
    inputs = inputs_here.astype(jnp.float32)
    norm_one_b = layer_norm(inputs, gain_one, shift_one).astype(bf)
    mixed = jnp.dot(norm_one_b, whole_in, preferred_element_type=jnp.float32)
    query_b = (mixed[:, :D] + query_bias).astype(bf)
    keys_b = mixed[:, D : D + HD].astype(bf)
    values_b = mixed[:, D + HD :].astype(bf)
    query_heads = query_b.reshape(count, heads, HD)

    def score_table():
        raw = (
            jnp.einsum("thd,sd->hts", query_heads, keys_b, preferred_element_type=jnp.float32)
            * scale
        )
        return jnp.where(allowed[None], raw, -1e30)

    scores = score_table()
    top = jnp.max(scores, axis=-1, keepdims=True)
    expo = jnp.exp(scores - top)
    total = jnp.sum(expo, axis=-1, keepdims=True)
    logsum = top + jnp.log(total)
    probs_b = (expo / total).astype(bf)
    attended_b = (
        jnp.einsum("hts,sd->thd", probs_b, values_b, preferred_element_type=jnp.float32)
        .reshape(count, D)
        .astype(bf)
    )
    middle = inputs + (
        jnp.dot(attended_b, whole_out, preferred_element_type=jnp.float32) + branch_bias
    )
    norm_two_b = layer_norm(middle, gain_two, shift_two).astype(bf)

    norm_all, active_b, grad_hidden_b, branch_parts, grad_norm_two, hidden_sums = ffn(
        groups,
        norm_two_b,
        grad_dealt.reshape(groups, count, D),
        part_up,
        part_down,
        hidden_bias_here.reshape(1, ff_here),
    )
    norm_all = norm_all.reshape(groups * count, D)
    active_b = active_b.reshape(groups * count, ff_here)
    grad_hidden_b = grad_hidden_b.reshape(groups * count, ff_here)
    down_grad = lax.psum_scatter(
        contract_rows(active_b, grad_all).astype(bf), "fsdp", scatter_dimension=0, tiled=True
    )
    up_grad_block = row_sum(parts, groups, grad_hidden_b, norm_all)
    branch_two = lax.psum_scatter(
        branch_parts.reshape(groups * count, D), "dp", scatter_dimension=0, tiled=True
    ).astype(jnp.float32)
    result = middle + (branch_two + output_bias)

    grad_y = grad_here.astype(jnp.float32)
    norm_value_two, pull_two = jax.vjp(layer_norm, middle, gain_two, shift_two)
    grad_middle_norm, grad_gain_two, grad_shift_two = pull_two(grad_norm_two)
    grad_middle = grad_y + grad_middle_norm
    grad_branch_b = grad_middle.astype(bf)
    grad_attended_b = contract_cols(grad_branch_b, whole_out).astype(bf)
    grad_heads = grad_attended_b.reshape(count, heads, HD)
    probs = jnp.exp(score_table() - logsum)
    probs_again_b = probs.astype(bf)
    grad_probs = jnp.einsum("thd,sd->hts", grad_heads, values_b, preferred_element_type=jnp.float32)
    grad_values_b = jnp.einsum(
        "hts,thd->sd", probs_again_b, grad_heads, preferred_element_type=jnp.float32
    ).astype(bf)
    weighted = jnp.sum(probs * grad_probs, axis=-1, keepdims=True)
    grad_scores_b = (probs * (grad_probs - weighted)).astype(bf)
    grad_query_b = (
        (
            jnp.einsum("hts,sd->thd", grad_scores_b, keys_b, preferred_element_type=jnp.float32)
            * scale
        )
        .reshape(count, D)
        .astype(bf)
    )
    grad_keys_b = (
        jnp.einsum("hts,thd->sd", grad_scores_b, query_heads, preferred_element_type=jnp.float32)
        * scale
    ).astype(bf)
    grad_mixed_b = jnp.concatenate([grad_query_b, grad_keys_b, grad_values_b], axis=1)
    grad_norm_one = contract_cols(grad_mixed_b, whole_in)
    norm_value_one, pull_one = jax.vjp(layer_norm, inputs, gain_one, shift_one)
    grad_inputs_norm, grad_gain_one, grad_shift_one = pull_one(grad_norm_one)
    grad_inputs = grad_middle + grad_inputs_norm
    hidden_whole = lax.dynamic_update_slice(
        jnp.zeros((FF,), jnp.float32), hidden_sums[0], (ff_start,)
    )
    vector_grad = jnp.concatenate(
        [
            jnp.stack(
                [
                    grad_gain_one,
                    grad_shift_one,
                    jnp.sum(grad_query_b.astype(jnp.float32), axis=0),
                    jnp.sum(grad_branch_b.astype(jnp.float32), axis=0),
                    grad_gain_two,
                    grad_shift_two,
                    jnp.sum(grad_y, axis=0),
                ],
                axis=0,
            ),
            hidden_whole.reshape(FF // D, D),
        ],
        axis=0,
    )
    vector_grad = vector_grad.reshape(NVEC, owners, rows).transpose(1, 0, 2)
    vector_grad = jnp.pad(vector_grad, ((0, 0), (0, 16 - NVEC), (0, 128 - rows)))
    small_part = jnp.concatenate(
        [
            contract_rows(norm_one_b, grad_mixed_b).astype(bf),
            contract_rows(attended_b, grad_branch_b).astype(bf),
        ],
        axis=1,
    )
    small_grad, back_result, back_grad, grad_up, vector_sum = finish_sums(
        parts,
        groups,
        small_part.reshape(groups // 2, 2, parts, rows, width_in + D),
        result.astype(bf).reshape(parts, piece, D),
        grad_inputs.astype(bf).reshape(parts, piece, D),
        up_grad_block.T.astype(bf).reshape(owners, rows, FF // owners),
        vector_grad,
    )
    grad_up = grad_up.transpose(1, 0, 2).reshape(rows, FF)
    vector_sum = jnp.sum(vector_sum, axis=0)
    grad_in = small_grad[:, :width_in]
    grad_out = small_grad[:, width_in : width_in + D]
    grad_vec = vector_sum[:NVEC, :rows].T
    in_new = adam_update(in_weight, in_first, in_second, grad_in, 1.0 / math.sqrt(D), decay_rate)
    out_new = adam_update(
        out_weight, out_first, out_second, grad_out, 1.0 / math.sqrt(D * 8 // TOK_DEV), decay_rate
    )
    up_new = adam_update(up_weight, up_first, up_second, grad_up, 1.0 / math.sqrt(D), decay_rate)
    down_new = adam_update(
        down_weight, down_first, down_second, down_grad, 1.0 / math.sqrt(FF), decay_rate
    )
    vec_new = adam_update(vectors, vector_first, vector_second, grad_vec, 0.1, 0.0)
    return (undeal(back_result), undeal(back_grad)) + in_new + out_new + up_new + down_new + vec_new


def solution(mesh):
    spec = P(("dp", "fsdp"), None)
    return jax.shard_map(
        shards,
        mesh=mesh,
        in_specs=(spec,) * 19,
        out_specs=(spec,) * 17,
        check_vma=False,
    )
```

```python
import functools
import math

import jax
import jax.numpy as jnp
from jax import lax
from jax.experimental import pallas as pl
from jax.experimental.pallas import tpu as pltpu
from jax.sharding import PartitionSpec as P

D = 2048
FF = 8192
HD = 128
TOK_DEV = 384
STEP = 5
NVEC = 11


eps_norm = 1e-05
beta_one = 0.5
beta_two = 0.5
adam_eps = 1e-08
decay_rate = 0.1


def layer_norm(values, gain, shift):
    centered = values - jnp.mean(values, axis=-1, keepdims=True)
    scaled = centered * lax.rsqrt(jnp.mean(centered * centered, axis=-1, keepdims=True) + eps_norm)
    return scaled * gain + shift


def gelu_tanh(values):
    return (
        0.5
        * values
        * (1.0 + jnp.tanh(0.7978845608028654 * (values + 0.044715 * values * values * values)))
    )


def segment_mask(sizes, count):
    ends = jnp.cumsum(sizes)
    places = jnp.arange(count, dtype=jnp.int32)
    labels = jnp.sum((places[:, None] >= ends[None, :]).astype(jnp.int32), axis=1)
    return (labels[:, None] == labels[None, :]) & (places[None, :] <= places[:, None])


def adam_update(weight, first, second, grad, rate, decay):
    grad = grad.astype(jnp.float32)
    first_new = beta_one * first + (1.0 - beta_one) * grad
    second_new = beta_two * second + (1.0 - beta_two) * grad * grad
    fix_one = 1.0 - beta_one**STEP
    fix_two = 1.0 - beta_two**STEP
    step_size = first_new / fix_one / (jnp.sqrt(second_new / fix_two) + adam_eps)
    weight_new = weight - rate * (step_size + decay * weight)
    return (weight_new, first_new, second_new)


def contract_rows(left, right):
    return lax.dot_general(
        left, right, (((0,), (0,)), ((), ())), preferred_element_type=jnp.float32
    )


def contract_cols(left, right):
    return lax.dot_general(
        left, right, (((1,), (1,)), ((), ())), preferred_element_type=jnp.float32
    )


MESH = pl.DeviceIdType.MESH
F32 = jnp.float32
BF = jnp.bfloat16


def wrap(value, count):
    return lax.rem(value + 2 * count, count)


def ring_place(index, parts):
    if parts != 8:
        return index
    z, y = lax.div(index, 2), lax.rem(index, 2)
    return z + y * (7 - 2 * z)


def ring_index(place, parts):
    place = wrap(place, parts)
    if parts != 8:
        return place
    back = lax.div(place, 4)
    return (1 - back) * 2 * place + back * (15 - 2 * place)


def remote(src, dst, send, recv, dp, fs):
    return pltpu.make_async_remote_copy(
        src_ref=src, dst_ref=dst, send_sem=send, recv_sem=recv, device_id=(dp, fs), device_id_type=MESH
    )


def lasting(micros):
    return pl.CostEstimate(
        flops=int(micros * 1.1e9), bytes_accessed=int(micros * 3.3e6), transcendentals=0
    )


def greet(targets):
    barrier = pltpu.get_barrier_semaphore()
    for dp, fs in targets:
        pl.semaphore_signal(barrier, inc=1, device_id=(dp, fs), device_id_type=MESH)
    pl.semaphore_wait(barrier, len(targets))


def greet_all(me, parts, owners):
    barrier = pltpu.get_barrier_semaphore()

    def one(i, carry):
        peer = wrap(me + i, owners)
        pl.semaphore_signal(
            barrier, inc=1, device_id=(lax.div(peer, parts), lax.rem(peer, parts)), device_id_type=MESH
        )
        return carry

    lax.fori_loop(1, owners, one, 0)
    pl.semaphore_wait(barrier, owners - 1)


def loop(low, high, body):
    def one(i, carry):
        body(i)
        return carry

    lax.fori_loop(low, high, one, 0)


def deal_copy(parts, dp, f, src, dst, send, recv, d, came=False):
    to = wrap(f + d, parts)
    place = wrap(f - d, parts) if came else f
    return remote(src.at[to], dst.at[place], send.at[d], recv.at[d], dp, to)


def owner_copy(me, parts, owners, src, dst, send, recv, d, came=False):
    to = wrap(me + d, owners)
    place = wrap(me - d, owners) if came else me
    return remote(
        src.at[to], dst.at[place], send.at[d], recv.at[d], lax.div(to, parts), lax.rem(to, parts)
    )


def spread_kernel(
    parts, groups,
    xd, gd, inb, ovb,
    xo, eall, win, wov,
    local, xs, xr, gs, gr, rs, rr, ns, nr, ss, sr, ens, enr, ess, esr,
):
    dp, f = lax.axis_index("dp"), lax.axis_index("fsdp")
    owners, rows_x = groups * parts, groups // 2
    x, core = lax.div(dp, 2), lax.rem(dp, 2)
    sib = x * 2 + 1 - core
    me = dp * parts + f
    p = ring_place(f, parts)
    nxt, prv = ring_index(p + 1, parts), ring_index(p - 1, parts)
    whole = (win, wov)
    mine = [
        pltpu.make_async_copy(inb, win.at[me], local.at[0]),
        pltpu.make_async_copy(ovb, wov.at[me], local.at[1]),
        pltpu.make_async_copy(xd.at[f], xo.at[f], local.at[2]),
        pltpu.make_async_copy(gd.at[f], eall.at[dp, f], local.at[3]),
    ]
    for copy in mine:
        copy.start()
    greet(
        [(dp, wrap(f + d, parts)) for d in range(1, parts)]
        + [(sib, f)]
        + [(wrap(x + dx, rows_x) * 2 + core, f) for dx in range(1, rows_x)]
    )
    for copy in mine:
        copy.wait()

    def x_copies(d, came=False):
        return deal_copy(parts, dp, f, xd, xo, xs, xr, d, came)

    def g_copies(d, came=False):
        return deal_copy(parts, dp, f, gd, eall.at[dp], gs, gr, d, came)

    def origin(h, s):
        return ring_index(p - s if h == 0 else p + s, parts)

    def ring_send(h, s):
        ref = whole[h].at[dp * parts + origin(h, s)]
        return remote(ref, ref, rs.at[h, s], rr.at[h, s], dp, nxt if h == 0 else prv)

    def ring_recv(h, s):
        ref = whole[h].at[dp * parts + origin(h, s)]
        return remote(ref, ref, rs.at[h, s - 1], rr.at[h, s - 1], dp, nxt if h == 0 else prv)

    def x_send(h, s, dx):
        ref = whole[h].at[dp * parts + origin(h, s)]
        to = wrap(x + dx, rows_x) * 2 + core
        return remote(ref, ref, ns.at[h, s, dx], nr.at[h, s, dx], to, f)

    def x_recv(h, s, dx):
        came = wrap(x - dx, rows_x) * 2 + core
        ref = whole[h].at[came * parts + origin(h, s)]
        return remote(ref, ref, ns.at[h, s, dx], nr.at[h, s, dx], came, f)

    def sib_send(h, s, dx):
        came = wrap(x - dx, rows_x) * 2 + core
        ref = whole[h].at[came * parts + origin(h, s)]
        return remote(ref, ref, ss.at[h, s, dx], sr.at[h, s, dx], sib, f)

    def sib_recv(h, s, dx):
        came = wrap(x - dx, rows_x) * 2 + 1 - core
        ref = whole[h].at[came * parts + origin(h, s)]
        return remote(ref, ref, ss.at[h, s, dx], sr.at[h, s, dx], sib, f)

    def e_x_send(d, dx):
        ref = eall.at[dp, wrap(f - d, parts)]
        to = wrap(x + dx, rows_x) * 2 + core
        return remote(ref, ref, ens.at[d, dx], enr.at[d, dx], to, f)

    def e_x_recv(d, dx):
        came = wrap(x - dx, rows_x) * 2 + core
        ref = eall.at[came, wrap(f - d, parts)]
        return remote(ref, ref, ens.at[d, dx], enr.at[d, dx], came, f)

    def e_sib_send(d, dx):
        came = wrap(x - dx, rows_x) * 2 + core
        ref = eall.at[came, wrap(f - d, parts)]
        return remote(ref, ref, ess.at[d, dx], esr.at[d, dx], sib, f)

    def e_sib_recv(d, dx):
        came = wrap(x - dx, rows_x) * 2 + 1 - core
        ref = eall.at[came, wrap(f - d, parts)]
        return remote(ref, ref, ess.at[d, dx], esr.at[d, dx], sib, f)

    def ring_step(s):
        for h in range(2):
            @pl.when(s > 0)
            def _():
                ring_recv(h, s).wait_recv()

            @pl.when(s < parts - 1)
            def _():
                ring_send(h, s).start()

            for dx in range(1, rows_x):
                x_send(h, s, dx).start()
            sib_send(h, s, 0).start()

    def e_step(d):
        @pl.when(d > 0)
        def _():
            g_copies(d, True).wait_recv()

        for dx in range(1, rows_x):
            e_x_send(d, dx).start()
        e_sib_send(d, 0).start()

    def relay(s):
        for h in range(2):
            for dx in range(1, rows_x):
                x_recv(h, s, dx).wait_recv()
                sib_send(h, s, dx).start()

    def e_relay(d):
        for dx in range(1, rows_x):
            e_x_recv(d, dx).wait_recv()
            e_sib_send(d, dx).start()

    def main(s):
        @pl.when(s < parts)
        def _():
            ring_step(s)

        @pl.when(s < parts - 1)
        def _():
            x_copies(s + 1).start()
            g_copies(s + 1).start()

        @pl.when((s >= 1) & (s <= parts))
        def _():
            e_step(s - 1)

        @pl.when((s >= 2) & (s < parts + 2))
        def _():
            relay(s - 2)

        @pl.when(s >= 3)
        def _():
            e_relay(s - 3)

    loop(0, parts + 3, main)

    def finish(s):
        for h in range(2):
            @pl.when(s < parts - 1)
            def _():
                ring_send(h, s).wait_send()

            for dx in range(1, rows_x):
                x_send(h, s, dx).wait_send()
            for dx in range(rows_x):
                sib_recv(h, s, dx).wait_recv()
                sib_send(h, s, dx).wait_send()
        for dx in range(1, rows_x):
            e_x_send(s, dx).wait_send()
        for dx in range(rows_x):
            e_sib_recv(s, dx).wait_recv()
            e_sib_send(s, dx).wait_send()

        @pl.when(s > 0)
        def _():
            x_copies(s, True).wait_recv()
            x_copies(s).wait_send()
            g_copies(s).wait_send()

    loop(0, parts, finish)


def exchange_kernel(parts, groups, src, dst, local, us, ur):
    dp, f = lax.axis_index("dp"), lax.axis_index("fsdp")
    owners = groups * parts
    me = dp * parts + f
    mine = pltpu.make_async_copy(src.at[me], dst.at[me], local)
    mine.start()
    greet_all(me, parts, owners)
    loop(1, owners, lambda d: owner_copy(me, parts, owners, src, dst, us, ur, d).start())
    mine.wait()

    def finish(d):
        owner_copy(me, parts, owners, src, dst, us, ur, d, True).wait_recv()
        owner_copy(me, parts, owners, src, dst, us, ur, d).wait_send()

    loop(1, owners, finish)


def exchange(parts, groups, src):
    owners = groups * parts
    dma = pltpu.SemaphoreType.DMA
    return pl.pallas_call(
        functools.partial(exchange_kernel, parts, groups),
        out_shape=jax.ShapeDtypeStruct(src.shape, BF),
        in_specs=[pl.BlockSpec(memory_space=pl.ANY)],
        out_specs=pl.BlockSpec(memory_space=pl.ANY),
        scratch_shapes=[dma(()), dma((owners,)), dma((owners,))],
        compiler_params=pltpu.CompilerParams(collective_id=5, has_side_effects=True),
        cost_estimate=lasting(25),
    )(src)


def spread(parts, groups, xd, gd, inb, ovb):
    owners, rows_x = groups * parts, groups // 2
    dma = pltpu.SemaphoreType.DMA
    return pl.pallas_call(
        functools.partial(spread_kernel, parts, groups),
        out_shape=(
            jax.ShapeDtypeStruct(xd.shape, BF),
            jax.ShapeDtypeStruct((groups,) + gd.shape, BF),
            jax.ShapeDtypeStruct((owners,) + inb.shape, BF),
            jax.ShapeDtypeStruct((owners,) + ovb.shape, BF),
        ),
        in_specs=[pl.BlockSpec(memory_space=pl.ANY)] * 4,
        out_specs=(pl.BlockSpec(memory_space=pl.ANY),) * 4,
        scratch_shapes=[
            dma((4,)),
            dma((parts,)), dma((parts,)), dma((parts,)), dma((parts,)),
            dma((2, parts)), dma((2, parts)),
            dma((2, parts, rows_x)), dma((2, parts, rows_x)),
            dma((2, parts, rows_x)), dma((2, parts, rows_x)),
            dma((parts, rows_x)), dma((parts, rows_x)),
            dma((parts, rows_x)), dma((parts, rows_x)),
        ],
        compiler_params=pltpu.CompilerParams(collective_id=0, has_side_effects=True),
        cost_estimate=lasting(200),
    )(xd, gd, inb, ovb)


def group_gather_kernel(groups, chunks, src, out, local, ns, nr, ss, sr):
    dp, f = lax.axis_index("dp"), lax.axis_index("fsdp")
    rows_x = groups // 2
    x, core = lax.div(dp, 2), lax.rem(dp, 2)
    sib = x * 2 + 1 - core
    size = src.shape[0] // chunks
    mine = pltpu.make_async_copy(src, out.at[dp], local)
    mine.start()
    greet([(sib, f)] + [(wrap(x + dx, rows_x) * 2 + core, f) for dx in range(1, rows_x)])

    def part(ref, k):
        return ref.at[pl.ds(k * size, size)]

    def x_send(k, dx):
        to = wrap(x + dx, rows_x) * 2 + core
        return remote(part(src, k), part(out.at[dp], k), ns.at[k, dx], nr.at[k, dx], to, f)

    def x_recv(k, dx):
        came = wrap(x - dx, rows_x) * 2 + core
        ref = part(out.at[came], k)
        return remote(ref, ref, ns.at[k, dx], nr.at[k, dx], came, f)

    def sib_send(k, dx):
        came = wrap(x - dx, rows_x) * 2 + core
        ref = part(out.at[came], k)
        return remote(part(src, k) if dx == 0 else ref, ref, ss.at[k, dx], sr.at[k, dx], sib, f)

    def sib_recv(k, dx):
        came = wrap(x - dx, rows_x) * 2 + 1 - core
        ref = part(out.at[came], k)
        return remote(ref, ref, ss.at[k, dx], sr.at[k, dx], sib, f)

    for k in range(chunks):
        for dx in range(1, rows_x):
            x_send(k, dx).start()
    for k in range(chunks):
        sib_send(k, 0).start()
    for k in range(chunks):
        for dx in range(1, rows_x):
            x_recv(k, dx).wait_recv()
            sib_send(k, dx).start()
    mine.wait()
    for k in range(chunks):
        for dx in range(rows_x):
            sib_recv(k, dx).wait_recv()
            sib_send(k, dx).wait_send()
        for dx in range(1, rows_x):
            x_send(k, dx).wait_send()


def group_gather(groups, src):
    chunks, rows_x = 4, groups // 2
    dma = pltpu.SemaphoreType.DMA
    return pl.pallas_call(
        functools.partial(group_gather_kernel, groups, chunks),
        out_shape=jax.ShapeDtypeStruct((groups,) + src.shape, BF),
        in_specs=[pl.BlockSpec(memory_space=pl.ANY)],
        out_specs=pl.BlockSpec(memory_space=pl.ANY),
        scratch_shapes=[dma(())] + [dma((chunks, rows_x))] * 4,
        compiler_params=pltpu.CompilerParams(collective_id=1, has_side_effects=True),
        cost_estimate=lasting(45),
    )(src)


def ffn_back_kernel(
    parts, groups, chunks,
    act, dhid, nrm, grd, w1, w2,
    down, up, dsum, ypart, got,
    acc, gotv, gone, wv, psib, sibr, xb, xrb, yb,
    rs, rr, gl, wl, gss, gsr, gns, gnr, ys,
):
    dp, f = lax.axis_index("dp"), lax.axis_index("fsdp")
    rows_x = groups // 2
    x, core = lax.div(dp, 2), lax.rem(dp, 2)
    sib = x * 2 + 1 - core
    p = ring_place(f, parts)
    nxt, prv = ring_index(p + 1, parts), ring_index(p - 1, parts)
    block, width = down.shape
    half, cut = width // 2, width // chunks
    count = dsum.shape[0]
    mats = ((act, grd, down), (dhid, nrm, up))
    w1_load = pltpu.make_async_copy(w1, wv, wl)
    w1_load.start()
    greet(
        [(dp, nxt), (dp, prv), (sib, f)]
        + [(wrap(x + dx, rows_x) * 2 + core, f) for dx in range(1, rows_x)]
    )

    def ring_copy(m, h, s):
        return remote(
            gone.at[m, h], got.at[m, h, s], rs.at[m, h, s], rr.at[m, h, s],
            dp, nxt if h == 0 else prv,
        )

    def products(s):
        for m in range(2):
            left, right = mats[m][:2]
            for h in range(2):
                c = ring_index(p - 1 - s if h == 0 else p + 1 + s, parts)
                acc[m, h] = lax.dot_general(
                    left[:, pl.ds(pl.multiple_of(c * block, block), block)],
                    right[:, h * half : (h + 1) * half],
                    (((0,), (0,)), ((), ())), preferred_element_type=F32,
                )

    def pass_on(s):
        for m in range(2):
            for h in range(2):
                fetch = pltpu.make_async_copy(got.at[m, h, s - 1], gotv.at[m, h], gl.at[m, h])
                store = pltpu.make_async_copy(
                    gone.at[m, h], mats[m][2].at[:, pl.ds(h * half, half)], gl.at[m, h]
                )

                @pl.when(s == 0)
                def _():
                    gone[m, h] = acc[m, h].astype(BF)

                @pl.when(s > 0)
                def _():
                    ring_copy(m, h, s - 1).wait_recv()
                    fetch.start()
                    ring_copy(m, h, s - 1).wait_send()
                    fetch.wait()
                    gone[m, h] = (acc[m, h] + gotv[m, h].astype(F32)).astype(BF)

                @pl.when(s < parts - 1)
                def _():
                    ring_copy(m, h, s).start()

                @pl.when(s == parts - 1)
                def _():
                    store.start()
                    store.wait()

    def cols(k):
        return pl.ds(pl.multiple_of(k * cut, cut), cut)

    def group_of(dx, c):
        return wrap(x + dx, rows_x) * 2 + (core if c == 0 else 1 - core)

    def rows_of(dx, c):
        return pl.ds(pl.multiple_of(group_of(dx, c) * count, count), count)

    def sum_sib(dx, k):
        return remote(
            psib.at[dx, :, cols(k)], sibr.at[dx, :, cols(k)], gss.at[dx, k], gsr.at[dx, k], sib, f
        )

    def sum_x(dx, k):
        to = wrap(x + dx, rows_x) * 2 + core
        return remote(
            xb.at[dx - 1, :, cols(k)], xrb.at[dx - 1, :, cols(k)],
            gns.at[dx, k], gnr.at[dx, k], to, f,
        )

    def other_side(n):
        dx, k = lax.div(n, chunks), lax.rem(n, chunks)
        dx = wrap(dx + 1, rows_x)
        psib[dx, :, cols(k)] = jnp.dot(
            dhid[rows_of(dx, 1), :], wv[:, cols(k)], preferred_element_type=F32
        ).astype(BF)
        sum_sib(dx, k).start()

    def own_side(n):
        dx, k = lax.div(n, chunks), lax.rem(n, chunks)
        dx = wrap(dx + 1, rows_x)
        dh = jnp.dot(dhid[rows_of(dx, 0), :], wv[:, cols(k)], preferred_element_type=F32)
        sum_sib(dx, k).wait_recv()
        dh = dh + sibr[dx, :, cols(k)].astype(F32)

        @pl.when(dx == 0)
        def _():
            dsum[:, cols(k)] = dh

        @pl.when(dx > 0)
        def _():
            xb[dx - 1, :, cols(k)] = dh.astype(BF)
            sum_x(dx, k).start()

    def collect(k):
        for dx in range(1, rows_x):
            sum_x(dx, k).wait_recv()
            dsum[:, cols(k)] += xrb[dx - 1, :, cols(k)].astype(F32)

    def y_copy(n):
        g, k = lax.div(n, chunks), lax.rem(n, chunks)
        return pltpu.make_async_copy(
            yb.at[lax.rem(n, 2)], ypart.at[g, :, cols(k)], ys.at[lax.rem(n, 2)]
        )

    def y_one(n):
        g, k = lax.div(n, chunks), lax.rem(n, chunks)

        @pl.when(n >= 2)
        def _():
            y_copy(n - 2).wait()

        yb[lax.rem(n, 2)] = jnp.dot(
            act[pl.ds(pl.multiple_of(g * count, count), count), :], wv[:, cols(k)],
            preferred_element_type=F32,
        ).astype(BF)
        y_copy(n).start()

    w2_load = pltpu.make_async_copy(w2, wv, wl)
    products(0)

    def step(s):
        pass_on(s)

        @pl.when(s < parts - 1)
        def _():
            products(s + 1)

        @pl.when(s == 0)
        def _():
            w1_load.wait()
            loop(0, rows_x * chunks, other_side)

        @pl.when(s == 1)
        def _():
            loop(0, rows_x * chunks, own_side)
            w2_load.start()

        @pl.when(s == 2)
        def _():
            w2_load.wait()
            loop(0, groups * chunks // 2, y_one)

        @pl.when(s == 3)
        def _():
            loop(groups * chunks // 2, groups * chunks, y_one)

        @pl.when(s == 4)
        def _():
            loop(0, chunks, collect)

    loop(0, parts, step)

    def last(k):
        for dx in range(rows_x):
            sum_sib(dx, k).wait_send()
        for dx in range(1, rows_x):
            sum_x(dx, k).wait_send()

    loop(0, chunks, last)
    y_copy(groups * chunks - 2).wait()
    y_copy(groups * chunks - 1).wait()


def ffn_back(parts, groups, act, dhid, nrm, grd, w1, w2):
    chunks, rows_x = 4, groups // 2
    units, width = w1.shape
    count = act.shape[0] // groups
    block, half = units // parts, width // 2
    dma = pltpu.SemaphoreType.DMA
    hbm = pl.BlockSpec(memory_space=pl.ANY)
    vmem = pl.BlockSpec(memory_space=pltpu.VMEM)
    outs = pl.pallas_call(
        functools.partial(ffn_back_kernel, parts, groups, chunks),
        out_shape=(
            jax.ShapeDtypeStruct((block, width), BF),
            jax.ShapeDtypeStruct((block, width), BF),
            jax.ShapeDtypeStruct((count, width), F32),
            jax.ShapeDtypeStruct((groups, count, width), BF),
            jax.ShapeDtypeStruct((2, 2, parts - 1, block, half), BF),
        ),
        in_specs=[vmem] * 4 + [hbm] * 2,
        out_specs=(hbm, hbm, vmem, hbm, hbm),
        scratch_shapes=[
            pltpu.VMEM((2, 2, block, half), F32),
            pltpu.VMEM((2, 2, block, half), BF),
            pltpu.VMEM((2, 2, block, half), BF),
            pltpu.VMEM((units, width), BF),
            pltpu.VMEM((rows_x, count, width), BF),
            pltpu.VMEM((rows_x, count, width), BF),
            pltpu.VMEM((rows_x - 1, count, width), BF),
            pltpu.VMEM((rows_x - 1, count, width), BF),
            pltpu.VMEM((2, count, width // chunks), BF),
            dma((2, 2, parts)), dma((2, 2, parts)), dma((2, 2)), dma(()),
            dma((rows_x, chunks)), dma((rows_x, chunks)),
            dma((rows_x, chunks)), dma((rows_x, chunks)),
            dma((2,)),
        ],
        compiler_params=pltpu.CompilerParams(
            collective_id=3, has_side_effects=True, vmem_limit_bytes=60 * 2**20
        ),
        cost_estimate=lasting(175),
    )(act, dhid, nrm, grd, w1, w2)
    return outs[:4]


def finish_kernel(
    parts, groups,
    grads, res, gx, upg, vec,
    total, res_out, gx_out, upg_out, vec_out,
    loc, sibr, xb, xrb, got, gone,
    local, ls, ss, sr, ns, nr, rs, rr, as_, ar, bs, br, us, ur, vs, vr,
):
    dp, f = lax.axis_index("dp"), lax.axis_index("fsdp")
    owners, rows_x = groups * parts, groups // 2
    x, core = lax.div(dp, 2), lax.rem(dp, 2)
    sib = x * 2 + 1 - core
    me = dp * parts + f
    p = ring_place(f, parts)
    nxt, prv = ring_index(p + 1, parts), ring_index(p - 1, parts)
    half = grads.shape[4] // 2
    mine = [
        pltpu.make_async_copy(res.at[f], res_out.at[f], local.at[0]),
        pltpu.make_async_copy(gx.at[f], gx_out.at[f], local.at[1]),
        pltpu.make_async_copy(upg.at[me], upg_out.at[me], local.at[2]),
        pltpu.make_async_copy(vec.at[me], vec_out.at[me], local.at[3]),
    ]
    for copy in mine:
        copy.start()
    greet_all(me, parts, owners)

    def chunk(h, s):
        return ring_index(p - 1 - s if h == 0 else p + 1 + s, parts)

    def sib_copy(h, s):
        piece = grads.at[:, 1 - core, chunk(h, s), :, pl.ds(h * half, half)]
        return remote(piece, sibr.at[h, s], ss.at[h, s], sr.at[h, s], sib, f)

    def own_copy(h, s):
        piece = grads.at[:, core, chunk(h, s), :, pl.ds(h * half, half)]
        return pltpu.make_async_copy(piece, loc.at[h, s], ls.at[h, s])

    def x_copy(h, s, dx):
        to = wrap(x + dx, rows_x) * 2 + core
        return remote(
            xb.at[h, s, dx - 1], xrb.at[h, s, dx - 1], ns.at[h, s, dx], nr.at[h, s, dx], to, f
        )

    def ring_copy(h, s):
        return remote(
            gone.at[h, s], got.at[h, s], rs.at[h, s], rr.at[h, s], dp, nxt if h == 0 else prv
        )

    def res_copies(d, came=False):
        return deal_copy(parts, dp, f, res, res_out, as_, ar, d, came)

    def gx_copies(d, came=False):
        return deal_copy(parts, dp, f, gx, gx_out, bs, br, d, came)

    def upg_copies(d, came=False):
        return owner_copy(me, parts, owners, upg, upg_out, us, ur, d, came)

    def vec_copies(d, came=False):
        return owner_copy(me, parts, owners, vec, vec_out, vs, vr, d, came)

    def begin(s):
        for h in range(2):
            sib_copy(h, s).start()
            own_copy(h, s).start()

    def pair(s):
        for h in range(2):
            sib_copy(h, s).wait_recv()
            own_copy(h, s).wait()
            for dx in range(1, rows_x):
                to = wrap(x + dx, rows_x)
                xb[h, s, dx - 1] = (sibr[h, s, to].astype(F32) + loc[h, s, to].astype(F32)).astype(BF)
                x_copy(h, s, dx).start()

    def step(s):
        for h in range(2):
            for dx in range(1, rows_x):
                x_copy(h, s, dx).wait_recv()

            def value():
                here = sibr[h, s, x].astype(F32) + loc[h, s, x].astype(F32)
                for dx in range(1, rows_x):
                    here = here + xrb[h, s, dx - 1].astype(F32)
                return here

            @pl.when(s == 0)
            def _():
                gone[h, s] = value().astype(BF)
                ring_copy(h, s).start()

            @pl.when((s > 0) & (s < parts - 1))
            def _():
                ring_copy(h, s - 1).wait_recv()
                gone[h, s] = (value() + got[h, s - 1].astype(F32)).astype(BF)
                ring_copy(h, s).start()

            @pl.when(s == parts - 1)
            def _():
                ring_copy(h, s - 1).wait_recv()
                total[:, h * half : (h + 1) * half] = value() + got[h, s - 1].astype(F32)

    each = -(-(owners - 1) // parts)
    ahead, near = min(4, parts), min(2, parts)
    for s in range(ahead):
        begin(s)
    for s in range(near):
        pair(s)

    def main(s):
        @pl.when(s < parts - ahead)
        def _():
            begin(s + ahead)

        @pl.when(s < parts - near)
        def _():
            pair(s + near)

        step(s)

        @pl.when(s < parts - 1)
        def _():
            res_copies(s + 1).start()
            gx_copies(s + 1).start()

        for j in range(each):
            d = s * each + 1 + j

            @pl.when(d < owners)
            def _():
                upg_copies(d).start()
                vec_copies(d).start()

    loop(0, parts, main)

    def finish(s):
        for h in range(2):
            sib_copy(h, s).wait_send()
            for dx in range(1, rows_x):
                x_copy(h, s, dx).wait_send()

            @pl.when(s < parts - 1)
            def _():
                ring_copy(h, s).wait_send()

        @pl.when(s > 0)
        def _():
            for copies in (res_copies, gx_copies):
                copies(s, True).wait_recv()
                copies(s).wait_send()

    loop(0, parts, finish)

    def owner_finish(d):
        for copies in (upg_copies, vec_copies):
            copies(d, True).wait_recv()
            copies(d).wait_send()

    loop(1, owners, owner_finish)
    for copy in mine:
        copy.wait()


def finish_sums(parts, groups, grads, res, gx, upg, vec):
    owners, rows_x = groups * parts, groups // 2
    rows, width = grads.shape[3:]
    half = width // 2
    dma = pltpu.SemaphoreType.DMA
    hbm = pl.BlockSpec(memory_space=pl.ANY)
    return pl.pallas_call(
        functools.partial(finish_kernel, parts, groups),
        out_shape=(
            jax.ShapeDtypeStruct((rows, width), F32),
            jax.ShapeDtypeStruct(res.shape, BF),
            jax.ShapeDtypeStruct(gx.shape, BF),
            jax.ShapeDtypeStruct(upg.shape, BF),
            jax.ShapeDtypeStruct(vec.shape, F32),
        ),
        in_specs=[hbm] * 5,
        out_specs=(pl.BlockSpec(memory_space=pltpu.VMEM),) + (hbm,) * 4,
        scratch_shapes=[
            pltpu.VMEM((2, parts, rows_x, rows, half), BF),
            pltpu.VMEM((2, parts, rows_x, rows, half), BF),
            pltpu.VMEM((2, parts, rows_x - 1, rows, half), BF),
            pltpu.VMEM((2, parts, rows_x - 1, rows, half), BF),
            pltpu.VMEM((2, parts, rows, half), BF),
            pltpu.VMEM((2, parts, rows, half), BF),
            dma((4,)),
            dma((2, parts)), dma((2, parts)), dma((2, parts)),
            dma((2, parts, rows_x)), dma((2, parts, rows_x)),
            dma((2, parts)), dma((2, parts)),
            dma((parts,)), dma((parts,)), dma((parts,)), dma((parts,)),
            dma((owners,)), dma((owners,)), dma((owners,)), dma((owners,)),
        ],
        compiler_params=pltpu.CompilerParams(
            collective_id=4, has_side_effects=True, vmem_limit_bytes=60 * 2**20
        ),
        cost_estimate=lasting(140),
    )(grads, res, gx, upg, vec)


def shards(
    tokens,
    cotangent,
    lengths,
    routing,
    in_weight,
    in_first,
    in_second,
    out_weight,
    out_first,
    out_second,
    up_weight,
    up_first,
    up_second,
    down_weight,
    down_first,
    down_second,
    vectors,
    vector_first,
    vector_second,
):
    bf = jnp.bfloat16
    heads = D // HD
    count = tokens.shape[0]
    parts = lax.axis_size("fsdp")
    groups = lax.axis_size("dp")
    both = ("dp", "fsdp")
    piece = count // parts
    width_in = D + 2 * HD
    slots = jnp.arange(parts, dtype=jnp.int32)
    order = routing[0]
    inverse = jnp.sum(jnp.where(order[:, None] == slots[None, :], slots[:, None], 0), axis=0)

    def deal(array):
        return jnp.take(array.reshape(parts, piece, D), inverse, axis=0)

    def undeal(array):
        return jnp.take(array, order, axis=0).reshape(count, D)

    rows = in_weight.shape[0]
    owners = groups * parts
    out_vec = jnp.concatenate(
        [out_weight.astype(bf), jnp.pad(vectors.astype(bf), ((0, 0), (0, 128 - NVEC)))], axis=1
    )
    up_pieces = up_weight.astype(bf).reshape(rows, owners, FF // owners).transpose(1, 0, 2)
    up_block, dealt, dealt_grad, out_vec = lax.optimization_barrier(
        (exchange(parts, groups, up_pieces), deal(tokens), deal(cotangent), out_vec)
    )
    x_dealt, grad_dealt, whole_in, whole_out = spread(
        parts, groups, dealt, dealt_grad, in_weight.astype(bf), out_vec
    )
    inputs_here = x_dealt.reshape(count, D)
    grad_all = grad_dealt.reshape(groups * count, D)
    grad_here = lax.dynamic_index_in_dim(
        grad_dealt, lax.axis_index("dp"), 0, keepdims=False
    ).reshape(count, D)
    whole_in = whole_in.reshape(D, width_in)
    whole_out = whole_out.reshape(D, D + 128)
    part_down = lax.all_gather(down_weight.astype(bf), "fsdp", axis=0, tiled=True)
    part_up = lax.all_gather(up_block.reshape(D, FF // owners).T, "fsdp", axis=0, tiled=True)

    table = whole_out[:, D : D + NVEC].astype(jnp.float32)
    whole_out = whole_out[:, :D]
    gain_one = table[:, 0]
    shift_one = table[:, 1]
    query_bias = table[:, 2]
    branch_bias = table[:, 3]
    gain_two = table[:, 4]
    shift_two = table[:, 5]
    output_bias = table[:, 6]
    hidden_bias = table[:, 7:].T.reshape(FF)
    ff_here = FF // groups
    ff_start = lax.axis_index("dp") * ff_here
    hidden_bias_here = lax.dynamic_slice(hidden_bias, (ff_start,), (ff_here,))
    allowed = segment_mask(lengths[0], count)
    scale = 1.0 / math.sqrt(HD)
    inputs = inputs_here.astype(jnp.float32)
    norm_one_b = layer_norm(inputs, gain_one, shift_one).astype(bf)
    mixed = jnp.dot(norm_one_b, whole_in, preferred_element_type=jnp.float32)
    query_b = (mixed[:, :D] + query_bias).astype(bf)
    keys_b = mixed[:, D : D + HD].astype(bf)
    values_b = mixed[:, D + HD :].astype(bf)
    query_heads = query_b.reshape(count, heads, HD)

    def score_table():
        raw = (
            jnp.einsum("thd,sd->hts", query_heads, keys_b, preferred_element_type=jnp.float32)
            * scale
        )
        return jnp.where(allowed[None], raw, -1e30)

    scores = score_table()
    top = jnp.max(scores, axis=-1, keepdims=True)
    expo = jnp.exp(scores - top)
    total = jnp.sum(expo, axis=-1, keepdims=True)
    logsum = top + jnp.log(total)
    probs_b = (expo / total).astype(bf)
    attended_b = (
        jnp.einsum("hts,sd->thd", probs_b, values_b, preferred_element_type=jnp.float32)
        .reshape(count, D)
        .astype(bf)
    )
    middle = inputs + (
        jnp.dot(attended_b, whole_out, preferred_element_type=jnp.float32) + branch_bias
    )
    norm_two_b = layer_norm(middle, gain_two, shift_two).astype(bf)

    fused = parts == 8 and groups == 4
    if fused:
        norm_all = group_gather(groups, norm_two_b).reshape(groups * count, D)
    else:
        norm_all = lax.all_gather(norm_two_b, "dp", axis=0, tiled=True)
    hidden = contract_cols(norm_all, part_up) + hidden_bias_here
    grad_active = contract_cols(grad_all, part_down)
    gelu_value, gelu_pull = jax.vjp(gelu_tanh, hidden)
    active_b = gelu_value.astype(bf)
    grad_hidden_b = gelu_pull(grad_active)[0].astype(bf)
    if fused:
        down_grad, up_grad_block, grad_norm_two, branch_parts = ffn_back(
            parts, groups, active_b, grad_hidden_b, norm_all, grad_all, part_up, part_down
        )
        branch_parts = branch_parts.reshape(groups * count, D)
    else:
        grad_norm_two = lax.psum_scatter(
            jnp.dot(grad_hidden_b, part_up, preferred_element_type=jnp.float32).astype(bf),
            "dp", scatter_dimension=0, tiled=True,
        ).astype(jnp.float32)
        up_grad_block = lax.psum_scatter(
            contract_rows(grad_hidden_b, norm_all).astype(bf),
            "fsdp", scatter_dimension=0, tiled=True,
        )
        down_grad = lax.psum_scatter(
            contract_rows(active_b, grad_all).astype(bf),
            "fsdp", scatter_dimension=0, tiled=True,
        )
        branch_parts = jnp.dot(active_b, part_down, preferred_element_type=jnp.float32).astype(bf)
    branch_two = lax.psum_scatter(
        branch_parts, "dp", scatter_dimension=0, tiled=True
    ).astype(jnp.float32)

    grad_y = grad_here.astype(jnp.float32)
    norm_value_two, pull_two = jax.vjp(layer_norm, middle, gain_two, shift_two)
    grad_middle_norm, grad_gain_two, grad_shift_two = pull_two(grad_norm_two)
    grad_middle = grad_y + grad_middle_norm
    grad_branch_b = grad_middle.astype(bf)
    grad_attended_b = contract_cols(grad_branch_b, whole_out).astype(bf)
    grad_heads = grad_attended_b.reshape(count, heads, HD)
    probs = jnp.exp(score_table() - logsum)
    probs_again_b = probs.astype(bf)
    grad_probs = jnp.einsum("thd,sd->hts", grad_heads, values_b, preferred_element_type=jnp.float32)
    grad_values_b = jnp.einsum(
        "hts,thd->sd", probs_again_b, grad_heads, preferred_element_type=jnp.float32
    ).astype(bf)
    weighted = jnp.sum(probs * grad_probs, axis=-1, keepdims=True)
    grad_scores_b = (probs * (grad_probs - weighted)).astype(bf)
    grad_query_b = (
        (
            jnp.einsum("hts,sd->thd", grad_scores_b, keys_b, preferred_element_type=jnp.float32)
            * scale
        )
        .reshape(count, D)
        .astype(bf)
    )
    grad_keys_b = (
        jnp.einsum("hts,thd->sd", grad_scores_b, query_heads, preferred_element_type=jnp.float32)
        * scale
    ).astype(bf)
    grad_mixed_b = jnp.concatenate([grad_query_b, grad_keys_b, grad_values_b], axis=1)
    grad_norm_one = contract_cols(grad_mixed_b, whole_in)
    norm_value_one, pull_one = jax.vjp(layer_norm, inputs, gain_one, shift_one)
    grad_inputs_norm, grad_gain_one, grad_shift_one = pull_one(grad_norm_one)
    grad_inputs = grad_middle + grad_inputs_norm
    middle_late, grad_inputs = lax.optimization_barrier((middle, grad_inputs))
    result = middle_late + (branch_two + output_bias)
    hidden_sums = jnp.sum(grad_hidden_b.astype(jnp.float32), axis=0)
    hidden_whole = lax.dynamic_update_slice(
        jnp.zeros((FF,), jnp.float32), hidden_sums, (ff_start,)
    )
    vector_grad = jnp.concatenate(
        [
            jnp.stack(
                [
                    grad_gain_one,
                    grad_shift_one,
                    jnp.sum(grad_query_b.astype(jnp.float32), axis=0),
                    jnp.sum(grad_branch_b.astype(jnp.float32), axis=0),
                    grad_gain_two,
                    grad_shift_two,
                    jnp.sum(grad_y, axis=0),
                ],
                axis=0,
            ),
            hidden_whole.reshape(FF // D, D),
        ],
        axis=0,
    )
    vector_grad = vector_grad.reshape(NVEC, owners, rows).transpose(1, 0, 2)
    vector_grad = jnp.pad(vector_grad, ((0, 0), (0, 16 - NVEC), (0, 128 - rows)))
    small_part = jnp.concatenate(
        [
            contract_rows(norm_one_b, grad_mixed_b).astype(bf),
            contract_rows(attended_b, grad_branch_b).astype(bf),
        ],
        axis=1,
    )
    small_grad, back_result, back_grad, grad_up, vector_sum = finish_sums(
        parts,
        groups,
        small_part.reshape(groups // 2, 2, parts, rows, width_in + D),
        result.astype(bf).reshape(parts, piece, D),
        grad_inputs.astype(bf).reshape(parts, piece, D),
        up_grad_block.T.astype(bf).reshape(owners, rows, FF // owners),
        vector_grad,
    )
    grad_up = grad_up.transpose(1, 0, 2).reshape(rows, FF)
    vector_sum = jnp.sum(vector_sum, axis=0)
    grad_in = small_grad[:, :width_in]
    grad_out = small_grad[:, width_in : width_in + D]
    grad_vec = vector_sum[:NVEC, :rows].T
    in_new = adam_update(in_weight, in_first, in_second, grad_in, 1.0 / math.sqrt(D), decay_rate)
    out_new = adam_update(
        out_weight, out_first, out_second, grad_out, 1.0 / math.sqrt(D * 8 // TOK_DEV), decay_rate
    )
    up_new = adam_update(up_weight, up_first, up_second, grad_up, 1.0 / math.sqrt(D), decay_rate)
    down_new = adam_update(
        down_weight, down_first, down_second, down_grad, 1.0 / math.sqrt(FF), decay_rate
    )
    vec_new = adam_update(vectors, vector_first, vector_second, grad_vec, 0.1, 0.0)
    return (undeal(back_result), undeal(back_grad)) + in_new + out_new + up_new + down_new + vec_new


def solution(mesh):
    spec = P(("dp", "fsdp"), None)
    return jax.shard_map(
        shards,
        mesh=mesh,
        in_specs=(spec,) * 19,
        out_specs=(spec,) * 17,
        check_vma=False,
    )
```

```python
import functools
import math

import jax
import jax.numpy as jnp
from jax import lax
from jax.experimental import pallas as pl
from jax.experimental.pallas import tpu as pltpu
from jax.sharding import PartitionSpec as P

D = 2048
FF = 8192
HD = 128
TOK_DEV = 384
STEP = 5
NVEC = 11


eps_norm = 1e-05
beta_one = 0.5
beta_two = 0.5
adam_eps = 1e-08
decay_rate = 0.1


def layer_norm(values, gain, shift):
    centered = values - jnp.mean(values, axis=-1, keepdims=True)
    scaled = centered * lax.rsqrt(jnp.mean(centered * centered, axis=-1, keepdims=True) + eps_norm)
    return scaled * gain + shift


def gelu_tanh(values):
    return (
        0.5
        * values
        * (1.0 + jnp.tanh(0.7978845608028654 * (values + 0.044715 * values * values * values)))
    )


def segment_mask(sizes, count):
    ends = jnp.cumsum(sizes)
    places = jnp.arange(count, dtype=jnp.int32)
    labels = jnp.sum((places[:, None] >= ends[None, :]).astype(jnp.int32), axis=1)
    return (labels[:, None] == labels[None, :]) & (places[None, :] <= places[:, None])


def adam_update(weight, first, second, grad, rate, decay):
    grad = grad.astype(jnp.float32)
    first_new = beta_one * first + (1.0 - beta_one) * grad
    second_new = beta_two * second + (1.0 - beta_two) * grad * grad
    fix_one = 1.0 - beta_one**STEP
    fix_two = 1.0 - beta_two**STEP
    step_size = first_new / fix_one / (jnp.sqrt(second_new / fix_two) + adam_eps)
    weight_new = weight - rate * (step_size + decay * weight)
    return (weight_new, first_new, second_new)


def contract_rows(left, right):
    return lax.dot_general(
        left, right, (((0,), (0,)), ((), ())), preferred_element_type=jnp.float32
    )


def contract_cols(left, right):
    return lax.dot_general(
        left, right, (((1,), (1,)), ((), ())), preferred_element_type=jnp.float32
    )


MESH = pl.DeviceIdType.MESH
F32 = jnp.float32
BF = jnp.bfloat16


def wrap(value, count):
    return lax.rem(value + 2 * count, count)


def ring_place(index, parts):
    if parts != 8:
        return index
    z, y = lax.div(index, 2), lax.rem(index, 2)
    return z + y * (7 - 2 * z)


def ring_index(place, parts):
    place = wrap(place, parts)
    if parts != 8:
        return place
    back = lax.div(place, 4)
    return (1 - back) * 2 * place + back * (15 - 2 * place)


def remote(src, dst, send, recv, dp, fs):
    return pltpu.make_async_remote_copy(
        src_ref=src, dst_ref=dst, send_sem=send, recv_sem=recv, device_id=(dp, fs), device_id_type=MESH
    )


def lasting(micros):
    return pl.CostEstimate(
        flops=int(micros * 1.1e9), bytes_accessed=int(micros * 3.3e6), transcendentals=0
    )


def greet(targets):
    barrier = pltpu.get_barrier_semaphore()
    for dp, fs in targets:
        pl.semaphore_signal(barrier, inc=1, device_id=(dp, fs), device_id_type=MESH)
    pl.semaphore_wait(barrier, len(targets))


def greet_all(me, parts, owners):
    barrier = pltpu.get_barrier_semaphore()

    def one(i, carry):
        peer = wrap(me + i, owners)
        pl.semaphore_signal(
            barrier, inc=1, device_id=(lax.div(peer, parts), lax.rem(peer, parts)), device_id_type=MESH
        )
        return carry

    lax.fori_loop(1, owners, one, 0)
    pl.semaphore_wait(barrier, owners - 1)


def loop(low, high, body):
    def one(i, carry):
        body(i)
        return carry

    lax.fori_loop(low, high, one, 0)


def deal_copy(parts, dp, f, src, dst, send, recv, d, came=False):
    to = wrap(f + d, parts)
    place = wrap(f - d, parts) if came else f
    return remote(src.at[to], dst.at[place], send.at[d], recv.at[d], dp, to)


def owner_copy(me, parts, owners, src, dst, send, recv, d, came=False):
    to = wrap(me + d, owners)
    place = wrap(me - d, owners) if came else me
    return remote(
        src.at[to], dst.at[place], send.at[d], recv.at[d], lax.div(to, parts), lax.rem(to, parts)
    )


def spread_kernel(
    parts, groups,
    xd, gd, inb, ovb,
    xo, eall, win, wov,
    local, xs, xr, gs, gr, rs, rr, ns, nr, ss, sr, ens, enr, ess, esr,
):
    dp, f = lax.axis_index("dp"), lax.axis_index("fsdp")
    owners, rows_x = groups * parts, groups // 2
    x, core = lax.div(dp, 2), lax.rem(dp, 2)
    sib = x * 2 + 1 - core
    me = dp * parts + f
    p = ring_place(f, parts)
    nxt, prv = ring_index(p + 1, parts), ring_index(p - 1, parts)
    whole = (win, wov)
    mine = [
        pltpu.make_async_copy(inb, win.at[me], local.at[0]),
        pltpu.make_async_copy(ovb, wov.at[me], local.at[1]),
        pltpu.make_async_copy(xd.at[f], xo.at[f], local.at[2]),
        pltpu.make_async_copy(gd.at[f], eall.at[dp, f], local.at[3]),
    ]
    for copy in mine:
        copy.start()
    greet(
        [(dp, wrap(f + d, parts)) for d in range(1, parts)]
        + [(sib, f)]
        + [(wrap(x + dx, rows_x) * 2 + core, f) for dx in range(1, rows_x)]
    )
    for copy in mine:
        copy.wait()

    def x_copies(d, came=False):
        return deal_copy(parts, dp, f, xd, xo, xs, xr, d, came)

    def g_copies(d, came=False):
        return deal_copy(parts, dp, f, gd, eall.at[dp], gs, gr, d, came)

    def origin(h, s):
        return ring_index(p - s if h == 0 else p + s, parts)

    def ring_send(h, s):
        ref = whole[h].at[dp * parts + origin(h, s)]
        return remote(ref, ref, rs.at[h, s], rr.at[h, s], dp, nxt if h == 0 else prv)

    def ring_recv(h, s):
        ref = whole[h].at[dp * parts + origin(h, s)]
        return remote(ref, ref, rs.at[h, s - 1], rr.at[h, s - 1], dp, nxt if h == 0 else prv)

    def x_send(h, s, dx):
        ref = whole[h].at[dp * parts + origin(h, s)]
        to = wrap(x + dx, rows_x) * 2 + core
        return remote(ref, ref, ns.at[h, s, dx], nr.at[h, s, dx], to, f)

    def x_recv(h, s, dx):
        came = wrap(x - dx, rows_x) * 2 + core
        ref = whole[h].at[came * parts + origin(h, s)]
        return remote(ref, ref, ns.at[h, s, dx], nr.at[h, s, dx], came, f)

    def sib_send(h, s, dx):
        came = wrap(x - dx, rows_x) * 2 + core
        ref = whole[h].at[came * parts + origin(h, s)]
        return remote(ref, ref, ss.at[h, s, dx], sr.at[h, s, dx], sib, f)

    def sib_recv(h, s, dx):
        came = wrap(x - dx, rows_x) * 2 + 1 - core
        ref = whole[h].at[came * parts + origin(h, s)]
        return remote(ref, ref, ss.at[h, s, dx], sr.at[h, s, dx], sib, f)

    def e_x_send(d, dx):
        ref = eall.at[dp, wrap(f - d, parts)]
        to = wrap(x + dx, rows_x) * 2 + core
        return remote(ref, ref, ens.at[d, dx], enr.at[d, dx], to, f)

    def e_x_recv(d, dx):
        came = wrap(x - dx, rows_x) * 2 + core
        ref = eall.at[came, wrap(f - d, parts)]
        return remote(ref, ref, ens.at[d, dx], enr.at[d, dx], came, f)

    def e_sib_send(d, dx):
        came = wrap(x - dx, rows_x) * 2 + core
        ref = eall.at[came, wrap(f - d, parts)]
        return remote(ref, ref, ess.at[d, dx], esr.at[d, dx], sib, f)

    def e_sib_recv(d, dx):
        came = wrap(x - dx, rows_x) * 2 + 1 - core
        ref = eall.at[came, wrap(f - d, parts)]
        return remote(ref, ref, ess.at[d, dx], esr.at[d, dx], sib, f)

    def ring_step(s):
        for h in range(2):
            @pl.when(s > 0)
            def _():
                ring_recv(h, s).wait_recv()

            @pl.when(s < parts - 1)
            def _():
                ring_send(h, s).start()

            for dx in range(1, rows_x):
                x_send(h, s, dx).start()
            sib_send(h, s, 0).start()

    def e_step(d):
        @pl.when(d > 0)
        def _():
            g_copies(d, True).wait_recv()

        for dx in range(1, rows_x):
            e_x_send(d, dx).start()
        e_sib_send(d, 0).start()

    def relay(s):
        for h in range(2):
            for dx in range(1, rows_x):
                x_recv(h, s, dx).wait_recv()
                sib_send(h, s, dx).start()

    def e_relay(d):
        for dx in range(1, rows_x):
            e_x_recv(d, dx).wait_recv()
            e_sib_send(d, dx).start()

    def main(s):
        @pl.when(s < parts)
        def _():
            ring_step(s)

        @pl.when(s < parts - 1)
        def _():
            x_copies(s + 1).start()
            g_copies(s + 1).start()

        @pl.when((s >= 1) & (s <= parts))
        def _():
            e_step(s - 1)

        @pl.when((s >= 2) & (s < parts + 2))
        def _():
            relay(s - 2)

        @pl.when(s >= 3)
        def _():
            e_relay(s - 3)

    loop(0, parts + 3, main)

    def finish(s):
        for h in range(2):
            @pl.when(s < parts - 1)
            def _():
                ring_send(h, s).wait_send()

            for dx in range(1, rows_x):
                x_send(h, s, dx).wait_send()
            for dx in range(rows_x):
                sib_recv(h, s, dx).wait_recv()
                sib_send(h, s, dx).wait_send()
        for dx in range(1, rows_x):
            e_x_send(s, dx).wait_send()
        for dx in range(rows_x):
            e_sib_recv(s, dx).wait_recv()
            e_sib_send(s, dx).wait_send()

        @pl.when(s > 0)
        def _():
            x_copies(s, True).wait_recv()
            x_copies(s).wait_send()
            g_copies(s).wait_send()

    loop(0, parts, finish)


def exchange_kernel(parts, groups, src, dst, local, us, ur):
    dp, f = lax.axis_index("dp"), lax.axis_index("fsdp")
    owners = groups * parts
    me = dp * parts + f
    mine = pltpu.make_async_copy(src.at[me], dst.at[me], local)
    mine.start()
    greet_all(me, parts, owners)
    loop(1, owners, lambda d: owner_copy(me, parts, owners, src, dst, us, ur, d).start())
    mine.wait()

    def finish(d):
        owner_copy(me, parts, owners, src, dst, us, ur, d, True).wait_recv()
        owner_copy(me, parts, owners, src, dst, us, ur, d).wait_send()

    loop(1, owners, finish)


def exchange(parts, groups, src):
    owners = groups * parts
    dma = pltpu.SemaphoreType.DMA
    return pl.pallas_call(
        functools.partial(exchange_kernel, parts, groups),
        out_shape=jax.ShapeDtypeStruct(src.shape, BF),
        in_specs=[pl.BlockSpec(memory_space=pl.ANY)],
        out_specs=pl.BlockSpec(memory_space=pl.ANY),
        scratch_shapes=[dma(()), dma((owners,)), dma((owners,))],
        compiler_params=pltpu.CompilerParams(collective_id=5, has_side_effects=True),
        cost_estimate=lasting(25),
    )(src)


def spread(parts, groups, xd, gd, inb, ovb):
    owners, rows_x = groups * parts, groups // 2
    dma = pltpu.SemaphoreType.DMA
    return pl.pallas_call(
        functools.partial(spread_kernel, parts, groups),
        out_shape=(
            jax.ShapeDtypeStruct(xd.shape, BF),
            jax.ShapeDtypeStruct((groups,) + gd.shape, BF),
            jax.ShapeDtypeStruct((owners,) + inb.shape, BF),
            jax.ShapeDtypeStruct((owners,) + ovb.shape, BF),
        ),
        in_specs=[pl.BlockSpec(memory_space=pl.ANY)] * 4,
        out_specs=(pl.BlockSpec(memory_space=pl.ANY),) * 4,
        scratch_shapes=[
            dma((4,)),
            dma((parts,)), dma((parts,)), dma((parts,)), dma((parts,)),
            dma((2, parts)), dma((2, parts)),
            dma((2, parts, rows_x)), dma((2, parts, rows_x)),
            dma((2, parts, rows_x)), dma((2, parts, rows_x)),
            dma((parts, rows_x)), dma((parts, rows_x)),
            dma((parts, rows_x)), dma((parts, rows_x)),
        ],
        compiler_params=pltpu.CompilerParams(collective_id=0, has_side_effects=True),
        cost_estimate=lasting(200),
    )(xd, gd, inb, ovb)


def group_gather_kernel(groups, chunks, src, out, local, ns, nr, ss, sr):
    dp, f = lax.axis_index("dp"), lax.axis_index("fsdp")
    rows_x = groups // 2
    x, core = lax.div(dp, 2), lax.rem(dp, 2)
    sib = x * 2 + 1 - core
    size = src.shape[0] // chunks
    mine = pltpu.make_async_copy(src, out.at[dp], local)
    mine.start()
    greet([(sib, f)] + [(wrap(x + dx, rows_x) * 2 + core, f) for dx in range(1, rows_x)])

    def part(ref, k):
        return ref.at[pl.ds(k * size, size)]

    def x_send(k, dx):
        to = wrap(x + dx, rows_x) * 2 + core
        return remote(part(src, k), part(out.at[dp], k), ns.at[k, dx], nr.at[k, dx], to, f)

    def x_recv(k, dx):
        came = wrap(x - dx, rows_x) * 2 + core
        ref = part(out.at[came], k)
        return remote(ref, ref, ns.at[k, dx], nr.at[k, dx], came, f)

    def sib_send(k, dx):
        came = wrap(x - dx, rows_x) * 2 + core
        ref = part(out.at[came], k)
        return remote(part(src, k) if dx == 0 else ref, ref, ss.at[k, dx], sr.at[k, dx], sib, f)

    def sib_recv(k, dx):
        came = wrap(x - dx, rows_x) * 2 + 1 - core
        ref = part(out.at[came], k)
        return remote(ref, ref, ss.at[k, dx], sr.at[k, dx], sib, f)

    for k in range(chunks):
        for dx in range(1, rows_x):
            x_send(k, dx).start()
    for k in range(chunks):
        sib_send(k, 0).start()
    for k in range(chunks):
        for dx in range(1, rows_x):
            x_recv(k, dx).wait_recv()
            sib_send(k, dx).start()
    mine.wait()
    for k in range(chunks):
        for dx in range(rows_x):
            sib_recv(k, dx).wait_recv()
            sib_send(k, dx).wait_send()
        for dx in range(1, rows_x):
            x_send(k, dx).wait_send()


def group_gather(groups, src):
    chunks, rows_x = 4, groups // 2
    dma = pltpu.SemaphoreType.DMA
    return pl.pallas_call(
        functools.partial(group_gather_kernel, groups, chunks),
        out_shape=jax.ShapeDtypeStruct((groups,) + src.shape, BF),
        in_specs=[pl.BlockSpec(memory_space=pl.ANY)],
        out_specs=pl.BlockSpec(memory_space=pl.ANY),
        scratch_shapes=[dma(())] + [dma((chunks, rows_x))] * 4,
        compiler_params=pltpu.CompilerParams(collective_id=1, has_side_effects=True),
        cost_estimate=lasting(45),
    )(src)


def ffn_back_kernel(
    parts, groups, chunks,
    act, dhid, nrm, grd, w1, w2,
    down, up, dsum, ysum,
    acc, got, gone, wv, psib, sibr, xb, xrb, total,
    rs, rr, gl, wl, gss, gsr, gns, gnr, free, used_sib, used_x,
):
    dp, f = lax.axis_index("dp"), lax.axis_index("fsdp")
    rows_x = groups // 2
    x, core = lax.div(dp, 2), lax.rem(dp, 2)
    sib = x * 2 + 1 - core
    p = ring_place(f, parts)
    nxt, prv = ring_index(p + 1, parts), ring_index(p - 1, parts)
    block, width = down.shape
    half, cut = width // 2, width // chunks
    count, slots = dsum.shape[0], got.shape[2]
    mats = ((act, grd, down), (dhid, nrm, up))
    w1_load = pltpu.make_async_copy(w1, wv, wl)
    w1_load.start()
    greet(
        [(dp, nxt), (dp, prv), (sib, f)]
        + [(wrap(x + dx, rows_x) * 2 + core, f) for dx in range(1, rows_x)]
    )

    def ring_copy(m, h, s):
        return remote(
            gone.at[m, h], got.at[m, h, lax.rem(s, slots)], rs.at[m, h, s], rr.at[m, h, s],
            dp, nxt if h == 0 else prv,
        )

    def products(s):
        for m in range(2):
            left, right = mats[m][:2]
            for h in range(2):
                c = ring_index(p - 1 - s if h == 0 else p + 1 + s, parts)
                acc[m, h] = lax.dot_general(
                    left[:, pl.ds(pl.multiple_of(c * block, block), block)],
                    right[:, h * half : (h + 1) * half],
                    (((0,), (0,)), ((), ())), preferred_element_type=F32,
                )

    def pass_on(s):
        for m in range(2):
            for h in range(2):
                store = pltpu.make_async_copy(
                    gone.at[m, h], mats[m][2].at[:, pl.ds(h * half, half)], gl.at[m, h]
                )

                @pl.when(s == 0)
                def _():
                    gone[m, h] = acc[m, h].astype(BF)

                @pl.when(s > 0)
                def _():
                    ring_copy(m, h, s - 1).wait_recv()
                    ring_copy(m, h, s - 1).wait_send()
                    gone[m, h] = (
                        acc[m, h] + got[m, h, lax.rem(s - 1, slots)].astype(F32)
                    ).astype(BF)

                @pl.when((s > 0) & (s - 1 + slots < parts - 1))
                def _():
                    pl.semaphore_signal(
                        free.at[m, h], inc=1, device_id=(dp, prv if h == 0 else nxt),
                        device_id_type=MESH,
                    )

                @pl.when((s >= slots) & (s < parts - 1))
                def _():
                    pl.semaphore_wait(free.at[m, h], 1)

                @pl.when(s < parts - 1)
                def _():
                    ring_copy(m, h, s).start()

                @pl.when(s == parts - 1)
                def _():
                    store.start()

    def stored():
        for m in range(2):
            for h in range(2):
                pltpu.make_async_copy(
                    gone.at[m, h], mats[m][2].at[:, pl.ds(h * half, half)], gl.at[m, h]
                ).wait()

    def cols(k):
        return pl.ds(pl.multiple_of(k * cut, cut), cut)

    def group_of(dx, c):
        return wrap(x + dx, rows_x) * 2 + (core if c == 0 else 1 - core)

    def rows_of(dx, c):
        return pl.ds(pl.multiple_of(group_of(dx, c) * count, count), count)

    rows_in = (dhid, act)

    def sum_sib(which, dx, k):
        return remote(
            psib.at[dx, :, cols(k)], sibr.at[dx, :, cols(k)],
            gss.at[which, dx, k], gsr.at[which, dx, k], sib, f,
        )

    def sum_x(which, dx, k):
        to = wrap(x + dx, rows_x) * 2 + core
        return remote(
            xb.at[dx - 1, :, cols(k)], xrb.at[dx - 1, :, cols(k)],
            gns.at[which, dx, k], gnr.at[which, dx, k], to, f,
        )

    def other_side(which, dx):
        def one(k):
            psib[dx, :, cols(k)] = jnp.dot(
                rows_in[which][rows_of(dx, 1), :], wv[:, cols(k)], preferred_element_type=F32
            ).astype(BF)
            sum_sib(which, dx, k).start()

        loop(0, chunks, one)

    def own_side(which, dx):
        def one(k):
            here = jnp.dot(
                rows_in[which][rows_of(dx, 0), :], wv[:, cols(k)], preferred_element_type=F32
            )
            sum_sib(which, dx, k).wait_recv()
            here = here + sibr[dx, :, cols(k)].astype(F32)
            if dx == 0:
                total[:, cols(k)] = here
            else:
                xb[dx - 1, :, cols(k)] = here.astype(BF)
                sum_x(which, dx, k).start()

        loop(0, chunks, one)

    def sent_sib(which):
        def one(k):
            for dx in range(rows_x):
                sum_sib(which, dx, k).wait_send()

        loop(0, chunks, one)

    def sent_x(which):
        def one(k):
            for dx in range(1, rows_x):
                sum_x(which, dx, k).wait_send()

        loop(0, chunks, one)

    def collect(which, out):
        def one(k):
            for dx in range(1, rows_x):
                sum_x(which, dx, k).wait_recv()
                total[:, cols(k)] += xrb[dx - 1, :, cols(k)].astype(F32)

        loop(0, chunks, one)
        copy = pltpu.make_async_copy(total, out, wl)
        copy.start()
        copy.wait()

    w2_load = pltpu.make_async_copy(w2, wv, wl)
    far = range(1, rows_x)
    products(0)

    def step(s):
        pass_on(s)

        @pl.when(s < parts - 1)
        def _():
            products(s + 1)

        @pl.when(s == 0)
        def _():
            w1_load.wait()
            for dx in far:
                other_side(0, dx)

        @pl.when(s == 1)
        def _():
            other_side(0, 0)

        @pl.when(s == 2)
        def _():
            for dx in far:
                own_side(0, dx)

        @pl.when(s == 3)
        def _():
            own_side(0, 0)
            w2_load.start()
            pl.semaphore_signal(used_sib, inc=1, device_id=(sib, f), device_id_type=MESH)
            sent_sib(0)

        @pl.when(s == 4)
        def _():
            w2_load.wait()
            pl.semaphore_wait(used_sib, 1)
            for dx in far:
                other_side(1, dx)
            other_side(1, 0)

        @pl.when(s == 5)
        def _():
            collect(0, dsum)
            for dx in far:
                pl.semaphore_signal(
                    used_x, inc=1, device_id=(wrap(x + dx, rows_x) * 2 + core, f), device_id_type=MESH
                )
            sent_x(0)
            pl.semaphore_wait(used_x, rows_x - 1)
            for dx in far:
                own_side(1, dx)

        @pl.when(s == 6)
        def _():
            own_side(1, 0)

    loop(0, parts, step)
    collect(1, ysum)
    sent_sib(1)
    sent_x(1)
    stored()


def ffn_back(parts, groups, act, dhid, nrm, grd, w1, w2):
    chunks, rows_x = 4, groups // 2
    units, width = w1.shape
    count = act.shape[0] // groups
    block, half = units // parts, width // 2
    dma = pltpu.SemaphoreType.DMA
    hbm = pl.BlockSpec(memory_space=pl.ANY)
    vmem = pl.BlockSpec(memory_space=pltpu.VMEM)
    return pl.pallas_call(
        functools.partial(ffn_back_kernel, parts, groups, chunks),
        out_shape=(
            jax.ShapeDtypeStruct((block, width), BF),
            jax.ShapeDtypeStruct((block, width), BF),
            jax.ShapeDtypeStruct((count, width), F32),
            jax.ShapeDtypeStruct((count, width), F32),
        ),
        in_specs=[vmem] * 4 + [hbm] * 2,
        out_specs=(hbm,) * 4,
        scratch_shapes=[
            pltpu.VMEM((2, 2, block, half), F32),
            pltpu.VMEM((2, 2, 3, block, half), BF),
            pltpu.VMEM((2, 2, block, half), BF),
            pltpu.VMEM((units, width), BF),
            pltpu.VMEM((rows_x, count, width), BF),
            pltpu.VMEM((rows_x, count, width), BF),
            pltpu.VMEM((rows_x - 1, count, width), BF),
            pltpu.VMEM((rows_x - 1, count, width), BF),
            pltpu.VMEM((count, width), F32),
            dma((2, 2, parts)), dma((2, 2, parts)), dma((2, 2)), dma(()),
            dma((2, rows_x, chunks)), dma((2, rows_x, chunks)),
            dma((2, rows_x, chunks)), dma((2, rows_x, chunks)),
            pltpu.SemaphoreType.REGULAR((2, 2)),
            pltpu.SemaphoreType.REGULAR,
            pltpu.SemaphoreType.REGULAR,
        ],
        compiler_params=pltpu.CompilerParams(
            collective_id=3, has_side_effects=True, vmem_limit_bytes=60 * 2**20
        ),
        cost_estimate=lasting(175),
    )(act, dhid, nrm, grd, w1, w2)


def finish_kernel(
    parts, groups,
    grads, res, gx, upg, vec,
    total, res_out, gx_out, upg_out, vec_out,
    loc, sibr, xb, xrb, got, gone,
    local, ls, ss, sr, ns, nr, rs, rr, as_, ar, bs, br, us, ur, vs, vr,
):
    dp, f = lax.axis_index("dp"), lax.axis_index("fsdp")
    owners, rows_x = groups * parts, groups // 2
    x, core = lax.div(dp, 2), lax.rem(dp, 2)
    sib = x * 2 + 1 - core
    me = dp * parts + f
    p = ring_place(f, parts)
    nxt, prv = ring_index(p + 1, parts), ring_index(p - 1, parts)
    half = grads.shape[4] // 2
    mine = [
        pltpu.make_async_copy(res.at[f], res_out.at[f], local.at[0]),
        pltpu.make_async_copy(gx.at[f], gx_out.at[f], local.at[1]),
        pltpu.make_async_copy(upg.at[me], upg_out.at[me], local.at[2]),
        pltpu.make_async_copy(vec.at[me], vec_out.at[me], local.at[3]),
    ]
    for copy in mine:
        copy.start()
    greet_all(me, parts, owners)

    def chunk(h, s):
        return ring_index(p - 1 - s if h == 0 else p + 1 + s, parts)

    def sib_copy(h, s):
        piece = grads.at[:, 1 - core, chunk(h, s), :, pl.ds(h * half, half)]
        return remote(piece, sibr.at[h, s], ss.at[h, s], sr.at[h, s], sib, f)

    def own_copy(h, s):
        piece = grads.at[:, core, chunk(h, s), :, pl.ds(h * half, half)]
        return pltpu.make_async_copy(piece, loc.at[h, s], ls.at[h, s])

    def x_copy(h, s, dx):
        to = wrap(x + dx, rows_x) * 2 + core
        return remote(
            xb.at[h, s, dx - 1], xrb.at[h, s, dx - 1], ns.at[h, s, dx], nr.at[h, s, dx], to, f
        )

    def ring_copy(h, s):
        return remote(
            gone.at[h, s], got.at[h, s], rs.at[h, s], rr.at[h, s], dp, nxt if h == 0 else prv
        )

    def res_copies(d, came=False):
        return deal_copy(parts, dp, f, res, res_out, as_, ar, d, came)

    def gx_copies(d, came=False):
        return deal_copy(parts, dp, f, gx, gx_out, bs, br, d, came)

    def upg_copies(d, came=False):
        return owner_copy(me, parts, owners, upg, upg_out, us, ur, d, came)

    def vec_copies(d, came=False):
        return owner_copy(me, parts, owners, vec, vec_out, vs, vr, d, came)

    def begin(s):
        for h in range(2):
            sib_copy(h, s).start()
            own_copy(h, s).start()

    def others(d):
        upg_copies(d).start()
        vec_copies(d).start()

    def returns(d):
        res_copies(d).start()
        gx_copies(d).start()

    def pair(s):
        for h in range(2):
            sib_copy(h, s).wait_recv()
            own_copy(h, s).wait()
            for dx in range(1, rows_x):
                to = wrap(x + dx, rows_x)
                xb[h, s, dx - 1] = (sibr[h, s, to].astype(F32) + loc[h, s, to].astype(F32)).astype(BF)
                x_copy(h, s, dx).start()

    def step(s):
        for h in range(2):
            for dx in range(1, rows_x):
                x_copy(h, s, dx).wait_recv()

            def value():
                here = sibr[h, s, x].astype(F32) + loc[h, s, x].astype(F32)
                for dx in range(1, rows_x):
                    here = here + xrb[h, s, dx - 1].astype(F32)
                return here

            @pl.when(s == 0)
            def _():
                gone[h, s] = value().astype(BF)
                ring_copy(h, s).start()

            @pl.when((s > 0) & (s < parts - 1))
            def _():
                ring_copy(h, s - 1).wait_recv()
                gone[h, s] = (value() + got[h, s - 1].astype(F32)).astype(BF)
                ring_copy(h, s).start()

            @pl.when(s == parts - 1)
            def _():
                ring_copy(h, s - 1).wait_recv()
                total[:, h * half : (h + 1) * half] = value() + got[h, s - 1].astype(F32)

    loop(0, parts, begin)
    loop(1, parts, returns)
    loop(1, owners, others)
    loop(0, parts, pair)
    loop(0, parts, step)

    def finish(s):
        for h in range(2):
            sib_copy(h, s).wait_send()
            for dx in range(1, rows_x):
                x_copy(h, s, dx).wait_send()

            @pl.when(s < parts - 1)
            def _():
                ring_copy(h, s).wait_send()

        @pl.when(s > 0)
        def _():
            for copies in (res_copies, gx_copies):
                copies(s, True).wait_recv()
                copies(s).wait_send()

    loop(0, parts, finish)

    def owner_finish(d):
        for copies in (upg_copies, vec_copies):
            copies(d, True).wait_recv()
            copies(d).wait_send()

    loop(1, owners, owner_finish)
    for copy in mine:
        copy.wait()


def finish_sums(parts, groups, grads, res, gx, upg, vec):
    owners, rows_x = groups * parts, groups // 2
    rows, width = grads.shape[3:]
    half = width // 2
    dma = pltpu.SemaphoreType.DMA
    hbm = pl.BlockSpec(memory_space=pl.ANY)
    return pl.pallas_call(
        functools.partial(finish_kernel, parts, groups),
        out_shape=(
            jax.ShapeDtypeStruct((rows, width), F32),
            jax.ShapeDtypeStruct(res.shape, BF),
            jax.ShapeDtypeStruct(gx.shape, BF),
            jax.ShapeDtypeStruct(upg.shape, BF),
            jax.ShapeDtypeStruct(vec.shape, F32),
        ),
        in_specs=[hbm] * 5,
        out_specs=(pl.BlockSpec(memory_space=pltpu.VMEM),) + (hbm,) * 4,
        scratch_shapes=[
            pltpu.VMEM((2, parts, rows_x, rows, half), BF),
            pltpu.VMEM((2, parts, rows_x, rows, half), BF),
            pltpu.VMEM((2, parts, rows_x - 1, rows, half), BF),
            pltpu.VMEM((2, parts, rows_x - 1, rows, half), BF),
            pltpu.VMEM((2, parts, rows, half), BF),
            pltpu.VMEM((2, parts, rows, half), BF),
            dma((4,)),
            dma((2, parts)), dma((2, parts)), dma((2, parts)),
            dma((2, parts, rows_x)), dma((2, parts, rows_x)),
            dma((2, parts)), dma((2, parts)),
            dma((parts,)), dma((parts,)), dma((parts,)), dma((parts,)),
            dma((owners,)), dma((owners,)), dma((owners,)), dma((owners,)),
        ],
        compiler_params=pltpu.CompilerParams(
            collective_id=4, has_side_effects=True, vmem_limit_bytes=60 * 2**20
        ),
        cost_estimate=lasting(140),
    )(grads, res, gx, upg, vec)


def shards(
    tokens,
    cotangent,
    lengths,
    routing,
    in_weight,
    in_first,
    in_second,
    out_weight,
    out_first,
    out_second,
    up_weight,
    up_first,
    up_second,
    down_weight,
    down_first,
    down_second,
    vectors,
    vector_first,
    vector_second,
):
    bf = jnp.bfloat16
    heads = D // HD
    count = tokens.shape[0]
    parts = lax.axis_size("fsdp")
    groups = lax.axis_size("dp")
    both = ("dp", "fsdp")
    piece = count // parts
    width_in = D + 2 * HD
    slots = jnp.arange(parts, dtype=jnp.int32)
    order = routing[0]
    inverse = jnp.sum(jnp.where(order[:, None] == slots[None, :], slots[:, None], 0), axis=0)

    def deal(array):
        return jnp.take(array.reshape(parts, piece, D), inverse, axis=0)

    def undeal(array):
        return jnp.take(array, order, axis=0).reshape(count, D)

    rows = in_weight.shape[0]
    owners = groups * parts
    out_vec = jnp.concatenate(
        [out_weight.astype(bf), jnp.pad(vectors.astype(bf), ((0, 0), (0, 128 - NVEC)))], axis=1
    )
    up_pieces = up_weight.astype(bf).reshape(rows, owners, FF // owners).transpose(1, 0, 2)
    up_block, dealt, dealt_grad, out_vec = lax.optimization_barrier(
        (exchange(parts, groups, up_pieces), deal(tokens), deal(cotangent), out_vec)
    )
    x_dealt, grad_dealt, whole_in, whole_out = spread(
        parts, groups, dealt, dealt_grad, in_weight.astype(bf), out_vec
    )
    inputs_here = x_dealt.reshape(count, D)
    grad_all = grad_dealt.reshape(groups * count, D)
    grad_here = lax.dynamic_index_in_dim(
        grad_dealt, lax.axis_index("dp"), 0, keepdims=False
    ).reshape(count, D)
    whole_in = whole_in.reshape(D, width_in)
    whole_out = whole_out.reshape(D, D + 128)
    part_down = lax.all_gather(down_weight.astype(bf), "fsdp", axis=0, tiled=True)
    part_up = lax.all_gather(up_block.reshape(D, FF // owners).T, "fsdp", axis=0, tiled=True)

    table = whole_out[:, D : D + NVEC].astype(jnp.float32)
    whole_out = whole_out[:, :D]
    gain_one = table[:, 0]
    shift_one = table[:, 1]
    query_bias = table[:, 2]
    branch_bias = table[:, 3]
    gain_two = table[:, 4]
    shift_two = table[:, 5]
    output_bias = table[:, 6]
    hidden_bias = table[:, 7:].T.reshape(FF)
    ff_here = FF // groups
    ff_start = lax.axis_index("dp") * ff_here
    hidden_bias_here = lax.dynamic_slice(hidden_bias, (ff_start,), (ff_here,))
    allowed = segment_mask(lengths[0], count)
    scale = 1.0 / math.sqrt(HD)
    inputs = inputs_here.astype(jnp.float32)
    norm_one_b = layer_norm(inputs, gain_one, shift_one).astype(bf)
    mixed = jnp.dot(norm_one_b, whole_in, preferred_element_type=jnp.float32)
    query_b = (mixed[:, :D] + query_bias).astype(bf)
    keys_b = mixed[:, D : D + HD].astype(bf)
    values_b = mixed[:, D + HD :].astype(bf)
    query_heads = query_b.reshape(count, heads, HD)

    def score_table():
        raw = (
            jnp.einsum("thd,sd->hts", query_heads, keys_b, preferred_element_type=jnp.float32)
            * scale
        )
        return jnp.where(allowed[None], raw, -1e30)

    scores = score_table()
    top = jnp.max(scores, axis=-1, keepdims=True)
    expo = jnp.exp(scores - top)
    total = jnp.sum(expo, axis=-1, keepdims=True)
    logsum = top + jnp.log(total)
    probs_b = (expo / total).astype(bf)
    attended_b = (
        jnp.einsum("hts,sd->thd", probs_b, values_b, preferred_element_type=jnp.float32)
        .reshape(count, D)
        .astype(bf)
    )
    middle = inputs + (
        jnp.dot(attended_b, whole_out, preferred_element_type=jnp.float32) + branch_bias
    )
    norm_two_b = layer_norm(middle, gain_two, shift_two).astype(bf)

    fused = parts == 8 and groups == 4
    if fused:
        norm_all = group_gather(groups, norm_two_b).reshape(groups * count, D)
    else:
        norm_all = lax.all_gather(norm_two_b, "dp", axis=0, tiled=True)
    hidden = contract_cols(norm_all, part_up) + hidden_bias_here
    grad_active = contract_cols(grad_all, part_down)
    gelu_value, gelu_pull = jax.vjp(gelu_tanh, hidden)
    active_b = gelu_value.astype(bf)
    grad_hidden_b = gelu_pull(grad_active)[0].astype(bf)
    if fused:
        down_grad, up_grad_block, grad_norm_two, branch_two = ffn_back(
            parts, groups, active_b, grad_hidden_b, norm_all, grad_all, part_up, part_down
        )
    else:
        grad_norm_two = lax.psum_scatter(
            jnp.dot(grad_hidden_b, part_up, preferred_element_type=jnp.float32).astype(bf),
            "dp", scatter_dimension=0, tiled=True,
        ).astype(jnp.float32)
        up_grad_block = lax.psum_scatter(
            contract_rows(grad_hidden_b, norm_all).astype(bf),
            "fsdp", scatter_dimension=0, tiled=True,
        )
        down_grad = lax.psum_scatter(
            contract_rows(active_b, grad_all).astype(bf),
            "fsdp", scatter_dimension=0, tiled=True,
        )
        branch_two = lax.psum_scatter(
            jnp.dot(active_b, part_down, preferred_element_type=jnp.float32).astype(bf),
            "dp", scatter_dimension=0, tiled=True,
        ).astype(jnp.float32)
    result = middle + (branch_two + output_bias)

    grad_y = grad_here.astype(jnp.float32)
    norm_value_two, pull_two = jax.vjp(layer_norm, middle, gain_two, shift_two)
    grad_middle_norm, grad_gain_two, grad_shift_two = pull_two(grad_norm_two)
    grad_middle = grad_y + grad_middle_norm
    grad_branch_b = grad_middle.astype(bf)
    grad_attended_b = contract_cols(grad_branch_b, whole_out).astype(bf)
    grad_heads = grad_attended_b.reshape(count, heads, HD)
    probs = jnp.exp(score_table() - logsum)
    probs_again_b = probs.astype(bf)
    grad_probs = jnp.einsum("thd,sd->hts", grad_heads, values_b, preferred_element_type=jnp.float32)
    grad_values_b = jnp.einsum(
        "hts,thd->sd", probs_again_b, grad_heads, preferred_element_type=jnp.float32
    ).astype(bf)
    weighted = jnp.sum(probs * grad_probs, axis=-1, keepdims=True)
    grad_scores_b = (probs * (grad_probs - weighted)).astype(bf)
    grad_query_b = (
        (
            jnp.einsum("hts,sd->thd", grad_scores_b, keys_b, preferred_element_type=jnp.float32)
            * scale
        )
        .reshape(count, D)
        .astype(bf)
    )
    grad_keys_b = (
        jnp.einsum("hts,thd->sd", grad_scores_b, query_heads, preferred_element_type=jnp.float32)
        * scale
    ).astype(bf)
    grad_mixed_b = jnp.concatenate([grad_query_b, grad_keys_b, grad_values_b], axis=1)
    grad_norm_one = contract_cols(grad_mixed_b, whole_in)
    norm_value_one, pull_one = jax.vjp(layer_norm, inputs, gain_one, shift_one)
    grad_inputs_norm, grad_gain_one, grad_shift_one = pull_one(grad_norm_one)
    grad_inputs = grad_middle + grad_inputs_norm
    hidden_sums = jnp.sum(grad_hidden_b.astype(jnp.float32), axis=0)
    hidden_whole = lax.dynamic_update_slice(
        jnp.zeros((FF,), jnp.float32), hidden_sums, (ff_start,)
    )
    vector_grad = jnp.concatenate(
        [
            jnp.stack(
                [
                    grad_gain_one,
                    grad_shift_one,
                    jnp.sum(grad_query_b.astype(jnp.float32), axis=0),
                    jnp.sum(grad_branch_b.astype(jnp.float32), axis=0),
                    grad_gain_two,
                    grad_shift_two,
                    jnp.sum(grad_y, axis=0),
                ],
                axis=0,
            ),
            hidden_whole.reshape(FF // D, D),
        ],
        axis=0,
    )
    vector_grad = vector_grad.reshape(NVEC, owners, rows).transpose(1, 0, 2)
    vector_grad = jnp.pad(vector_grad, ((0, 0), (0, 16 - NVEC), (0, 128 - rows)))
    small_part = jnp.concatenate(
        [
            contract_rows(norm_one_b, grad_mixed_b).astype(bf),
            contract_rows(attended_b, grad_branch_b).astype(bf),
        ],
        axis=1,
    )
    small_grad, back_result, back_grad, grad_up, vector_sum = finish_sums(
        parts,
        groups,
        small_part.reshape(groups // 2, 2, parts, rows, width_in + D),
        result.astype(bf).reshape(parts, piece, D),
        grad_inputs.astype(bf).reshape(parts, piece, D),
        up_grad_block.T.astype(bf).reshape(owners, rows, FF // owners),
        vector_grad,
    )
    grad_up = grad_up.transpose(1, 0, 2).reshape(rows, FF)
    vector_sum = jnp.sum(vector_sum, axis=0)
    grad_in = small_grad[:, :width_in]
    grad_out = small_grad[:, width_in : width_in + D]
    grad_vec = vector_sum[:NVEC, :rows].T
    in_new = adam_update(in_weight, in_first, in_second, grad_in, 1.0 / math.sqrt(D), decay_rate)
    out_new = adam_update(
        out_weight, out_first, out_second, grad_out, 1.0 / math.sqrt(D * 8 // TOK_DEV), decay_rate
    )
    up_new = adam_update(up_weight, up_first, up_second, grad_up, 1.0 / math.sqrt(D), decay_rate)
    down_new = adam_update(
        down_weight, down_first, down_second, down_grad, 1.0 / math.sqrt(FF), decay_rate
    )
    vec_new = adam_update(vectors, vector_first, vector_second, grad_vec, 0.1, 0.0)
    return (undeal(back_result), undeal(back_grad)) + in_new + out_new + up_new + down_new + vec_new


def solution(mesh):
    spec = P(("dp", "fsdp"), None)
    return jax.shard_map(
        shards,
        mesh=mesh,
        in_specs=(spec,) * 19,
        out_specs=(spec,) * 17,
        check_vma=False,
    )
```

```python
import functools
import math

import jax
import jax.numpy as jnp
from jax import lax
from jax.experimental import pallas as pl
from jax.experimental.pallas import tpu as pltpu
from jax.sharding import PartitionSpec as P

D = 2048
FF = 8192
HD = 128
TOK_DEV = 384
STEP = 5
NVEC = 11


eps_norm = 1e-05
beta_one = 0.5
beta_two = 0.5
adam_eps = 1e-08
decay_rate = 0.1


def layer_norm(values, gain, shift):
    centered = values - jnp.mean(values, axis=-1, keepdims=True)
    scaled = centered * lax.rsqrt(jnp.mean(centered * centered, axis=-1, keepdims=True) + eps_norm)
    return scaled * gain + shift


def gelu_tanh(values):
    return (
        0.5
        * values
        * (1.0 + jnp.tanh(0.7978845608028654 * (values + 0.044715 * values * values * values)))
    )


def segment_mask(sizes, count):
    ends = jnp.cumsum(sizes)
    places = jnp.arange(count, dtype=jnp.int32)
    labels = jnp.sum((places[:, None] >= ends[None, :]).astype(jnp.int32), axis=1)
    return (labels[:, None] == labels[None, :]) & (places[None, :] <= places[:, None])


def adam_update(weight, first, second, grad, rate, decay):
    grad = grad.astype(jnp.float32)
    first_new = beta_one * first + (1.0 - beta_one) * grad
    second_new = beta_two * second + (1.0 - beta_two) * grad * grad
    fix_one = 1.0 - beta_one**STEP
    fix_two = 1.0 - beta_two**STEP
    step_size = first_new / fix_one / (jnp.sqrt(second_new / fix_two) + adam_eps)
    weight_new = weight - rate * (step_size + decay * weight)
    return (weight_new, first_new, second_new)


def contract_rows(left, right):
    return lax.dot_general(
        left, right, (((0,), (0,)), ((), ())), preferred_element_type=jnp.float32
    )


def contract_cols(left, right):
    return lax.dot_general(
        left, right, (((1,), (1,)), ((), ())), preferred_element_type=jnp.float32
    )


MESH = pl.DeviceIdType.MESH
F32 = jnp.float32
BF = jnp.bfloat16


def wrap(value, count):
    return lax.rem(value + 2 * count, count)


def ring_place(index, parts):
    if parts != 8:
        return index
    z, y = lax.div(index, 2), lax.rem(index, 2)
    return z + y * (7 - 2 * z)


def ring_index(place, parts):
    place = wrap(place, parts)
    if parts != 8:
        return place
    back = lax.div(place, 4)
    return (1 - back) * 2 * place + back * (15 - 2 * place)


def remote(src, dst, send, recv, dp, fs):
    return pltpu.make_async_remote_copy(
        src_ref=src, dst_ref=dst, send_sem=send, recv_sem=recv, device_id=(dp, fs), device_id_type=MESH
    )


def lasting(micros):
    return pl.CostEstimate(
        flops=int(micros * 1.1e9), bytes_accessed=int(micros * 3.3e6), transcendentals=0
    )


def greet(targets):
    barrier = pltpu.get_barrier_semaphore()
    for dp, fs in targets:
        pl.semaphore_signal(barrier, inc=1, device_id=(dp, fs), device_id_type=MESH)
    pl.semaphore_wait(barrier, len(targets))


def greet_all(me, parts, owners):
    barrier = pltpu.get_barrier_semaphore()

    def one(i, carry):
        peer = wrap(me + i, owners)
        pl.semaphore_signal(
            barrier, inc=1, device_id=(lax.div(peer, parts), lax.rem(peer, parts)), device_id_type=MESH
        )
        return carry

    lax.fori_loop(1, owners, one, 0)
    pl.semaphore_wait(barrier, owners - 1)


def loop(low, high, body):
    def one(i, carry):
        body(i)
        return carry

    lax.fori_loop(low, high, one, 0)


def deal_copy(parts, dp, f, src, dst, send, recv, d, came=False):
    to = wrap(f + d, parts)
    place = wrap(f - d, parts) if came else f
    return remote(src.at[to], dst.at[place], send.at[d], recv.at[d], dp, to)


def owner_copy(me, parts, owners, src, dst, send, recv, d, came=False):
    to = wrap(me + d, owners)
    place = wrap(me - d, owners) if came else me
    return remote(
        src.at[to], dst.at[place], send.at[d], recv.at[d], lax.div(to, parts), lax.rem(to, parts)
    )


def spread_kernel(
    parts, groups,
    xd, gd, inb, ovb,
    xo, eall, win, wov,
    local, xs, xr, gs, gr, rs, rr, ns, nr, ss, sr, ens, enr, ess, esr,
):
    dp, f = lax.axis_index("dp"), lax.axis_index("fsdp")
    owners, rows_x = groups * parts, groups // 2
    x, core = lax.div(dp, 2), lax.rem(dp, 2)
    sib = x * 2 + 1 - core
    me = dp * parts + f
    p = ring_place(f, parts)
    nxt, prv = ring_index(p + 1, parts), ring_index(p - 1, parts)
    whole = (win, wov)
    mine = [
        pltpu.make_async_copy(inb, win.at[me], local.at[0]),
        pltpu.make_async_copy(ovb, wov.at[me], local.at[1]),
        pltpu.make_async_copy(xd.at[f], xo.at[f], local.at[2]),
        pltpu.make_async_copy(gd.at[f], eall.at[dp, f], local.at[3]),
    ]
    for copy in mine:
        copy.start()
    greet(
        [(dp, wrap(f + d, parts)) for d in range(1, parts)]
        + [(sib, f)]
        + [(wrap(x + dx, rows_x) * 2 + core, f) for dx in range(1, rows_x)]
    )
    for copy in mine:
        copy.wait()

    def x_copies(d, came=False):
        return deal_copy(parts, dp, f, xd, xo, xs, xr, d, came)

    def g_copies(d, came=False):
        return deal_copy(parts, dp, f, gd, eall.at[dp], gs, gr, d, came)

    def origin(h, s):
        return ring_index(p - s if h == 0 else p + s, parts)

    def ring_send(h, s):
        ref = whole[h].at[dp * parts + origin(h, s)]
        return remote(ref, ref, rs.at[h, s], rr.at[h, s], dp, nxt if h == 0 else prv)

    def ring_recv(h, s):
        ref = whole[h].at[dp * parts + origin(h, s)]
        return remote(ref, ref, rs.at[h, s - 1], rr.at[h, s - 1], dp, nxt if h == 0 else prv)

    def x_send(h, s, dx):
        ref = whole[h].at[dp * parts + origin(h, s)]
        to = wrap(x + dx, rows_x) * 2 + core
        return remote(ref, ref, ns.at[h, s, dx], nr.at[h, s, dx], to, f)

    def x_recv(h, s, dx):
        came = wrap(x - dx, rows_x) * 2 + core
        ref = whole[h].at[came * parts + origin(h, s)]
        return remote(ref, ref, ns.at[h, s, dx], nr.at[h, s, dx], came, f)

    def sib_send(h, s, dx):
        came = wrap(x - dx, rows_x) * 2 + core
        ref = whole[h].at[came * parts + origin(h, s)]
        return remote(ref, ref, ss.at[h, s, dx], sr.at[h, s, dx], sib, f)

    def sib_recv(h, s, dx):
        came = wrap(x - dx, rows_x) * 2 + 1 - core
        ref = whole[h].at[came * parts + origin(h, s)]
        return remote(ref, ref, ss.at[h, s, dx], sr.at[h, s, dx], sib, f)

    def e_x_send(d, dx):
        ref = eall.at[dp, wrap(f - d, parts)]
        to = wrap(x + dx, rows_x) * 2 + core
        return remote(ref, ref, ens.at[d, dx], enr.at[d, dx], to, f)

    def e_x_recv(d, dx):
        came = wrap(x - dx, rows_x) * 2 + core
        ref = eall.at[came, wrap(f - d, parts)]
        return remote(ref, ref, ens.at[d, dx], enr.at[d, dx], came, f)

    def e_sib_send(d, dx):
        came = wrap(x - dx, rows_x) * 2 + core
        ref = eall.at[came, wrap(f - d, parts)]
        return remote(ref, ref, ess.at[d, dx], esr.at[d, dx], sib, f)

    def e_sib_recv(d, dx):
        came = wrap(x - dx, rows_x) * 2 + 1 - core
        ref = eall.at[came, wrap(f - d, parts)]
        return remote(ref, ref, ess.at[d, dx], esr.at[d, dx], sib, f)

    def ring_step(s):
        for h in range(2):
            @pl.when(s > 0)
            def _():
                ring_recv(h, s).wait_recv()

            @pl.when(s < parts - 1)
            def _():
                ring_send(h, s).start()

            for dx in range(1, rows_x):
                x_send(h, s, dx).start()
            sib_send(h, s, 0).start()

    def e_step(d):
        @pl.when(d > 0)
        def _():
            g_copies(d, True).wait_recv()

        for dx in range(1, rows_x):
            e_x_send(d, dx).start()
        e_sib_send(d, 0).start()

    def relay(s):
        for h in range(2):
            for dx in range(1, rows_x):
                x_recv(h, s, dx).wait_recv()
                sib_send(h, s, dx).start()

    def e_relay(d):
        for dx in range(1, rows_x):
            e_x_recv(d, dx).wait_recv()
            e_sib_send(d, dx).start()

    def main(s):
        @pl.when(s < parts)
        def _():
            ring_step(s)

        @pl.when(s < parts - 1)
        def _():
            x_copies(s + 1).start()
            g_copies(s + 1).start()

        @pl.when((s >= 1) & (s <= parts))
        def _():
            e_step(s - 1)

        @pl.when((s >= 2) & (s < parts + 2))
        def _():
            relay(s - 2)

        @pl.when(s >= 3)
        def _():
            e_relay(s - 3)

    loop(0, parts + 3, main)

    def finish(s):
        for h in range(2):
            @pl.when(s < parts - 1)
            def _():
                ring_send(h, s).wait_send()

            for dx in range(1, rows_x):
                x_send(h, s, dx).wait_send()
            for dx in range(rows_x):
                sib_recv(h, s, dx).wait_recv()
                sib_send(h, s, dx).wait_send()
        for dx in range(1, rows_x):
            e_x_send(s, dx).wait_send()
        for dx in range(rows_x):
            e_sib_recv(s, dx).wait_recv()
            e_sib_send(s, dx).wait_send()

        @pl.when(s > 0)
        def _():
            x_copies(s, True).wait_recv()
            x_copies(s).wait_send()
            g_copies(s).wait_send()

    loop(0, parts, finish)


def exchange_kernel(parts, groups, src, dst, local, us, ur):
    dp, f = lax.axis_index("dp"), lax.axis_index("fsdp")
    owners = groups * parts
    me = dp * parts + f
    mine = pltpu.make_async_copy(src.at[me], dst.at[me], local)
    mine.start()
    greet_all(me, parts, owners)
    loop(1, owners, lambda d: owner_copy(me, parts, owners, src, dst, us, ur, d).start())
    mine.wait()

    def finish(d):
        owner_copy(me, parts, owners, src, dst, us, ur, d, True).wait_recv()
        owner_copy(me, parts, owners, src, dst, us, ur, d).wait_send()

    loop(1, owners, finish)


def exchange(parts, groups, src):
    owners = groups * parts
    dma = pltpu.SemaphoreType.DMA
    return pl.pallas_call(
        functools.partial(exchange_kernel, parts, groups),
        out_shape=jax.ShapeDtypeStruct(src.shape, BF),
        in_specs=[pl.BlockSpec(memory_space=pl.ANY)],
        out_specs=pl.BlockSpec(memory_space=pl.ANY),
        scratch_shapes=[dma(()), dma((owners,)), dma((owners,))],
        compiler_params=pltpu.CompilerParams(collective_id=5, has_side_effects=True),
        cost_estimate=lasting(25),
    )(src)


def spread(parts, groups, xd, gd, inb, ovb):
    owners, rows_x = groups * parts, groups // 2
    dma = pltpu.SemaphoreType.DMA
    return pl.pallas_call(
        functools.partial(spread_kernel, parts, groups),
        out_shape=(
            jax.ShapeDtypeStruct(xd.shape, BF),
            jax.ShapeDtypeStruct((groups,) + gd.shape, BF),
            jax.ShapeDtypeStruct((owners,) + inb.shape, BF),
            jax.ShapeDtypeStruct((owners,) + ovb.shape, BF),
        ),
        in_specs=[pl.BlockSpec(memory_space=pl.ANY)] * 4,
        out_specs=(pl.BlockSpec(memory_space=pl.ANY),) * 4,
        scratch_shapes=[
            dma((4,)),
            dma((parts,)), dma((parts,)), dma((parts,)), dma((parts,)),
            dma((2, parts)), dma((2, parts)),
            dma((2, parts, rows_x)), dma((2, parts, rows_x)),
            dma((2, parts, rows_x)), dma((2, parts, rows_x)),
            dma((parts, rows_x)), dma((parts, rows_x)),
            dma((parts, rows_x)), dma((parts, rows_x)),
        ],
        compiler_params=pltpu.CompilerParams(collective_id=0, has_side_effects=True),
        cost_estimate=lasting(200),
    )(xd, gd, inb, ovb)


def group_gather_kernel(groups, chunks, src, out, local, ns, nr, ss, sr):
    dp, f = lax.axis_index("dp"), lax.axis_index("fsdp")
    rows_x = groups // 2
    x, core = lax.div(dp, 2), lax.rem(dp, 2)
    sib = x * 2 + 1 - core
    size = src.shape[0] // chunks
    mine = pltpu.make_async_copy(src, out.at[dp], local)
    mine.start()
    greet([(sib, f)] + [(wrap(x + dx, rows_x) * 2 + core, f) for dx in range(1, rows_x)])

    def part(ref, k):
        return ref.at[pl.ds(k * size, size)]

    def x_send(k, dx):
        to = wrap(x + dx, rows_x) * 2 + core
        return remote(part(src, k), part(out.at[dp], k), ns.at[k, dx], nr.at[k, dx], to, f)

    def x_recv(k, dx):
        came = wrap(x - dx, rows_x) * 2 + core
        ref = part(out.at[came], k)
        return remote(ref, ref, ns.at[k, dx], nr.at[k, dx], came, f)

    def sib_send(k, dx):
        came = wrap(x - dx, rows_x) * 2 + core
        ref = part(out.at[came], k)
        return remote(part(src, k) if dx == 0 else ref, ref, ss.at[k, dx], sr.at[k, dx], sib, f)

    def sib_recv(k, dx):
        came = wrap(x - dx, rows_x) * 2 + 1 - core
        ref = part(out.at[came], k)
        return remote(ref, ref, ss.at[k, dx], sr.at[k, dx], sib, f)

    for k in range(chunks):
        for dx in range(1, rows_x):
            x_send(k, dx).start()
    for k in range(chunks):
        sib_send(k, 0).start()
    for k in range(chunks):
        for dx in range(1, rows_x):
            x_recv(k, dx).wait_recv()
            sib_send(k, dx).start()
    mine.wait()
    for k in range(chunks):
        for dx in range(rows_x):
            sib_recv(k, dx).wait_recv()
            sib_send(k, dx).wait_send()
        for dx in range(1, rows_x):
            x_send(k, dx).wait_send()


def group_gather(groups, src):
    chunks, rows_x = 4, groups // 2
    dma = pltpu.SemaphoreType.DMA
    return pl.pallas_call(
        functools.partial(group_gather_kernel, groups, chunks),
        out_shape=jax.ShapeDtypeStruct((groups,) + src.shape, BF),
        in_specs=[pl.BlockSpec(memory_space=pl.ANY)],
        out_specs=pl.BlockSpec(memory_space=pl.ANY),
        scratch_shapes=[dma(())] + [dma((chunks, rows_x))] * 4,
        compiler_params=pltpu.CompilerParams(collective_id=1, has_side_effects=True),
        cost_estimate=lasting(45),
    )(src)


def ffn_back_kernel(
    parts, groups, chunks,
    act_t, dhid_t, nrm, grd, act, dhid, w1, w2,
    down, up, dsum, ysum,
    acc, got, gone, wv, psib, sibr, xb, xrb, total, some,
    rs, rr, gl, wl, sl, gss, gsr, gns, gnr, free, used_sib, used_x,
):
    dp, f = lax.axis_index("dp"), lax.axis_index("fsdp")
    rows_x = groups // 2
    x, core = lax.div(dp, 2), lax.rem(dp, 2)
    sib = x * 2 + 1 - core
    p = ring_place(f, parts)
    nxt, prv = ring_index(p + 1, parts), ring_index(p - 1, parts)
    block, width = down.shape
    half, cut = width // 2, width // chunks
    count, slots = dsum.shape[0], got.shape[2]
    mats = ((act_t, grd, down), (dhid_t, nrm, up))
    w1_load = pltpu.make_async_copy(w1, wv, wl)
    w1_load.start()
    greet(
        [(dp, nxt), (dp, prv), (sib, f)]
        + [(wrap(x + dx, rows_x) * 2 + core, f) for dx in range(1, rows_x)]
    )

    def ring_copy(m, h, s):
        return remote(
            gone.at[m, h], got.at[m, h, lax.rem(s, slots)], rs.at[m, h, s], rr.at[m, h, s],
            dp, nxt if h == 0 else prv,
        )

    def products(s):
        for m in range(2):
            left, right = mats[m][:2]
            for h in range(2):
                c = ring_index(p - 1 - s if h == 0 else p + 1 + s, parts)
                acc[m, h] = jnp.dot(
                    left[pl.ds(pl.multiple_of(c * block, block), block), :],
                    right[:, h * half : (h + 1) * half],
                    preferred_element_type=F32,
                )

    def pass_on(s):
        for m in range(2):
            for h in range(2):
                store = pltpu.make_async_copy(
                    gone.at[m, h], mats[m][2].at[:, pl.ds(h * half, half)], gl.at[m, h]
                )

                @pl.when(s == 0)
                def _():
                    gone[m, h] = acc[m, h].astype(BF)

                @pl.when(s > 0)
                def _():
                    ring_copy(m, h, s - 1).wait_recv()
                    ring_copy(m, h, s - 1).wait_send()
                    gone[m, h] = (
                        acc[m, h] + got[m, h, lax.rem(s - 1, slots)].astype(F32)
                    ).astype(BF)

                @pl.when((s > 0) & (s - 1 + slots < parts - 1))
                def _():
                    pl.semaphore_signal(
                        free.at[m, h], inc=1, device_id=(dp, prv if h == 0 else nxt),
                        device_id_type=MESH,
                    )

                @pl.when((s >= slots) & (s < parts - 1))
                def _():
                    pl.semaphore_wait(free.at[m, h], 1)

                @pl.when(s < parts - 1)
                def _():
                    ring_copy(m, h, s).start()

                @pl.when(s == parts - 1)
                def _():
                    store.start()

    def stored():
        for m in range(2):
            for h in range(2):
                pltpu.make_async_copy(
                    gone.at[m, h], mats[m][2].at[:, pl.ds(h * half, half)], gl.at[m, h]
                ).wait()

    def cols(k):
        return pl.ds(pl.multiple_of(k * cut, cut), cut)

    def group_of(dx, c):
        return wrap(x + dx, rows_x) * 2 + (core if c == 0 else 1 - core)

    def rows_of(dx, c):
        return pl.ds(pl.multiple_of(group_of(dx, c) * count, count), count)

    rows_in = (dhid, act)

    def sum_sib(which, dx, k):
        return remote(
            psib.at[dx, :, cols(k)], sibr.at[dx, :, cols(k)],
            gss.at[which, dx, k], gsr.at[which, dx, k], sib, f,
        )

    def sum_x(which, dx, k):
        to = wrap(x + dx, rows_x) * 2 + core
        return remote(
            xb.at[dx - 1, :, cols(k)], xrb.at[dx - 1, :, cols(k)],
            gns.at[which, dx, k], gnr.at[which, dx, k], to, f,
        )

    def take_rows(which, dx, c):
        copy = pltpu.make_async_copy(rows_in[which].at[rows_of(dx, c)], some, sl)
        copy.start()
        copy.wait()

    def other_side(which, dx):
        take_rows(which, dx, 1)

        def one(k):
            psib[dx, :, cols(k)] = jnp.dot(
                some[...], wv[:, cols(k)], preferred_element_type=F32
            ).astype(BF)
            sum_sib(which, dx, k).start()

        loop(0, chunks, one)

    def own_side(which, dx):
        take_rows(which, dx, 0)

        def one(k):
            here = jnp.dot(
                some[...], wv[:, cols(k)], preferred_element_type=F32
            )
            sum_sib(which, dx, k).wait_recv()
            here = here + sibr[dx, :, cols(k)].astype(F32)
            if dx == 0:
                total[:, cols(k)] = here
            else:
                xb[dx - 1, :, cols(k)] = here.astype(BF)
                sum_x(which, dx, k).start()

        loop(0, chunks, one)

    def sent_sib(which):
        def one(k):
            for dx in range(rows_x):
                sum_sib(which, dx, k).wait_send()

        loop(0, chunks, one)

    def sent_x(which):
        def one(k):
            for dx in range(1, rows_x):
                sum_x(which, dx, k).wait_send()

        loop(0, chunks, one)

    def collect(which, out):
        def one(k):
            for dx in range(1, rows_x):
                sum_x(which, dx, k).wait_recv()
                total[:, cols(k)] += xrb[dx - 1, :, cols(k)].astype(F32)

        loop(0, chunks, one)
        copy = pltpu.make_async_copy(total, out, wl)
        copy.start()
        copy.wait()

    w2_load = pltpu.make_async_copy(w2, wv, wl)
    far = range(1, rows_x)
    products(0)

    def step(s):
        pass_on(s)

        @pl.when(s < parts - 1)
        def _():
            products(s + 1)

        @pl.when(s == 0)
        def _():
            w1_load.wait()
            for dx in far:
                other_side(0, dx)

        @pl.when(s == 1)
        def _():
            other_side(0, 0)

        @pl.when(s == 2)
        def _():
            for dx in far:
                own_side(0, dx)

        @pl.when(s == 3)
        def _():
            own_side(0, 0)
            w2_load.start()
            pl.semaphore_signal(used_sib, inc=1, device_id=(sib, f), device_id_type=MESH)
            sent_sib(0)

        @pl.when(s == 4)
        def _():
            w2_load.wait()
            pl.semaphore_wait(used_sib, 1)
            for dx in far:
                other_side(1, dx)
            other_side(1, 0)

        @pl.when(s == 5)
        def _():
            collect(0, dsum)
            for dx in far:
                pl.semaphore_signal(
                    used_x, inc=1, device_id=(wrap(x + dx, rows_x) * 2 + core, f), device_id_type=MESH
                )
            sent_x(0)
            pl.semaphore_wait(used_x, rows_x - 1)
            for dx in far:
                own_side(1, dx)

        @pl.when(s == 6)
        def _():
            own_side(1, 0)

    loop(0, parts, step)
    collect(1, ysum)
    sent_sib(1)
    sent_x(1)
    stored()


def ffn_back(parts, groups, act, dhid, nrm, grd, w1, w2):
    chunks, rows_x = 4, groups // 2
    units, width = w1.shape
    count = act.shape[0] // groups
    block, half = units // parts, width // 2
    dma = pltpu.SemaphoreType.DMA
    hbm = pl.BlockSpec(memory_space=pl.ANY)
    vmem = pl.BlockSpec(memory_space=pltpu.VMEM)
    return pl.pallas_call(
        functools.partial(ffn_back_kernel, parts, groups, chunks),
        out_shape=(
            jax.ShapeDtypeStruct((block, width), BF),
            jax.ShapeDtypeStruct((block, width), BF),
            jax.ShapeDtypeStruct((count, width), F32),
            jax.ShapeDtypeStruct((count, width), F32),
        ),
        in_specs=[vmem] * 4 + [hbm] * 4,
        out_specs=(hbm,) * 4,
        scratch_shapes=[
            pltpu.VMEM((2, 2, block, half), F32),
            pltpu.VMEM((2, 2, 2, block, half), BF),
            pltpu.VMEM((2, 2, block, half), BF),
            pltpu.VMEM((units, width), BF),
            pltpu.VMEM((rows_x, count, width), BF),
            pltpu.VMEM((rows_x, count, width), BF),
            pltpu.VMEM((rows_x - 1, count, width), BF),
            pltpu.VMEM((rows_x - 1, count, width), BF),
            pltpu.VMEM((count, width), F32),
            pltpu.VMEM((count, units), BF),
            dma((2, 2, parts)), dma((2, 2, parts)), dma((2, 2)), dma(()), dma(()),
            dma((2, rows_x, chunks)), dma((2, rows_x, chunks)),
            dma((2, rows_x, chunks)), dma((2, rows_x, chunks)),
            pltpu.SemaphoreType.REGULAR((2, 2)),
            pltpu.SemaphoreType.REGULAR,
            pltpu.SemaphoreType.REGULAR,
        ],
        compiler_params=pltpu.CompilerParams(
            collective_id=3, has_side_effects=True, vmem_limit_bytes=60 * 2**20
        ),
        cost_estimate=lasting(175),
    )(act.T, dhid.T, nrm, grd, act, dhid, w1, w2)


def finish_kernel(
    parts, groups,
    grad_a, grad_b, res, gx, upg, vec,
    total_a, total_b, res_out, gx_out, upg_out, vec_out,
    loc_a, loc_b, sibr_a, sibr_b, xb_a, xb_b, xrb_a, xrb_b, got_a, got_b, gone_a, gone_b,
    local, ls, ss, sr, ns, nr, rs, rr, as_, ar, bs, br, us, ur, vs, vr,
):
    dp, f = lax.axis_index("dp"), lax.axis_index("fsdp")
    owners, rows_x = groups * parts, groups // 2
    x, core = lax.div(dp, 2), lax.rem(dp, 2)
    sib = x * 2 + 1 - core
    me = dp * parts + f
    p = ring_place(f, parts)
    nxt, prv = ring_index(p + 1, parts), ring_index(p - 1, parts)
    grads, total = (grad_a, grad_b), (total_a, total_b)
    loc, sibr, xb, xrb = (loc_a, loc_b), (sibr_a, sibr_b), (xb_a, xb_b), (xrb_a, xrb_b)
    got, gone = (got_a, got_b), (gone_a, gone_b)
    mine = [
        pltpu.make_async_copy(res.at[f], res_out.at[f], local.at[0]),
        pltpu.make_async_copy(gx.at[f], gx_out.at[f], local.at[1]),
        pltpu.make_async_copy(upg.at[me], upg_out.at[me], local.at[2]),
        pltpu.make_async_copy(vec.at[me], vec_out.at[me], local.at[3]),
    ]
    for copy in mine:
        copy.start()
    greet_all(me, parts, owners)

    def chunk(h, s):
        return ring_index(p - 1 - s if h == 0 else p + 1 + s, parts)

    def sib_copy(h, s):
        piece = grads[h].at[:, 1 - core, chunk(h, s)]
        return remote(piece, sibr[h].at[s], ss.at[h, s], sr.at[h, s], sib, f)

    def own_copy(h, s):
        piece = grads[h].at[:, core, chunk(h, s)]
        return pltpu.make_async_copy(piece, loc[h].at[s], ls.at[h, s])

    def x_copy(h, s, dx):
        to = wrap(x + dx, rows_x) * 2 + core
        return remote(
            xb[h].at[s, dx - 1], xrb[h].at[s, dx - 1], ns.at[h, s, dx], nr.at[h, s, dx], to, f
        )

    def ring_copy(h, s):
        return remote(
            gone[h].at[s], got[h].at[s], rs.at[h, s], rr.at[h, s], dp, nxt if h == 0 else prv
        )

    def res_copies(d, came=False):
        return deal_copy(parts, dp, f, res, res_out, as_, ar, d, came)

    def gx_copies(d, came=False):
        return deal_copy(parts, dp, f, gx, gx_out, bs, br, d, came)

    def upg_copies(d, came=False):
        return owner_copy(me, parts, owners, upg, upg_out, us, ur, d, came)

    def vec_copies(d, came=False):
        return owner_copy(me, parts, owners, vec, vec_out, vs, vr, d, came)

    def begin(s):
        for h in range(2):
            sib_copy(h, s).start()
            own_copy(h, s).start()

    def others(d):
        upg_copies(d).start()
        vec_copies(d).start()

    def returns(d):
        res_copies(d).start()
        gx_copies(d).start()

    def pair(s):
        for h in range(2):
            sib_copy(h, s).wait_recv()
            own_copy(h, s).wait()
            for dx in range(1, rows_x):
                to = wrap(x + dx, rows_x)
                xb[h][s, dx - 1] = (sibr[h][s, to].astype(F32) + loc[h][s, to].astype(F32)).astype(BF)
                x_copy(h, s, dx).start()

    def step(s):
        for h in range(2):
            for dx in range(1, rows_x):
                x_copy(h, s, dx).wait_recv()

            def value():
                here = sibr[h][s, x].astype(F32) + loc[h][s, x].astype(F32)
                for dx in range(1, rows_x):
                    here = here + xrb[h][s, dx - 1].astype(F32)
                return here

            @pl.when(s == 0)
            def _():
                gone[h][s] = value().astype(BF)
                ring_copy(h, s).start()

            @pl.when((s > 0) & (s < parts - 1))
            def _():
                ring_copy(h, s - 1).wait_recv()
                gone[h][s] = (value() + got[h][s - 1].astype(F32)).astype(BF)
                ring_copy(h, s).start()

            @pl.when(s == parts - 1)
            def _():
                ring_copy(h, s - 1).wait_recv()
                total[h][...] = value() + got[h][s - 1].astype(F32)

    loop(0, parts, begin)
    loop(1, parts, returns)
    loop(1, owners, others)
    loop(0, parts, pair)
    loop(0, parts, step)

    def finish(s):
        for h in range(2):
            sib_copy(h, s).wait_send()
            for dx in range(1, rows_x):
                x_copy(h, s, dx).wait_send()

            @pl.when(s < parts - 1)
            def _():
                ring_copy(h, s).wait_send()

        @pl.when(s > 0)
        def _():
            for copies in (res_copies, gx_copies):
                copies(s, True).wait_recv()
                copies(s).wait_send()

    loop(0, parts, finish)

    def owner_finish(d):
        for copies in (upg_copies, vec_copies):
            copies(d, True).wait_recv()
            copies(d).wait_send()

    loop(1, owners, owner_finish)
    for copy in mine:
        copy.wait()


def finish_sums(parts, groups, grad_a, grad_b, res, gx, upg, vec):
    owners, rows_x = groups * parts, groups // 2
    rows = grad_a.shape[3]
    widths = (grad_a.shape[4], grad_b.shape[4])
    dma = pltpu.SemaphoreType.DMA
    hbm = pl.BlockSpec(memory_space=pl.ANY)
    return pl.pallas_call(
        functools.partial(finish_kernel, parts, groups),
        out_shape=(
            jax.ShapeDtypeStruct((rows, widths[0]), F32),
            jax.ShapeDtypeStruct((rows, widths[1]), F32),
            jax.ShapeDtypeStruct(res.shape, BF),
            jax.ShapeDtypeStruct(gx.shape, BF),
            jax.ShapeDtypeStruct(upg.shape, BF),
            jax.ShapeDtypeStruct(vec.shape, F32),
        ),
        in_specs=[hbm] * 6,
        out_specs=(pl.BlockSpec(memory_space=pltpu.VMEM),) * 2 + (hbm,) * 4,
        scratch_shapes=[
            *(
                pltpu.VMEM(lead + (rows, width), BF)
                for lead in (
                    (parts, rows_x), (parts, rows_x), (parts, rows_x - 1), (parts, rows_x - 1),
                    (parts,), (parts,),
                )
                for width in widths
            ),
            dma((4,)),
            dma((2, parts)), dma((2, parts)), dma((2, parts)),
            dma((2, parts, rows_x)), dma((2, parts, rows_x)),
            dma((2, parts)), dma((2, parts)),
            dma((parts,)), dma((parts,)), dma((parts,)), dma((parts,)),
            dma((owners,)), dma((owners,)), dma((owners,)), dma((owners,)),
        ],
        compiler_params=pltpu.CompilerParams(
            collective_id=4, has_side_effects=True, vmem_limit_bytes=60 * 2**20
        ),
        cost_estimate=lasting(140),
    )(grad_a, grad_b, res, gx, upg, vec)


def shards(
    tokens,
    cotangent,
    lengths,
    routing,
    in_weight,
    in_first,
    in_second,
    out_weight,
    out_first,
    out_second,
    up_weight,
    up_first,
    up_second,
    down_weight,
    down_first,
    down_second,
    vectors,
    vector_first,
    vector_second,
):
    bf = jnp.bfloat16
    heads = D // HD
    count = tokens.shape[0]
    parts = lax.axis_size("fsdp")
    groups = lax.axis_size("dp")
    both = ("dp", "fsdp")
    piece = count // parts
    width_in = D + 2 * HD
    slots = jnp.arange(parts, dtype=jnp.int32)
    order = routing[0]
    inverse = jnp.sum(jnp.where(order[:, None] == slots[None, :], slots[:, None], 0), axis=0)

    def deal(array):
        return jnp.take(array.reshape(parts, piece, D), inverse, axis=0)

    def undeal(array):
        return jnp.take(array, order, axis=0).reshape(count, D)

    rows = in_weight.shape[0]
    owners = groups * parts
    out_vec = jnp.concatenate(
        [out_weight.astype(bf), jnp.pad(vectors.astype(bf), ((0, 0), (0, 128 - NVEC)))], axis=1
    )
    up_pieces = up_weight.astype(bf).reshape(rows, owners, FF // owners).transpose(1, 0, 2)
    up_block, dealt, dealt_grad, out_vec = lax.optimization_barrier(
        (exchange(parts, groups, up_pieces), deal(tokens), deal(cotangent), out_vec)
    )
    x_dealt, grad_dealt, whole_in, whole_out = spread(
        parts, groups, dealt, dealt_grad, in_weight.astype(bf), out_vec
    )
    inputs_here = x_dealt.reshape(count, D)
    grad_all = grad_dealt.reshape(groups * count, D)
    grad_here = lax.dynamic_index_in_dim(
        grad_dealt, lax.axis_index("dp"), 0, keepdims=False
    ).reshape(count, D)
    whole_in = whole_in.reshape(D, width_in)
    whole_out = whole_out.reshape(D, D + 128)
    part_down = lax.all_gather(down_weight.astype(bf), "fsdp", axis=0, tiled=True)
    part_up = lax.all_gather(up_block.reshape(D, FF // owners).T, "fsdp", axis=0, tiled=True)

    table = whole_out[:, D : D + NVEC].astype(jnp.float32)
    whole_out = whole_out[:, :D]
    gain_one = table[:, 0]
    shift_one = table[:, 1]
    query_bias = table[:, 2]
    branch_bias = table[:, 3]
    gain_two = table[:, 4]
    shift_two = table[:, 5]
    output_bias = table[:, 6]
    hidden_bias = table[:, 7:].T.reshape(FF)
    ff_here = FF // groups
    ff_start = lax.axis_index("dp") * ff_here
    hidden_bias_here = lax.dynamic_slice(hidden_bias, (ff_start,), (ff_here,))
    allowed = segment_mask(lengths[0], count)
    scale = 1.0 / math.sqrt(HD)
    inputs = inputs_here.astype(jnp.float32)
    norm_one_b = layer_norm(inputs, gain_one, shift_one).astype(bf)
    mixed = jnp.dot(norm_one_b, whole_in, preferred_element_type=jnp.float32)
    query_b = (mixed[:, :D] + query_bias).astype(bf)
    keys_b = mixed[:, D : D + HD].astype(bf)
    values_b = mixed[:, D + HD :].astype(bf)
    query_heads = query_b.reshape(count, heads, HD)

    def score_table():
        raw = (
            jnp.einsum("thd,sd->hts", query_heads, keys_b, preferred_element_type=jnp.float32)
            * scale
        )
        return jnp.where(allowed[None], raw, -1e30)

    scores = score_table()
    top = jnp.max(scores, axis=-1, keepdims=True)
    expo = jnp.exp(scores - top)
    total = jnp.sum(expo, axis=-1, keepdims=True)
    logsum = top + jnp.log(total)
    probs_b = (expo / total).astype(bf)
    attended_b = (
        jnp.einsum("hts,sd->thd", probs_b, values_b, preferred_element_type=jnp.float32)
        .reshape(count, D)
        .astype(bf)
    )
    middle = inputs + (
        jnp.dot(attended_b, whole_out, preferred_element_type=jnp.float32) + branch_bias
    )
    norm_two_b = layer_norm(middle, gain_two, shift_two).astype(bf)

    fused = parts == 8 and groups == 4
    if fused:
        norm_all = group_gather(groups, norm_two_b).reshape(groups * count, D)
    else:
        norm_all = lax.all_gather(norm_two_b, "dp", axis=0, tiled=True)
    hidden = contract_cols(norm_all, part_up) + hidden_bias_here
    grad_active = contract_cols(grad_all, part_down)
    gelu_value, gelu_pull = jax.vjp(gelu_tanh, hidden)
    active_b = gelu_value.astype(bf)
    grad_hidden_b = gelu_pull(grad_active)[0].astype(bf)
    active_b, grad_hidden_b = lax.optimization_barrier((active_b, grad_hidden_b))
    if fused:
        down_grad, up_grad_block, grad_norm_two, branch_two = ffn_back(
            parts, groups, active_b, grad_hidden_b, norm_all, grad_all, part_up, part_down
        )
    else:
        grad_norm_two = lax.psum_scatter(
            jnp.dot(grad_hidden_b, part_up, preferred_element_type=jnp.float32).astype(bf),
            "dp", scatter_dimension=0, tiled=True,
        ).astype(jnp.float32)
        up_grad_block = lax.psum_scatter(
            contract_rows(grad_hidden_b, norm_all).astype(bf),
            "fsdp", scatter_dimension=0, tiled=True,
        )
        down_grad = lax.psum_scatter(
            contract_rows(active_b, grad_all).astype(bf),
            "fsdp", scatter_dimension=0, tiled=True,
        )
        branch_two = lax.psum_scatter(
            jnp.dot(active_b, part_down, preferred_element_type=jnp.float32).astype(bf),
            "dp", scatter_dimension=0, tiled=True,
        ).astype(jnp.float32)
    result = middle + (branch_two + output_bias)

    grad_y = grad_here.astype(jnp.float32)
    norm_value_two, pull_two = jax.vjp(layer_norm, middle, gain_two, shift_two)
    grad_middle_norm, grad_gain_two, grad_shift_two = pull_two(grad_norm_two)
    grad_middle = grad_y + grad_middle_norm
    grad_branch_b = grad_middle.astype(bf)
    grad_attended_b = contract_cols(grad_branch_b, whole_out).astype(bf)
    grad_heads = grad_attended_b.reshape(count, heads, HD)
    probs = jnp.exp(score_table() - logsum)
    probs_again_b = probs.astype(bf)
    grad_probs = jnp.einsum("thd,sd->hts", grad_heads, values_b, preferred_element_type=jnp.float32)
    grad_values_b = jnp.einsum(
        "hts,thd->sd", probs_again_b, grad_heads, preferred_element_type=jnp.float32
    ).astype(bf)
    weighted = jnp.sum(probs * grad_probs, axis=-1, keepdims=True)
    grad_scores_b = (probs * (grad_probs - weighted)).astype(bf)
    grad_query_b = (
        (
            jnp.einsum("hts,sd->thd", grad_scores_b, keys_b, preferred_element_type=jnp.float32)
            * scale
        )
        .reshape(count, D)
        .astype(bf)
    )
    grad_keys_b = (
        jnp.einsum("hts,thd->sd", grad_scores_b, query_heads, preferred_element_type=jnp.float32)
        * scale
    ).astype(bf)
    grad_mixed_b = jnp.concatenate([grad_query_b, grad_keys_b, grad_values_b], axis=1)
    grad_norm_one = contract_cols(grad_mixed_b, whole_in)
    norm_value_one, pull_one = jax.vjp(layer_norm, inputs, gain_one, shift_one)
    grad_inputs_norm, grad_gain_one, grad_shift_one = pull_one(grad_norm_one)
    grad_inputs = grad_middle + grad_inputs_norm
    hidden_sums = jnp.sum(grad_hidden_b.astype(jnp.float32), axis=0)
    hidden_whole = lax.dynamic_update_slice(
        jnp.zeros((FF,), jnp.float32), hidden_sums, (ff_start,)
    )
    vector_grad = jnp.concatenate(
        [
            jnp.stack(
                [
                    grad_gain_one,
                    grad_shift_one,
                    jnp.sum(grad_query_b.astype(jnp.float32), axis=0),
                    jnp.sum(grad_branch_b.astype(jnp.float32), axis=0),
                    grad_gain_two,
                    grad_shift_two,
                    jnp.sum(grad_y, axis=0),
                ],
                axis=0,
            ),
            hidden_whole.reshape(FF // D, D),
        ],
        axis=0,
    )
    vector_grad = vector_grad.reshape(NVEC, owners, rows).transpose(1, 0, 2)
    vector_grad = jnp.pad(vector_grad, ((0, 0), (0, 16 - NVEC), (0, 128 - rows)))
    grad_in, grad_out, back_result, back_grad, grad_up, vector_sum = finish_sums(
        parts,
        groups,
        contract_rows(norm_one_b, grad_mixed_b)
        .astype(bf)
        .reshape(groups // 2, 2, parts, rows, width_in),
        contract_rows(attended_b, grad_branch_b).astype(bf).reshape(groups // 2, 2, parts, rows, D),
        result.astype(bf).reshape(parts, piece, D),
        grad_inputs.astype(bf).reshape(parts, piece, D),
        up_grad_block.T.astype(bf).reshape(owners, rows, FF // owners),
        vector_grad,
    )
    grad_up = grad_up.transpose(1, 0, 2).reshape(rows, FF)
    vector_sum = jnp.sum(vector_sum, axis=0)
    grad_vec = vector_sum[:NVEC, :rows].T
    in_new = adam_update(in_weight, in_first, in_second, grad_in, 1.0 / math.sqrt(D), decay_rate)
    out_new = adam_update(
        out_weight, out_first, out_second, grad_out, 1.0 / math.sqrt(D * 8 // TOK_DEV), decay_rate
    )
    up_new = adam_update(up_weight, up_first, up_second, grad_up, 1.0 / math.sqrt(D), decay_rate)
    down_new = adam_update(
        down_weight, down_first, down_second, down_grad, 1.0 / math.sqrt(FF), decay_rate
    )
    vec_new = adam_update(vectors, vector_first, vector_second, grad_vec, 0.1, 0.0)
    return (undeal(back_result), undeal(back_grad)) + in_new + out_new + up_new + down_new + vec_new


def solution(mesh):
    spec = P(("dp", "fsdp"), None)
    return jax.shard_map(
        shards,
        mesh=mesh,
        in_specs=(spec,) * 19,
        out_specs=(spec,) * 17,
        check_vma=False,
    )
```

```python
import functools
import math

import jax
import jax.numpy as jnp
from jax import lax
from jax.experimental import pallas as pl
from jax.experimental.pallas import tpu as pltpu
from jax.sharding import PartitionSpec as P

D = 2048
FF = 8192
HD = 128
TOK_DEV = 384
STEP = 5
NVEC = 11


eps_norm = 1e-05
beta_one = 0.5
beta_two = 0.5
adam_eps = 1e-08
decay_rate = 0.1


def layer_norm(values, gain, shift):
    centered = values - jnp.mean(values, axis=-1, keepdims=True)
    scaled = centered * lax.rsqrt(jnp.mean(centered * centered, axis=-1, keepdims=True) + eps_norm)
    return scaled * gain + shift


def gelu_tanh(values):
    return (
        0.5
        * values
        * (1.0 + jnp.tanh(0.7978845608028654 * (values + 0.044715 * values * values * values)))
    )


def segment_mask(sizes, count):
    ends = jnp.cumsum(sizes)
    places = jnp.arange(count, dtype=jnp.int32)
    labels = jnp.sum((places[:, None] >= ends[None, :]).astype(jnp.int32), axis=1)
    return (labels[:, None] == labels[None, :]) & (places[None, :] <= places[:, None])


def adam_update(weight, first, second, grad, rate, decay):
    grad = grad.astype(jnp.float32)
    first_new = beta_one * first + (1.0 - beta_one) * grad
    second_new = beta_two * second + (1.0 - beta_two) * grad * grad
    fix_one = 1.0 - beta_one**STEP
    fix_two = 1.0 - beta_two**STEP
    step_size = first_new / fix_one / (jnp.sqrt(second_new / fix_two) + adam_eps)
    weight_new = weight - rate * (step_size + decay * weight)
    return (weight_new, first_new, second_new)


def contract_rows(left, right):
    return lax.dot_general(
        left, right, (((0,), (0,)), ((), ())), preferred_element_type=jnp.float32
    )


def contract_cols(left, right):
    return lax.dot_general(
        left, right, (((1,), (1,)), ((), ())), preferred_element_type=jnp.float32
    )


MESH = pl.DeviceIdType.MESH
F32 = jnp.float32
BF = jnp.bfloat16


def wrap(value, count):
    return lax.rem(value + 2 * count, count)


def ring_place(index, parts):
    if parts != 8:
        return index
    z, y = lax.div(index, 2), lax.rem(index, 2)
    return z + y * (7 - 2 * z)


def ring_index(place, parts):
    place = wrap(place, parts)
    if parts != 8:
        return place
    back = lax.div(place, 4)
    return (1 - back) * 2 * place + back * (15 - 2 * place)


def remote(src, dst, send, recv, dp, fs):
    return pltpu.make_async_remote_copy(
        src_ref=src, dst_ref=dst, send_sem=send, recv_sem=recv, device_id=(dp, fs), device_id_type=MESH
    )


def lasting(micros):
    return pl.CostEstimate(
        flops=int(micros * 1.1e9), bytes_accessed=int(micros * 3.3e6), transcendentals=0
    )


def greet(targets):
    barrier = pltpu.get_barrier_semaphore()
    for dp, fs in targets:
        pl.semaphore_signal(barrier, inc=1, device_id=(dp, fs), device_id_type=MESH)
    pl.semaphore_wait(barrier, len(targets))


def greet_all(me, parts, owners):
    barrier = pltpu.get_barrier_semaphore()

    def one(i, carry):
        peer = wrap(me + i, owners)
        pl.semaphore_signal(
            barrier, inc=1, device_id=(lax.div(peer, parts), lax.rem(peer, parts)), device_id_type=MESH
        )
        return carry

    lax.fori_loop(1, owners, one, 0)
    pl.semaphore_wait(barrier, owners - 1)


def loop(low, high, body):
    def one(i, carry):
        body(i)
        return carry

    lax.fori_loop(low, high, one, 0)


def deal_copy(parts, dp, f, src, dst, send, recv, d, came=False):
    to = wrap(f + d, parts)
    place = wrap(f - d, parts) if came else f
    return remote(src.at[to], dst.at[place], send.at[d], recv.at[d], dp, to)


def owner_copy(me, parts, owners, src, dst, send, recv, d, came=False):
    to = wrap(me + d, owners)
    place = wrap(me - d, owners) if came else me
    return remote(
        src.at[to], dst.at[place], send.at[d], recv.at[d], lax.div(to, parts), lax.rem(to, parts)
    )


def spread_kernel(
    parts, groups,
    xd, gd, inb, ovb,
    xo, eall, win, wov,
    local, xs, xr, gs, gr, rs, rr, ns, nr, ss, sr, ens, enr, ess, esr,
):
    dp, f = lax.axis_index("dp"), lax.axis_index("fsdp")
    owners, rows_x = groups * parts, groups // 2
    x, core = lax.div(dp, 2), lax.rem(dp, 2)
    sib = x * 2 + 1 - core
    me = dp * parts + f
    p = ring_place(f, parts)
    nxt, prv = ring_index(p + 1, parts), ring_index(p - 1, parts)
    whole = (win, wov)
    mine = [
        pltpu.make_async_copy(inb, win.at[me], local.at[0]),
        pltpu.make_async_copy(ovb, wov.at[me], local.at[1]),
        pltpu.make_async_copy(xd.at[f], xo.at[f], local.at[2]),
        pltpu.make_async_copy(gd.at[f], eall.at[dp, f], local.at[3]),
    ]
    for copy in mine:
        copy.start()
    greet(
        [(dp, wrap(f + d, parts)) for d in range(1, parts)]
        + [(sib, f)]
        + [(wrap(x + dx, rows_x) * 2 + core, f) for dx in range(1, rows_x)]
    )
    for copy in mine:
        copy.wait()

    def x_copies(d, came=False):
        return deal_copy(parts, dp, f, xd, xo, xs, xr, d, came)

    def g_copies(d, came=False):
        return deal_copy(parts, dp, f, gd, eall.at[dp], gs, gr, d, came)

    def origin(h, s):
        return ring_index(p - s if h == 0 else p + s, parts)

    def ring_send(h, s):
        ref = whole[h].at[dp * parts + origin(h, s)]
        return remote(ref, ref, rs.at[h, s], rr.at[h, s], dp, nxt if h == 0 else prv)

    def ring_recv(h, s):
        ref = whole[h].at[dp * parts + origin(h, s)]
        return remote(ref, ref, rs.at[h, s - 1], rr.at[h, s - 1], dp, nxt if h == 0 else prv)

    def x_send(h, s, dx):
        ref = whole[h].at[dp * parts + origin(h, s)]
        to = wrap(x + dx, rows_x) * 2 + core
        return remote(ref, ref, ns.at[h, s, dx], nr.at[h, s, dx], to, f)

    def x_recv(h, s, dx):
        came = wrap(x - dx, rows_x) * 2 + core
        ref = whole[h].at[came * parts + origin(h, s)]
        return remote(ref, ref, ns.at[h, s, dx], nr.at[h, s, dx], came, f)

    def sib_send(h, s, dx):
        came = wrap(x - dx, rows_x) * 2 + core
        ref = whole[h].at[came * parts + origin(h, s)]
        return remote(ref, ref, ss.at[h, s, dx], sr.at[h, s, dx], sib, f)

    def sib_recv(h, s, dx):
        came = wrap(x - dx, rows_x) * 2 + 1 - core
        ref = whole[h].at[came * parts + origin(h, s)]
        return remote(ref, ref, ss.at[h, s, dx], sr.at[h, s, dx], sib, f)

    def e_x_send(d, dx):
        ref = eall.at[dp, wrap(f - d, parts)]
        to = wrap(x + dx, rows_x) * 2 + core
        return remote(ref, ref, ens.at[d, dx], enr.at[d, dx], to, f)

    def e_x_recv(d, dx):
        came = wrap(x - dx, rows_x) * 2 + core
        ref = eall.at[came, wrap(f - d, parts)]
        return remote(ref, ref, ens.at[d, dx], enr.at[d, dx], came, f)

    def e_sib_send(d, dx):
        came = wrap(x - dx, rows_x) * 2 + core
        ref = eall.at[came, wrap(f - d, parts)]
        return remote(ref, ref, ess.at[d, dx], esr.at[d, dx], sib, f)

    def e_sib_recv(d, dx):
        came = wrap(x - dx, rows_x) * 2 + 1 - core
        ref = eall.at[came, wrap(f - d, parts)]
        return remote(ref, ref, ess.at[d, dx], esr.at[d, dx], sib, f)

    def ring_step(s):
        for h in range(2):
            @pl.when(s > 0)
            def _():
                ring_recv(h, s).wait_recv()

            @pl.when(s < parts - 1)
            def _():
                ring_send(h, s).start()

            for dx in range(1, rows_x):
                x_send(h, s, dx).start()
            sib_send(h, s, 0).start()

    def e_step(d):
        @pl.when(d > 0)
        def _():
            g_copies(d, True).wait_recv()

        for dx in range(1, rows_x):
            e_x_send(d, dx).start()
        e_sib_send(d, 0).start()

    def relay(s):
        for h in range(2):
            for dx in range(1, rows_x):
                x_recv(h, s, dx).wait_recv()
                sib_send(h, s, dx).start()

    def e_relay(d):
        for dx in range(1, rows_x):
            e_x_recv(d, dx).wait_recv()
            e_sib_send(d, dx).start()

    def main(s):
        @pl.when(s < parts)
        def _():
            ring_step(s)

        @pl.when(s < parts - 1)
        def _():
            x_copies(s + 1).start()
            g_copies(s + 1).start()

        @pl.when((s >= 1) & (s <= parts))
        def _():
            e_step(s - 1)

        @pl.when((s >= 2) & (s < parts + 2))
        def _():
            relay(s - 2)

        @pl.when(s >= 3)
        def _():
            e_relay(s - 3)

    loop(0, parts + 3, main)

    def finish(s):
        for h in range(2):
            @pl.when(s < parts - 1)
            def _():
                ring_send(h, s).wait_send()

            for dx in range(1, rows_x):
                x_send(h, s, dx).wait_send()
            for dx in range(rows_x):
                sib_recv(h, s, dx).wait_recv()
                sib_send(h, s, dx).wait_send()
        for dx in range(1, rows_x):
            e_x_send(s, dx).wait_send()
        for dx in range(rows_x):
            e_sib_recv(s, dx).wait_recv()
            e_sib_send(s, dx).wait_send()

        @pl.when(s > 0)
        def _():
            x_copies(s, True).wait_recv()
            x_copies(s).wait_send()
            g_copies(s).wait_send()

    loop(0, parts, finish)


def exchange_kernel(parts, groups, src, dst, local, us, ur):
    dp, f = lax.axis_index("dp"), lax.axis_index("fsdp")
    owners = groups * parts
    me = dp * parts + f
    mine = pltpu.make_async_copy(src.at[me], dst.at[me], local)
    mine.start()
    greet_all(me, parts, owners)
    loop(1, owners, lambda d: owner_copy(me, parts, owners, src, dst, us, ur, d).start())
    mine.wait()

    def finish(d):
        owner_copy(me, parts, owners, src, dst, us, ur, d, True).wait_recv()
        owner_copy(me, parts, owners, src, dst, us, ur, d).wait_send()

    loop(1, owners, finish)


def exchange(parts, groups, src):
    owners = groups * parts
    dma = pltpu.SemaphoreType.DMA
    return pl.pallas_call(
        functools.partial(exchange_kernel, parts, groups),
        out_shape=jax.ShapeDtypeStruct(src.shape, BF),
        in_specs=[pl.BlockSpec(memory_space=pl.ANY)],
        out_specs=pl.BlockSpec(memory_space=pl.ANY),
        scratch_shapes=[dma(()), dma((owners,)), dma((owners,))],
        compiler_params=pltpu.CompilerParams(collective_id=5, has_side_effects=True),
        cost_estimate=lasting(25),
    )(src)


def spread(parts, groups, xd, gd, inb, ovb):
    owners, rows_x = groups * parts, groups // 2
    dma = pltpu.SemaphoreType.DMA
    return pl.pallas_call(
        functools.partial(spread_kernel, parts, groups),
        out_shape=(
            jax.ShapeDtypeStruct(xd.shape, BF),
            jax.ShapeDtypeStruct((groups,) + gd.shape, BF),
            jax.ShapeDtypeStruct((owners,) + inb.shape, BF),
            jax.ShapeDtypeStruct((owners,) + ovb.shape, BF),
        ),
        in_specs=[pl.BlockSpec(memory_space=pl.ANY)] * 4,
        out_specs=(pl.BlockSpec(memory_space=pl.ANY),) * 4,
        scratch_shapes=[
            dma((4,)),
            dma((parts,)), dma((parts,)), dma((parts,)), dma((parts,)),
            dma((2, parts)), dma((2, parts)),
            dma((2, parts, rows_x)), dma((2, parts, rows_x)),
            dma((2, parts, rows_x)), dma((2, parts, rows_x)),
            dma((parts, rows_x)), dma((parts, rows_x)),
            dma((parts, rows_x)), dma((parts, rows_x)),
        ],
        compiler_params=pltpu.CompilerParams(collective_id=0, has_side_effects=True),
        cost_estimate=lasting(200),
    )(xd, gd, inb, ovb)


def group_gather_kernel(groups, chunks, src, out, local, ns, nr, ss, sr):
    dp, f = lax.axis_index("dp"), lax.axis_index("fsdp")
    rows_x = groups // 2
    x, core = lax.div(dp, 2), lax.rem(dp, 2)
    sib = x * 2 + 1 - core
    size = src.shape[0] // chunks
    mine = pltpu.make_async_copy(src, out.at[dp], local)
    mine.start()
    greet([(sib, f)] + [(wrap(x + dx, rows_x) * 2 + core, f) for dx in range(1, rows_x)])

    def part(ref, k):
        return ref.at[pl.ds(k * size, size)]

    def x_send(k, dx):
        to = wrap(x + dx, rows_x) * 2 + core
        return remote(part(src, k), part(out.at[dp], k), ns.at[k, dx], nr.at[k, dx], to, f)

    def x_recv(k, dx):
        came = wrap(x - dx, rows_x) * 2 + core
        ref = part(out.at[came], k)
        return remote(ref, ref, ns.at[k, dx], nr.at[k, dx], came, f)

    def sib_send(k, dx):
        came = wrap(x - dx, rows_x) * 2 + core
        ref = part(out.at[came], k)
        return remote(part(src, k) if dx == 0 else ref, ref, ss.at[k, dx], sr.at[k, dx], sib, f)

    def sib_recv(k, dx):
        came = wrap(x - dx, rows_x) * 2 + 1 - core
        ref = part(out.at[came], k)
        return remote(ref, ref, ss.at[k, dx], sr.at[k, dx], sib, f)

    for k in range(chunks):
        for dx in range(1, rows_x):
            x_send(k, dx).start()
    for k in range(chunks):
        sib_send(k, 0).start()
    for k in range(chunks):
        for dx in range(1, rows_x):
            x_recv(k, dx).wait_recv()
            sib_send(k, dx).start()
    mine.wait()
    for k in range(chunks):
        for dx in range(rows_x):
            sib_recv(k, dx).wait_recv()
            sib_send(k, dx).wait_send()
        for dx in range(1, rows_x):
            x_send(k, dx).wait_send()


def group_gather(groups, src):
    chunks, rows_x = 4, groups // 2
    dma = pltpu.SemaphoreType.DMA
    return pl.pallas_call(
        functools.partial(group_gather_kernel, groups, chunks),
        out_shape=jax.ShapeDtypeStruct((groups,) + src.shape, BF),
        in_specs=[pl.BlockSpec(memory_space=pl.ANY)],
        out_specs=pl.BlockSpec(memory_space=pl.ANY),
        scratch_shapes=[dma(())] + [dma((chunks, rows_x))] * 4,
        compiler_params=pltpu.CompilerParams(collective_id=1, has_side_effects=True),
        cost_estimate=lasting(45),
    )(src)


def ffn_back_kernel(
    parts, groups, chunks, streams,
    grad, act, dhid, w1, w2,
    out, dsum, ysum,
    loc, got, gone, w1v, w2v, some, psib, sibr, xb, xrb,
    ll, ol, rs, rr, wl, sl, gss, gsr, gns, gnr,
):
    dp, f = lax.axis_index("dp"), lax.axis_index("fsdp")
    rows_x = groups // 2
    x, core = lax.div(dp, 2), lax.rem(dp, 2)
    sib = x * 2 + 1 - core
    p = ring_place(f, parts)
    nxt, prv = ring_index(p + 1, parts), ring_index(p - 1, parts)
    block, width = out.shape
    part, cut = width // streams, width // chunks
    count = dsum.shape[0]
    far = range(1, rows_x)

    def local_copy(h, s):
        c = ring_index(p - 1 - s if h % 2 == 0 else p + 1 + s, parts)
        return pltpu.make_async_copy(
            grad.at[pl.ds(pl.multiple_of(c * block, block), block), pl.ds(h * part, part)],
            loc.at[lax.rem(s, 2), h], ll.at[lax.rem(s, 2), h],
        )

    w_loads = (
        pltpu.make_async_copy(w1, w1v, wl.at[0]),
        pltpu.make_async_copy(w2, w2v, wl.at[1]),
    )
    for s in range(2):
        for h in range(streams):
            local_copy(h, s).start()
    for load in w_loads:
        load.start()
    greet(
        [(dp, nxt), (dp, prv), (sib, f)]
        + [(wrap(x + dx, rows_x) * 2 + core, f) for dx in range(1, rows_x)]
    )

    def ring_copy(h, s):
        return remote(
            gone.at[lax.rem(s, 2), h], got.at[h, s], rs.at[h, s], rr.at[h, s],
            dp, nxt if h % 2 == 0 else prv,
        )

    def out_copy(h):
        return pltpu.make_async_copy(
            gone.at[lax.rem(parts - 1, 2), h], out.at[:, pl.ds(h * part, part)], ol.at[h]
        )

    def pass_on(s):
        slot = lax.rem(s, 2)
        for h in range(streams):
            local_copy(h, s).wait()

            @pl.when(s >= 2)
            def _():
                ring_copy(h, s - 2).wait_send()

            @pl.when(s == 0)
            def _():
                gone[slot, h] = loc[slot, h]

            @pl.when(s > 0)
            def _():
                ring_copy(h, s - 1).wait_recv()
                gone[slot, h] = (
                    loc[slot, h].astype(F32) + got[h, s - 1].astype(F32)
                ).astype(BF)

            @pl.when(s < parts - 1)
            def _():
                ring_copy(h, s).start()

            @pl.when(s == parts - 1)
            def _():
                out_copy(h).start()

            @pl.when(s < parts - 2)
            def _():
                local_copy(h, s + 2).start()

    def cols(k):
        return pl.ds(pl.multiple_of(k * cut, cut), cut)

    def rows_of(dx, c):
        group = wrap(x + dx, rows_x) * 2 + (core if c == 0 else 1 - core)
        return pl.ds(pl.multiple_of(group * count, count), count)

    rows_in, weights, totals = (dhid, act), (w1v, w2v), (dsum, ysum)

    def sum_sib(which, k):
        return remote(
            psib.at[which, :, :, cols(k)], sibr.at[which, :, :, cols(k)],
            gss.at[which, k], gsr.at[which, k], sib, f,
        )

    def sum_x(which, dx, k):
        to = wrap(x + dx, rows_x) * 2 + core
        return remote(
            xb.at[which, dx - 1, :, cols(k)], xrb.at[which, dx - 1, :, cols(k)],
            gns.at[which, dx, k], gnr.at[which, dx, k], to, f,
        )

    def take_rows(which, c):
        copies = [
            pltpu.make_async_copy(
                rows_in[which].at[rows_of(dx, c)], some.at[pl.ds(dx * count, count)], sl.at[dx]
            )
            for dx in range(rows_x)
        ]
        for copy in copies:
            copy.start()
        for copy in copies:
            copy.wait()

    def other_side(which):
        take_rows(which, 1)

        def one(k):
            psib[which, :, :, cols(k)] = (
                jnp.dot(some[...], weights[which][:, cols(k)], preferred_element_type=F32)
                .astype(BF)
                .reshape(rows_x, count, cut)
            )
            sum_sib(which, k).start()

        loop(0, chunks, one)

    def own_side(which):
        take_rows(which, 0)

        def one(k):
            here = jnp.dot(some[...], weights[which][:, cols(k)], preferred_element_type=F32)
            sum_sib(which, k).wait_recv()
            here = here.reshape(rows_x, count, cut) + sibr[which, :, :, cols(k)].astype(F32)
            for dx in far:
                xb[which, dx - 1, :, cols(k)] = here[dx].astype(BF)
                sum_x(which, dx, k).start()
            totals[which][:, cols(k)] = here[0]

        loop(0, chunks, one)

    def collect(which):
        def one(k):
            for dx in far:
                sum_x(which, dx, k).wait_recv()
                totals[which][:, cols(k)] += xrb[which, dx - 1, :, cols(k)].astype(F32)

        loop(0, chunks, one)

    def step(s):
        pass_on(s)

        @pl.when(s == 0)
        def _():
            w_loads[0].wait()
            other_side(0)

        @pl.when(s == 1)
        def _():
            own_side(0)

        @pl.when(s == 2)
        def _():
            w_loads[1].wait()
            other_side(1)

        @pl.when(s == 3)
        def _():
            own_side(1)

        @pl.when(s == 4)
        def _():
            collect(0)

    loop(0, parts, step)
    collect(1)
    for h in range(streams):
        ring_copy(h, parts - 2).wait_send()
        out_copy(h).wait()
    for which in range(2):
        for k in range(chunks):
            sum_sib(which, k).wait_send()
            for dx in far:
                sum_x(which, dx, k).wait_send()


def ffn_back(parts, groups, grad, act, dhid, w1, w2):
    chunks, streams, rows_x = 4, 4, groups // 2
    units, width = w1.shape
    count = act.shape[0] // groups
    block, part = units // parts, width // streams
    dma = pltpu.SemaphoreType.DMA
    hbm = pl.BlockSpec(memory_space=pl.ANY)
    vmem = pl.BlockSpec(memory_space=pltpu.VMEM)
    return pl.pallas_call(
        functools.partial(ffn_back_kernel, parts, groups, chunks, streams),
        out_shape=(
            jax.ShapeDtypeStruct((block, width), BF),
            jax.ShapeDtypeStruct((count, width), F32),
            jax.ShapeDtypeStruct((count, width), F32),
        ),
        in_specs=[hbm] * 5,
        out_specs=(hbm, vmem, vmem),
        scratch_shapes=[
            pltpu.VMEM((2, streams, block, part), BF),
            pltpu.VMEM((streams, parts - 1, block, part), BF),
            pltpu.VMEM((2, streams, block, part), BF),
            pltpu.VMEM((units, width), BF),
            pltpu.VMEM((units, width), BF),
            pltpu.VMEM((rows_x * count, units), BF),
            pltpu.VMEM((2, rows_x, count, width), BF),
            pltpu.VMEM((2, rows_x, count, width), BF),
            pltpu.VMEM((2, rows_x - 1, count, width), BF),
            pltpu.VMEM((2, rows_x - 1, count, width), BF),
            dma((2, streams)), dma((streams,)),
            dma((streams, parts)), dma((streams, parts)), dma((2,)), dma((rows_x,)),
            dma((2, chunks)), dma((2, chunks)),
            dma((2, rows_x, chunks)), dma((2, rows_x, chunks)),
        ],
        compiler_params=pltpu.CompilerParams(
            collective_id=3, has_side_effects=True, vmem_limit_bytes=60 * 2**20
        ),
        cost_estimate=lasting(110),
    )(grad, act, dhid, w1, w2)


def finish_kernel(
    parts, groups,
    grad_a, grad_b, res, gx, upg, vec,
    total_a, total_b, res_out, gx_out, upg_out, vec_out,
    loc_a, loc_b, sibr_a, sibr_b, xb_a, xb_b, xrb_a, xrb_b, got_a, got_b, gone_a, gone_b,
    local, ls, ss, sr, ns, nr, rs, rr, as_, ar, bs, br, us, ur, vs, vr,
):
    dp, f = lax.axis_index("dp"), lax.axis_index("fsdp")
    owners, rows_x = groups * parts, groups // 2
    x, core = lax.div(dp, 2), lax.rem(dp, 2)
    sib = x * 2 + 1 - core
    me = dp * parts + f
    p = ring_place(f, parts)
    nxt, prv = ring_index(p + 1, parts), ring_index(p - 1, parts)
    grads, total = (grad_a, grad_b), (total_a, total_b)
    loc, sibr, xb, xrb = (loc_a, loc_b), (sibr_a, sibr_b), (xb_a, xb_b), (xrb_a, xrb_b)
    got, gone = (got_a, got_b), (gone_a, gone_b)
    mine = [
        pltpu.make_async_copy(res.at[f], res_out.at[f], local.at[0]),
        pltpu.make_async_copy(gx.at[f], gx_out.at[f], local.at[1]),
        pltpu.make_async_copy(upg.at[me], upg_out.at[me], local.at[2]),
        pltpu.make_async_copy(vec.at[me], vec_out.at[me], local.at[3]),
    ]
    for copy in mine:
        copy.start()
    greet_all(me, parts, owners)

    def chunk(h, s):
        return ring_index(p - 1 - s if h == 0 else p + 1 + s, parts)

    def sib_copy(h, s):
        piece = grads[h].at[:, 1 - core, chunk(h, s)]
        return remote(piece, sibr[h].at[s], ss.at[h, s], sr.at[h, s], sib, f)

    def own_copy(h, s):
        piece = grads[h].at[:, core, chunk(h, s)]
        return pltpu.make_async_copy(piece, loc[h].at[s], ls.at[h, s])

    def x_copy(h, s, dx):
        to = wrap(x + dx, rows_x) * 2 + core
        return remote(
            xb[h].at[s, dx - 1], xrb[h].at[s, dx - 1], ns.at[h, s, dx], nr.at[h, s, dx], to, f
        )

    def ring_copy(h, s):
        return remote(
            gone[h].at[s], got[h].at[s], rs.at[h, s], rr.at[h, s], dp, nxt if h == 0 else prv
        )

    def res_copies(d, came=False):
        return deal_copy(parts, dp, f, res, res_out, as_, ar, d, came)

    def gx_copies(d, came=False):
        return deal_copy(parts, dp, f, gx, gx_out, bs, br, d, came)

    def upg_copies(d, came=False):
        return owner_copy(me, parts, owners, upg, upg_out, us, ur, d, came)

    def vec_copies(d, came=False):
        return owner_copy(me, parts, owners, vec, vec_out, vs, vr, d, came)

    def begin(s):
        for h in range(2):
            sib_copy(h, s).start()
            own_copy(h, s).start()

    def others(d):
        upg_copies(d).start()
        vec_copies(d).start()

    def returns(d):
        res_copies(d).start()
        gx_copies(d).start()

    def pair(s):
        for h in range(2):
            sib_copy(h, s).wait_recv()
            own_copy(h, s).wait()
            for dx in range(1, rows_x):
                to = wrap(x + dx, rows_x)
                xb[h][s, dx - 1] = (sibr[h][s, to].astype(F32) + loc[h][s, to].astype(F32)).astype(BF)
                x_copy(h, s, dx).start()

    def step(s):
        for h in range(2):
            for dx in range(1, rows_x):
                x_copy(h, s, dx).wait_recv()

            def value():
                here = sibr[h][s, x].astype(F32) + loc[h][s, x].astype(F32)
                for dx in range(1, rows_x):
                    here = here + xrb[h][s, dx - 1].astype(F32)
                return here

            @pl.when(s == 0)
            def _():
                gone[h][s] = value().astype(BF)
                ring_copy(h, s).start()

            @pl.when((s > 0) & (s < parts - 1))
            def _():
                ring_copy(h, s - 1).wait_recv()
                gone[h][s] = (value() + got[h][s - 1].astype(F32)).astype(BF)
                ring_copy(h, s).start()

            @pl.when(s == parts - 1)
            def _():
                ring_copy(h, s - 1).wait_recv()
                total[h][...] = value() + got[h][s - 1].astype(F32)

    loop(0, parts, begin)
    loop(1, parts, returns)
    loop(1, owners, others)
    loop(0, parts, pair)
    loop(0, parts, step)

    def finish(s):
        for h in range(2):
            sib_copy(h, s).wait_send()
            for dx in range(1, rows_x):
                x_copy(h, s, dx).wait_send()

            @pl.when(s < parts - 1)
            def _():
                ring_copy(h, s).wait_send()

        @pl.when(s > 0)
        def _():
            for copies in (res_copies, gx_copies):
                copies(s, True).wait_recv()
                copies(s).wait_send()

    loop(0, parts, finish)

    def owner_finish(d):
        for copies in (upg_copies, vec_copies):
            copies(d, True).wait_recv()
            copies(d).wait_send()

    loop(1, owners, owner_finish)
    for copy in mine:
        copy.wait()


def finish_sums(parts, groups, grad_a, grad_b, res, gx, upg, vec):
    owners, rows_x = groups * parts, groups // 2
    rows = grad_a.shape[3]
    widths = (grad_a.shape[4], grad_b.shape[4])
    dma = pltpu.SemaphoreType.DMA
    hbm = pl.BlockSpec(memory_space=pl.ANY)
    return pl.pallas_call(
        functools.partial(finish_kernel, parts, groups),
        out_shape=(
            jax.ShapeDtypeStruct((rows, widths[0]), F32),
            jax.ShapeDtypeStruct((rows, widths[1]), F32),
            jax.ShapeDtypeStruct(res.shape, BF),
            jax.ShapeDtypeStruct(gx.shape, BF),
            jax.ShapeDtypeStruct(upg.shape, BF),
            jax.ShapeDtypeStruct(vec.shape, F32),
        ),
        in_specs=[hbm] * 6,
        out_specs=(pl.BlockSpec(memory_space=pltpu.VMEM),) * 2 + (hbm,) * 4,
        scratch_shapes=[
            *(
                pltpu.VMEM(lead + (rows, width), BF)
                for lead in (
                    (parts, rows_x), (parts, rows_x), (parts, rows_x - 1), (parts, rows_x - 1),
                    (parts,), (parts,),
                )
                for width in widths
            ),
            dma((4,)),
            dma((2, parts)), dma((2, parts)), dma((2, parts)),
            dma((2, parts, rows_x)), dma((2, parts, rows_x)),
            dma((2, parts)), dma((2, parts)),
            dma((parts,)), dma((parts,)), dma((parts,)), dma((parts,)),
            dma((owners,)), dma((owners,)), dma((owners,)), dma((owners,)),
        ],
        compiler_params=pltpu.CompilerParams(
            collective_id=4, has_side_effects=True, vmem_limit_bytes=60 * 2**20
        ),
        cost_estimate=lasting(140),
    )(grad_a, grad_b, res, gx, upg, vec)


def shards(
    tokens,
    cotangent,
    lengths,
    routing,
    in_weight,
    in_first,
    in_second,
    out_weight,
    out_first,
    out_second,
    up_weight,
    up_first,
    up_second,
    down_weight,
    down_first,
    down_second,
    vectors,
    vector_first,
    vector_second,
):
    bf = jnp.bfloat16
    heads = D // HD
    count = tokens.shape[0]
    parts = lax.axis_size("fsdp")
    groups = lax.axis_size("dp")
    both = ("dp", "fsdp")
    piece = count // parts
    width_in = D + 2 * HD
    slots = jnp.arange(parts, dtype=jnp.int32)
    order = routing[0]
    inverse = jnp.sum(jnp.where(order[:, None] == slots[None, :], slots[:, None], 0), axis=0)

    def deal(array):
        return jnp.take(array.reshape(parts, piece, D), inverse, axis=0)

    def undeal(array):
        return jnp.take(array, order, axis=0).reshape(count, D)

    rows = in_weight.shape[0]
    owners = groups * parts
    out_vec = jnp.concatenate(
        [out_weight.astype(bf), jnp.pad(vectors.astype(bf), ((0, 0), (0, 128 - NVEC)))], axis=1
    )
    up_pieces = up_weight.astype(bf).reshape(rows, owners, FF // owners).transpose(1, 0, 2)
    up_block, dealt, dealt_grad, out_vec = lax.optimization_barrier(
        (exchange(parts, groups, up_pieces), deal(tokens), deal(cotangent), out_vec)
    )
    x_dealt, grad_dealt, whole_in, whole_out = spread(
        parts, groups, dealt, dealt_grad, in_weight.astype(bf), out_vec
    )
    inputs_here = x_dealt.reshape(count, D)
    grad_all = grad_dealt.reshape(groups * count, D)
    grad_here = lax.dynamic_index_in_dim(
        grad_dealt, lax.axis_index("dp"), 0, keepdims=False
    ).reshape(count, D)
    whole_in = whole_in.reshape(D, width_in)
    whole_out = whole_out.reshape(D, D + 128)
    part_down = lax.all_gather(down_weight.astype(bf), "fsdp", axis=0, tiled=True)
    part_up = lax.all_gather(up_block.reshape(D, FF // owners).T, "fsdp", axis=0, tiled=True)

    table = whole_out[:, D : D + NVEC].astype(jnp.float32)
    whole_out = whole_out[:, :D]
    gain_one = table[:, 0]
    shift_one = table[:, 1]
    query_bias = table[:, 2]
    branch_bias = table[:, 3]
    gain_two = table[:, 4]
    shift_two = table[:, 5]
    output_bias = table[:, 6]
    hidden_bias = table[:, 7:].T.reshape(FF)
    ff_here = FF // groups
    ff_start = lax.axis_index("dp") * ff_here
    hidden_bias_here = lax.dynamic_slice(hidden_bias, (ff_start,), (ff_here,))
    allowed = segment_mask(lengths[0], count)
    scale = 1.0 / math.sqrt(HD)
    inputs = inputs_here.astype(jnp.float32)
    norm_one_b = layer_norm(inputs, gain_one, shift_one).astype(bf)
    mixed = jnp.dot(norm_one_b, whole_in, preferred_element_type=jnp.float32)
    query_b = (mixed[:, :D] + query_bias).astype(bf)
    keys_b = mixed[:, D : D + HD].astype(bf)
    values_b = mixed[:, D + HD :].astype(bf)
    query_heads = query_b.reshape(count, heads, HD)

    def score_table():
        raw = (
            jnp.einsum("thd,sd->hts", query_heads, keys_b, preferred_element_type=jnp.float32)
            * scale
        )
        return jnp.where(allowed[None], raw, -1e30)

    scores = score_table()
    top = jnp.max(scores, axis=-1, keepdims=True)
    expo = jnp.exp(scores - top)
    total = jnp.sum(expo, axis=-1, keepdims=True)
    logsum = top + jnp.log(total)
    probs_b = (expo / total).astype(bf)
    attended_b = (
        jnp.einsum("hts,sd->thd", probs_b, values_b, preferred_element_type=jnp.float32)
        .reshape(count, D)
        .astype(bf)
    )
    middle = inputs + (
        jnp.dot(attended_b, whole_out, preferred_element_type=jnp.float32) + branch_bias
    )
    norm_two_b = layer_norm(middle, gain_two, shift_two).astype(bf)

    fused = parts == 8 and groups == 4
    if fused:
        norm_all = group_gather(groups, norm_two_b).reshape(groups * count, D)
    else:
        norm_all = lax.all_gather(norm_two_b, "dp", axis=0, tiled=True)
    hidden = contract_cols(norm_all, part_up) + hidden_bias_here
    grad_active = contract_cols(grad_all, part_down)
    gelu_value, gelu_pull = jax.vjp(gelu_tanh, hidden)
    active_b = gelu_value.astype(bf)
    grad_hidden_b = gelu_pull(grad_active)[0].astype(bf)
    down_parts = contract_rows(active_b, grad_all).astype(bf)
    up_parts = contract_rows(grad_hidden_b, norm_all).astype(bf)
    down_parts, up_parts = lax.optimization_barrier((down_parts, up_parts))
    down_grad = lax.psum_scatter(down_parts, "fsdp", scatter_dimension=0, tiled=True)
    if fused:
        up_grad_block, grad_norm_two, branch_two = ffn_back(
            parts, groups, up_parts, active_b, grad_hidden_b, part_up, part_down
        )
    else:
        up_grad_block = lax.psum_scatter(up_parts, "fsdp", scatter_dimension=0, tiled=True)
        grad_norm_two = lax.psum_scatter(
            jnp.dot(grad_hidden_b, part_up, preferred_element_type=jnp.float32).astype(bf),
            "dp", scatter_dimension=0, tiled=True,
        ).astype(jnp.float32)
        branch_two = lax.psum_scatter(
            jnp.dot(active_b, part_down, preferred_element_type=jnp.float32).astype(bf),
            "dp", scatter_dimension=0, tiled=True,
        ).astype(jnp.float32)
    result = middle + (branch_two + output_bias)

    grad_y = grad_here.astype(jnp.float32)
    norm_value_two, pull_two = jax.vjp(layer_norm, middle, gain_two, shift_two)
    grad_middle_norm, grad_gain_two, grad_shift_two = pull_two(grad_norm_two)
    grad_middle = grad_y + grad_middle_norm
    grad_branch_b = grad_middle.astype(bf)
    grad_attended_b = contract_cols(grad_branch_b, whole_out).astype(bf)
    grad_heads = grad_attended_b.reshape(count, heads, HD)
    probs = jnp.exp(score_table() - logsum)
    probs_again_b = probs.astype(bf)
    grad_probs = jnp.einsum("thd,sd->hts", grad_heads, values_b, preferred_element_type=jnp.float32)
    grad_values_b = jnp.einsum(
        "hts,thd->sd", probs_again_b, grad_heads, preferred_element_type=jnp.float32
    ).astype(bf)
    weighted = jnp.sum(probs * grad_probs, axis=-1, keepdims=True)
    grad_scores_b = (probs * (grad_probs - weighted)).astype(bf)
    grad_query_b = (
        (
            jnp.einsum("hts,sd->thd", grad_scores_b, keys_b, preferred_element_type=jnp.float32)
            * scale
        )
        .reshape(count, D)
        .astype(bf)
    )
    grad_keys_b = (
        jnp.einsum("hts,thd->sd", grad_scores_b, query_heads, preferred_element_type=jnp.float32)
        * scale
    ).astype(bf)
    grad_mixed_b = jnp.concatenate([grad_query_b, grad_keys_b, grad_values_b], axis=1)
    down_grad, grad_mixed_b = lax.optimization_barrier((down_grad, grad_mixed_b))
    grad_norm_one = contract_cols(grad_mixed_b, whole_in)
    norm_value_one, pull_one = jax.vjp(layer_norm, inputs, gain_one, shift_one)
    grad_inputs_norm, grad_gain_one, grad_shift_one = pull_one(grad_norm_one)
    grad_inputs = grad_middle + grad_inputs_norm
    hidden_sums = jnp.sum(grad_hidden_b.astype(jnp.float32), axis=0)
    hidden_whole = lax.dynamic_update_slice(
        jnp.zeros((FF,), jnp.float32), hidden_sums, (ff_start,)
    )
    vector_grad = jnp.concatenate(
        [
            jnp.stack(
                [
                    grad_gain_one,
                    grad_shift_one,
                    jnp.sum(grad_query_b.astype(jnp.float32), axis=0),
                    jnp.sum(grad_branch_b.astype(jnp.float32), axis=0),
                    grad_gain_two,
                    grad_shift_two,
                    jnp.sum(grad_y, axis=0),
                ],
                axis=0,
            ),
            hidden_whole.reshape(FF // D, D),
        ],
        axis=0,
    )
    vector_grad = vector_grad.reshape(NVEC, owners, rows).transpose(1, 0, 2)
    vector_grad = jnp.pad(vector_grad, ((0, 0), (0, 16 - NVEC), (0, 128 - rows)))
    grad_in, grad_out, back_result, back_grad, grad_up, vector_sum = finish_sums(
        parts,
        groups,
        contract_rows(norm_one_b, grad_mixed_b)
        .astype(bf)
        .reshape(groups // 2, 2, parts, rows, width_in),
        contract_rows(attended_b, grad_branch_b).astype(bf).reshape(groups // 2, 2, parts, rows, D),
        result.astype(bf).reshape(parts, piece, D),
        grad_inputs.astype(bf).reshape(parts, piece, D),
        up_grad_block.T.astype(bf).reshape(owners, rows, FF // owners),
        vector_grad,
    )
    grad_up = grad_up.transpose(1, 0, 2).reshape(rows, FF)
    vector_sum = jnp.sum(vector_sum, axis=0)
    grad_vec = vector_sum[:NVEC, :rows].T
    in_new = adam_update(in_weight, in_first, in_second, grad_in, 1.0 / math.sqrt(D), decay_rate)
    out_new = adam_update(
        out_weight, out_first, out_second, grad_out, 1.0 / math.sqrt(D * 8 // TOK_DEV), decay_rate
    )
    up_new = adam_update(up_weight, up_first, up_second, grad_up, 1.0 / math.sqrt(D), decay_rate)
    down_new = adam_update(
        down_weight, down_first, down_second, down_grad, 1.0 / math.sqrt(FF), decay_rate
    )
    vec_new = adam_update(vectors, vector_first, vector_second, grad_vec, 0.1, 0.0)
    return (undeal(back_result), undeal(back_grad)) + in_new + out_new + up_new + down_new + vec_new


def solution(mesh):
    spec = P(("dp", "fsdp"), None)
    return jax.shard_map(
        shards,
        mesh=mesh,
        in_specs=(spec,) * 19,
        out_specs=(spec,) * 17,
        check_vma=False,
    )
```

```python
import functools
import math

import jax
import jax.numpy as jnp
from jax import lax
from jax.experimental import pallas as pl
from jax.experimental.pallas import tpu as pltpu
from jax.sharding import PartitionSpec as P

D = 2048
FF = 8192
HD = 128
TOK_DEV = 384
STEP = 5
NVEC = 11


eps_norm = 1e-05
beta_one = 0.5
beta_two = 0.5
adam_eps = 1e-08
decay_rate = 0.1


def layer_norm(values, gain, shift):
    centered = values - jnp.mean(values, axis=-1, keepdims=True)
    scaled = centered * lax.rsqrt(jnp.mean(centered * centered, axis=-1, keepdims=True) + eps_norm)
    return scaled * gain + shift


def gelu_tanh(values):
    return (
        0.5
        * values
        * (1.0 + jnp.tanh(0.7978845608028654 * (values + 0.044715 * values * values * values)))
    )


def segment_mask(sizes, count):
    ends = jnp.cumsum(sizes)
    places = jnp.arange(count, dtype=jnp.int32)
    labels = jnp.sum((places[:, None] >= ends[None, :]).astype(jnp.int32), axis=1)
    return (labels[:, None] == labels[None, :]) & (places[None, :] <= places[:, None])


def adam_update(weight, first, second, grad, rate, decay):
    grad = grad.astype(jnp.float32)
    first_new = beta_one * first + (1.0 - beta_one) * grad
    second_new = beta_two * second + (1.0 - beta_two) * grad * grad
    fix_one = 1.0 - beta_one**STEP
    fix_two = 1.0 - beta_two**STEP
    step_size = first_new / fix_one / (jnp.sqrt(second_new / fix_two) + adam_eps)
    weight_new = weight - rate * (step_size + decay * weight)
    return (weight_new, first_new, second_new)


def contract_rows(left, right):
    return lax.dot_general(
        left, right, (((0,), (0,)), ((), ())), preferred_element_type=jnp.float32
    )


def contract_cols(left, right):
    return lax.dot_general(
        left, right, (((1,), (1,)), ((), ())), preferred_element_type=jnp.float32
    )


MESH = pl.DeviceIdType.MESH
F32 = jnp.float32
BF = jnp.bfloat16


def wrap(value, count):
    return lax.rem(value + 2 * count, count)


def ring_place(index, parts):
    if parts != 8:
        return index
    z, y = lax.div(index, 2), lax.rem(index, 2)
    return z + y * (7 - 2 * z)


def ring_index(place, parts):
    place = wrap(place, parts)
    if parts != 8:
        return place
    back = lax.div(place, 4)
    return (1 - back) * 2 * place + back * (15 - 2 * place)


def remote(src, dst, send, recv, dp, fs):
    return pltpu.make_async_remote_copy(
        src_ref=src, dst_ref=dst, send_sem=send, recv_sem=recv, device_id=(dp, fs), device_id_type=MESH
    )


def lasting(micros):
    return pl.CostEstimate(
        flops=int(micros * 1.1e9), bytes_accessed=int(micros * 3.3e6), transcendentals=0
    )


def greet(targets):
    barrier = pltpu.get_barrier_semaphore()
    for dp, fs in targets:
        pl.semaphore_signal(barrier, inc=1, device_id=(dp, fs), device_id_type=MESH)
    pl.semaphore_wait(barrier, len(targets))


def greet_all(me, parts, owners):
    barrier = pltpu.get_barrier_semaphore()

    def one(i, carry):
        peer = wrap(me + i, owners)
        pl.semaphore_signal(
            barrier, inc=1, device_id=(lax.div(peer, parts), lax.rem(peer, parts)), device_id_type=MESH
        )
        return carry

    lax.fori_loop(1, owners, one, 0)
    pl.semaphore_wait(barrier, owners - 1)


def loop(low, high, body):
    def one(i, carry):
        body(i)
        return carry

    lax.fori_loop(low, high, one, 0)


def deal_copy(parts, dp, f, src, dst, send, recv, d, came=False):
    to = wrap(f + d, parts)
    place = wrap(f - d, parts) if came else f
    return remote(src.at[to], dst.at[place], send.at[d], recv.at[d], dp, to)


def owner_copy(me, parts, owners, src, dst, send, recv, d, came=False):
    to = wrap(me + d, owners)
    place = wrap(me - d, owners) if came else me
    return remote(
        src.at[to], dst.at[place], send.at[d], recv.at[d], lax.div(to, parts), lax.rem(to, parts)
    )


def spread_kernel(
    parts, groups,
    xd, gd, inb, ovb,
    xo, eall, win, wov,
    local, xs, xr, gs, gr, rs, rr, ns, nr, ss, sr, ens, enr, ess, esr,
):
    dp, f = lax.axis_index("dp"), lax.axis_index("fsdp")
    owners, rows_x = groups * parts, groups // 2
    x, core = lax.div(dp, 2), lax.rem(dp, 2)
    sib = x * 2 + 1 - core
    me = dp * parts + f
    p = ring_place(f, parts)
    nxt, prv = ring_index(p + 1, parts), ring_index(p - 1, parts)
    whole = (win, wov)
    mine = [
        pltpu.make_async_copy(inb, win.at[me], local.at[0]),
        pltpu.make_async_copy(ovb, wov.at[me], local.at[1]),
        pltpu.make_async_copy(xd.at[f], xo.at[f], local.at[2]),
        pltpu.make_async_copy(gd.at[f], eall.at[dp, f], local.at[3]),
    ]
    for copy in mine:
        copy.start()
    greet(
        [(dp, wrap(f + d, parts)) for d in range(1, parts)]
        + [(sib, f)]
        + [(wrap(x + dx, rows_x) * 2 + core, f) for dx in range(1, rows_x)]
    )
    for copy in mine:
        copy.wait()

    def x_copies(d, came=False):
        return deal_copy(parts, dp, f, xd, xo, xs, xr, d, came)

    def g_copies(d, came=False):
        return deal_copy(parts, dp, f, gd, eall.at[dp], gs, gr, d, came)

    def origin(h, s):
        return ring_index(p - s if h == 0 else p + s, parts)

    def ring_send(h, s):
        ref = whole[h].at[dp * parts + origin(h, s)]
        return remote(ref, ref, rs.at[h, s], rr.at[h, s], dp, nxt if h == 0 else prv)

    def ring_recv(h, s):
        ref = whole[h].at[dp * parts + origin(h, s)]
        return remote(ref, ref, rs.at[h, s - 1], rr.at[h, s - 1], dp, nxt if h == 0 else prv)

    def x_send(h, s, dx):
        ref = whole[h].at[dp * parts + origin(h, s)]
        to = wrap(x + dx, rows_x) * 2 + core
        return remote(ref, ref, ns.at[h, s, dx], nr.at[h, s, dx], to, f)

    def x_recv(h, s, dx):
        came = wrap(x - dx, rows_x) * 2 + core
        ref = whole[h].at[came * parts + origin(h, s)]
        return remote(ref, ref, ns.at[h, s, dx], nr.at[h, s, dx], came, f)

    def sib_send(h, s, dx):
        came = wrap(x - dx, rows_x) * 2 + core
        ref = whole[h].at[came * parts + origin(h, s)]
        return remote(ref, ref, ss.at[h, s, dx], sr.at[h, s, dx], sib, f)

    def sib_recv(h, s, dx):
        came = wrap(x - dx, rows_x) * 2 + 1 - core
        ref = whole[h].at[came * parts + origin(h, s)]
        return remote(ref, ref, ss.at[h, s, dx], sr.at[h, s, dx], sib, f)

    def e_x_send(d, dx):
        ref = eall.at[dp, wrap(f - d, parts)]
        to = wrap(x + dx, rows_x) * 2 + core
        return remote(ref, ref, ens.at[d, dx], enr.at[d, dx], to, f)

    def e_x_recv(d, dx):
        came = wrap(x - dx, rows_x) * 2 + core
        ref = eall.at[came, wrap(f - d, parts)]
        return remote(ref, ref, ens.at[d, dx], enr.at[d, dx], came, f)

    def e_sib_send(d, dx):
        came = wrap(x - dx, rows_x) * 2 + core
        ref = eall.at[came, wrap(f - d, parts)]
        return remote(ref, ref, ess.at[d, dx], esr.at[d, dx], sib, f)

    def e_sib_recv(d, dx):
        came = wrap(x - dx, rows_x) * 2 + 1 - core
        ref = eall.at[came, wrap(f - d, parts)]
        return remote(ref, ref, ess.at[d, dx], esr.at[d, dx], sib, f)

    def ring_step(s):
        for h in range(2):
            @pl.when(s > 0)
            def _():
                ring_recv(h, s).wait_recv()

            @pl.when(s < parts - 1)
            def _():
                ring_send(h, s).start()

            for dx in range(1, rows_x):
                x_send(h, s, dx).start()
            sib_send(h, s, 0).start()

    def e_step(d):
        @pl.when(d > 0)
        def _():
            g_copies(d, True).wait_recv()

        for dx in range(1, rows_x):
            e_x_send(d, dx).start()
        e_sib_send(d, 0).start()

    def relay(s):
        for h in range(2):
            for dx in range(1, rows_x):
                x_recv(h, s, dx).wait_recv()
                sib_send(h, s, dx).start()

    def e_relay(d):
        for dx in range(1, rows_x):
            e_x_recv(d, dx).wait_recv()
            e_sib_send(d, dx).start()

    def main(s):
        @pl.when(s < parts)
        def _():
            ring_step(s)

        @pl.when(s < parts - 1)
        def _():
            x_copies(s + 1).start()
            g_copies(s + 1).start()

        @pl.when((s >= 1) & (s <= parts))
        def _():
            e_step(s - 1)

        @pl.when((s >= 2) & (s < parts + 2))
        def _():
            relay(s - 2)

        @pl.when(s >= 3)
        def _():
            e_relay(s - 3)

    loop(0, parts + 3, main)

    def finish(s):
        for h in range(2):
            @pl.when(s < parts - 1)
            def _():
                ring_send(h, s).wait_send()

            for dx in range(1, rows_x):
                x_send(h, s, dx).wait_send()
            for dx in range(rows_x):
                sib_recv(h, s, dx).wait_recv()
                sib_send(h, s, dx).wait_send()
        for dx in range(1, rows_x):
            e_x_send(s, dx).wait_send()
        for dx in range(rows_x):
            e_sib_recv(s, dx).wait_recv()
            e_sib_send(s, dx).wait_send()

        @pl.when(s > 0)
        def _():
            x_copies(s, True).wait_recv()
            x_copies(s).wait_send()
            g_copies(s).wait_send()

    loop(0, parts, finish)


def exchange_kernel(parts, groups, src, dst, local, us, ur):
    dp, f = lax.axis_index("dp"), lax.axis_index("fsdp")
    owners = groups * parts
    me = dp * parts + f
    mine = pltpu.make_async_copy(src.at[me], dst.at[me], local)
    mine.start()
    greet_all(me, parts, owners)
    loop(1, owners, lambda d: owner_copy(me, parts, owners, src, dst, us, ur, d).start())
    mine.wait()

    def finish(d):
        owner_copy(me, parts, owners, src, dst, us, ur, d, True).wait_recv()
        owner_copy(me, parts, owners, src, dst, us, ur, d).wait_send()

    loop(1, owners, finish)


def exchange(parts, groups, src):
    owners = groups * parts
    dma = pltpu.SemaphoreType.DMA
    return pl.pallas_call(
        functools.partial(exchange_kernel, parts, groups),
        out_shape=jax.ShapeDtypeStruct(src.shape, BF),
        in_specs=[pl.BlockSpec(memory_space=pl.ANY)],
        out_specs=pl.BlockSpec(memory_space=pl.ANY),
        scratch_shapes=[dma(()), dma((owners,)), dma((owners,))],
        compiler_params=pltpu.CompilerParams(collective_id=5, has_side_effects=True),
        cost_estimate=lasting(25),
    )(src)


def spread(parts, groups, xd, gd, inb, ovb):
    owners, rows_x = groups * parts, groups // 2
    dma = pltpu.SemaphoreType.DMA
    return pl.pallas_call(
        functools.partial(spread_kernel, parts, groups),
        out_shape=(
            jax.ShapeDtypeStruct(xd.shape, BF),
            jax.ShapeDtypeStruct((groups,) + gd.shape, BF),
            jax.ShapeDtypeStruct((owners,) + inb.shape, BF),
            jax.ShapeDtypeStruct((owners,) + ovb.shape, BF),
        ),
        in_specs=[pl.BlockSpec(memory_space=pl.ANY)] * 4,
        out_specs=(pl.BlockSpec(memory_space=pl.ANY),) * 4,
        scratch_shapes=[
            dma((4,)),
            dma((parts,)), dma((parts,)), dma((parts,)), dma((parts,)),
            dma((2, parts)), dma((2, parts)),
            dma((2, parts, rows_x)), dma((2, parts, rows_x)),
            dma((2, parts, rows_x)), dma((2, parts, rows_x)),
            dma((parts, rows_x)), dma((parts, rows_x)),
            dma((parts, rows_x)), dma((parts, rows_x)),
        ],
        compiler_params=pltpu.CompilerParams(collective_id=0, has_side_effects=True),
        cost_estimate=lasting(200),
    )(xd, gd, inb, ovb)


def group_gather_kernel(groups, chunks, src, out, local, ns, nr, ss, sr):
    dp, f = lax.axis_index("dp"), lax.axis_index("fsdp")
    rows_x = groups // 2
    x, core = lax.div(dp, 2), lax.rem(dp, 2)
    sib = x * 2 + 1 - core
    size = src.shape[0] // chunks
    mine = pltpu.make_async_copy(src, out.at[dp], local)
    mine.start()
    greet([(sib, f)] + [(wrap(x + dx, rows_x) * 2 + core, f) for dx in range(1, rows_x)])

    def part(ref, k):
        return ref.at[pl.ds(k * size, size)]

    def x_send(k, dx):
        to = wrap(x + dx, rows_x) * 2 + core
        return remote(part(src, k), part(out.at[dp], k), ns.at[k, dx], nr.at[k, dx], to, f)

    def x_recv(k, dx):
        came = wrap(x - dx, rows_x) * 2 + core
        ref = part(out.at[came], k)
        return remote(ref, ref, ns.at[k, dx], nr.at[k, dx], came, f)

    def sib_send(k, dx):
        came = wrap(x - dx, rows_x) * 2 + core
        ref = part(out.at[came], k)
        return remote(part(src, k) if dx == 0 else ref, ref, ss.at[k, dx], sr.at[k, dx], sib, f)

    def sib_recv(k, dx):
        came = wrap(x - dx, rows_x) * 2 + 1 - core
        ref = part(out.at[came], k)
        return remote(ref, ref, ss.at[k, dx], sr.at[k, dx], sib, f)

    for k in range(chunks):
        for dx in range(1, rows_x):
            x_send(k, dx).start()
    for k in range(chunks):
        sib_send(k, 0).start()
    for k in range(chunks):
        for dx in range(1, rows_x):
            x_recv(k, dx).wait_recv()
            sib_send(k, dx).start()
    mine.wait()
    for k in range(chunks):
        for dx in range(rows_x):
            sib_recv(k, dx).wait_recv()
            sib_send(k, dx).wait_send()
        for dx in range(1, rows_x):
            x_send(k, dx).wait_send()


def group_gather(groups, src):
    chunks, rows_x = 4, groups // 2
    dma = pltpu.SemaphoreType.DMA
    return pl.pallas_call(
        functools.partial(group_gather_kernel, groups, chunks),
        out_shape=jax.ShapeDtypeStruct((groups,) + src.shape, BF),
        in_specs=[pl.BlockSpec(memory_space=pl.ANY)],
        out_specs=pl.BlockSpec(memory_space=pl.ANY),
        scratch_shapes=[dma(())] + [dma((chunks, rows_x))] * 4,
        compiler_params=pltpu.CompilerParams(collective_id=1, has_side_effects=True),
        cost_estimate=lasting(45),
    )(src)


def ffn_back_kernel(
    parts, groups, chunks, streams,
    grad_a, grad_b, act, dhid, w1, w2,
    out_a, out_b, dsum, ysum,
    loc, got, gone, wv, some, psib, sibr, xb, xrb,
    ll, ol, rs, rr, wl, sl, gss, gsr, gns, gnr,
):
    grads, outs = (grad_a, grad_b), (out_a, out_b)
    dp, f = lax.axis_index("dp"), lax.axis_index("fsdp")
    rows_x = groups // 2
    x, core = lax.div(dp, 2), lax.rem(dp, 2)
    sib = x * 2 + 1 - core
    p = ring_place(f, parts)
    nxt, prv = ring_index(p + 1, parts), ring_index(p - 1, parts)
    block, width = out_a.shape
    part, cut = width * 2 // streams, width // chunks
    count = dsum.shape[0]
    far = range(1, rows_x)

    def local_copy(h, s):
        c = ring_index(p - 1 - s if h // 2 % 2 == 0 else p + 1 + s, parts)
        return pltpu.make_async_copy(
            grads[h % 2].at[
                pl.ds(pl.multiple_of(c * block, block), block), pl.ds(h // 2 * part, part)
            ],
            loc.at[lax.rem(s, 2), h], ll.at[lax.rem(s, 2), h],
        )

    w_loads = (
        pltpu.make_async_copy(w1, wv, wl.at[0]),
        pltpu.make_async_copy(w2, wv, wl.at[1]),
    )
    for s in range(2):
        for h in range(streams):
            local_copy(h, s).start()
    w_loads[0].start()
    greet(
        [(dp, nxt), (dp, prv), (sib, f)]
        + [(wrap(x + dx, rows_x) * 2 + core, f) for dx in range(1, rows_x)]
    )

    def ring_copy(h, s):
        return remote(
            gone.at[lax.rem(s, 2), h], got.at[h, s], rs.at[h, s], rr.at[h, s],
            dp, nxt if h // 2 % 2 == 0 else prv,
        )

    def out_copy(h):
        return pltpu.make_async_copy(
            gone.at[lax.rem(parts - 1, 2), h],
            outs[h % 2].at[:, pl.ds(h // 2 * part, part)],
            ol.at[h],
        )

    def pass_on(s):
        slot = lax.rem(s, 2)
        for h in range(streams):
            local_copy(h, s).wait()

            @pl.when(s >= 2)
            def _():
                ring_copy(h, s - 2).wait_send()

            @pl.when(s == 0)
            def _():
                gone[slot, h] = loc[slot, h]

            @pl.when(s > 0)
            def _():
                ring_copy(h, s - 1).wait_recv()
                gone[slot, h] = (
                    loc[slot, h].astype(F32) + got[h, s - 1].astype(F32)
                ).astype(BF)

            @pl.when(s < parts - 1)
            def _():
                ring_copy(h, s).start()

            @pl.when(s == parts - 1)
            def _():
                out_copy(h).start()

            @pl.when(s < parts - 2)
            def _():
                local_copy(h, s + 2).start()

    def cols(k):
        return pl.ds(pl.multiple_of(k * cut, cut), cut)

    def rows_of(dx, c):
        group = wrap(x + dx, rows_x) * 2 + (core if c == 0 else 1 - core)
        return pl.ds(pl.multiple_of(group * count, count), count)

    rows_in, totals = (dhid, act), (dsum, ysum)

    def sum_sib(which, k):
        return remote(
            psib.at[:, :, cols(k)], sibr.at[which, :, :, cols(k)],
            gss.at[which, k], gsr.at[which, k], sib, f,
        )

    def sum_x(which, dx, k):
        to = wrap(x + dx, rows_x) * 2 + core
        return remote(
            xb.at[dx - 1, :, cols(k)], xrb.at[which, dx - 1, :, cols(k)],
            gns.at[which, dx, k], gnr.at[which, dx, k], to, f,
        )

    def take_rows(which, c):
        copies = [
            pltpu.make_async_copy(
                rows_in[which].at[rows_of(dx, c)], some.at[pl.ds(dx * count, count)], sl.at[dx]
            )
            for dx in range(rows_x)
        ]
        for copy in copies:
            copy.start()
        for copy in copies:
            copy.wait()

    def other_side(which):
        take_rows(which, 1)

        def one(k):
            psib[:, :, cols(k)] = (
                jnp.dot(some[...], wv[:, cols(k)], preferred_element_type=F32)
                .astype(BF)
                .reshape(rows_x, count, cut)
            )
            sum_sib(which, k).start()

        loop(0, chunks, one)

    def own_side(which):
        take_rows(which, 0)

        def one(k):
            here = jnp.dot(some[...], wv[:, cols(k)], preferred_element_type=F32)
            sum_sib(which, k).wait_recv()
            here = here.reshape(rows_x, count, cut) + sibr[which, :, :, cols(k)].astype(F32)
            for dx in far:
                xb[dx - 1, :, cols(k)] = here[dx].astype(BF)
                sum_x(which, dx, k).start()
            totals[which][:, cols(k)] = here[0]

        loop(0, chunks, one)

    def collect(which):
        def one(k):
            for dx in far:
                sum_x(which, dx, k).wait_recv()
                totals[which][:, cols(k)] += xrb[which, dx - 1, :, cols(k)].astype(F32)

        loop(0, chunks, one)

    def sent_sib(which):
        loop(0, chunks, lambda k: sum_sib(which, k).wait_send())

    def sent_x(which):
        for dx in far:
            loop(0, chunks, lambda k: sum_x(which, dx, k).wait_send())

    def step(s):
        pass_on(s)

        @pl.when(s == 0)
        def _():
            w_loads[0].wait()
            other_side(0)

        @pl.when(s == 1)
        def _():
            own_side(0)
            w_loads[1].start()

        @pl.when(s == 2)
        def _():
            w_loads[1].wait()
            sent_sib(0)
            other_side(1)

        @pl.when(s == 3)
        def _():
            sent_x(0)
            own_side(1)

        @pl.when(s == 4)
        def _():
            collect(0)

    loop(0, parts, step)
    collect(1)
    for h in range(streams):
        ring_copy(h, parts - 2).wait_send()
        out_copy(h).wait()
    sent_sib(1)
    sent_x(1)


def ffn_back(parts, groups, grad_a, grad_b, act, dhid, w1, w2):
    chunks, streams, rows_x = 4, 8, groups // 2
    units, width = w1.shape
    count = act.shape[0] // groups
    block, part = units // parts, width * 2 // streams
    dma = pltpu.SemaphoreType.DMA
    hbm = pl.BlockSpec(memory_space=pl.ANY)
    vmem = pl.BlockSpec(memory_space=pltpu.VMEM)
    return pl.pallas_call(
        functools.partial(ffn_back_kernel, parts, groups, chunks, streams),
        out_shape=(
            jax.ShapeDtypeStruct((block, width), BF),
            jax.ShapeDtypeStruct((block, width), BF),
            jax.ShapeDtypeStruct((count, width), F32),
            jax.ShapeDtypeStruct((count, width), F32),
        ),
        in_specs=[hbm] * 6,
        out_specs=(hbm, hbm, vmem, vmem),
        scratch_shapes=[
            pltpu.VMEM((2, streams, block, part), BF),
            pltpu.VMEM((streams, parts - 1, block, part), BF),
            pltpu.VMEM((2, streams, block, part), BF),
            pltpu.VMEM((units, width), BF),
            pltpu.VMEM((rows_x * count, units), BF),
            pltpu.VMEM((rows_x, count, width), BF),
            pltpu.VMEM((2, rows_x, count, width), BF),
            pltpu.VMEM((rows_x - 1, count, width), BF),
            pltpu.VMEM((2, rows_x - 1, count, width), BF),
            dma((2, streams)), dma((streams,)),
            dma((streams, parts)), dma((streams, parts)), dma((2,)), dma((rows_x,)),
            dma((2, chunks)), dma((2, chunks)),
            dma((2, rows_x, chunks)), dma((2, rows_x, chunks)),
        ],
        compiler_params=pltpu.CompilerParams(
            collective_id=3, has_side_effects=True, vmem_limit_bytes=60 * 2**20
        ),
        cost_estimate=lasting(165),
    )(grad_a, grad_b, act, dhid, w1, w2)


def finish_kernel(
    parts, groups,
    grad_a, grad_b, gx, upg, vec,
    total_a, total_b, gx_out, upg_out, vec_out,
    loc_a, loc_b, sibr_a, sibr_b, xb_a, xb_b, xrb_a, xrb_b, got_a, got_b, gone_a, gone_b,
    local, ls, ss, sr, ns, nr, rs, rr, bs, br, us, ur, vs, vr,
):
    dp, f = lax.axis_index("dp"), lax.axis_index("fsdp")
    owners, rows_x = groups * parts, groups // 2
    x, core = lax.div(dp, 2), lax.rem(dp, 2)
    sib = x * 2 + 1 - core
    me = dp * parts + f
    p = ring_place(f, parts)
    nxt, prv = ring_index(p + 1, parts), ring_index(p - 1, parts)
    grads, total = (grad_a, grad_b), (total_a, total_b)
    loc, sibr, xb, xrb = (loc_a, loc_b), (sibr_a, sibr_b), (xb_a, xb_b), (xrb_a, xrb_b)
    got, gone = (got_a, got_b), (gone_a, gone_b)
    mine = [
        pltpu.make_async_copy(gx.at[f], gx_out.at[f], local.at[0]),
        pltpu.make_async_copy(vec.at[me], vec_out.at[me], local.at[1]),
        pltpu.make_async_copy(upg.at[me], upg_out.at[me], local.at[2]),
    ]
    for copy in mine:
        copy.start()
    greet_all(me, parts, owners)

    def chunk(h, s):
        return ring_index(p - 1 - s if h == 0 else p + 1 + s, parts)

    def sib_copy(h, s):
        piece = grads[h].at[:, 1 - core, chunk(h, s)]
        return remote(piece, sibr[h].at[s], ss.at[h, s], sr.at[h, s], sib, f)

    def own_copy(h, s):
        piece = grads[h].at[:, core, chunk(h, s)]
        return pltpu.make_async_copy(piece, loc[h].at[s], ls.at[h, s])

    def x_copy(h, s, dx):
        to = wrap(x + dx, rows_x) * 2 + core
        return remote(
            xb[h].at[s, dx - 1], xrb[h].at[s, dx - 1], ns.at[h, s, dx], nr.at[h, s, dx], to, f
        )

    def ring_copy(h, s):
        return remote(
            gone[h].at[s], got[h].at[s], rs.at[h, s], rr.at[h, s], dp, nxt if h == 0 else prv
        )

    def gx_copies(d, came=False):
        return deal_copy(parts, dp, f, gx, gx_out, bs, br, d, came)

    def upg_copies(d, came=False):
        return owner_copy(me, parts, owners, upg, upg_out, us, ur, d, came)

    def vec_copies(d, came=False):
        return owner_copy(me, parts, owners, vec, vec_out, vs, vr, d, came)

    def begin(s):
        for h in range(2):
            sib_copy(h, s).start()
            own_copy(h, s).start()

    def others(d):
        upg_copies(d).start()
        vec_copies(d).start()

    def returns(d):
        gx_copies(d).start()

    def pair(s):
        for h in range(2):
            sib_copy(h, s).wait_recv()
            own_copy(h, s).wait()
            for dx in range(1, rows_x):
                to = wrap(x + dx, rows_x)
                xb[h][s, dx - 1] = (sibr[h][s, to].astype(F32) + loc[h][s, to].astype(F32)).astype(BF)
                x_copy(h, s, dx).start()

    def step(s):
        for h in range(2):
            for dx in range(1, rows_x):
                x_copy(h, s, dx).wait_recv()

            def value():
                here = sibr[h][s, x].astype(F32) + loc[h][s, x].astype(F32)
                for dx in range(1, rows_x):
                    here = here + xrb[h][s, dx - 1].astype(F32)
                return here

            @pl.when(s == 0)
            def _():
                gone[h][s] = value().astype(BF)
                ring_copy(h, s).start()

            @pl.when((s > 0) & (s < parts - 1))
            def _():
                ring_copy(h, s - 1).wait_recv()
                gone[h][s] = (value() + got[h][s - 1].astype(F32)).astype(BF)
                ring_copy(h, s).start()

            @pl.when(s == parts - 1)
            def _():
                ring_copy(h, s - 1).wait_recv()
                total[h][...] = value() + got[h][s - 1].astype(F32)

    loop(0, parts, begin)
    loop(1, parts, returns)
    loop(1, owners, others)
    loop(0, parts, pair)
    loop(0, parts, step)

    def finish(s):
        for h in range(2):
            sib_copy(h, s).wait_send()
            for dx in range(1, rows_x):
                x_copy(h, s, dx).wait_send()

            @pl.when(s < parts - 1)
            def _():
                ring_copy(h, s).wait_send()

        @pl.when(s > 0)
        def _():
            gx_copies(s, True).wait_recv()
            gx_copies(s).wait_send()

    loop(0, parts, finish)

    def owner_finish(d):
        for copies in (upg_copies, vec_copies):
            copies(d, True).wait_recv()
            copies(d).wait_send()

    loop(1, owners, owner_finish)
    for copy in mine:
        copy.wait()


def finish_sums(parts, groups, grad_a, grad_b, gx, upg, vec):
    owners, rows_x = groups * parts, groups // 2
    rows = grad_a.shape[3]
    widths = (grad_a.shape[4], grad_b.shape[4])
    dma = pltpu.SemaphoreType.DMA
    hbm = pl.BlockSpec(memory_space=pl.ANY)
    return pl.pallas_call(
        functools.partial(finish_kernel, parts, groups),
        out_shape=(
            jax.ShapeDtypeStruct((rows, widths[0]), F32),
            jax.ShapeDtypeStruct((rows, widths[1]), F32),
            jax.ShapeDtypeStruct(gx.shape, BF),
            jax.ShapeDtypeStruct(upg.shape, BF),
            jax.ShapeDtypeStruct(vec.shape, F32),
        ),
        in_specs=[hbm] * 5,
        out_specs=(pl.BlockSpec(memory_space=pltpu.VMEM),) * 2 + (hbm,) * 3,
        scratch_shapes=[
            *(
                pltpu.VMEM(lead + (rows, width), BF)
                for lead in (
                    (parts, rows_x), (parts, rows_x), (parts, rows_x - 1), (parts, rows_x - 1),
                    (parts,), (parts,),
                )
                for width in widths
            ),
            dma((3,)),
            dma((2, parts)), dma((2, parts)), dma((2, parts)),
            dma((2, parts, rows_x)), dma((2, parts, rows_x)),
            dma((2, parts)), dma((2, parts)),
            dma((parts,)), dma((parts,)),
            dma((owners,)), dma((owners,)), dma((owners,)), dma((owners,)),
        ],
        compiler_params=pltpu.CompilerParams(
            collective_id=4, has_side_effects=True, vmem_limit_bytes=60 * 2**20
        ),
        cost_estimate=lasting(115),
    )(grad_a, grad_b, gx, upg, vec)


def shards(
    tokens,
    cotangent,
    lengths,
    routing,
    in_weight,
    in_first,
    in_second,
    out_weight,
    out_first,
    out_second,
    up_weight,
    up_first,
    up_second,
    down_weight,
    down_first,
    down_second,
    vectors,
    vector_first,
    vector_second,
):
    bf = jnp.bfloat16
    heads = D // HD
    count = tokens.shape[0]
    parts = lax.axis_size("fsdp")
    groups = lax.axis_size("dp")
    both = ("dp", "fsdp")
    piece = count // parts
    width_in = D + 2 * HD
    slots = jnp.arange(parts, dtype=jnp.int32)
    order = routing[0]
    inverse = jnp.sum(jnp.where(order[:, None] == slots[None, :], slots[:, None], 0), axis=0)

    def deal(array):
        return jnp.take(array.reshape(parts, piece, D), inverse, axis=0)

    def undeal(array):
        return jnp.take(array, order, axis=0).reshape(count, D)

    rows = in_weight.shape[0]
    owners = groups * parts
    out_vec = jnp.concatenate(
        [out_weight.astype(bf), jnp.pad(vectors.astype(bf), ((0, 0), (0, 128 - NVEC)))], axis=1
    )
    up_pieces = up_weight.astype(bf).reshape(rows, owners, FF // owners).transpose(1, 0, 2)
    up_block, dealt, dealt_grad, out_vec = lax.optimization_barrier(
        (exchange(parts, groups, up_pieces), deal(tokens), deal(cotangent), out_vec)
    )
    x_dealt, grad_dealt, whole_in, whole_out = spread(
        parts, groups, dealt, dealt_grad, in_weight.astype(bf), out_vec
    )
    inputs_here = x_dealt.reshape(count, D)
    grad_all = grad_dealt.reshape(groups * count, D)
    grad_here = lax.dynamic_index_in_dim(
        grad_dealt, lax.axis_index("dp"), 0, keepdims=False
    ).reshape(count, D)
    whole_in = whole_in.reshape(D, width_in)
    whole_out = whole_out.reshape(D, D + 128)
    part_down = lax.all_gather(down_weight.astype(bf), "fsdp", axis=0, tiled=True)
    part_up = lax.all_gather(up_block.reshape(D, FF // owners).T, "fsdp", axis=0, tiled=True)

    table = whole_out[:, D : D + NVEC].astype(jnp.float32)
    whole_out = whole_out[:, :D]
    gain_one = table[:, 0]
    shift_one = table[:, 1]
    query_bias = table[:, 2]
    branch_bias = table[:, 3]
    gain_two = table[:, 4]
    shift_two = table[:, 5]
    output_bias = table[:, 6]
    hidden_bias = table[:, 7:].T.reshape(FF)
    ff_here = FF // groups
    ff_start = lax.axis_index("dp") * ff_here
    hidden_bias_here = lax.dynamic_slice(hidden_bias, (ff_start,), (ff_here,))
    allowed = segment_mask(lengths[0], count)
    scale = 1.0 / math.sqrt(HD)
    inputs = inputs_here.astype(jnp.float32)
    norm_one_b = layer_norm(inputs, gain_one, shift_one).astype(bf)
    mixed = jnp.dot(norm_one_b, whole_in, preferred_element_type=jnp.float32)
    query_b = (mixed[:, :D] + query_bias).astype(bf)
    keys_b = mixed[:, D : D + HD].astype(bf)
    values_b = mixed[:, D + HD :].astype(bf)
    query_heads = query_b.reshape(count, heads, HD)

    def score_table():
        raw = (
            jnp.einsum("thd,sd->hts", query_heads, keys_b, preferred_element_type=jnp.float32)
            * scale
        )
        return jnp.where(allowed[None], raw, -1e30)

    scores = score_table()
    top = jnp.max(scores, axis=-1, keepdims=True)
    expo = jnp.exp(scores - top)
    total = jnp.sum(expo, axis=-1, keepdims=True)
    logsum = top + jnp.log(total)
    probs_b = (expo / total).astype(bf)
    attended_b = (
        jnp.einsum("hts,sd->thd", probs_b, values_b, preferred_element_type=jnp.float32)
        .reshape(count, D)
        .astype(bf)
    )
    middle = inputs + (
        jnp.dot(attended_b, whole_out, preferred_element_type=jnp.float32) + branch_bias
    )
    norm_two_b = layer_norm(middle, gain_two, shift_two).astype(bf)

    fused = parts == 8 and groups == 4
    if fused:
        norm_all = group_gather(groups, norm_two_b).reshape(groups * count, D)
    else:
        norm_all = lax.all_gather(norm_two_b, "dp", axis=0, tiled=True)
    hidden = contract_cols(norm_all, part_up) + hidden_bias_here
    grad_active = contract_cols(grad_all, part_down)
    gelu_value, gelu_pull = jax.vjp(gelu_tanh, hidden)
    active_b = gelu_value.astype(bf)
    grad_hidden_b = gelu_pull(grad_active)[0].astype(bf)
    down_parts = contract_rows(active_b, grad_all).astype(bf)
    up_parts = contract_rows(grad_hidden_b, norm_all).astype(bf)
    if fused:
        down_grad, up_grad_block, grad_norm_two, branch_two = ffn_back(
            parts, groups, down_parts, up_parts, active_b, grad_hidden_b, part_up, part_down
        )
    else:
        down_grad = lax.psum_scatter(down_parts, "fsdp", scatter_dimension=0, tiled=True)
        up_grad_block = lax.psum_scatter(up_parts, "fsdp", scatter_dimension=0, tiled=True)
        grad_norm_two = lax.psum_scatter(
            jnp.dot(grad_hidden_b, part_up, preferred_element_type=jnp.float32).astype(bf),
            "dp", scatter_dimension=0, tiled=True,
        ).astype(jnp.float32)
        branch_two = lax.psum_scatter(
            jnp.dot(active_b, part_down, preferred_element_type=jnp.float32).astype(bf),
            "dp", scatter_dimension=0, tiled=True,
        ).astype(jnp.float32)
    result = middle + (branch_two + output_bias)

    grad_y = grad_here.astype(jnp.float32)
    norm_value_two, pull_two = jax.vjp(layer_norm, middle, gain_two, shift_two)
    grad_middle_norm, grad_gain_two, grad_shift_two = pull_two(grad_norm_two)
    grad_middle = grad_y + grad_middle_norm
    grad_branch_b = grad_middle.astype(bf)
    grad_attended_b = contract_cols(grad_branch_b, whole_out).astype(bf)
    grad_heads = grad_attended_b.reshape(count, heads, HD)
    probs = jnp.exp(score_table() - logsum)
    probs_again_b = probs.astype(bf)
    grad_probs = jnp.einsum("thd,sd->hts", grad_heads, values_b, preferred_element_type=jnp.float32)
    grad_values_b = jnp.einsum(
        "hts,thd->sd", probs_again_b, grad_heads, preferred_element_type=jnp.float32
    ).astype(bf)
    weighted = jnp.sum(probs * grad_probs, axis=-1, keepdims=True)
    grad_scores_b = (probs * (grad_probs - weighted)).astype(bf)
    place = lax.axis_index("fsdp")
    offsets = jnp.arange(parts, dtype=jnp.int32)
    leaving = jnp.take(
        result.astype(bf).reshape(parts, piece, D), lax.rem(place + offsets, parts), axis=0
    )
    by_offset = [leaving[0]] + [
        lax.ppermute(leaving[d], "fsdp", [(i, (i + d) % parts) for i in range(parts)])
        for d in range(1, parts)
    ]
    early, late = parts * 3 // 8 + 1, parts * 6 // 8
    by_offset[:early], grad_scores_b = lax.optimization_barrier((by_offset[:early], grad_scores_b))
    grad_query_b = (
        (
            jnp.einsum("hts,sd->thd", grad_scores_b, keys_b, preferred_element_type=jnp.float32)
            * scale
        )
        .reshape(count, D)
        .astype(bf)
    )
    grad_keys_b = (
        jnp.einsum("hts,thd->sd", grad_scores_b, query_heads, preferred_element_type=jnp.float32)
        * scale
    ).astype(bf)
    grad_mixed_b = jnp.concatenate([grad_query_b, grad_keys_b, grad_values_b], axis=1)
    by_offset[early:late], grad_mixed_b = lax.optimization_barrier(
        (by_offset[early:late], grad_mixed_b)
    )
    grad_norm_one = contract_cols(grad_mixed_b, whole_in)
    norm_value_one, pull_one = jax.vjp(layer_norm, inputs, gain_one, shift_one)
    grad_inputs_norm, grad_gain_one, grad_shift_one = pull_one(grad_norm_one)
    grad_inputs = grad_middle + grad_inputs_norm
    by_offset[late:], grad_inputs = lax.optimization_barrier((by_offset[late:], grad_inputs))
    hidden_sums = jnp.sum(grad_hidden_b.astype(jnp.float32), axis=0)
    hidden_whole = lax.dynamic_update_slice(
        jnp.zeros((FF,), jnp.float32), hidden_sums, (ff_start,)
    )
    vector_grad = jnp.concatenate(
        [
            jnp.stack(
                [
                    grad_gain_one,
                    grad_shift_one,
                    jnp.sum(grad_query_b.astype(jnp.float32), axis=0),
                    jnp.sum(grad_branch_b.astype(jnp.float32), axis=0),
                    grad_gain_two,
                    grad_shift_two,
                    jnp.sum(grad_y, axis=0),
                ],
                axis=0,
            ),
            hidden_whole.reshape(FF // D, D),
        ],
        axis=0,
    )
    vector_grad = vector_grad.reshape(NVEC, owners, rows).transpose(1, 0, 2)
    vector_grad = jnp.pad(vector_grad, ((0, 0), (0, 16 - NVEC), (0, 128 - rows)))
    grad_in, grad_out, back_grad, grad_up, vector_sum = finish_sums(
        parts,
        groups,
        contract_rows(norm_one_b, grad_mixed_b)
        .astype(bf)
        .reshape(groups // 2, 2, parts, rows, width_in),
        contract_rows(attended_b, grad_branch_b).astype(bf).reshape(groups // 2, 2, parts, rows, D),
        grad_inputs.astype(bf).reshape(parts, piece, D),
        up_grad_block.T.astype(bf).reshape(owners, rows, FF // owners),
        vector_grad,
    )
    grad_up = grad_up.transpose(1, 0, 2).reshape(rows, FF)
    vector_sum = jnp.sum(vector_sum, axis=0)
    grad_vec = vector_sum[:NVEC, :rows].T
    in_new = adam_update(in_weight, in_first, in_second, grad_in, 1.0 / math.sqrt(D), decay_rate)
    out_new = adam_update(
        out_weight, out_first, out_second, grad_out, 1.0 / math.sqrt(D * 8 // TOK_DEV), decay_rate
    )
    up_new = adam_update(up_weight, up_first, up_second, grad_up, 1.0 / math.sqrt(D), decay_rate)
    down_new = adam_update(
        down_weight, down_first, down_second, down_grad, 1.0 / math.sqrt(FF), decay_rate
    )
    vec_new = adam_update(vectors, vector_first, vector_second, grad_vec, 0.1, 0.0)
    result_here = jnp.take(
        jnp.stack(by_offset), lax.rem(place - order + parts, parts), axis=0
    ).reshape(count, D)
    return (result_here, undeal(back_grad)) + in_new + out_new + up_new + down_new + vec_new


def solution(mesh):
    spec = P(("dp", "fsdp"), None)
    return jax.shard_map(
        shards,
        mesh=mesh,
        in_specs=(spec,) * 19,
        out_specs=(spec,) * 17,
        check_vma=False,
    )
```

```python
import functools
import math

import jax
import jax.numpy as jnp
from jax import lax
from jax.experimental import pallas as pl
from jax.experimental.pallas import tpu as pltpu
from jax.sharding import PartitionSpec as P

D = 2048
FF = 8192
HD = 128
TOK_DEV = 384
STEP = 5
NVEC = 11


eps_norm = 1e-05
beta_one = 0.5
beta_two = 0.5
adam_eps = 1e-08
decay_rate = 0.1


def layer_norm(values, gain, shift):
    centered = values - jnp.mean(values, axis=-1, keepdims=True)
    scaled = centered * lax.rsqrt(jnp.mean(centered * centered, axis=-1, keepdims=True) + eps_norm)
    return scaled * gain + shift


def gelu_tanh(values):
    return (
        0.5
        * values
        * (1.0 + jnp.tanh(0.7978845608028654 * (values + 0.044715 * values * values * values)))
    )


def segment_mask(sizes, count):
    ends = jnp.cumsum(sizes)
    places = jnp.arange(count, dtype=jnp.int32)
    labels = jnp.sum((places[:, None] >= ends[None, :]).astype(jnp.int32), axis=1)
    return (labels[:, None] == labels[None, :]) & (places[None, :] <= places[:, None])


def adam_update(weight, first, second, grad, rate, decay):
    grad = grad.astype(jnp.float32)
    first_new = beta_one * first + (1.0 - beta_one) * grad
    second_new = beta_two * second + (1.0 - beta_two) * grad * grad
    fix_one = 1.0 - beta_one**STEP
    fix_two = 1.0 - beta_two**STEP
    step_size = first_new / fix_one / (jnp.sqrt(second_new / fix_two) + adam_eps)
    weight_new = weight - rate * (step_size + decay * weight)
    return (weight_new, first_new, second_new)


def contract_rows(left, right):
    return lax.dot_general(
        left, right, (((0,), (0,)), ((), ())), preferred_element_type=jnp.float32
    )


def contract_cols(left, right):
    return lax.dot_general(
        left, right, (((1,), (1,)), ((), ())), preferred_element_type=jnp.float32
    )


MESH = pl.DeviceIdType.MESH
F32 = jnp.float32
BF = jnp.bfloat16


def wrap(value, count):
    return lax.rem(value + 2 * count, count)


def ring_place(index, parts):
    if parts != 8:
        return index
    z, y = lax.div(index, 2), lax.rem(index, 2)
    return z + y * (7 - 2 * z)


def ring_index(place, parts):
    place = wrap(place, parts)
    if parts != 8:
        return place
    back = lax.div(place, 4)
    return (1 - back) * 2 * place + back * (15 - 2 * place)


def remote(src, dst, send, recv, dp, fs):
    return pltpu.make_async_remote_copy(
        src_ref=src, dst_ref=dst, send_sem=send, recv_sem=recv, device_id=(dp, fs), device_id_type=MESH
    )


def lasting(micros):
    return pl.CostEstimate(
        flops=int(micros * 1.1e9), bytes_accessed=int(micros * 3.3e6), transcendentals=0
    )


def greet(targets):
    barrier = pltpu.get_barrier_semaphore()
    for dp, fs in targets:
        pl.semaphore_signal(barrier, inc=1, device_id=(dp, fs), device_id_type=MESH)
    pl.semaphore_wait(barrier, len(targets))


def greet_all(me, parts, owners):
    barrier = pltpu.get_barrier_semaphore()

    def one(i, carry):
        peer = wrap(me + i, owners)
        pl.semaphore_signal(
            barrier, inc=1, device_id=(lax.div(peer, parts), lax.rem(peer, parts)), device_id_type=MESH
        )
        return carry

    lax.fori_loop(1, owners, one, 0)
    pl.semaphore_wait(barrier, owners - 1)


def loop(low, high, body):
    def one(i, carry):
        body(i)
        return carry

    lax.fori_loop(low, high, one, 0)


def deal_copy(parts, dp, f, src, dst, send, recv, d, came=False):
    to = wrap(f + d, parts)
    place = wrap(f - d, parts) if came else f
    return remote(src.at[to], dst.at[place], send.at[d], recv.at[d], dp, to)


def owner_copy(me, parts, owners, src, dst, send, recv, d, came=False):
    to = wrap(me + d, owners)
    place = wrap(me - d, owners) if came else me
    return remote(
        src.at[to], dst.at[place], send.at[d], recv.at[d], lax.div(to, parts), lax.rem(to, parts)
    )


def spread_kernel(
    parts, groups,
    xd, gd, inb, ovb,
    xo, eall, win, wov,
    local, xs, xr, gs, gr, rs, rr, ns, nr, ss, sr, ens, enr, ess, esr,
):
    dp, f = lax.axis_index("dp"), lax.axis_index("fsdp")
    owners, rows_x = groups * parts, groups // 2
    x, core = lax.div(dp, 2), lax.rem(dp, 2)
    sib = x * 2 + 1 - core
    me = dp * parts + f
    p = ring_place(f, parts)
    nxt, prv = ring_index(p + 1, parts), ring_index(p - 1, parts)
    whole = (win, wov)
    mine = [
        pltpu.make_async_copy(inb, win.at[me], local.at[0]),
        pltpu.make_async_copy(ovb, wov.at[me], local.at[1]),
        pltpu.make_async_copy(xd.at[f], xo.at[f], local.at[2]),
        pltpu.make_async_copy(gd.at[f], eall.at[dp, f], local.at[3]),
    ]
    for copy in mine:
        copy.start()
    greet(
        [(dp, wrap(f + d, parts)) for d in range(1, parts)]
        + [(sib, f)]
        + [(wrap(x + dx, rows_x) * 2 + core, f) for dx in range(1, rows_x)]
    )
    for copy in mine:
        copy.wait()

    def x_copies(d, came=False):
        return deal_copy(parts, dp, f, xd, xo, xs, xr, d, came)

    def g_copies(d, came=False):
        return deal_copy(parts, dp, f, gd, eall.at[dp], gs, gr, d, came)

    def origin(h, s):
        return ring_index(p - s if h == 0 else p + s, parts)

    def ring_send(h, s):
        ref = whole[h].at[dp * parts + origin(h, s)]
        return remote(ref, ref, rs.at[h, s], rr.at[h, s], dp, nxt if h == 0 else prv)

    def ring_recv(h, s):
        ref = whole[h].at[dp * parts + origin(h, s)]
        return remote(ref, ref, rs.at[h, s - 1], rr.at[h, s - 1], dp, nxt if h == 0 else prv)

    def x_send(h, s, dx):
        ref = whole[h].at[dp * parts + origin(h, s)]
        to = wrap(x + dx, rows_x) * 2 + core
        return remote(ref, ref, ns.at[h, s, dx], nr.at[h, s, dx], to, f)

    def x_recv(h, s, dx):
        came = wrap(x - dx, rows_x) * 2 + core
        ref = whole[h].at[came * parts + origin(h, s)]
        return remote(ref, ref, ns.at[h, s, dx], nr.at[h, s, dx], came, f)

    def sib_send(h, s, dx):
        came = wrap(x - dx, rows_x) * 2 + core
        ref = whole[h].at[came * parts + origin(h, s)]
        return remote(ref, ref, ss.at[h, s, dx], sr.at[h, s, dx], sib, f)

    def sib_recv(h, s, dx):
        came = wrap(x - dx, rows_x) * 2 + 1 - core
        ref = whole[h].at[came * parts + origin(h, s)]
        return remote(ref, ref, ss.at[h, s, dx], sr.at[h, s, dx], sib, f)

    def e_x_send(d, dx):
        ref = eall.at[dp, wrap(f - d, parts)]
        to = wrap(x + dx, rows_x) * 2 + core
        return remote(ref, ref, ens.at[d, dx], enr.at[d, dx], to, f)

    def e_x_recv(d, dx):
        came = wrap(x - dx, rows_x) * 2 + core
        ref = eall.at[came, wrap(f - d, parts)]
        return remote(ref, ref, ens.at[d, dx], enr.at[d, dx], came, f)

    def e_sib_send(d, dx):
        came = wrap(x - dx, rows_x) * 2 + core
        ref = eall.at[came, wrap(f - d, parts)]
        return remote(ref, ref, ess.at[d, dx], esr.at[d, dx], sib, f)

    def e_sib_recv(d, dx):
        came = wrap(x - dx, rows_x) * 2 + 1 - core
        ref = eall.at[came, wrap(f - d, parts)]
        return remote(ref, ref, ess.at[d, dx], esr.at[d, dx], sib, f)

    def ring_step(s):
        for h in range(2):
            @pl.when(s > 0)
            def _():
                ring_recv(h, s).wait_recv()

            @pl.when(s < parts - 1)
            def _():
                ring_send(h, s).start()

            for dx in range(1, rows_x):
                x_send(h, s, dx).start()
            sib_send(h, s, 0).start()

    def e_step(d):
        @pl.when(d > 0)
        def _():
            g_copies(d, True).wait_recv()

        for dx in range(1, rows_x):
            e_x_send(d, dx).start()
        e_sib_send(d, 0).start()

    def relay(s):
        for h in range(2):
            for dx in range(1, rows_x):
                x_recv(h, s, dx).wait_recv()
                sib_send(h, s, dx).start()

    def e_relay(d):
        for dx in range(1, rows_x):
            e_x_recv(d, dx).wait_recv()
            e_sib_send(d, dx).start()

    def main(s):
        @pl.when(s < parts)
        def _():
            ring_step(s)

        @pl.when(s < parts - 1)
        def _():
            x_copies(s + 1).start()
            g_copies(s + 1).start()

        @pl.when((s >= 1) & (s <= parts))
        def _():
            e_step(s - 1)

        @pl.when((s >= 2) & (s < parts + 2))
        def _():
            relay(s - 2)

        @pl.when(s >= 3)
        def _():
            e_relay(s - 3)

    loop(0, parts + 3, main)

    def finish(s):
        for h in range(2):
            @pl.when(s < parts - 1)
            def _():
                ring_send(h, s).wait_send()

            for dx in range(1, rows_x):
                x_send(h, s, dx).wait_send()
            for dx in range(rows_x):
                sib_recv(h, s, dx).wait_recv()
                sib_send(h, s, dx).wait_send()
        for dx in range(1, rows_x):
            e_x_send(s, dx).wait_send()
        for dx in range(rows_x):
            e_sib_recv(s, dx).wait_recv()
            e_sib_send(s, dx).wait_send()

        @pl.when(s > 0)
        def _():
            x_copies(s, True).wait_recv()
            x_copies(s).wait_send()
            g_copies(s).wait_send()

    loop(0, parts, finish)


def exchange_kernel(parts, groups, src, dst, local, us, ur):
    dp, f = lax.axis_index("dp"), lax.axis_index("fsdp")
    owners = groups * parts
    me = dp * parts + f
    mine = pltpu.make_async_copy(src.at[me], dst.at[me], local)
    mine.start()
    greet_all(me, parts, owners)
    loop(1, owners, lambda d: owner_copy(me, parts, owners, src, dst, us, ur, d).start())
    mine.wait()

    def finish(d):
        owner_copy(me, parts, owners, src, dst, us, ur, d, True).wait_recv()
        owner_copy(me, parts, owners, src, dst, us, ur, d).wait_send()

    loop(1, owners, finish)


def exchange(parts, groups, src):
    owners = groups * parts
    dma = pltpu.SemaphoreType.DMA
    return pl.pallas_call(
        functools.partial(exchange_kernel, parts, groups),
        out_shape=jax.ShapeDtypeStruct(src.shape, BF),
        in_specs=[pl.BlockSpec(memory_space=pl.ANY)],
        out_specs=pl.BlockSpec(memory_space=pl.ANY),
        scratch_shapes=[dma(()), dma((owners,)), dma((owners,))],
        compiler_params=pltpu.CompilerParams(collective_id=5, has_side_effects=True),
        cost_estimate=lasting(25),
    )(src)


def spread(parts, groups, xd, gd, inb, ovb):
    owners, rows_x = groups * parts, groups // 2
    dma = pltpu.SemaphoreType.DMA
    return pl.pallas_call(
        functools.partial(spread_kernel, parts, groups),
        out_shape=(
            jax.ShapeDtypeStruct(xd.shape, BF),
            jax.ShapeDtypeStruct((groups,) + gd.shape, BF),
            jax.ShapeDtypeStruct((owners,) + inb.shape, BF),
            jax.ShapeDtypeStruct((owners,) + ovb.shape, BF),
        ),
        in_specs=[pl.BlockSpec(memory_space=pl.ANY)] * 4,
        out_specs=(pl.BlockSpec(memory_space=pl.ANY),) * 4,
        scratch_shapes=[
            dma((4,)),
            dma((parts,)), dma((parts,)), dma((parts,)), dma((parts,)),
            dma((2, parts)), dma((2, parts)),
            dma((2, parts, rows_x)), dma((2, parts, rows_x)),
            dma((2, parts, rows_x)), dma((2, parts, rows_x)),
            dma((parts, rows_x)), dma((parts, rows_x)),
            dma((parts, rows_x)), dma((parts, rows_x)),
        ],
        compiler_params=pltpu.CompilerParams(collective_id=0, has_side_effects=True),
        cost_estimate=lasting(200),
    )(xd, gd, inb, ovb)


def group_gather_kernel(groups, chunks, src, out, local, ns, nr, ss, sr):
    dp, f = lax.axis_index("dp"), lax.axis_index("fsdp")
    rows_x = groups // 2
    x, core = lax.div(dp, 2), lax.rem(dp, 2)
    sib = x * 2 + 1 - core
    size = src.shape[0] // chunks
    mine = pltpu.make_async_copy(src, out.at[dp], local)
    mine.start()
    greet([(sib, f)] + [(wrap(x + dx, rows_x) * 2 + core, f) for dx in range(1, rows_x)])

    def part(ref, k):
        return ref.at[pl.ds(k * size, size)]

    def x_send(k, dx):
        to = wrap(x + dx, rows_x) * 2 + core
        return remote(part(src, k), part(out.at[dp], k), ns.at[k, dx], nr.at[k, dx], to, f)

    def x_recv(k, dx):
        came = wrap(x - dx, rows_x) * 2 + core
        ref = part(out.at[came], k)
        return remote(ref, ref, ns.at[k, dx], nr.at[k, dx], came, f)

    def sib_send(k, dx):
        came = wrap(x - dx, rows_x) * 2 + core
        ref = part(out.at[came], k)
        return remote(part(src, k) if dx == 0 else ref, ref, ss.at[k, dx], sr.at[k, dx], sib, f)

    def sib_recv(k, dx):
        came = wrap(x - dx, rows_x) * 2 + 1 - core
        ref = part(out.at[came], k)
        return remote(ref, ref, ss.at[k, dx], sr.at[k, dx], sib, f)

    for k in range(chunks):
        for dx in range(1, rows_x):
            x_send(k, dx).start()
    for k in range(chunks):
        sib_send(k, 0).start()
    for k in range(chunks):
        for dx in range(1, rows_x):
            x_recv(k, dx).wait_recv()
            sib_send(k, dx).start()
    mine.wait()
    for k in range(chunks):
        for dx in range(rows_x):
            sib_recv(k, dx).wait_recv()
            sib_send(k, dx).wait_send()
        for dx in range(1, rows_x):
            x_send(k, dx).wait_send()


def group_gather(groups, src):
    chunks, rows_x = 4, groups // 2
    dma = pltpu.SemaphoreType.DMA
    return pl.pallas_call(
        functools.partial(group_gather_kernel, groups, chunks),
        out_shape=jax.ShapeDtypeStruct((groups,) + src.shape, BF),
        in_specs=[pl.BlockSpec(memory_space=pl.ANY)],
        out_specs=pl.BlockSpec(memory_space=pl.ANY),
        scratch_shapes=[dma(())] + [dma((chunks, rows_x))] * 4,
        compiler_params=pltpu.CompilerParams(collective_id=1, has_side_effects=True),
        cost_estimate=lasting(45),
    )(src)


def ffn_back_kernel(
    parts, groups, chunks, streams,
    grad, act, dhid, w1, w2,
    out, dsum, ysum,
    loc, got, gone, w1v, w2v, some, psib, sibr, xb, xrb,
    ll, ol, rs, rr, wl, sl, gss, gsr, gns, gnr,
):
    dp, f = lax.axis_index("dp"), lax.axis_index("fsdp")
    rows_x = groups // 2
    x, core = lax.div(dp, 2), lax.rem(dp, 2)
    sib = x * 2 + 1 - core
    p = ring_place(f, parts)
    nxt, prv = ring_index(p + 1, parts), ring_index(p - 1, parts)
    block, width = out.shape
    part, cut = width // streams, width // chunks
    count = dsum.shape[0]
    far = range(1, rows_x)

    def local_copy(h, s):
        c = ring_index(p - 1 - s if h % 2 == 0 else p + 1 + s, parts)
        return pltpu.make_async_copy(
            grad.at[pl.ds(pl.multiple_of(c * block, block), block), pl.ds(h * part, part)],
            loc.at[lax.rem(s, 2), h], ll.at[lax.rem(s, 2), h],
        )

    w_loads = (
        pltpu.make_async_copy(w1, w1v, wl.at[0]),
        pltpu.make_async_copy(w2, w2v, wl.at[1]),
    )
    for s in range(2):
        for h in range(streams):
            local_copy(h, s).start()
    for load in w_loads:
        load.start()
    greet(
        [(dp, nxt), (dp, prv), (sib, f)]
        + [(wrap(x + dx, rows_x) * 2 + core, f) for dx in range(1, rows_x)]
    )

    def ring_copy(h, s):
        return remote(
            gone.at[lax.rem(s, 2), h], got.at[h, s], rs.at[h, s], rr.at[h, s],
            dp, nxt if h % 2 == 0 else prv,
        )

    def out_copy(h):
        return pltpu.make_async_copy(
            gone.at[lax.rem(parts - 1, 2), h], out.at[:, pl.ds(h * part, part)], ol.at[h]
        )

    def pass_on(s):
        slot = lax.rem(s, 2)
        for h in range(streams):
            local_copy(h, s).wait()

            @pl.when(s >= 2)
            def _():
                ring_copy(h, s - 2).wait_send()

            @pl.when(s == 0)
            def _():
                gone[slot, h] = loc[slot, h]

            @pl.when(s > 0)
            def _():
                ring_copy(h, s - 1).wait_recv()
                gone[slot, h] = (
                    loc[slot, h].astype(F32) + got[h, s - 1].astype(F32)
                ).astype(BF)

            @pl.when(s < parts - 1)
            def _():
                ring_copy(h, s).start()

            @pl.when(s == parts - 1)
            def _():
                out_copy(h).start()

            @pl.when(s < parts - 2)
            def _():
                local_copy(h, s + 2).start()

    def cols(k):
        return pl.ds(pl.multiple_of(k * cut, cut), cut)

    def rows_of(dx, c):
        group = wrap(x + dx, rows_x) * 2 + (core if c == 0 else 1 - core)
        return pl.ds(pl.multiple_of(group * count, count), count)

    rows_in, weights, totals = (dhid, act), (w1v, w2v), (dsum, ysum)

    def sum_sib(which, k):
        return remote(
            psib.at[which, :, :, cols(k)], sibr.at[which, :, :, cols(k)],
            gss.at[which, k], gsr.at[which, k], sib, f,
        )

    def sum_x(which, dx, k):
        to = wrap(x + dx, rows_x) * 2 + core
        return remote(
            xb.at[which, dx - 1, :, cols(k)], xrb.at[which, dx - 1, :, cols(k)],
            gns.at[which, dx, k], gnr.at[which, dx, k], to, f,
        )

    def take_rows(which, c):
        copies = [
            pltpu.make_async_copy(
                rows_in[which].at[rows_of(dx, c)], some.at[pl.ds(dx * count, count)], sl.at[dx]
            )
            for dx in range(rows_x)
        ]
        for copy in copies:
            copy.start()
        for copy in copies:
            copy.wait()

    def other_side(which):
        take_rows(which, 1)

        def one(k):
            psib[which, :, :, cols(k)] = (
                jnp.dot(some[...], weights[which][:, cols(k)], preferred_element_type=F32)
                .astype(BF)
                .reshape(rows_x, count, cut)
            )
            sum_sib(which, k).start()

        loop(0, chunks, one)

    def own_side(which):
        take_rows(which, 0)

        def one(k):
            here = jnp.dot(some[...], weights[which][:, cols(k)], preferred_element_type=F32)
            sum_sib(which, k).wait_recv()
            here = here.reshape(rows_x, count, cut) + sibr[which, :, :, cols(k)].astype(F32)
            for dx in far:
                xb[which, dx - 1, :, cols(k)] = here[dx].astype(BF)
                sum_x(which, dx, k).start()
            totals[which][:, cols(k)] = here[0]

        loop(0, chunks, one)

    def collect(which):
        def one(k):
            for dx in far:
                sum_x(which, dx, k).wait_recv()
                totals[which][:, cols(k)] += xrb[which, dx - 1, :, cols(k)].astype(F32)

        loop(0, chunks, one)

    def step(s):
        pass_on(s)

        @pl.when(s == 0)
        def _():
            w_loads[0].wait()
            other_side(0)

        @pl.when(s == 1)
        def _():
            own_side(0)

        @pl.when(s == 2)
        def _():
            w_loads[1].wait()
            other_side(1)

        @pl.when(s == 3)
        def _():
            own_side(1)

        @pl.when(s == 4)
        def _():
            collect(0)

    loop(0, parts, step)
    collect(1)
    for h in range(streams):
        ring_copy(h, parts - 2).wait_send()
        out_copy(h).wait()
    for which in range(2):
        for k in range(chunks):
            sum_sib(which, k).wait_send()
            for dx in far:
                sum_x(which, dx, k).wait_send()


def ffn_back(parts, groups, grad, act, dhid, w1, w2):
    chunks, streams, rows_x = 4, 4, groups // 2
    units, width = w1.shape
    count = act.shape[0] // groups
    block, part = units // parts, width // streams
    dma = pltpu.SemaphoreType.DMA
    hbm = pl.BlockSpec(memory_space=pl.ANY)
    vmem = pl.BlockSpec(memory_space=pltpu.VMEM)
    return pl.pallas_call(
        functools.partial(ffn_back_kernel, parts, groups, chunks, streams),
        out_shape=(
            jax.ShapeDtypeStruct((block, width), BF),
            jax.ShapeDtypeStruct((count, width), F32),
            jax.ShapeDtypeStruct((count, width), F32),
        ),
        in_specs=[hbm] * 5,
        out_specs=(hbm, vmem, vmem),
        scratch_shapes=[
            pltpu.VMEM((2, streams, block, part), BF),
            pltpu.VMEM((streams, parts - 1, block, part), BF),
            pltpu.VMEM((2, streams, block, part), BF),
            pltpu.VMEM((units, width), BF),
            pltpu.VMEM((units, width), BF),
            pltpu.VMEM((rows_x * count, units), BF),
            pltpu.VMEM((2, rows_x, count, width), BF),
            pltpu.VMEM((2, rows_x, count, width), BF),
            pltpu.VMEM((2, rows_x - 1, count, width), BF),
            pltpu.VMEM((2, rows_x - 1, count, width), BF),
            dma((2, streams)), dma((streams,)),
            dma((streams, parts)), dma((streams, parts)), dma((2,)), dma((rows_x,)),
            dma((2, chunks)), dma((2, chunks)),
            dma((2, rows_x, chunks)), dma((2, rows_x, chunks)),
        ],
        compiler_params=pltpu.CompilerParams(
            collective_id=3, has_side_effects=True, vmem_limit_bytes=60 * 2**20
        ),
        cost_estimate=lasting(110),
    )(grad, act, dhid, w1, w2)


def finish_kernel(
    parts, groups,
    grad_a, grad_b, gx, upg, vec,
    total_a, total_b, gx_out, upg_out, vec_out,
    loc_a, loc_b, sibr_a, sibr_b, xb_a, xb_b, xrb_a, xrb_b, got_a, got_b, gone_a, gone_b,
    local, ls, ss, sr, ns, nr, rs, rr, bs, br, us, ur, vs, vr,
):
    dp, f = lax.axis_index("dp"), lax.axis_index("fsdp")
    owners, rows_x = groups * parts, groups // 2
    x, core = lax.div(dp, 2), lax.rem(dp, 2)
    sib = x * 2 + 1 - core
    me = dp * parts + f
    p = ring_place(f, parts)
    nxt, prv = ring_index(p + 1, parts), ring_index(p - 1, parts)
    grads, total = (grad_a, grad_b), (total_a, total_b)
    loc, sibr, xb, xrb = (loc_a, loc_b), (sibr_a, sibr_b), (xb_a, xb_b), (xrb_a, xrb_b)
    got, gone = (got_a, got_b), (gone_a, gone_b)
    mine = [
        pltpu.make_async_copy(gx.at[f], gx_out.at[f], local.at[0]),
        pltpu.make_async_copy(vec.at[me], vec_out.at[me], local.at[1]),
        pltpu.make_async_copy(upg.at[me], upg_out.at[me], local.at[2]),
    ]
    for copy in mine:
        copy.start()
    greet_all(me, parts, owners)

    def chunk(h, s):
        return ring_index(p - 1 - s if h == 0 else p + 1 + s, parts)

    def sib_copy(h, s):
        piece = grads[h].at[:, 1 - core, chunk(h, s)]
        return remote(piece, sibr[h].at[s], ss.at[h, s], sr.at[h, s], sib, f)

    def own_copy(h, s):
        piece = grads[h].at[:, core, chunk(h, s)]
        return pltpu.make_async_copy(piece, loc[h].at[s], ls.at[h, s])

    def x_copy(h, s, dx):
        to = wrap(x + dx, rows_x) * 2 + core
        return remote(
            xb[h].at[s, dx - 1], xrb[h].at[s, dx - 1], ns.at[h, s, dx], nr.at[h, s, dx], to, f
        )

    def ring_copy(h, s):
        return remote(
            gone[h].at[s], got[h].at[s], rs.at[h, s], rr.at[h, s], dp, nxt if h == 0 else prv
        )

    def gx_copies(d, came=False):
        return deal_copy(parts, dp, f, gx, gx_out, bs, br, d, came)

    def upg_copies(d, came=False):
        return owner_copy(me, parts, owners, upg, upg_out, us, ur, d, came)

    def vec_copies(d, came=False):
        return owner_copy(me, parts, owners, vec, vec_out, vs, vr, d, came)

    def begin(s):
        for h in range(2):
            sib_copy(h, s).start()
            own_copy(h, s).start()

    def others(d):
        upg_copies(d).start()
        vec_copies(d).start()

    def returns(d):
        gx_copies(d).start()

    def pair(s):
        for h in range(2):
            sib_copy(h, s).wait_recv()
            own_copy(h, s).wait()
            for dx in range(1, rows_x):
                to = wrap(x + dx, rows_x)
                xb[h][s, dx - 1] = (sibr[h][s, to].astype(F32) + loc[h][s, to].astype(F32)).astype(BF)
                x_copy(h, s, dx).start()

    def step(s):
        for h in range(2):
            for dx in range(1, rows_x):
                x_copy(h, s, dx).wait_recv()

            def value():
                here = sibr[h][s, x].astype(F32) + loc[h][s, x].astype(F32)
                for dx in range(1, rows_x):
                    here = here + xrb[h][s, dx - 1].astype(F32)
                return here

            @pl.when(s == 0)
            def _():
                gone[h][s] = value().astype(BF)
                ring_copy(h, s).start()

            @pl.when((s > 0) & (s < parts - 1))
            def _():
                ring_copy(h, s - 1).wait_recv()
                gone[h][s] = (value() + got[h][s - 1].astype(F32)).astype(BF)
                ring_copy(h, s).start()

            @pl.when(s == parts - 1)
            def _():
                ring_copy(h, s - 1).wait_recv()
                total[h][...] = value() + got[h][s - 1].astype(F32)

    loop(0, parts, begin)
    loop(1, parts, returns)
    loop(1, owners, others)
    loop(0, parts, pair)
    loop(0, parts, step)

    def finish(s):
        for h in range(2):
            sib_copy(h, s).wait_send()
            for dx in range(1, rows_x):
                x_copy(h, s, dx).wait_send()

            @pl.when(s < parts - 1)
            def _():
                ring_copy(h, s).wait_send()

        @pl.when(s > 0)
        def _():
            gx_copies(s, True).wait_recv()
            gx_copies(s).wait_send()

    loop(0, parts, finish)

    def owner_finish(d):
        for copies in (upg_copies, vec_copies):
            copies(d, True).wait_recv()
            copies(d).wait_send()

    loop(1, owners, owner_finish)
    for copy in mine:
        copy.wait()


def finish_sums(parts, groups, grad_a, grad_b, gx, upg, vec):
    owners, rows_x = groups * parts, groups // 2
    rows = grad_a.shape[3]
    widths = (grad_a.shape[4], grad_b.shape[4])
    dma = pltpu.SemaphoreType.DMA
    hbm = pl.BlockSpec(memory_space=pl.ANY)
    return pl.pallas_call(
        functools.partial(finish_kernel, parts, groups),
        out_shape=(
            jax.ShapeDtypeStruct((rows, widths[0]), F32),
            jax.ShapeDtypeStruct((rows, widths[1]), F32),
            jax.ShapeDtypeStruct(gx.shape, BF),
            jax.ShapeDtypeStruct(upg.shape, BF),
            jax.ShapeDtypeStruct(vec.shape, F32),
        ),
        in_specs=[hbm] * 5,
        out_specs=(pl.BlockSpec(memory_space=pltpu.VMEM),) * 2 + (hbm,) * 3,
        scratch_shapes=[
            *(
                pltpu.VMEM(lead + (rows, width), BF)
                for lead in (
                    (parts, rows_x), (parts, rows_x), (parts, rows_x - 1), (parts, rows_x - 1),
                    (parts,), (parts,),
                )
                for width in widths
            ),
            dma((3,)),
            dma((2, parts)), dma((2, parts)), dma((2, parts)),
            dma((2, parts, rows_x)), dma((2, parts, rows_x)),
            dma((2, parts)), dma((2, parts)),
            dma((parts,)), dma((parts,)),
            dma((owners,)), dma((owners,)), dma((owners,)), dma((owners,)),
        ],
        compiler_params=pltpu.CompilerParams(
            collective_id=4, has_side_effects=True, vmem_limit_bytes=60 * 2**20
        ),
        cost_estimate=lasting(1),
    )(grad_a, grad_b, gx, upg, vec)


def shards(
    tokens,
    cotangent,
    lengths,
    routing,
    in_weight,
    in_first,
    in_second,
    out_weight,
    out_first,
    out_second,
    up_weight,
    up_first,
    up_second,
    down_weight,
    down_first,
    down_second,
    vectors,
    vector_first,
    vector_second,
):
    bf = jnp.bfloat16
    heads = D // HD
    count = tokens.shape[0]
    parts = lax.axis_size("fsdp")
    groups = lax.axis_size("dp")
    both = ("dp", "fsdp")
    piece = count // parts
    width_in = D + 2 * HD
    slots = jnp.arange(parts, dtype=jnp.int32)
    order = routing[0]
    inverse = jnp.sum(jnp.where(order[:, None] == slots[None, :], slots[:, None], 0), axis=0)

    def deal(array):
        return jnp.take(array.reshape(parts, piece, D), inverse, axis=0)

    def undeal(array):
        return jnp.take(array, order, axis=0).reshape(count, D)

    rows = in_weight.shape[0]
    owners = groups * parts
    out_vec = jnp.concatenate(
        [out_weight.astype(bf), jnp.pad(vectors.astype(bf), ((0, 0), (0, 128 - NVEC)))], axis=1
    )
    up_pieces = up_weight.astype(bf).reshape(rows, owners, FF // owners).transpose(1, 0, 2)
    up_block, dealt, dealt_grad, out_vec = lax.optimization_barrier(
        (exchange(parts, groups, up_pieces), deal(tokens), deal(cotangent), out_vec)
    )
    x_dealt, grad_dealt, whole_in, whole_out = spread(
        parts, groups, dealt, dealt_grad, in_weight.astype(bf), out_vec
    )
    inputs_here = x_dealt.reshape(count, D)
    grad_all = grad_dealt.reshape(groups * count, D)
    grad_here = lax.dynamic_index_in_dim(
        grad_dealt, lax.axis_index("dp"), 0, keepdims=False
    ).reshape(count, D)
    whole_in = whole_in.reshape(D, width_in)
    whole_out = whole_out.reshape(D, D + 128)
    part_down = lax.all_gather(down_weight.astype(bf), "fsdp", axis=0, tiled=True)
    part_up = lax.all_gather(up_block.reshape(D, FF // owners).T, "fsdp", axis=0, tiled=True)

    table = whole_out[:, D : D + NVEC].astype(jnp.float32)
    whole_out = whole_out[:, :D]
    gain_one = table[:, 0]
    shift_one = table[:, 1]
    query_bias = table[:, 2]
    branch_bias = table[:, 3]
    gain_two = table[:, 4]
    shift_two = table[:, 5]
    output_bias = table[:, 6]
    hidden_bias = table[:, 7:].T.reshape(FF)
    ff_here = FF // groups
    ff_start = lax.axis_index("dp") * ff_here
    hidden_bias_here = lax.dynamic_slice(hidden_bias, (ff_start,), (ff_here,))
    allowed = segment_mask(lengths[0], count)
    scale = 1.0 / math.sqrt(HD)
    inputs = inputs_here.astype(jnp.float32)
    norm_one_b = layer_norm(inputs, gain_one, shift_one).astype(bf)
    mixed = jnp.dot(norm_one_b, whole_in, preferred_element_type=jnp.float32)
    query_b = (mixed[:, :D] + query_bias).astype(bf)
    keys_b = mixed[:, D : D + HD].astype(bf)
    values_b = mixed[:, D + HD :].astype(bf)
    query_heads = query_b.reshape(count, heads, HD)

    def score_table():
        raw = (
            jnp.einsum("thd,sd->hts", query_heads, keys_b, preferred_element_type=jnp.float32)
            * scale
        )
        return jnp.where(allowed[None], raw, -1e30)

    scores = score_table()
    top = jnp.max(scores, axis=-1, keepdims=True)
    expo = jnp.exp(scores - top)
    total = jnp.sum(expo, axis=-1, keepdims=True)
    logsum = top + jnp.log(total)
    probs_b = (expo / total).astype(bf)
    attended_b = (
        jnp.einsum("hts,sd->thd", probs_b, values_b, preferred_element_type=jnp.float32)
        .reshape(count, D)
        .astype(bf)
    )
    middle = inputs + (
        jnp.dot(attended_b, whole_out, preferred_element_type=jnp.float32) + branch_bias
    )
    norm_two_b = layer_norm(middle, gain_two, shift_two).astype(bf)

    fused = parts == 8 and groups == 4
    if fused:
        norm_all = group_gather(groups, norm_two_b).reshape(groups * count, D)
    else:
        norm_all = lax.all_gather(norm_two_b, "dp", axis=0, tiled=True)
    hidden = contract_cols(norm_all, part_up) + hidden_bias_here
    grad_active = contract_cols(grad_all, part_down)
    gelu_value, gelu_pull = jax.vjp(gelu_tanh, hidden)
    active_b = gelu_value.astype(bf)
    grad_hidden_b = gelu_pull(grad_active)[0].astype(bf)
    down_parts = [
        contract_rows(active_b, grad_all[:, h * D // 2 : (h + 1) * D // 2]).astype(bf)
        for h in range(2)
    ]
    up_parts = contract_rows(grad_hidden_b, norm_all).astype(bf)
    down_parts, up_parts = lax.optimization_barrier((down_parts, up_parts))
    down_half = [
        lax.psum_scatter(item, "fsdp", scatter_dimension=0, tiled=True) for item in down_parts
    ]
    if fused:
        up_grad_block, grad_norm_two, branch_two = ffn_back(
            parts, groups, up_parts, active_b, grad_hidden_b, part_up, part_down
        )
    else:
        up_grad_block = lax.psum_scatter(up_parts, "fsdp", scatter_dimension=0, tiled=True)
        grad_norm_two = lax.psum_scatter(
            jnp.dot(grad_hidden_b, part_up, preferred_element_type=jnp.float32).astype(bf),
            "dp", scatter_dimension=0, tiled=True,
        ).astype(jnp.float32)
        branch_two = lax.psum_scatter(
            jnp.dot(active_b, part_down, preferred_element_type=jnp.float32).astype(bf),
            "dp", scatter_dimension=0, tiled=True,
        ).astype(jnp.float32)
    result = middle + (branch_two + output_bias)

    grad_y = grad_here.astype(jnp.float32)
    norm_value_two, pull_two = jax.vjp(layer_norm, middle, gain_two, shift_two)
    grad_middle_norm, grad_gain_two, grad_shift_two = pull_two(grad_norm_two)
    grad_middle = grad_y + grad_middle_norm
    grad_branch_b = grad_middle.astype(bf)
    grad_attended_b = contract_cols(grad_branch_b, whole_out).astype(bf)
    grad_heads = grad_attended_b.reshape(count, heads, HD)
    probs = jnp.exp(score_table() - logsum)
    probs_again_b = probs.astype(bf)
    grad_probs = jnp.einsum("thd,sd->hts", grad_heads, values_b, preferred_element_type=jnp.float32)
    grad_values_b = jnp.einsum(
        "hts,thd->sd", probs_again_b, grad_heads, preferred_element_type=jnp.float32
    ).astype(bf)
    weighted = jnp.sum(probs * grad_probs, axis=-1, keepdims=True)
    grad_scores_b = (probs * (grad_probs - weighted)).astype(bf)
    place = lax.axis_index("fsdp")
    offsets = jnp.arange(parts, dtype=jnp.int32)
    leaving = jnp.take(
        result.astype(bf).reshape(parts, piece, D), lax.rem(place + offsets, parts), axis=0
    )
    by_offset = [leaving[0]] + [
        lax.ppermute(leaving[d], "fsdp", [(i, (i + d) % parts) for i in range(parts)])
        for d in range(1, parts)
    ]
    early, late = parts * 3 // 8 + 1, parts * 6 // 8
    by_offset[:early], grad_scores_b = lax.optimization_barrier((by_offset[:early], grad_scores_b))
    grad_query_b = (
        (
            jnp.einsum("hts,sd->thd", grad_scores_b, keys_b, preferred_element_type=jnp.float32)
            * scale
        )
        .reshape(count, D)
        .astype(bf)
    )
    grad_keys_b = (
        jnp.einsum("hts,thd->sd", grad_scores_b, query_heads, preferred_element_type=jnp.float32)
        * scale
    ).astype(bf)
    grad_mixed_b = jnp.concatenate([grad_query_b, grad_keys_b, grad_values_b], axis=1)
    by_offset[early:late], grad_mixed_b = lax.optimization_barrier(
        (by_offset[early:late], grad_mixed_b)
    )
    down_half[0], grad_mixed_b = lax.optimization_barrier((down_half[0], grad_mixed_b))
    grad_norm_one = contract_cols(grad_mixed_b, whole_in)
    norm_value_one, pull_one = jax.vjp(layer_norm, inputs, gain_one, shift_one)
    grad_inputs_norm, grad_gain_one, grad_shift_one = pull_one(grad_norm_one)
    grad_inputs = grad_middle + grad_inputs_norm
    by_offset[late:], grad_inputs = lax.optimization_barrier((by_offset[late:], grad_inputs))
    hidden_sums = jnp.sum(grad_hidden_b.astype(jnp.float32), axis=0)
    hidden_whole = lax.dynamic_update_slice(
        jnp.zeros((FF,), jnp.float32), hidden_sums, (ff_start,)
    )
    vector_grad = jnp.concatenate(
        [
            jnp.stack(
                [
                    grad_gain_one,
                    grad_shift_one,
                    jnp.sum(grad_query_b.astype(jnp.float32), axis=0),
                    jnp.sum(grad_branch_b.astype(jnp.float32), axis=0),
                    grad_gain_two,
                    grad_shift_two,
                    jnp.sum(grad_y, axis=0),
                ],
                axis=0,
            ),
            hidden_whole.reshape(FF // D, D),
        ],
        axis=0,
    )
    vector_grad = vector_grad.reshape(NVEC, owners, rows).transpose(1, 0, 2)
    vector_grad = jnp.pad(vector_grad, ((0, 0), (0, 16 - NVEC), (0, 128 - rows)))
    grad_in, grad_out, back_grad, grad_up, vector_sum = finish_sums(
        parts,
        groups,
        contract_rows(norm_one_b, grad_mixed_b)
        .astype(bf)
        .reshape(groups // 2, 2, parts, rows, width_in),
        contract_rows(attended_b, grad_branch_b).astype(bf).reshape(groups // 2, 2, parts, rows, D),
        grad_inputs.astype(bf).reshape(parts, piece, D),
        up_grad_block.T.astype(bf).reshape(owners, rows, FF // owners),
        vector_grad,
    )
    grad_up = grad_up.transpose(1, 0, 2).reshape(rows, FF)
    vector_sum = jnp.sum(vector_sum, axis=0)
    grad_vec = vector_sum[:NVEC, :rows].T
    down_grad = jnp.concatenate(down_half, axis=1)
    in_new = adam_update(in_weight, in_first, in_second, grad_in, 1.0 / math.sqrt(D), decay_rate)
    out_new = adam_update(
        out_weight, out_first, out_second, grad_out, 1.0 / math.sqrt(D * 8 // TOK_DEV), decay_rate
    )
    up_new = adam_update(up_weight, up_first, up_second, grad_up, 1.0 / math.sqrt(D), decay_rate)
    down_new = adam_update(
        down_weight, down_first, down_second, down_grad, 1.0 / math.sqrt(FF), decay_rate
    )
    vec_new = adam_update(vectors, vector_first, vector_second, grad_vec, 0.1, 0.0)
    result_here = jnp.take(
        jnp.stack(by_offset), lax.rem(place - order + parts, parts), axis=0
    ).reshape(count, D)
    return (result_here, undeal(back_grad)) + in_new + out_new + up_new + down_new + vec_new


def solution(mesh):
    spec = P(("dp", "fsdp"), None)
    return jax.shard_map(
        shards,
        mesh=mesh,
        in_specs=(spec,) * 19,
        out_specs=(spec,) * 17,
        check_vma=False,
    )
```

```python
import functools
import math

import jax
import jax.numpy as jnp
from jax import lax
from jax.experimental import pallas as pl
from jax.experimental.pallas import tpu as pltpu
from jax.sharding import PartitionSpec as P

D = 2048
FF = 8192
HD = 128
TOK_DEV = 384
STEP = 5
NVEC = 11


eps_norm = 1e-05
beta_one = 0.5
beta_two = 0.5
adam_eps = 1e-08
decay_rate = 0.1


def layer_norm(values, gain, shift):
    centered = values - jnp.mean(values, axis=-1, keepdims=True)
    scaled = centered * lax.rsqrt(jnp.mean(centered * centered, axis=-1, keepdims=True) + eps_norm)
    return scaled * gain + shift


def gelu_tanh(values):
    return (
        0.5
        * values
        * (1.0 + jnp.tanh(0.7978845608028654 * (values + 0.044715 * values * values * values)))
    )


def segment_mask(sizes, count):
    ends = jnp.cumsum(sizes)
    places = jnp.arange(count, dtype=jnp.int32)
    labels = jnp.sum((places[:, None] >= ends[None, :]).astype(jnp.int32), axis=1)
    return (labels[:, None] == labels[None, :]) & (places[None, :] <= places[:, None])


def adam_update(weight, first, second, grad, rate, decay):
    grad = grad.astype(jnp.float32)
    first_new = beta_one * first + (1.0 - beta_one) * grad
    second_new = beta_two * second + (1.0 - beta_two) * grad * grad
    fix_one = 1.0 - beta_one**STEP
    fix_two = 1.0 - beta_two**STEP
    step_size = first_new / fix_one / (jnp.sqrt(second_new / fix_two) + adam_eps)
    weight_new = weight - rate * (step_size + decay * weight)
    return (weight_new, first_new, second_new)


def contract_rows(left, right):
    return lax.dot_general(
        left, right, (((0,), (0,)), ((), ())), preferred_element_type=jnp.float32
    )


def contract_cols(left, right):
    return lax.dot_general(
        left, right, (((1,), (1,)), ((), ())), preferred_element_type=jnp.float32
    )


MESH = pl.DeviceIdType.MESH
F32 = jnp.float32
BF = jnp.bfloat16


def wrap(value, count):
    return lax.rem(value + 2 * count, count)


def ring_place(index, parts):
    if parts != 8:
        return index
    z, y = lax.div(index, 2), lax.rem(index, 2)
    return z + y * (7 - 2 * z)


def ring_index(place, parts):
    place = wrap(place, parts)
    if parts != 8:
        return place
    back = lax.div(place, 4)
    return (1 - back) * 2 * place + back * (15 - 2 * place)


def remote(src, dst, send, recv, dp, fs):
    return pltpu.make_async_remote_copy(
        src_ref=src, dst_ref=dst, send_sem=send, recv_sem=recv, device_id=(dp, fs), device_id_type=MESH
    )


def lasting(micros):
    return pl.CostEstimate(
        flops=int(micros * 1.1e9), bytes_accessed=int(micros * 3.3e6), transcendentals=0
    )


def greet(targets):
    barrier = pltpu.get_barrier_semaphore()
    for dp, fs in targets:
        pl.semaphore_signal(barrier, inc=1, device_id=(dp, fs), device_id_type=MESH)
    pl.semaphore_wait(barrier, len(targets))


def greet_all(me, parts, owners):
    barrier = pltpu.get_barrier_semaphore()

    def one(i, carry):
        peer = wrap(me + i, owners)
        pl.semaphore_signal(
            barrier, inc=1, device_id=(lax.div(peer, parts), lax.rem(peer, parts)), device_id_type=MESH
        )
        return carry

    lax.fori_loop(1, owners, one, 0)
    pl.semaphore_wait(barrier, owners - 1)


def loop(low, high, body):
    def one(i, carry):
        body(i)
        return carry

    lax.fori_loop(low, high, one, 0)


def deal_copy(parts, dp, f, src, dst, send, recv, d, came=False):
    to = wrap(f + d, parts)
    place = wrap(f - d, parts) if came else f
    return remote(src.at[to], dst.at[place], send.at[d], recv.at[d], dp, to)


def owner_copy(me, parts, owners, src, dst, send, recv, d, came=False):
    to = wrap(me + d, owners)
    place = wrap(me - d, owners) if came else me
    return remote(
        src.at[to], dst.at[place], send.at[d], recv.at[d], lax.div(to, parts), lax.rem(to, parts)
    )


def spread_kernel(
    parts, groups,
    xd, gd, inb, ovb,
    xo, eall, win, wov,
    local, xs, xr, gs, gr, rs, rr, ns, nr, ss, sr, ens, enr, ess, esr,
):
    dp, f = lax.axis_index("dp"), lax.axis_index("fsdp")
    owners, rows_x = groups * parts, groups // 2
    x, core = lax.div(dp, 2), lax.rem(dp, 2)
    sib = x * 2 + 1 - core
    me = dp * parts + f
    p = ring_place(f, parts)
    nxt, prv = ring_index(p + 1, parts), ring_index(p - 1, parts)
    whole = (win, wov)
    mine = [
        pltpu.make_async_copy(inb, win.at[me], local.at[0]),
        pltpu.make_async_copy(ovb, wov.at[me], local.at[1]),
        pltpu.make_async_copy(xd.at[f], xo.at[f], local.at[2]),
        pltpu.make_async_copy(gd.at[f], eall.at[dp, f], local.at[3]),
    ]
    for copy in mine:
        copy.start()
    greet(
        [(dp, wrap(f + d, parts)) for d in range(1, parts)]
        + [(sib, f)]
        + [(wrap(x + dx, rows_x) * 2 + core, f) for dx in range(1, rows_x)]
    )
    for copy in mine:
        copy.wait()

    def x_copies(d, came=False):
        return deal_copy(parts, dp, f, xd, xo, xs, xr, d, came)

    def g_copies(d, came=False):
        return deal_copy(parts, dp, f, gd, eall.at[dp], gs, gr, d, came)

    def origin(h, s):
        return ring_index(p - s if h == 0 else p + s, parts)

    def ring_send(h, s):
        ref = whole[h].at[dp * parts + origin(h, s)]
        return remote(ref, ref, rs.at[h, s], rr.at[h, s], dp, nxt if h == 0 else prv)

    def ring_recv(h, s):
        ref = whole[h].at[dp * parts + origin(h, s)]
        return remote(ref, ref, rs.at[h, s - 1], rr.at[h, s - 1], dp, nxt if h == 0 else prv)

    def x_send(h, s, dx):
        ref = whole[h].at[dp * parts + origin(h, s)]
        to = wrap(x + dx, rows_x) * 2 + core
        return remote(ref, ref, ns.at[h, s, dx], nr.at[h, s, dx], to, f)

    def x_recv(h, s, dx):
        came = wrap(x - dx, rows_x) * 2 + core
        ref = whole[h].at[came * parts + origin(h, s)]
        return remote(ref, ref, ns.at[h, s, dx], nr.at[h, s, dx], came, f)

    def sib_send(h, s, dx):
        came = wrap(x - dx, rows_x) * 2 + core
        ref = whole[h].at[came * parts + origin(h, s)]
        return remote(ref, ref, ss.at[h, s, dx], sr.at[h, s, dx], sib, f)

    def sib_recv(h, s, dx):
        came = wrap(x - dx, rows_x) * 2 + 1 - core
        ref = whole[h].at[came * parts + origin(h, s)]
        return remote(ref, ref, ss.at[h, s, dx], sr.at[h, s, dx], sib, f)

    def e_x_send(d, dx):
        ref = eall.at[dp, wrap(f - d, parts)]
        to = wrap(x + dx, rows_x) * 2 + core
        return remote(ref, ref, ens.at[d, dx], enr.at[d, dx], to, f)

    def e_x_recv(d, dx):
        came = wrap(x - dx, rows_x) * 2 + core
        ref = eall.at[came, wrap(f - d, parts)]
        return remote(ref, ref, ens.at[d, dx], enr.at[d, dx], came, f)

    def e_sib_send(d, dx):
        came = wrap(x - dx, rows_x) * 2 + core
        ref = eall.at[came, wrap(f - d, parts)]
        return remote(ref, ref, ess.at[d, dx], esr.at[d, dx], sib, f)

    def e_sib_recv(d, dx):
        came = wrap(x - dx, rows_x) * 2 + 1 - core
        ref = eall.at[came, wrap(f - d, parts)]
        return remote(ref, ref, ess.at[d, dx], esr.at[d, dx], sib, f)

    def ring_step(s):
        for h in range(2):
            @pl.when(s > 0)
            def _():
                ring_recv(h, s).wait_recv()

            @pl.when(s < parts - 1)
            def _():
                ring_send(h, s).start()

            for dx in range(1, rows_x):
                x_send(h, s, dx).start()
            sib_send(h, s, 0).start()

    def e_step(d):
        @pl.when(d > 0)
        def _():
            g_copies(d, True).wait_recv()

        for dx in range(1, rows_x):
            e_x_send(d, dx).start()
        e_sib_send(d, 0).start()

    def relay(s):
        for h in range(2):
            for dx in range(1, rows_x):
                x_recv(h, s, dx).wait_recv()
                sib_send(h, s, dx).start()

    def e_relay(d):
        for dx in range(1, rows_x):
            e_x_recv(d, dx).wait_recv()
            e_sib_send(d, dx).start()

    def main(s):
        @pl.when(s < parts)
        def _():
            ring_step(s)

        @pl.when(s < parts - 1)
        def _():
            x_copies(s + 1).start()
            g_copies(s + 1).start()

        @pl.when((s >= 1) & (s <= parts))
        def _():
            e_step(s - 1)

        @pl.when((s >= 2) & (s < parts + 2))
        def _():
            relay(s - 2)

        @pl.when(s >= 3)
        def _():
            e_relay(s - 3)

    loop(0, parts + 3, main)

    def finish(s):
        for h in range(2):
            @pl.when(s < parts - 1)
            def _():
                ring_send(h, s).wait_send()

            for dx in range(1, rows_x):
                x_send(h, s, dx).wait_send()
            for dx in range(rows_x):
                sib_recv(h, s, dx).wait_recv()
                sib_send(h, s, dx).wait_send()
        for dx in range(1, rows_x):
            e_x_send(s, dx).wait_send()
        for dx in range(rows_x):
            e_sib_recv(s, dx).wait_recv()
            e_sib_send(s, dx).wait_send()

        @pl.when(s > 0)
        def _():
            x_copies(s, True).wait_recv()
            x_copies(s).wait_send()
            g_copies(s).wait_send()

    loop(0, parts, finish)


def exchange_kernel(parts, groups, src, dst, local, us, ur):
    dp, f = lax.axis_index("dp"), lax.axis_index("fsdp")
    owners = groups * parts
    me = dp * parts + f
    mine = pltpu.make_async_copy(src.at[me], dst.at[me], local)
    mine.start()
    greet_all(me, parts, owners)
    loop(1, owners, lambda d: owner_copy(me, parts, owners, src, dst, us, ur, d).start())
    mine.wait()

    def finish(d):
        owner_copy(me, parts, owners, src, dst, us, ur, d, True).wait_recv()
        owner_copy(me, parts, owners, src, dst, us, ur, d).wait_send()

    loop(1, owners, finish)


def exchange(parts, groups, src):
    owners = groups * parts
    dma = pltpu.SemaphoreType.DMA
    return pl.pallas_call(
        functools.partial(exchange_kernel, parts, groups),
        out_shape=jax.ShapeDtypeStruct(src.shape, BF),
        in_specs=[pl.BlockSpec(memory_space=pl.ANY)],
        out_specs=pl.BlockSpec(memory_space=pl.ANY),
        scratch_shapes=[dma(()), dma((owners,)), dma((owners,))],
        compiler_params=pltpu.CompilerParams(collective_id=5, has_side_effects=True),
        cost_estimate=lasting(25),
    )(src)


def spread(parts, groups, xd, gd, inb, ovb):
    owners, rows_x = groups * parts, groups // 2
    dma = pltpu.SemaphoreType.DMA
    return pl.pallas_call(
        functools.partial(spread_kernel, parts, groups),
        out_shape=(
            jax.ShapeDtypeStruct(xd.shape, BF),
            jax.ShapeDtypeStruct((groups,) + gd.shape, BF),
            jax.ShapeDtypeStruct((owners,) + inb.shape, BF),
            jax.ShapeDtypeStruct((owners,) + ovb.shape, BF),
        ),
        in_specs=[pl.BlockSpec(memory_space=pl.ANY)] * 4,
        out_specs=(pl.BlockSpec(memory_space=pl.ANY),) * 4,
        scratch_shapes=[
            dma((4,)),
            dma((parts,)), dma((parts,)), dma((parts,)), dma((parts,)),
            dma((2, parts)), dma((2, parts)),
            dma((2, parts, rows_x)), dma((2, parts, rows_x)),
            dma((2, parts, rows_x)), dma((2, parts, rows_x)),
            dma((parts, rows_x)), dma((parts, rows_x)),
            dma((parts, rows_x)), dma((parts, rows_x)),
        ],
        compiler_params=pltpu.CompilerParams(collective_id=0, has_side_effects=True),
        cost_estimate=lasting(200),
    )(xd, gd, inb, ovb)


def group_gather_kernel(groups, chunks, src, out, local, ns, nr, ss, sr):
    dp, f = lax.axis_index("dp"), lax.axis_index("fsdp")
    rows_x = groups // 2
    x, core = lax.div(dp, 2), lax.rem(dp, 2)
    sib = x * 2 + 1 - core
    size = src.shape[0] // chunks
    mine = pltpu.make_async_copy(src, out.at[dp], local)
    mine.start()
    greet([(sib, f)] + [(wrap(x + dx, rows_x) * 2 + core, f) for dx in range(1, rows_x)])

    def part(ref, k):
        return ref.at[pl.ds(k * size, size)]

    def x_send(k, dx):
        to = wrap(x + dx, rows_x) * 2 + core
        return remote(part(src, k), part(out.at[dp], k), ns.at[k, dx], nr.at[k, dx], to, f)

    def x_recv(k, dx):
        came = wrap(x - dx, rows_x) * 2 + core
        ref = part(out.at[came], k)
        return remote(ref, ref, ns.at[k, dx], nr.at[k, dx], came, f)

    def sib_send(k, dx):
        came = wrap(x - dx, rows_x) * 2 + core
        ref = part(out.at[came], k)
        return remote(part(src, k) if dx == 0 else ref, ref, ss.at[k, dx], sr.at[k, dx], sib, f)

    def sib_recv(k, dx):
        came = wrap(x - dx, rows_x) * 2 + 1 - core
        ref = part(out.at[came], k)
        return remote(ref, ref, ss.at[k, dx], sr.at[k, dx], sib, f)

    for k in range(chunks):
        for dx in range(1, rows_x):
            x_send(k, dx).start()
    for k in range(chunks):
        sib_send(k, 0).start()
    for k in range(chunks):
        for dx in range(1, rows_x):
            x_recv(k, dx).wait_recv()
            sib_send(k, dx).start()
    mine.wait()
    for k in range(chunks):
        for dx in range(rows_x):
            sib_recv(k, dx).wait_recv()
            sib_send(k, dx).wait_send()
        for dx in range(1, rows_x):
            x_send(k, dx).wait_send()


def group_gather(groups, src):
    chunks, rows_x = 4, groups // 2
    dma = pltpu.SemaphoreType.DMA
    return pl.pallas_call(
        functools.partial(group_gather_kernel, groups, chunks),
        out_shape=jax.ShapeDtypeStruct((groups,) + src.shape, BF),
        in_specs=[pl.BlockSpec(memory_space=pl.ANY)],
        out_specs=pl.BlockSpec(memory_space=pl.ANY),
        scratch_shapes=[dma(())] + [dma((chunks, rows_x))] * 4,
        compiler_params=pltpu.CompilerParams(collective_id=1, has_side_effects=True),
        cost_estimate=lasting(45),
    )(src)


def ffn_back_kernel(
    parts, groups, chunks, streams,
    grad, act, dhid, w1, w2,
    out, dsum, ysum,
    loc, got, gone, w1v, w2v, some, psib, sibr, xb, xrb,
    ll, ol, rs, rr, wl, sl, gss, gsr, gns, gnr,
):
    dp, f = lax.axis_index("dp"), lax.axis_index("fsdp")
    rows_x = groups // 2
    x, core = lax.div(dp, 2), lax.rem(dp, 2)
    sib = x * 2 + 1 - core
    p = ring_place(f, parts)
    nxt, prv = ring_index(p + 1, parts), ring_index(p - 1, parts)
    block, width = out.shape
    part, cut = width // streams, width // chunks
    count = dsum.shape[0]
    far = range(1, rows_x)

    def local_copy(h, s):
        c = ring_index(p - 1 - s if h % 2 == 0 else p + 1 + s, parts)
        return pltpu.make_async_copy(
            grad.at[pl.ds(pl.multiple_of(c * block, block), block), pl.ds(h * part, part)],
            loc.at[lax.rem(s, 2), h], ll.at[lax.rem(s, 2), h],
        )

    w_loads = (
        pltpu.make_async_copy(w1, w1v, wl.at[0]),
        pltpu.make_async_copy(w2, w2v, wl.at[1]),
    )
    for s in range(2):
        for h in range(streams):
            local_copy(h, s).start()
    for load in w_loads:
        load.start()
    greet(
        [(dp, nxt), (dp, prv), (sib, f)]
        + [(wrap(x + dx, rows_x) * 2 + core, f) for dx in range(1, rows_x)]
    )

    def ring_copy(h, s):
        return remote(
            gone.at[lax.rem(s, 2), h], got.at[h, s], rs.at[h, s], rr.at[h, s],
            dp, nxt if h % 2 == 0 else prv,
        )

    def out_copy(h):
        return pltpu.make_async_copy(
            gone.at[lax.rem(parts - 1, 2), h], out.at[:, pl.ds(h * part, part)], ol.at[h]
        )

    def pass_on(s):
        slot = lax.rem(s, 2)
        for h in range(streams):
            local_copy(h, s).wait()

            @pl.when(s >= 2)
            def _():
                ring_copy(h, s - 2).wait_send()

            @pl.when(s == 0)
            def _():
                gone[slot, h] = loc[slot, h]

            @pl.when(s > 0)
            def _():
                ring_copy(h, s - 1).wait_recv()
                gone[slot, h] = (
                    loc[slot, h].astype(F32) + got[h, s - 1].astype(F32)
                ).astype(BF)

            @pl.when(s < parts - 1)
            def _():
                ring_copy(h, s).start()

            @pl.when(s == parts - 1)
            def _():
                out_copy(h).start()

            @pl.when(s < parts - 2)
            def _():
                local_copy(h, s + 2).start()

    def cols(k):
        return pl.ds(pl.multiple_of(k * cut, cut), cut)

    def rows_of(dx, c):
        group = wrap(x + dx, rows_x) * 2 + (core if c == 0 else 1 - core)
        return pl.ds(pl.multiple_of(group * count, count), count)

    rows_in, weights, totals = (dhid, act), (w1v, w2v), (dsum, ysum)

    def sum_sib(which, k):
        return remote(
            psib.at[which, :, :, cols(k)], sibr.at[which, :, :, cols(k)],
            gss.at[which, k], gsr.at[which, k], sib, f,
        )

    def sum_x(which, dx, k):
        to = wrap(x + dx, rows_x) * 2 + core
        return remote(
            xb.at[which, dx - 1, :, cols(k)], xrb.at[which, dx - 1, :, cols(k)],
            gns.at[which, dx, k], gnr.at[which, dx, k], to, f,
        )

    def take_rows(which, c):
        copies = [
            pltpu.make_async_copy(
                rows_in[which].at[rows_of(dx, c)], some.at[pl.ds(dx * count, count)], sl.at[dx]
            )
            for dx in range(rows_x)
        ]
        for copy in copies:
            copy.start()
        for copy in copies:
            copy.wait()

    def other_side(which):
        take_rows(which, 1)

        def one(k):
            psib[which, :, :, cols(k)] = (
                jnp.dot(some[...], weights[which][:, cols(k)], preferred_element_type=F32)
                .astype(BF)
                .reshape(rows_x, count, cut)
            )
            sum_sib(which, k).start()

        loop(0, chunks, one)

    def own_side(which):
        take_rows(which, 0)

        def one(k):
            here = jnp.dot(some[...], weights[which][:, cols(k)], preferred_element_type=F32)
            sum_sib(which, k).wait_recv()
            here = here.reshape(rows_x, count, cut) + sibr[which, :, :, cols(k)].astype(F32)
            for dx in far:
                xb[which, dx - 1, :, cols(k)] = here[dx].astype(BF)
                sum_x(which, dx, k).start()
            totals[which][:, cols(k)] = here[0]

        loop(0, chunks, one)

    def collect(which):
        def one(k):
            for dx in far:
                sum_x(which, dx, k).wait_recv()
                totals[which][:, cols(k)] += xrb[which, dx - 1, :, cols(k)].astype(F32)

        loop(0, chunks, one)

    def step(s):
        pass_on(s)

        @pl.when(s == 0)
        def _():
            w_loads[0].wait()
            other_side(0)

        @pl.when(s == 1)
        def _():
            own_side(0)

        @pl.when(s == 2)
        def _():
            w_loads[1].wait()
            other_side(1)

        @pl.when(s == 3)
        def _():
            own_side(1)

        @pl.when(s == 4)
        def _():
            collect(0)

    loop(0, parts, step)
    collect(1)
    for h in range(streams):
        ring_copy(h, parts - 2).wait_send()
        out_copy(h).wait()
    for which in range(2):
        for k in range(chunks):
            sum_sib(which, k).wait_send()
            for dx in far:
                sum_x(which, dx, k).wait_send()


def ffn_back(parts, groups, grad, act, dhid, w1, w2):
    chunks, streams, rows_x = 4, 4, groups // 2
    units, width = w1.shape
    count = act.shape[0] // groups
    block, part = units // parts, width // streams
    dma = pltpu.SemaphoreType.DMA
    hbm = pl.BlockSpec(memory_space=pl.ANY)
    vmem = pl.BlockSpec(memory_space=pltpu.VMEM)
    return pl.pallas_call(
        functools.partial(ffn_back_kernel, parts, groups, chunks, streams),
        out_shape=(
            jax.ShapeDtypeStruct((block, width), BF),
            jax.ShapeDtypeStruct((count, width), F32),
            jax.ShapeDtypeStruct((count, width), F32),
        ),
        in_specs=[hbm] * 5,
        out_specs=(hbm, vmem, vmem),
        scratch_shapes=[
            pltpu.VMEM((2, streams, block, part), BF),
            pltpu.VMEM((streams, parts - 1, block, part), BF),
            pltpu.VMEM((2, streams, block, part), BF),
            pltpu.VMEM((units, width), BF),
            pltpu.VMEM((units, width), BF),
            pltpu.VMEM((rows_x * count, units), BF),
            pltpu.VMEM((2, rows_x, count, width), BF),
            pltpu.VMEM((2, rows_x, count, width), BF),
            pltpu.VMEM((2, rows_x - 1, count, width), BF),
            pltpu.VMEM((2, rows_x - 1, count, width), BF),
            dma((2, streams)), dma((streams,)),
            dma((streams, parts)), dma((streams, parts)), dma((2,)), dma((rows_x,)),
            dma((2, chunks)), dma((2, chunks)),
            dma((2, rows_x, chunks)), dma((2, rows_x, chunks)),
        ],
        compiler_params=pltpu.CompilerParams(
            collective_id=3, has_side_effects=True, vmem_limit_bytes=60 * 2**20
        ),
        cost_estimate=lasting(110),
    )(grad, act, dhid, w1, w2)


def finish_kernel(
    parts, groups,
    grad_a, grad_b, res, gx, upg, vec,
    total_a, total_b, res_out, gx_out, upg_out, vec_out,
    loc_a, loc_b, sibr_a, sibr_b, xb_a, xb_b, xrb_a, xrb_b, got_a, got_b, gone_a, gone_b,
    local, ls, ss, sr, ns, nr, rs, rr, as_, ar, bs, br, us, ur, vs, vr,
):
    dp, f = lax.axis_index("dp"), lax.axis_index("fsdp")
    owners, rows_x = groups * parts, groups // 2
    x, core = lax.div(dp, 2), lax.rem(dp, 2)
    sib = x * 2 + 1 - core
    me = dp * parts + f
    p = ring_place(f, parts)
    nxt, prv = ring_index(p + 1, parts), ring_index(p - 1, parts)
    grads, total = (grad_a, grad_b), (total_a, total_b)
    loc, sibr, xb, xrb = (loc_a, loc_b), (sibr_a, sibr_b), (xb_a, xb_b), (xrb_a, xrb_b)
    got, gone = (got_a, got_b), (gone_a, gone_b)
    mine = [
        pltpu.make_async_copy(res.at[f], res_out.at[f], local.at[0]),
        pltpu.make_async_copy(gx.at[f], gx_out.at[f], local.at[1]),
        pltpu.make_async_copy(upg.at[me], upg_out.at[me], local.at[2]),
        pltpu.make_async_copy(vec.at[me], vec_out.at[me], local.at[3]),
    ]
    for copy in mine:
        copy.start()
    greet_all(me, parts, owners)

    def chunk(h, s):
        return ring_index(p - 1 - s if h == 0 else p + 1 + s, parts)

    def sib_copy(h, s):
        piece = grads[h].at[:, 1 - core, chunk(h, s)]
        return remote(piece, sibr[h].at[s], ss.at[h, s], sr.at[h, s], sib, f)

    def own_copy(h, s):
        piece = grads[h].at[:, core, chunk(h, s)]
        return pltpu.make_async_copy(piece, loc[h].at[s], ls.at[h, s])

    def x_copy(h, s, dx):
        to = wrap(x + dx, rows_x) * 2 + core
        return remote(
            xb[h].at[s, dx - 1], xrb[h].at[s, dx - 1], ns.at[h, s, dx], nr.at[h, s, dx], to, f
        )

    def ring_copy(h, s):
        return remote(
            gone[h].at[s], got[h].at[s], rs.at[h, s], rr.at[h, s], dp, nxt if h == 0 else prv
        )

    def res_copies(d, came=False):
        return deal_copy(parts, dp, f, res, res_out, as_, ar, d, came)

    def gx_copies(d, came=False):
        return deal_copy(parts, dp, f, gx, gx_out, bs, br, d, came)

    def upg_copies(d, came=False):
        return owner_copy(me, parts, owners, upg, upg_out, us, ur, d, came)

    def vec_copies(d, came=False):
        return owner_copy(me, parts, owners, vec, vec_out, vs, vr, d, came)

    def begin(s):
        for h in range(2):
            sib_copy(h, s).start()
            own_copy(h, s).start()

    def others(d):
        upg_copies(d).start()
        vec_copies(d).start()

    def returns(d):
        res_copies(d).start()
        gx_copies(d).start()

    def pair(s):
        for h in range(2):
            sib_copy(h, s).wait_recv()
            own_copy(h, s).wait()
            for dx in range(1, rows_x):
                to = wrap(x + dx, rows_x)
                xb[h][s, dx - 1] = (sibr[h][s, to].astype(F32) + loc[h][s, to].astype(F32)).astype(BF)
                x_copy(h, s, dx).start()

    def step(s):
        for h in range(2):
            for dx in range(1, rows_x):
                x_copy(h, s, dx).wait_recv()

            def value():
                here = sibr[h][s, x].astype(F32) + loc[h][s, x].astype(F32)
                for dx in range(1, rows_x):
                    here = here + xrb[h][s, dx - 1].astype(F32)
                return here

            @pl.when(s == 0)
            def _():
                gone[h][s] = value().astype(BF)
                ring_copy(h, s).start()

            @pl.when((s > 0) & (s < parts - 1))
            def _():
                ring_copy(h, s - 1).wait_recv()
                gone[h][s] = (value() + got[h][s - 1].astype(F32)).astype(BF)
                ring_copy(h, s).start()

            @pl.when(s == parts - 1)
            def _():
                ring_copy(h, s - 1).wait_recv()
                total[h][...] = value() + got[h][s - 1].astype(F32)

    loop(0, parts, begin)
    loop(1, parts, returns)
    loop(1, owners, others)
    loop(0, parts, pair)
    loop(0, parts, step)

    def finish(s):
        for h in range(2):
            sib_copy(h, s).wait_send()
            for dx in range(1, rows_x):
                x_copy(h, s, dx).wait_send()

            @pl.when(s < parts - 1)
            def _():
                ring_copy(h, s).wait_send()

        @pl.when(s > 0)
        def _():
            for copies in (res_copies, gx_copies):
                copies(s, True).wait_recv()
                copies(s).wait_send()

    loop(0, parts, finish)

    def owner_finish(d):
        for copies in (upg_copies, vec_copies):
            copies(d, True).wait_recv()
            copies(d).wait_send()

    loop(1, owners, owner_finish)
    for copy in mine:
        copy.wait()


def finish_sums(parts, groups, grad_a, grad_b, res, gx, upg, vec):
    owners, rows_x = groups * parts, groups // 2
    rows = grad_a.shape[3]
    widths = (grad_a.shape[4], grad_b.shape[4])
    dma = pltpu.SemaphoreType.DMA
    hbm = pl.BlockSpec(memory_space=pl.ANY)
    return pl.pallas_call(
        functools.partial(finish_kernel, parts, groups),
        out_shape=(
            jax.ShapeDtypeStruct((rows, widths[0]), F32),
            jax.ShapeDtypeStruct((rows, widths[1]), F32),
            jax.ShapeDtypeStruct(res.shape, BF),
            jax.ShapeDtypeStruct(gx.shape, BF),
            jax.ShapeDtypeStruct(upg.shape, BF),
            jax.ShapeDtypeStruct(vec.shape, F32),
        ),
        in_specs=[hbm] * 6,
        out_specs=(pl.BlockSpec(memory_space=pltpu.VMEM),) * 2 + (hbm,) * 4,
        scratch_shapes=[
            *(
                pltpu.VMEM(lead + (rows, width), BF)
                for lead in (
                    (parts, rows_x), (parts, rows_x), (parts, rows_x - 1), (parts, rows_x - 1),
                    (parts,), (parts,),
                )
                for width in widths
            ),
            dma((4,)),
            dma((2, parts)), dma((2, parts)), dma((2, parts)),
            dma((2, parts, rows_x)), dma((2, parts, rows_x)),
            dma((2, parts)), dma((2, parts)),
            dma((parts,)), dma((parts,)), dma((parts,)), dma((parts,)),
            dma((owners,)), dma((owners,)), dma((owners,)), dma((owners,)),
        ],
        compiler_params=pltpu.CompilerParams(
            collective_id=4, has_side_effects=True, vmem_limit_bytes=60 * 2**20
        ),
        cost_estimate=lasting(1),
    )(grad_a, grad_b, res, gx, upg, vec)


def shards(
    tokens,
    cotangent,
    lengths,
    routing,
    in_weight,
    in_first,
    in_second,
    out_weight,
    out_first,
    out_second,
    up_weight,
    up_first,
    up_second,
    down_weight,
    down_first,
    down_second,
    vectors,
    vector_first,
    vector_second,
):
    bf = jnp.bfloat16
    heads = D // HD
    count = tokens.shape[0]
    parts = lax.axis_size("fsdp")
    groups = lax.axis_size("dp")
    both = ("dp", "fsdp")
    piece = count // parts
    width_in = D + 2 * HD
    slots = jnp.arange(parts, dtype=jnp.int32)
    order = routing[0]
    inverse = jnp.sum(jnp.where(order[:, None] == slots[None, :], slots[:, None], 0), axis=0)

    def deal(array):
        return jnp.take(array.reshape(parts, piece, D), inverse, axis=0)

    def undeal(array):
        return jnp.take(array, order, axis=0).reshape(count, D)

    rows = in_weight.shape[0]
    owners = groups * parts
    out_vec = jnp.concatenate(
        [out_weight.astype(bf), jnp.pad(vectors.astype(bf), ((0, 0), (0, 128 - NVEC)))], axis=1
    )
    up_pieces = up_weight.astype(bf).reshape(rows, owners, FF // owners).transpose(1, 0, 2)
    up_block, dealt, dealt_grad, out_vec = lax.optimization_barrier(
        (exchange(parts, groups, up_pieces), deal(tokens), deal(cotangent), out_vec)
    )
    x_dealt, grad_dealt, whole_in, whole_out = spread(
        parts, groups, dealt, dealt_grad, in_weight.astype(bf), out_vec
    )
    inputs_here = x_dealt.reshape(count, D)
    grad_all = grad_dealt.reshape(groups * count, D)
    grad_here = lax.dynamic_index_in_dim(
        grad_dealt, lax.axis_index("dp"), 0, keepdims=False
    ).reshape(count, D)
    whole_in = whole_in.reshape(D, width_in)
    whole_out = whole_out.reshape(D, D + 128)
    part_down = lax.all_gather(down_weight.astype(bf), "fsdp", axis=0, tiled=True)
    part_up = lax.all_gather(up_block.reshape(D, FF // owners).T, "fsdp", axis=0, tiled=True)

    table = whole_out[:, D : D + NVEC].astype(jnp.float32)
    whole_out = whole_out[:, :D]
    gain_one = table[:, 0]
    shift_one = table[:, 1]
    query_bias = table[:, 2]
    branch_bias = table[:, 3]
    gain_two = table[:, 4]
    shift_two = table[:, 5]
    output_bias = table[:, 6]
    hidden_bias = table[:, 7:].T.reshape(FF)
    ff_here = FF // groups
    ff_start = lax.axis_index("dp") * ff_here
    hidden_bias_here = lax.dynamic_slice(hidden_bias, (ff_start,), (ff_here,))
    allowed = segment_mask(lengths[0], count)
    scale = 1.0 / math.sqrt(HD)
    inputs = inputs_here.astype(jnp.float32)
    norm_one_b = layer_norm(inputs, gain_one, shift_one).astype(bf)
    mixed = jnp.dot(norm_one_b, whole_in, preferred_element_type=jnp.float32)
    query_b = (mixed[:, :D] + query_bias).astype(bf)
    keys_b = mixed[:, D : D + HD].astype(bf)
    values_b = mixed[:, D + HD :].astype(bf)
    query_heads = query_b.reshape(count, heads, HD)

    def score_table():
        raw = (
            jnp.einsum("thd,sd->hts", query_heads, keys_b, preferred_element_type=jnp.float32)
            * scale
        )
        return jnp.where(allowed[None], raw, -1e30)

    scores = score_table()
    top = jnp.max(scores, axis=-1, keepdims=True)
    expo = jnp.exp(scores - top)
    total = jnp.sum(expo, axis=-1, keepdims=True)
    logsum = top + jnp.log(total)
    probs_b = (expo / total).astype(bf)
    attended_b = (
        jnp.einsum("hts,sd->thd", probs_b, values_b, preferred_element_type=jnp.float32)
        .reshape(count, D)
        .astype(bf)
    )
    middle = inputs + (
        jnp.dot(attended_b, whole_out, preferred_element_type=jnp.float32) + branch_bias
    )
    norm_two_b = layer_norm(middle, gain_two, shift_two).astype(bf)

    fused = parts == 8 and groups == 4
    if fused:
        norm_all = group_gather(groups, norm_two_b).reshape(groups * count, D)
    else:
        norm_all = lax.all_gather(norm_two_b, "dp", axis=0, tiled=True)
    hidden = contract_cols(norm_all, part_up) + hidden_bias_here
    grad_active = contract_cols(grad_all, part_down)
    gelu_value, gelu_pull = jax.vjp(gelu_tanh, hidden)
    active_b = gelu_value.astype(bf)
    grad_hidden_b = gelu_pull(grad_active)[0].astype(bf)
    down_parts = contract_rows(active_b, grad_all).astype(bf)
    up_parts = contract_rows(grad_hidden_b, norm_all).astype(bf)
    down_parts, up_parts = lax.optimization_barrier((down_parts, up_parts))
    if fused:
        up_grad_block, grad_norm_two, branch_two = ffn_back(
            parts, groups, up_parts, active_b, grad_hidden_b, part_up, part_down
        )
    else:
        up_grad_block = lax.psum_scatter(up_parts, "fsdp", scatter_dimension=0, tiled=True)
        grad_norm_two = lax.psum_scatter(
            jnp.dot(grad_hidden_b, part_up, preferred_element_type=jnp.float32).astype(bf),
            "dp", scatter_dimension=0, tiled=True,
        ).astype(jnp.float32)
        branch_two = lax.psum_scatter(
            jnp.dot(active_b, part_down, preferred_element_type=jnp.float32).astype(bf),
            "dp", scatter_dimension=0, tiled=True,
        ).astype(jnp.float32)
    down_parts, up_grad_block = lax.optimization_barrier((down_parts, up_grad_block))
    down_grad = lax.psum_scatter(down_parts, "fsdp", scatter_dimension=0, tiled=True)
    result = middle + (branch_two + output_bias)

    grad_y = grad_here.astype(jnp.float32)
    norm_value_two, pull_two = jax.vjp(layer_norm, middle, gain_two, shift_two)
    grad_middle_norm, grad_gain_two, grad_shift_two = pull_two(grad_norm_two)
    grad_middle = grad_y + grad_middle_norm
    grad_branch_b = grad_middle.astype(bf)
    grad_attended_b = contract_cols(grad_branch_b, whole_out).astype(bf)
    grad_heads = grad_attended_b.reshape(count, heads, HD)
    probs = jnp.exp(score_table() - logsum)
    probs_again_b = probs.astype(bf)
    grad_probs = jnp.einsum("thd,sd->hts", grad_heads, values_b, preferred_element_type=jnp.float32)
    grad_values_b = jnp.einsum(
        "hts,thd->sd", probs_again_b, grad_heads, preferred_element_type=jnp.float32
    ).astype(bf)
    weighted = jnp.sum(probs * grad_probs, axis=-1, keepdims=True)
    grad_scores_b = (probs * (grad_probs - weighted)).astype(bf)
    grad_query_b = (
        (
            jnp.einsum("hts,sd->thd", grad_scores_b, keys_b, preferred_element_type=jnp.float32)
            * scale
        )
        .reshape(count, D)
        .astype(bf)
    )
    grad_keys_b = (
        jnp.einsum("hts,thd->sd", grad_scores_b, query_heads, preferred_element_type=jnp.float32)
        * scale
    ).astype(bf)
    grad_mixed_b = jnp.concatenate([grad_query_b, grad_keys_b, grad_values_b], axis=1)
    grad_norm_one = contract_cols(grad_mixed_b, whole_in)
    norm_value_one, pull_one = jax.vjp(layer_norm, inputs, gain_one, shift_one)
    grad_inputs_norm, grad_gain_one, grad_shift_one = pull_one(grad_norm_one)
    grad_inputs = grad_middle + grad_inputs_norm
    hidden_sums = jnp.sum(grad_hidden_b.astype(jnp.float32), axis=0)
    hidden_whole = lax.dynamic_update_slice(
        jnp.zeros((FF,), jnp.float32), hidden_sums, (ff_start,)
    )
    vector_grad = jnp.concatenate(
        [
            jnp.stack(
                [
                    grad_gain_one,
                    grad_shift_one,
                    jnp.sum(grad_query_b.astype(jnp.float32), axis=0),
                    jnp.sum(grad_branch_b.astype(jnp.float32), axis=0),
                    grad_gain_two,
                    grad_shift_two,
                    jnp.sum(grad_y, axis=0),
                ],
                axis=0,
            ),
            hidden_whole.reshape(FF // D, D),
        ],
        axis=0,
    )
    vector_grad = vector_grad.reshape(NVEC, owners, rows).transpose(1, 0, 2)
    vector_grad = jnp.pad(vector_grad, ((0, 0), (0, 16 - NVEC), (0, 128 - rows)))
    grad_in, grad_out, back_result, back_grad, grad_up, vector_sum = finish_sums(
        parts,
        groups,
        contract_rows(norm_one_b, grad_mixed_b)
        .astype(bf)
        .reshape(groups // 2, 2, parts, rows, width_in),
        contract_rows(attended_b, grad_branch_b).astype(bf).reshape(groups // 2, 2, parts, rows, D),
        result.astype(bf).reshape(parts, piece, D),
        grad_inputs.astype(bf).reshape(parts, piece, D),
        up_grad_block.T.astype(bf).reshape(owners, rows, FF // owners),
        vector_grad,
    )
    grad_up = grad_up.transpose(1, 0, 2).reshape(rows, FF)
    vector_sum = jnp.sum(vector_sum, axis=0)
    grad_vec = vector_sum[:NVEC, :rows].T
    in_new = adam_update(in_weight, in_first, in_second, grad_in, 1.0 / math.sqrt(D), decay_rate)
    out_new = adam_update(
        out_weight, out_first, out_second, grad_out, 1.0 / math.sqrt(D * 8 // TOK_DEV), decay_rate
    )
    up_new = adam_update(up_weight, up_first, up_second, grad_up, 1.0 / math.sqrt(D), decay_rate)
    down_new = adam_update(
        down_weight, down_first, down_second, down_grad, 1.0 / math.sqrt(FF), decay_rate
    )
    vec_new = adam_update(vectors, vector_first, vector_second, grad_vec, 0.1, 0.0)
    return (undeal(back_result), undeal(back_grad)) + in_new + out_new + up_new + down_new + vec_new


def solution(mesh):
    spec = P(("dp", "fsdp"), None)
    return jax.shard_map(
        shards,
        mesh=mesh,
        in_specs=(spec,) * 19,
        out_specs=(spec,) * 17,
        check_vma=False,
    )
```

```python
import functools
import math

import jax
import jax.numpy as jnp
from jax import lax
from jax.experimental import pallas as pl
from jax.experimental.pallas import tpu as pltpu
from jax.sharding import PartitionSpec as P

D = 2048
FF = 8192
HD = 128
TOK_DEV = 384
STEP = 5
NVEC = 11


eps_norm = 1e-05
beta_one = 0.5
beta_two = 0.5
adam_eps = 1e-08
decay_rate = 0.1


def layer_norm(values, gain, shift):
    centered = values - jnp.mean(values, axis=-1, keepdims=True)
    scaled = centered * lax.rsqrt(jnp.mean(centered * centered, axis=-1, keepdims=True) + eps_norm)
    return scaled * gain + shift


def gelu_tanh(values):
    return (
        0.5
        * values
        * (1.0 + jnp.tanh(0.7978845608028654 * (values + 0.044715 * values * values * values)))
    )


def segment_mask(sizes, count):
    ends = jnp.cumsum(sizes)
    places = jnp.arange(count, dtype=jnp.int32)
    labels = jnp.sum((places[:, None] >= ends[None, :]).astype(jnp.int32), axis=1)
    return (labels[:, None] == labels[None, :]) & (places[None, :] <= places[:, None])


def adam_update(weight, first, second, grad, rate, decay):
    grad = grad.astype(jnp.float32)
    first_new = beta_one * first + (1.0 - beta_one) * grad
    second_new = beta_two * second + (1.0 - beta_two) * grad * grad
    fix_one = 1.0 - beta_one**STEP
    fix_two = 1.0 - beta_two**STEP
    step_size = first_new / fix_one / (jnp.sqrt(second_new / fix_two) + adam_eps)
    weight_new = weight - rate * (step_size + decay * weight)
    return (weight_new, first_new, second_new)


def contract_rows(left, right):
    return lax.dot_general(
        left, right, (((0,), (0,)), ((), ())), preferred_element_type=jnp.float32
    )


def contract_cols(left, right):
    return lax.dot_general(
        left, right, (((1,), (1,)), ((), ())), preferred_element_type=jnp.float32
    )


MESH = pl.DeviceIdType.MESH
F32 = jnp.float32
BF = jnp.bfloat16


def wrap(value, count):
    return lax.rem(value + 2 * count, count)


def ring_place(index, parts):
    if parts != 8:
        return index
    z, y = lax.div(index, 2), lax.rem(index, 2)
    return z + y * (7 - 2 * z)


def ring_index(place, parts):
    place = wrap(place, parts)
    if parts != 8:
        return place
    back = lax.div(place, 4)
    return (1 - back) * 2 * place + back * (15 - 2 * place)


def remote(src, dst, send, recv, dp, fs):
    return pltpu.make_async_remote_copy(
        src_ref=src, dst_ref=dst, send_sem=send, recv_sem=recv, device_id=(dp, fs), device_id_type=MESH
    )


def lasting(micros):
    return pl.CostEstimate(
        flops=int(micros * 1.1e9), bytes_accessed=int(micros * 3.3e6), transcendentals=0
    )


def greet(targets):
    barrier = pltpu.get_barrier_semaphore()
    for dp, fs in targets:
        pl.semaphore_signal(barrier, inc=1, device_id=(dp, fs), device_id_type=MESH)
    pl.semaphore_wait(barrier, len(targets))


def greet_all(me, parts, owners):
    barrier = pltpu.get_barrier_semaphore()

    def one(i, carry):
        peer = wrap(me + i, owners)
        pl.semaphore_signal(
            barrier, inc=1, device_id=(lax.div(peer, parts), lax.rem(peer, parts)), device_id_type=MESH
        )
        return carry

    lax.fori_loop(1, owners, one, 0)
    pl.semaphore_wait(barrier, owners - 1)


def loop(low, high, body):
    def one(i, carry):
        body(i)
        return carry

    lax.fori_loop(low, high, one, 0)


def deal_copy(parts, dp, f, src, dst, send, recv, d, came=False):
    to = wrap(f + d, parts)
    place = wrap(f - d, parts) if came else f
    return remote(src.at[to], dst.at[place], send.at[d], recv.at[d], dp, to)


def owner_copy(me, parts, owners, src, dst, send, recv, d, came=False):
    to = wrap(me + d, owners)
    place = wrap(me - d, owners) if came else me
    return remote(
        src.at[to], dst.at[place], send.at[d], recv.at[d], lax.div(to, parts), lax.rem(to, parts)
    )


def spread_kernel(
    parts, groups,
    xd, gd, inb, ovb,
    xo, eall, win, wov,
    local, xs, xr, gs, gr, rs, rr, ns, nr, ss, sr, ens, enr, ess, esr,
):
    dp, f = lax.axis_index("dp"), lax.axis_index("fsdp")
    owners, rows_x = groups * parts, groups // 2
    x, core = lax.div(dp, 2), lax.rem(dp, 2)
    sib = x * 2 + 1 - core
    me = dp * parts + f
    p = ring_place(f, parts)
    nxt, prv = ring_index(p + 1, parts), ring_index(p - 1, parts)
    whole = (win, wov)
    mine = [
        pltpu.make_async_copy(inb, win.at[me], local.at[0]),
        pltpu.make_async_copy(ovb, wov.at[me], local.at[1]),
        pltpu.make_async_copy(xd.at[f], xo.at[f], local.at[2]),
        pltpu.make_async_copy(gd.at[f], eall.at[dp, f], local.at[3]),
    ]
    for copy in mine:
        copy.start()
    greet(
        [(dp, wrap(f + d, parts)) for d in range(1, parts)]
        + [(sib, f)]
        + [(wrap(x + dx, rows_x) * 2 + core, f) for dx in range(1, rows_x)]
    )
    for copy in mine:
        copy.wait()

    def x_copies(d, came=False):
        return deal_copy(parts, dp, f, xd, xo, xs, xr, d, came)

    def g_copies(d, came=False):
        return deal_copy(parts, dp, f, gd, eall.at[dp], gs, gr, d, came)

    def origin(h, s):
        return ring_index(p - s if h == 0 else p + s, parts)

    def ring_send(h, s):
        ref = whole[h].at[dp * parts + origin(h, s)]
        return remote(ref, ref, rs.at[h, s], rr.at[h, s], dp, nxt if h == 0 else prv)

    def ring_recv(h, s):
        ref = whole[h].at[dp * parts + origin(h, s)]
        return remote(ref, ref, rs.at[h, s - 1], rr.at[h, s - 1], dp, nxt if h == 0 else prv)

    def x_send(h, s, dx):
        ref = whole[h].at[dp * parts + origin(h, s)]
        to = wrap(x + dx, rows_x) * 2 + core
        return remote(ref, ref, ns.at[h, s, dx], nr.at[h, s, dx], to, f)

    def x_recv(h, s, dx):
        came = wrap(x - dx, rows_x) * 2 + core
        ref = whole[h].at[came * parts + origin(h, s)]
        return remote(ref, ref, ns.at[h, s, dx], nr.at[h, s, dx], came, f)

    def sib_send(h, s, dx):
        came = wrap(x - dx, rows_x) * 2 + core
        ref = whole[h].at[came * parts + origin(h, s)]
        return remote(ref, ref, ss.at[h, s, dx], sr.at[h, s, dx], sib, f)

    def sib_recv(h, s, dx):
        came = wrap(x - dx, rows_x) * 2 + 1 - core
        ref = whole[h].at[came * parts + origin(h, s)]
        return remote(ref, ref, ss.at[h, s, dx], sr.at[h, s, dx], sib, f)

    def e_x_send(d, dx):
        ref = eall.at[dp, wrap(f - d, parts)]
        to = wrap(x + dx, rows_x) * 2 + core
        return remote(ref, ref, ens.at[d, dx], enr.at[d, dx], to, f)

    def e_x_recv(d, dx):
        came = wrap(x - dx, rows_x) * 2 + core
        ref = eall.at[came, wrap(f - d, parts)]
        return remote(ref, ref, ens.at[d, dx], enr.at[d, dx], came, f)

    def e_sib_send(d, dx):
        came = wrap(x - dx, rows_x) * 2 + core
        ref = eall.at[came, wrap(f - d, parts)]
        return remote(ref, ref, ess.at[d, dx], esr.at[d, dx], sib, f)

    def e_sib_recv(d, dx):
        came = wrap(x - dx, rows_x) * 2 + 1 - core
        ref = eall.at[came, wrap(f - d, parts)]
        return remote(ref, ref, ess.at[d, dx], esr.at[d, dx], sib, f)

    def ring_step(s):
        for h in range(2):
            @pl.when(s > 0)
            def _():
                ring_recv(h, s).wait_recv()

            @pl.when(s < parts - 1)
            def _():
                ring_send(h, s).start()

            for dx in range(1, rows_x):
                x_send(h, s, dx).start()
            sib_send(h, s, 0).start()

    def e_step(d):
        @pl.when(d > 0)
        def _():
            g_copies(d, True).wait_recv()

        for dx in range(1, rows_x):
            e_x_send(d, dx).start()
        e_sib_send(d, 0).start()

    def relay(s):
        for h in range(2):
            for dx in range(1, rows_x):
                x_recv(h, s, dx).wait_recv()
                sib_send(h, s, dx).start()

    def e_relay(d):
        for dx in range(1, rows_x):
            e_x_recv(d, dx).wait_recv()
            e_sib_send(d, dx).start()

    def main(s):
        @pl.when(s < parts)
        def _():
            ring_step(s)

        @pl.when(s < parts - 1)
        def _():
            x_copies(s + 1).start()
            g_copies(s + 1).start()

        @pl.when((s >= 1) & (s <= parts))
        def _():
            e_step(s - 1)

        @pl.when((s >= 2) & (s < parts + 2))
        def _():
            relay(s - 2)

        @pl.when(s >= 3)
        def _():
            e_relay(s - 3)

    loop(0, parts + 3, main)

    def finish(s):
        for h in range(2):
            @pl.when(s < parts - 1)
            def _():
                ring_send(h, s).wait_send()

            for dx in range(1, rows_x):
                x_send(h, s, dx).wait_send()
            for dx in range(rows_x):
                sib_recv(h, s, dx).wait_recv()
                sib_send(h, s, dx).wait_send()
        for dx in range(1, rows_x):
            e_x_send(s, dx).wait_send()
        for dx in range(rows_x):
            e_sib_recv(s, dx).wait_recv()
            e_sib_send(s, dx).wait_send()

        @pl.when(s > 0)
        def _():
            x_copies(s, True).wait_recv()
            x_copies(s).wait_send()
            g_copies(s).wait_send()

    loop(0, parts, finish)


def exchange_kernel(parts, groups, src, dst, local, us, ur):
    dp, f = lax.axis_index("dp"), lax.axis_index("fsdp")
    owners = groups * parts
    me = dp * parts + f
    mine = pltpu.make_async_copy(src.at[me], dst.at[me], local)
    mine.start()
    greet_all(me, parts, owners)
    loop(1, owners, lambda d: owner_copy(me, parts, owners, src, dst, us, ur, d).start())
    mine.wait()

    def finish(d):
        owner_copy(me, parts, owners, src, dst, us, ur, d, True).wait_recv()
        owner_copy(me, parts, owners, src, dst, us, ur, d).wait_send()

    loop(1, owners, finish)


def exchange(parts, groups, src):
    owners = groups * parts
    dma = pltpu.SemaphoreType.DMA
    return pl.pallas_call(
        functools.partial(exchange_kernel, parts, groups),
        out_shape=jax.ShapeDtypeStruct(src.shape, BF),
        in_specs=[pl.BlockSpec(memory_space=pl.ANY)],
        out_specs=pl.BlockSpec(memory_space=pl.ANY),
        scratch_shapes=[dma(()), dma((owners,)), dma((owners,))],
        compiler_params=pltpu.CompilerParams(collective_id=5, has_side_effects=True),
        cost_estimate=lasting(25),
    )(src)


def spread(parts, groups, xd, gd, inb, ovb):
    owners, rows_x = groups * parts, groups // 2
    dma = pltpu.SemaphoreType.DMA
    return pl.pallas_call(
        functools.partial(spread_kernel, parts, groups),
        out_shape=(
            jax.ShapeDtypeStruct(xd.shape, BF),
            jax.ShapeDtypeStruct((groups,) + gd.shape, BF),
            jax.ShapeDtypeStruct((owners,) + inb.shape, BF),
            jax.ShapeDtypeStruct((owners,) + ovb.shape, BF),
        ),
        in_specs=[pl.BlockSpec(memory_space=pl.ANY)] * 4,
        out_specs=(pl.BlockSpec(memory_space=pl.ANY),) * 4,
        scratch_shapes=[
            dma((4,)),
            dma((parts,)), dma((parts,)), dma((parts,)), dma((parts,)),
            dma((2, parts)), dma((2, parts)),
            dma((2, parts, rows_x)), dma((2, parts, rows_x)),
            dma((2, parts, rows_x)), dma((2, parts, rows_x)),
            dma((parts, rows_x)), dma((parts, rows_x)),
            dma((parts, rows_x)), dma((parts, rows_x)),
        ],
        compiler_params=pltpu.CompilerParams(collective_id=0, has_side_effects=True),
        cost_estimate=lasting(200),
    )(xd, gd, inb, ovb)


def group_gather_kernel(groups, chunks, src, out, local, ns, nr, ss, sr):
    dp, f = lax.axis_index("dp"), lax.axis_index("fsdp")
    rows_x = groups // 2
    x, core = lax.div(dp, 2), lax.rem(dp, 2)
    sib = x * 2 + 1 - core
    size = src.shape[0] // chunks
    mine = pltpu.make_async_copy(src, out.at[dp], local)
    mine.start()
    greet([(sib, f)] + [(wrap(x + dx, rows_x) * 2 + core, f) for dx in range(1, rows_x)])

    def part(ref, k):
        return ref.at[pl.ds(k * size, size)]

    def x_send(k, dx):
        to = wrap(x + dx, rows_x) * 2 + core
        return remote(part(src, k), part(out.at[dp], k), ns.at[k, dx], nr.at[k, dx], to, f)

    def x_recv(k, dx):
        came = wrap(x - dx, rows_x) * 2 + core
        ref = part(out.at[came], k)
        return remote(ref, ref, ns.at[k, dx], nr.at[k, dx], came, f)

    def sib_send(k, dx):
        came = wrap(x - dx, rows_x) * 2 + core
        ref = part(out.at[came], k)
        return remote(part(src, k) if dx == 0 else ref, ref, ss.at[k, dx], sr.at[k, dx], sib, f)

    def sib_recv(k, dx):
        came = wrap(x - dx, rows_x) * 2 + 1 - core
        ref = part(out.at[came], k)
        return remote(ref, ref, ss.at[k, dx], sr.at[k, dx], sib, f)

    for k in range(chunks):
        for dx in range(1, rows_x):
            x_send(k, dx).start()
    for k in range(chunks):
        sib_send(k, 0).start()
    for k in range(chunks):
        for dx in range(1, rows_x):
            x_recv(k, dx).wait_recv()
            sib_send(k, dx).start()
    mine.wait()
    for k in range(chunks):
        for dx in range(rows_x):
            sib_recv(k, dx).wait_recv()
            sib_send(k, dx).wait_send()
        for dx in range(1, rows_x):
            x_send(k, dx).wait_send()


def group_gather(groups, src):
    chunks, rows_x = 4, groups // 2
    dma = pltpu.SemaphoreType.DMA
    return pl.pallas_call(
        functools.partial(group_gather_kernel, groups, chunks),
        out_shape=jax.ShapeDtypeStruct((groups,) + src.shape, BF),
        in_specs=[pl.BlockSpec(memory_space=pl.ANY)],
        out_specs=pl.BlockSpec(memory_space=pl.ANY),
        scratch_shapes=[dma(())] + [dma((chunks, rows_x))] * 4,
        compiler_params=pltpu.CompilerParams(collective_id=1, has_side_effects=True),
        cost_estimate=lasting(45),
    )(src)


def ffn_back_kernel(
    parts, groups, chunks, streams,
    grad, act, dhid, w1, w2, base,
    out, dsum, back,
    ysum, leaving, loc, got, gone, wv, some, psib, sibr, xb, xrb,
    ll, ol, rs, rr, wl, sl, gss, gsr, gns, gnr, bs, br, bl,
):
    dp, f = lax.axis_index("dp"), lax.axis_index("fsdp")
    rows_x = groups // 2
    x, core = lax.div(dp, 2), lax.rem(dp, 2)
    sib = x * 2 + 1 - core
    p = ring_place(f, parts)
    nxt, prv = ring_index(p + 1, parts), ring_index(p - 1, parts)
    block, width = out.shape
    part, cut = width // streams, width // chunks
    count = dsum.shape[0]
    far = range(1, rows_x)

    def local_copy(h, s):
        c = ring_index(p - 1 - s if h % 2 == 0 else p + 1 + s, parts)
        return pltpu.make_async_copy(
            grad.at[
                pl.ds(pl.multiple_of(c * block, block), block), pl.ds(h * part, part)
            ],
            loc.at[lax.rem(s, 2), h], ll.at[lax.rem(s, 2), h],
        )

    w_loads = (
        pltpu.make_async_copy(w2, wv, wl.at[0]),
        pltpu.make_async_copy(w1, wv, wl.at[1]),
    )
    for s in range(2):
        for h in range(streams):
            local_copy(h, s).start()
    w_loads[0].start()
    greet(
        [(dp, wrap(f + d, parts)) for d in range(1, parts)]
        + [(sib, f)]
        + [(wrap(x + dx, rows_x) * 2 + core, f) for dx in range(1, rows_x)]
    )

    def ring_copy(h, s):
        return remote(
            gone.at[lax.rem(s, 2), h], got.at[h, s], rs.at[h, s], rr.at[h, s],
            dp, nxt if h % 2 == 0 else prv,
        )

    def out_copy(h):
        return pltpu.make_async_copy(
            gone.at[lax.rem(parts - 1, 2), h],
            out.at[:, pl.ds(h * part, part)],
            ol.at[h],
        )

    def pass_on(s):
        slot = lax.rem(s, 2)
        for h in range(streams):
            local_copy(h, s).wait()

            @pl.when(s >= 2)
            def _():
                ring_copy(h, s - 2).wait_send()

            @pl.when(s == 0)
            def _():
                gone[slot, h] = loc[slot, h]

            @pl.when(s > 0)
            def _():
                ring_copy(h, s - 1).wait_recv()
                gone[slot, h] = (
                    loc[slot, h].astype(F32) + got[h, s - 1].astype(F32)
                ).astype(BF)

            @pl.when(s < parts - 1)
            def _():
                ring_copy(h, s).start()

            @pl.when(s == parts - 1)
            def _():
                out_copy(h).start()

            @pl.when(s < parts - 2)
            def _():
                local_copy(h, s + 2).start()

    def cols(k):
        return pl.ds(pl.multiple_of(k * cut, cut), cut)

    def rows_of(dx, c):
        group = wrap(x + dx, rows_x) * 2 + (core if c == 0 else 1 - core)
        return pl.ds(pl.multiple_of(group * count, count), count)

    rows_in, totals = (act, dhid), (ysum, dsum)

    def sum_sib(which, k):
        return remote(
            psib.at[:, :, cols(k)], sibr.at[which, :, :, cols(k)],
            gss.at[which, k], gsr.at[which, k], sib, f,
        )

    def sum_x(which, dx, k):
        to = wrap(x + dx, rows_x) * 2 + core
        return remote(
            xb.at[dx - 1, :, cols(k)], xrb.at[which, dx - 1, :, cols(k)],
            gns.at[which, dx, k], gnr.at[which, dx, k], to, f,
        )

    def take_rows(which, c):
        copies = [
            pltpu.make_async_copy(
                rows_in[which].at[rows_of(dx, c)], some.at[pl.ds(dx * count, count)], sl.at[dx]
            )
            for dx in range(rows_x)
        ]
        for copy in copies:
            copy.start()
        for copy in copies:
            copy.wait()

    def other_side(which):
        take_rows(which, 1)

        def one(k):
            psib[:, :, cols(k)] = (
                jnp.dot(some[...], wv[:, cols(k)], preferred_element_type=F32)
                .astype(BF)
                .reshape(rows_x, count, cut)
            )
            sum_sib(which, k).start()

        loop(0, chunks, one)

    def own_side(which):
        take_rows(which, 0)

        def one(k):
            here = jnp.dot(some[...], wv[:, cols(k)], preferred_element_type=F32)
            sum_sib(which, k).wait_recv()
            here = here.reshape(rows_x, count, cut) + sibr[which, :, :, cols(k)].astype(F32)
            for dx in far:
                xb[dx - 1, :, cols(k)] = here[dx].astype(BF)
                sum_x(which, dx, k).start()
            totals[which][:, cols(k)] = here[0]

        loop(0, chunks, one)

    def collect(which):
        def one(k):
            for dx in far:
                sum_x(which, dx, k).wait_recv()
                totals[which][:, cols(k)] += xrb[which, dx - 1, :, cols(k)].astype(F32)

        loop(0, chunks, one)

    def back_copy(d, came=False):
        return deal_copy(parts, dp, f, leaving, back, bs, br, d, came)

    def own_back():
        return pltpu.make_async_copy(leaving.at[f], back.at[f], bl)

    def send_back():
        piece = count // parts

        def one(j):
            rows = pl.ds(pl.multiple_of(j * piece, piece), piece)
            leaving[j] = (base[rows, :] + ysum[rows, :]).astype(BF)

        loop(0, parts, one)
        own_back().start()
        loop(1, parts, lambda d: back_copy(d).start())

    def sent_sib(which):
        loop(0, chunks, lambda k: sum_sib(which, k).wait_send())

    def sent_x(which):
        for dx in far:
            loop(0, chunks, lambda k: sum_x(which, dx, k).wait_send())

    def step(s):
        pass_on(s)

        @pl.when(s == 0)
        def _():
            w_loads[0].wait()
            other_side(0)

        @pl.when(s == 1)
        def _():
            own_side(0)
            w_loads[1].start()

        @pl.when(s == 2)
        def _():
            w_loads[1].wait()
            sent_sib(0)
            other_side(1)

        @pl.when(s == 3)
        def _():
            collect(0)
            send_back()
            sent_x(0)
            own_side(1)

    loop(0, parts, step)
    collect(1)
    for h in range(streams):
        ring_copy(h, parts - 2).wait_send()
        out_copy(h).wait()
    sent_sib(1)
    sent_x(1)
    own_back().wait()

    def returned(d):
        back_copy(d, True).wait_recv()
        back_copy(d).wait_send()

    loop(1, parts, returned)


def ffn_back(parts, groups, grad, act, dhid, w1, w2, base):
    chunks, streams, rows_x = 4, 4, groups // 2
    units, width = w1.shape
    count = act.shape[0] // groups
    block, part, piece = units // parts, width // streams, count // parts
    dma = pltpu.SemaphoreType.DMA
    hbm = pl.BlockSpec(memory_space=pl.ANY)
    vmem = pl.BlockSpec(memory_space=pltpu.VMEM)
    return pl.pallas_call(
        functools.partial(ffn_back_kernel, parts, groups, chunks, streams),
        out_shape=(
            jax.ShapeDtypeStruct((block, width), BF),
            jax.ShapeDtypeStruct((count, width), F32),
            jax.ShapeDtypeStruct((parts, piece, width), BF),
        ),
        in_specs=[hbm] * 5 + [vmem],
        out_specs=(hbm, vmem, hbm),
        scratch_shapes=[
            pltpu.VMEM((count, width), F32),
            pltpu.VMEM((parts, piece, width), BF),
            pltpu.VMEM((2, streams, block, part), BF),
            pltpu.VMEM((streams, parts - 1, block, part), BF),
            pltpu.VMEM((2, streams, block, part), BF),
            pltpu.VMEM((units, width), BF),
            pltpu.VMEM((rows_x * count, units), BF),
            pltpu.VMEM((rows_x, count, width), BF),
            pltpu.VMEM((2, rows_x, count, width), BF),
            pltpu.VMEM((rows_x - 1, count, width), BF),
            pltpu.VMEM((2, rows_x - 1, count, width), BF),
            dma((2, streams)), dma((streams,)),
            dma((streams, parts)), dma((streams, parts)), dma((2,)), dma((rows_x,)),
            dma((2, chunks)), dma((2, chunks)),
            dma((2, rows_x, chunks)), dma((2, rows_x, chunks)),
            dma((parts,)), dma((parts,)), dma(()),
        ],
        compiler_params=pltpu.CompilerParams(
            collective_id=3, has_side_effects=True, vmem_limit_bytes=60 * 2**20
        ),
        cost_estimate=lasting(130),
    )(grad, act, dhid, w1, w2, base)


def finish_kernel(
    parts, groups,
    grad_a, grad_b, gx, upg, vec,
    total_a, total_b, gx_out, upg_out, vec_out,
    loc_a, loc_b, sibr_a, sibr_b, xb_a, xb_b, xrb_a, xrb_b, got_a, got_b, gone_a, gone_b,
    local, ls, ss, sr, ns, nr, rs, rr, bs, br, us, ur, vs, vr,
):
    dp, f = lax.axis_index("dp"), lax.axis_index("fsdp")
    owners, rows_x = groups * parts, groups // 2
    x, core = lax.div(dp, 2), lax.rem(dp, 2)
    sib = x * 2 + 1 - core
    me = dp * parts + f
    p = ring_place(f, parts)
    nxt, prv = ring_index(p + 1, parts), ring_index(p - 1, parts)
    grads, total = (grad_a, grad_b), (total_a, total_b)
    loc, sibr, xb, xrb = (loc_a, loc_b), (sibr_a, sibr_b), (xb_a, xb_b), (xrb_a, xrb_b)
    got, gone = (got_a, got_b), (gone_a, gone_b)
    mine = [
        pltpu.make_async_copy(gx.at[f], gx_out.at[f], local.at[0]),
        pltpu.make_async_copy(vec.at[me], vec_out.at[me], local.at[1]),
        pltpu.make_async_copy(upg.at[me], upg_out.at[me], local.at[2]),
    ]
    for copy in mine:
        copy.start()
    greet_all(me, parts, owners)

    def chunk(h, s):
        return ring_index(p - 1 - s if h == 0 else p + 1 + s, parts)

    def sib_copy(h, s):
        piece = grads[h].at[:, 1 - core, chunk(h, s)]
        return remote(piece, sibr[h].at[s], ss.at[h, s], sr.at[h, s], sib, f)

    def own_copy(h, s):
        piece = grads[h].at[:, core, chunk(h, s)]
        return pltpu.make_async_copy(piece, loc[h].at[s], ls.at[h, s])

    def x_copy(h, s, dx):
        to = wrap(x + dx, rows_x) * 2 + core
        return remote(
            xb[h].at[s, dx - 1], xrb[h].at[s, dx - 1], ns.at[h, s, dx], nr.at[h, s, dx], to, f
        )

    def ring_copy(h, s):
        return remote(
            gone[h].at[s], got[h].at[s], rs.at[h, s], rr.at[h, s], dp, nxt if h == 0 else prv
        )

    def gx_copies(d, came=False):
        return deal_copy(parts, dp, f, gx, gx_out, bs, br, d, came)

    def upg_copies(d, came=False):
        return owner_copy(me, parts, owners, upg, upg_out, us, ur, d, came)

    def vec_copies(d, came=False):
        return owner_copy(me, parts, owners, vec, vec_out, vs, vr, d, came)

    def begin(s):
        for h in range(2):
            sib_copy(h, s).start()
            own_copy(h, s).start()

    def others(d):
        upg_copies(d).start()
        vec_copies(d).start()

    def returns(d):
        gx_copies(d).start()

    def pair(s):
        for h in range(2):
            sib_copy(h, s).wait_recv()
            own_copy(h, s).wait()
            for dx in range(1, rows_x):
                to = wrap(x + dx, rows_x)
                xb[h][s, dx - 1] = (sibr[h][s, to].astype(F32) + loc[h][s, to].astype(F32)).astype(BF)
                x_copy(h, s, dx).start()

    def step(s):
        for h in range(2):
            for dx in range(1, rows_x):
                x_copy(h, s, dx).wait_recv()

            def value():
                here = sibr[h][s, x].astype(F32) + loc[h][s, x].astype(F32)
                for dx in range(1, rows_x):
                    here = here + xrb[h][s, dx - 1].astype(F32)
                return here

            @pl.when(s == 0)
            def _():
                gone[h][s] = value().astype(BF)
                ring_copy(h, s).start()

            @pl.when((s > 0) & (s < parts - 1))
            def _():
                ring_copy(h, s - 1).wait_recv()
                gone[h][s] = (value() + got[h][s - 1].astype(F32)).astype(BF)
                ring_copy(h, s).start()

            @pl.when(s == parts - 1)
            def _():
                ring_copy(h, s - 1).wait_recv()
                total[h][...] = value() + got[h][s - 1].astype(F32)

    loop(0, parts, begin)
    loop(1, parts, returns)
    loop(1, owners, others)
    loop(0, parts, pair)
    loop(0, parts, step)

    def finish(s):
        for h in range(2):
            sib_copy(h, s).wait_send()
            for dx in range(1, rows_x):
                x_copy(h, s, dx).wait_send()

            @pl.when(s < parts - 1)
            def _():
                ring_copy(h, s).wait_send()

        @pl.when(s > 0)
        def _():
            gx_copies(s, True).wait_recv()
            gx_copies(s).wait_send()

    loop(0, parts, finish)

    def owner_finish(d):
        for copies in (upg_copies, vec_copies):
            copies(d, True).wait_recv()
            copies(d).wait_send()

    loop(1, owners, owner_finish)
    for copy in mine:
        copy.wait()


def finish_sums(parts, groups, grad_a, grad_b, gx, upg, vec):
    owners, rows_x = groups * parts, groups // 2
    rows = grad_a.shape[3]
    widths = (grad_a.shape[4], grad_b.shape[4])
    dma = pltpu.SemaphoreType.DMA
    hbm = pl.BlockSpec(memory_space=pl.ANY)
    return pl.pallas_call(
        functools.partial(finish_kernel, parts, groups),
        out_shape=(
            jax.ShapeDtypeStruct((rows, widths[0]), F32),
            jax.ShapeDtypeStruct((rows, widths[1]), F32),
            jax.ShapeDtypeStruct(gx.shape, BF),
            jax.ShapeDtypeStruct(upg.shape, BF),
            jax.ShapeDtypeStruct(vec.shape, F32),
        ),
        in_specs=[hbm] * 5,
        out_specs=(pl.BlockSpec(memory_space=pltpu.VMEM),) * 2 + (hbm,) * 3,
        scratch_shapes=[
            *(
                pltpu.VMEM(lead + (rows, width), BF)
                for lead in (
                    (parts, rows_x), (parts, rows_x), (parts, rows_x - 1), (parts, rows_x - 1),
                    (parts,), (parts,),
                )
                for width in widths
            ),
            dma((3,)),
            dma((2, parts)), dma((2, parts)), dma((2, parts)),
            dma((2, parts, rows_x)), dma((2, parts, rows_x)),
            dma((2, parts)), dma((2, parts)),
            dma((parts,)), dma((parts,)),
            dma((owners,)), dma((owners,)), dma((owners,)), dma((owners,)),
        ],
        compiler_params=pltpu.CompilerParams(
            collective_id=4, has_side_effects=True, vmem_limit_bytes=60 * 2**20
        ),
        cost_estimate=lasting(1),
    )(grad_a, grad_b, gx, upg, vec)


def shards(
    tokens,
    cotangent,
    lengths,
    routing,
    in_weight,
    in_first,
    in_second,
    out_weight,
    out_first,
    out_second,
    up_weight,
    up_first,
    up_second,
    down_weight,
    down_first,
    down_second,
    vectors,
    vector_first,
    vector_second,
):
    bf = jnp.bfloat16
    heads = D // HD
    count = tokens.shape[0]
    parts = lax.axis_size("fsdp")
    groups = lax.axis_size("dp")
    both = ("dp", "fsdp")
    piece = count // parts
    width_in = D + 2 * HD
    slots = jnp.arange(parts, dtype=jnp.int32)
    order = routing[0]
    inverse = jnp.sum(jnp.where(order[:, None] == slots[None, :], slots[:, None], 0), axis=0)

    def deal(array):
        return jnp.take(array.reshape(parts, piece, D), inverse, axis=0)

    def undeal(array):
        return jnp.take(array, order, axis=0).reshape(count, D)

    rows = in_weight.shape[0]
    owners = groups * parts
    out_vec = jnp.concatenate(
        [out_weight.astype(bf), jnp.pad(vectors.astype(bf), ((0, 0), (0, 128 - NVEC)))], axis=1
    )
    up_pieces = up_weight.astype(bf).reshape(rows, owners, FF // owners).transpose(1, 0, 2)
    up_block, dealt, dealt_grad, out_vec = lax.optimization_barrier(
        (exchange(parts, groups, up_pieces), deal(tokens), deal(cotangent), out_vec)
    )
    x_dealt, grad_dealt, whole_in, whole_out = spread(
        parts, groups, dealt, dealt_grad, in_weight.astype(bf), out_vec
    )
    inputs_here = x_dealt.reshape(count, D)
    grad_all = grad_dealt.reshape(groups * count, D)
    grad_here = lax.dynamic_index_in_dim(
        grad_dealt, lax.axis_index("dp"), 0, keepdims=False
    ).reshape(count, D)
    whole_in = whole_in.reshape(D, width_in)
    whole_out = whole_out.reshape(D, D + 128)
    part_down = lax.all_gather(down_weight.astype(bf), "fsdp", axis=0, tiled=True)
    part_up = lax.all_gather(up_block.reshape(D, FF // owners).T, "fsdp", axis=0, tiled=True)

    table = whole_out[:, D : D + NVEC].astype(jnp.float32)
    whole_out = whole_out[:, :D]
    gain_one = table[:, 0]
    shift_one = table[:, 1]
    query_bias = table[:, 2]
    branch_bias = table[:, 3]
    gain_two = table[:, 4]
    shift_two = table[:, 5]
    output_bias = table[:, 6]
    hidden_bias = table[:, 7:].T.reshape(FF)
    ff_here = FF // groups
    ff_start = lax.axis_index("dp") * ff_here
    hidden_bias_here = lax.dynamic_slice(hidden_bias, (ff_start,), (ff_here,))
    allowed = segment_mask(lengths[0], count)
    scale = 1.0 / math.sqrt(HD)
    inputs = inputs_here.astype(jnp.float32)
    norm_one_b = layer_norm(inputs, gain_one, shift_one).astype(bf)
    mixed = jnp.dot(norm_one_b, whole_in, preferred_element_type=jnp.float32)
    query_b = (mixed[:, :D] + query_bias).astype(bf)
    keys_b = mixed[:, D : D + HD].astype(bf)
    values_b = mixed[:, D + HD :].astype(bf)
    query_heads = query_b.reshape(count, heads, HD)

    def score_table():
        raw = (
            jnp.einsum("thd,sd->hts", query_heads, keys_b, preferred_element_type=jnp.float32)
            * scale
        )
        return jnp.where(allowed[None], raw, -1e30)

    scores = score_table()
    top = jnp.max(scores, axis=-1, keepdims=True)
    expo = jnp.exp(scores - top)
    total = jnp.sum(expo, axis=-1, keepdims=True)
    logsum = top + jnp.log(total)
    probs_b = (expo / total).astype(bf)
    attended_b = (
        jnp.einsum("hts,sd->thd", probs_b, values_b, preferred_element_type=jnp.float32)
        .reshape(count, D)
        .astype(bf)
    )
    middle = inputs + (
        jnp.dot(attended_b, whole_out, preferred_element_type=jnp.float32) + branch_bias
    )
    norm_two_b = layer_norm(middle, gain_two, shift_two).astype(bf)

    fused = parts == 8 and groups == 4
    if fused:
        norm_all = group_gather(groups, norm_two_b).reshape(groups * count, D)
    else:
        norm_all = lax.all_gather(norm_two_b, "dp", axis=0, tiled=True)
    hidden = contract_cols(norm_all, part_up) + hidden_bias_here
    grad_active = contract_cols(grad_all, part_down)
    gelu_value, gelu_pull = jax.vjp(gelu_tanh, hidden)
    active_b = gelu_value.astype(bf)
    grad_hidden_b = gelu_pull(grad_active)[0].astype(bf)
    down_parts = contract_rows(active_b, grad_all).astype(bf)
    up_parts = contract_rows(grad_hidden_b, norm_all).astype(bf)
    down_parts, up_parts = lax.optimization_barrier((down_parts, up_parts))
    if fused:
        up_grad_block, grad_norm_two, back_result = ffn_back(
            parts, groups, up_parts, active_b, grad_hidden_b, part_up, part_down,
            middle + output_bias,
        )
    else:
        up_grad_block = lax.psum_scatter(up_parts, "fsdp", scatter_dimension=0, tiled=True)
        grad_norm_two = lax.psum_scatter(
            jnp.dot(grad_hidden_b, part_up, preferred_element_type=jnp.float32).astype(bf),
            "dp", scatter_dimension=0, tiled=True,
        ).astype(jnp.float32)
        branch_two = lax.psum_scatter(
            jnp.dot(active_b, part_down, preferred_element_type=jnp.float32).astype(bf),
            "dp", scatter_dimension=0, tiled=True,
        ).astype(jnp.float32)
        back_result = lax.all_to_all(
            (middle + (branch_two + output_bias)).astype(bf),
            "fsdp", split_axis=0, concat_axis=0, tiled=True,
        ).reshape(parts, piece, D)
    down_parts, up_grad_block = lax.optimization_barrier((down_parts, up_grad_block))
    down_grad = lax.psum_scatter(down_parts, "fsdp", scatter_dimension=0, tiled=True)

    grad_y = grad_here.astype(jnp.float32)
    norm_value_two, pull_two = jax.vjp(layer_norm, middle, gain_two, shift_two)
    grad_middle_norm, grad_gain_two, grad_shift_two = pull_two(grad_norm_two)
    grad_middle = grad_y + grad_middle_norm
    grad_branch_b = grad_middle.astype(bf)
    grad_attended_b = contract_cols(grad_branch_b, whole_out).astype(bf)
    grad_heads = grad_attended_b.reshape(count, heads, HD)
    probs = jnp.exp(score_table() - logsum)
    probs_again_b = probs.astype(bf)
    grad_probs = jnp.einsum("thd,sd->hts", grad_heads, values_b, preferred_element_type=jnp.float32)
    grad_values_b = jnp.einsum(
        "hts,thd->sd", probs_again_b, grad_heads, preferred_element_type=jnp.float32
    ).astype(bf)
    weighted = jnp.sum(probs * grad_probs, axis=-1, keepdims=True)
    grad_scores_b = (probs * (grad_probs - weighted)).astype(bf)
    grad_query_b = (
        (
            jnp.einsum("hts,sd->thd", grad_scores_b, keys_b, preferred_element_type=jnp.float32)
            * scale
        )
        .reshape(count, D)
        .astype(bf)
    )
    grad_keys_b = (
        jnp.einsum("hts,thd->sd", grad_scores_b, query_heads, preferred_element_type=jnp.float32)
        * scale
    ).astype(bf)
    grad_mixed_b = jnp.concatenate([grad_query_b, grad_keys_b, grad_values_b], axis=1)
    grad_norm_one = contract_cols(grad_mixed_b, whole_in)
    norm_value_one, pull_one = jax.vjp(layer_norm, inputs, gain_one, shift_one)
    grad_inputs_norm, grad_gain_one, grad_shift_one = pull_one(grad_norm_one)
    grad_inputs = grad_middle + grad_inputs_norm
    hidden_sums = jnp.sum(grad_hidden_b.astype(jnp.float32), axis=0)
    hidden_whole = lax.dynamic_update_slice(
        jnp.zeros((FF,), jnp.float32), hidden_sums, (ff_start,)
    )
    vector_grad = jnp.concatenate(
        [
            jnp.stack(
                [
                    grad_gain_one,
                    grad_shift_one,
                    jnp.sum(grad_query_b.astype(jnp.float32), axis=0),
                    jnp.sum(grad_branch_b.astype(jnp.float32), axis=0),
                    grad_gain_two,
                    grad_shift_two,
                    jnp.sum(grad_y, axis=0),
                ],
                axis=0,
            ),
            hidden_whole.reshape(FF // D, D),
        ],
        axis=0,
    )
    vector_grad = vector_grad.reshape(NVEC, owners, rows).transpose(1, 0, 2)
    vector_grad = jnp.pad(vector_grad, ((0, 0), (0, 16 - NVEC), (0, 128 - rows)))
    grad_in, grad_out, back_grad, grad_up, vector_sum = finish_sums(
        parts,
        groups,
        contract_rows(norm_one_b, grad_mixed_b)
        .astype(bf)
        .reshape(groups // 2, 2, parts, rows, width_in),
        contract_rows(attended_b, grad_branch_b).astype(bf).reshape(groups // 2, 2, parts, rows, D),
        grad_inputs.astype(bf).reshape(parts, piece, D),
        up_grad_block.T.astype(bf).reshape(owners, rows, FF // owners),
        vector_grad,
    )
    grad_up = grad_up.transpose(1, 0, 2).reshape(rows, FF)
    vector_sum = jnp.sum(vector_sum, axis=0)
    grad_vec = vector_sum[:NVEC, :rows].T
    in_new = adam_update(in_weight, in_first, in_second, grad_in, 1.0 / math.sqrt(D), decay_rate)
    out_new = adam_update(
        out_weight, out_first, out_second, grad_out, 1.0 / math.sqrt(D * 8 // TOK_DEV), decay_rate
    )
    up_new = adam_update(up_weight, up_first, up_second, grad_up, 1.0 / math.sqrt(D), decay_rate)
    down_new = adam_update(
        down_weight, down_first, down_second, down_grad, 1.0 / math.sqrt(FF), decay_rate
    )
    vec_new = adam_update(vectors, vector_first, vector_second, grad_vec, 0.1, 0.0)
    return (undeal(back_result), undeal(back_grad)) + in_new + out_new + up_new + down_new + vec_new


def solution(mesh):
    spec = P(("dp", "fsdp"), None)
    return jax.shard_map(
        shards,
        mesh=mesh,
        in_specs=(spec,) * 19,
        out_specs=(spec,) * 17,
        check_vma=False,
    )
```

```python
import functools
import math

import jax
import jax.numpy as jnp
from jax import lax
from jax.experimental import pallas as pl
from jax.experimental.pallas import tpu as pltpu
from jax.sharding import PartitionSpec as P

D = 2048
FF = 8192
HD = 128
TOK_DEV = 384
STEP = 5
NVEC = 11


eps_norm = 1e-05
beta_one = 0.5
beta_two = 0.5
adam_eps = 1e-08
decay_rate = 0.1


def layer_norm(values, gain, shift):
    centered = values - jnp.mean(values, axis=-1, keepdims=True)
    scaled = centered * lax.rsqrt(jnp.mean(centered * centered, axis=-1, keepdims=True) + eps_norm)
    return scaled * gain + shift


def gelu_tanh(values):
    return (
        0.5
        * values
        * (1.0 + jnp.tanh(0.7978845608028654 * (values + 0.044715 * values * values * values)))
    )


def segment_mask(sizes, count):
    ends = jnp.cumsum(sizes)
    places = jnp.arange(count, dtype=jnp.int32)
    labels = jnp.sum((places[:, None] >= ends[None, :]).astype(jnp.int32), axis=1)
    return (labels[:, None] == labels[None, :]) & (places[None, :] <= places[:, None])


def adam_update(weight, first, second, grad, rate, decay):
    grad = grad.astype(jnp.float32)
    first_new = beta_one * first + (1.0 - beta_one) * grad
    second_new = beta_two * second + (1.0 - beta_two) * grad * grad
    fix_one = 1.0 - beta_one**STEP
    fix_two = 1.0 - beta_two**STEP
    step_size = first_new / fix_one / (jnp.sqrt(second_new / fix_two) + adam_eps)
    weight_new = weight - rate * (step_size + decay * weight)
    return (weight_new, first_new, second_new)


def contract_rows(left, right):
    return lax.dot_general(
        left, right, (((0,), (0,)), ((), ())), preferred_element_type=jnp.float32
    )


def contract_cols(left, right):
    return lax.dot_general(
        left, right, (((1,), (1,)), ((), ())), preferred_element_type=jnp.float32
    )


MESH = pl.DeviceIdType.MESH
F32 = jnp.float32
BF = jnp.bfloat16


def wrap(value, count):
    return lax.rem(value + 2 * count, count)


def ring_place(index, parts):
    if parts != 8:
        return index
    z, y = lax.div(index, 2), lax.rem(index, 2)
    return z + y * (7 - 2 * z)


def ring_index(place, parts):
    place = wrap(place, parts)
    if parts != 8:
        return place
    back = lax.div(place, 4)
    return (1 - back) * 2 * place + back * (15 - 2 * place)


def remote(src, dst, send, recv, dp, fs):
    return pltpu.make_async_remote_copy(
        src_ref=src, dst_ref=dst, send_sem=send, recv_sem=recv, device_id=(dp, fs), device_id_type=MESH
    )


def lasting(micros):
    return pl.CostEstimate(
        flops=int(micros * 1.1e9), bytes_accessed=int(micros * 3.3e6), transcendentals=0
    )


def greet(targets):
    barrier = pltpu.get_barrier_semaphore()
    for dp, fs in targets:
        pl.semaphore_signal(barrier, inc=1, device_id=(dp, fs), device_id_type=MESH)
    pl.semaphore_wait(barrier, len(targets))


def greet_all(me, parts, owners):
    barrier = pltpu.get_barrier_semaphore()

    def one(i, carry):
        peer = wrap(me + i, owners)
        pl.semaphore_signal(
            barrier, inc=1, device_id=(lax.div(peer, parts), lax.rem(peer, parts)), device_id_type=MESH
        )
        return carry

    lax.fori_loop(1, owners, one, 0)
    pl.semaphore_wait(barrier, owners - 1)


def loop(low, high, body):
    def one(i, carry):
        body(i)
        return carry

    lax.fori_loop(low, high, one, 0)


def deal_copy(parts, dp, f, src, dst, send, recv, d, came=False):
    to = wrap(f + d, parts)
    place = wrap(f - d, parts) if came else f
    return remote(src.at[to], dst.at[place], send.at[d], recv.at[d], dp, to)


def owner_copy(me, parts, owners, src, dst, send, recv, d, came=False):
    to = wrap(me + d, owners)
    place = wrap(me - d, owners) if came else me
    return remote(
        src.at[to], dst.at[place], send.at[d], recv.at[d], lax.div(to, parts), lax.rem(to, parts)
    )


def spread_kernel(
    parts, groups,
    xd, gd, inb, ovb,
    xo, eall, win, wov,
    local, xs, xr, gs, gr, rs, rr, ns, nr, ss, sr, ens, enr, ess, esr,
):
    dp, f = lax.axis_index("dp"), lax.axis_index("fsdp")
    owners, rows_x = groups * parts, groups // 2
    x, core = lax.div(dp, 2), lax.rem(dp, 2)
    sib = x * 2 + 1 - core
    me = dp * parts + f
    p = ring_place(f, parts)
    nxt, prv = ring_index(p + 1, parts), ring_index(p - 1, parts)
    whole = (win, wov)
    mine = [
        pltpu.make_async_copy(inb, win.at[me], local.at[0]),
        pltpu.make_async_copy(ovb, wov.at[me], local.at[1]),
        pltpu.make_async_copy(xd.at[f], xo.at[f], local.at[2]),
        pltpu.make_async_copy(gd.at[f], eall.at[dp, f], local.at[3]),
    ]
    for copy in mine:
        copy.start()
    greet(
        [(dp, wrap(f + d, parts)) for d in range(1, parts)]
        + [(sib, f)]
        + [(wrap(x + dx, rows_x) * 2 + core, f) for dx in range(1, rows_x)]
    )
    for copy in mine:
        copy.wait()

    def x_copies(d, came=False):
        return deal_copy(parts, dp, f, xd, xo, xs, xr, d, came)

    def g_copies(d, came=False):
        return deal_copy(parts, dp, f, gd, eall.at[dp], gs, gr, d, came)

    def origin(h, s):
        return ring_index(p - s if h == 0 else p + s, parts)

    def ring_send(h, s):
        ref = whole[h].at[dp * parts + origin(h, s)]
        return remote(ref, ref, rs.at[h, s], rr.at[h, s], dp, nxt if h == 0 else prv)

    def ring_recv(h, s):
        ref = whole[h].at[dp * parts + origin(h, s)]
        return remote(ref, ref, rs.at[h, s - 1], rr.at[h, s - 1], dp, nxt if h == 0 else prv)

    def x_send(h, s, dx):
        ref = whole[h].at[dp * parts + origin(h, s)]
        to = wrap(x + dx, rows_x) * 2 + core
        return remote(ref, ref, ns.at[h, s, dx], nr.at[h, s, dx], to, f)

    def x_recv(h, s, dx):
        came = wrap(x - dx, rows_x) * 2 + core
        ref = whole[h].at[came * parts + origin(h, s)]
        return remote(ref, ref, ns.at[h, s, dx], nr.at[h, s, dx], came, f)

    def sib_send(h, s, dx):
        came = wrap(x - dx, rows_x) * 2 + core
        ref = whole[h].at[came * parts + origin(h, s)]
        return remote(ref, ref, ss.at[h, s, dx], sr.at[h, s, dx], sib, f)

    def sib_recv(h, s, dx):
        came = wrap(x - dx, rows_x) * 2 + 1 - core
        ref = whole[h].at[came * parts + origin(h, s)]
        return remote(ref, ref, ss.at[h, s, dx], sr.at[h, s, dx], sib, f)

    def e_x_send(d, dx):
        ref = eall.at[dp, wrap(f - d, parts)]
        to = wrap(x + dx, rows_x) * 2 + core
        return remote(ref, ref, ens.at[d, dx], enr.at[d, dx], to, f)

    def e_x_recv(d, dx):
        came = wrap(x - dx, rows_x) * 2 + core
        ref = eall.at[came, wrap(f - d, parts)]
        return remote(ref, ref, ens.at[d, dx], enr.at[d, dx], came, f)

    def e_sib_send(d, dx):
        came = wrap(x - dx, rows_x) * 2 + core
        ref = eall.at[came, wrap(f - d, parts)]
        return remote(ref, ref, ess.at[d, dx], esr.at[d, dx], sib, f)

    def e_sib_recv(d, dx):
        came = wrap(x - dx, rows_x) * 2 + 1 - core
        ref = eall.at[came, wrap(f - d, parts)]
        return remote(ref, ref, ess.at[d, dx], esr.at[d, dx], sib, f)

    def ring_step(s):
        for h in range(2):
            @pl.when(s > 0)
            def _():
                ring_recv(h, s).wait_recv()

            @pl.when(s < parts - 1)
            def _():
                ring_send(h, s).start()

            for dx in range(1, rows_x):
                x_send(h, s, dx).start()
            sib_send(h, s, 0).start()

    def e_step(d):
        @pl.when(d > 0)
        def _():
            g_copies(d, True).wait_recv()

        for dx in range(1, rows_x):
            e_x_send(d, dx).start()
        e_sib_send(d, 0).start()

    def relay(s):
        for h in range(2):
            for dx in range(1, rows_x):
                x_recv(h, s, dx).wait_recv()
                sib_send(h, s, dx).start()

    def e_relay(d):
        for dx in range(1, rows_x):
            e_x_recv(d, dx).wait_recv()
            e_sib_send(d, dx).start()

    def main(s):
        @pl.when(s < parts)
        def _():
            ring_step(s)

        @pl.when(s < parts - 1)
        def _():
            x_copies(s + 1).start()
            g_copies(s + 1).start()

        @pl.when((s >= 1) & (s <= parts))
        def _():
            e_step(s - 1)

        @pl.when((s >= 2) & (s < parts + 2))
        def _():
            relay(s - 2)

        @pl.when(s >= 3)
        def _():
            e_relay(s - 3)

    loop(0, parts + 3, main)

    def finish(s):
        for h in range(2):
            @pl.when(s < parts - 1)
            def _():
                ring_send(h, s).wait_send()

            for dx in range(1, rows_x):
                x_send(h, s, dx).wait_send()
            for dx in range(rows_x):
                sib_recv(h, s, dx).wait_recv()
                sib_send(h, s, dx).wait_send()
        for dx in range(1, rows_x):
            e_x_send(s, dx).wait_send()
        for dx in range(rows_x):
            e_sib_recv(s, dx).wait_recv()
            e_sib_send(s, dx).wait_send()

        @pl.when(s > 0)
        def _():
            x_copies(s, True).wait_recv()
            x_copies(s).wait_send()
            g_copies(s).wait_send()

    loop(0, parts, finish)


def exchange_kernel(parts, groups, src, dst, local, us, ur):
    dp, f = lax.axis_index("dp"), lax.axis_index("fsdp")
    owners = groups * parts
    me = dp * parts + f
    mine = pltpu.make_async_copy(src.at[me], dst.at[me], local)
    mine.start()
    greet_all(me, parts, owners)
    loop(1, owners, lambda d: owner_copy(me, parts, owners, src, dst, us, ur, d).start())
    mine.wait()

    def finish(d):
        owner_copy(me, parts, owners, src, dst, us, ur, d, True).wait_recv()
        owner_copy(me, parts, owners, src, dst, us, ur, d).wait_send()

    loop(1, owners, finish)


def exchange(parts, groups, src):
    owners = groups * parts
    dma = pltpu.SemaphoreType.DMA
    return pl.pallas_call(
        functools.partial(exchange_kernel, parts, groups),
        out_shape=jax.ShapeDtypeStruct(src.shape, BF),
        in_specs=[pl.BlockSpec(memory_space=pl.ANY)],
        out_specs=pl.BlockSpec(memory_space=pl.ANY),
        scratch_shapes=[dma(()), dma((owners,)), dma((owners,))],
        compiler_params=pltpu.CompilerParams(collective_id=5, has_side_effects=True),
        cost_estimate=lasting(25),
    )(src)


def spread(parts, groups, xd, gd, inb, ovb):
    owners, rows_x = groups * parts, groups // 2
    dma = pltpu.SemaphoreType.DMA
    return pl.pallas_call(
        functools.partial(spread_kernel, parts, groups),
        out_shape=(
            jax.ShapeDtypeStruct(xd.shape, BF),
            jax.ShapeDtypeStruct((groups,) + gd.shape, BF),
            jax.ShapeDtypeStruct((owners,) + inb.shape, BF),
            jax.ShapeDtypeStruct((owners,) + ovb.shape, BF),
        ),
        in_specs=[pl.BlockSpec(memory_space=pl.ANY)] * 4,
        out_specs=(pl.BlockSpec(memory_space=pl.ANY),) * 4,
        scratch_shapes=[
            dma((4,)),
            dma((parts,)), dma((parts,)), dma((parts,)), dma((parts,)),
            dma((2, parts)), dma((2, parts)),
            dma((2, parts, rows_x)), dma((2, parts, rows_x)),
            dma((2, parts, rows_x)), dma((2, parts, rows_x)),
            dma((parts, rows_x)), dma((parts, rows_x)),
            dma((parts, rows_x)), dma((parts, rows_x)),
        ],
        compiler_params=pltpu.CompilerParams(collective_id=0, has_side_effects=True),
        cost_estimate=lasting(200),
    )(xd, gd, inb, ovb)


def group_gather_kernel(groups, chunks, src, out, local, ns, nr, ss, sr):
    dp, f = lax.axis_index("dp"), lax.axis_index("fsdp")
    rows_x = groups // 2
    x, core = lax.div(dp, 2), lax.rem(dp, 2)
    sib = x * 2 + 1 - core
    size = src.shape[0] // chunks
    mine = pltpu.make_async_copy(src, out.at[dp], local)
    mine.start()
    greet([(sib, f)] + [(wrap(x + dx, rows_x) * 2 + core, f) for dx in range(1, rows_x)])

    def part(ref, k):
        return ref.at[pl.ds(k * size, size)]

    def x_send(k, dx):
        to = wrap(x + dx, rows_x) * 2 + core
        return remote(part(src, k), part(out.at[dp], k), ns.at[k, dx], nr.at[k, dx], to, f)

    def x_recv(k, dx):
        came = wrap(x - dx, rows_x) * 2 + core
        ref = part(out.at[came], k)
        return remote(ref, ref, ns.at[k, dx], nr.at[k, dx], came, f)

    def sib_send(k, dx):
        came = wrap(x - dx, rows_x) * 2 + core
        ref = part(out.at[came], k)
        return remote(part(src, k) if dx == 0 else ref, ref, ss.at[k, dx], sr.at[k, dx], sib, f)

    def sib_recv(k, dx):
        came = wrap(x - dx, rows_x) * 2 + 1 - core
        ref = part(out.at[came], k)
        return remote(ref, ref, ss.at[k, dx], sr.at[k, dx], sib, f)

    for k in range(chunks):
        for dx in range(1, rows_x):
            x_send(k, dx).start()
    for k in range(chunks):
        sib_send(k, 0).start()
    for k in range(chunks):
        for dx in range(1, rows_x):
            x_recv(k, dx).wait_recv()
            sib_send(k, dx).start()
    mine.wait()
    for k in range(chunks):
        for dx in range(rows_x):
            sib_recv(k, dx).wait_recv()
            sib_send(k, dx).wait_send()
        for dx in range(1, rows_x):
            x_send(k, dx).wait_send()


def group_gather(groups, src):
    chunks, rows_x = 4, groups // 2
    dma = pltpu.SemaphoreType.DMA
    return pl.pallas_call(
        functools.partial(group_gather_kernel, groups, chunks),
        out_shape=jax.ShapeDtypeStruct((groups,) + src.shape, BF),
        in_specs=[pl.BlockSpec(memory_space=pl.ANY)],
        out_specs=pl.BlockSpec(memory_space=pl.ANY),
        scratch_shapes=[dma(())] + [dma((chunks, rows_x))] * 4,
        compiler_params=pltpu.CompilerParams(collective_id=1, has_side_effects=True),
        cost_estimate=lasting(45),
    )(src)


def ffn_back_kernel(
    parts, groups, chunks, streams,
    grad, act, dhid, w1, w2, base,
    out, dsum, back,
    ysum, leaving, loc, got, gone, wv, some, psib, sibr, xb, xrb,
    ll, ol, rs, rr, wl, sl, gss, gsr, gns, gnr, bs, br, bl,
):
    dp, f = lax.axis_index("dp"), lax.axis_index("fsdp")
    rows_x = groups // 2
    x, core = lax.div(dp, 2), lax.rem(dp, 2)
    sib = x * 2 + 1 - core
    p = ring_place(f, parts)
    nxt, prv = ring_index(p + 1, parts), ring_index(p - 1, parts)
    block, width = out.shape
    part, cut = width // streams, width // chunks
    count = dsum.shape[0]
    far, mid = range(1, rows_x), chunks // 2

    def local_copy(h, s):
        c = ring_index(p - 1 - s if h % 2 == 0 else p + 1 + s, parts)
        return pltpu.make_async_copy(
            grad.at[
                pl.ds(pl.multiple_of(c * block, block), block), pl.ds(h * part, part)
            ],
            loc.at[lax.rem(s, 2), h], ll.at[lax.rem(s, 2), h],
        )

    w_loads = (
        pltpu.make_async_copy(w2, wv, wl.at[0]),
        pltpu.make_async_copy(w1, wv, wl.at[1]),
    )
    for s in range(2):
        for h in range(streams):
            local_copy(h, s).start()
    w_loads[0].start()
    greet(
        [(dp, wrap(f + d, parts)) for d in range(1, parts)]
        + [(sib, f)]
        + [(wrap(x + dx, rows_x) * 2 + core, f) for dx in range(1, rows_x)]
    )

    def ring_copy(h, s):
        return remote(
            gone.at[lax.rem(s, 2), h], got.at[h, s], rs.at[h, s], rr.at[h, s],
            dp, nxt if h % 2 == 0 else prv,
        )

    def out_copy(h):
        return pltpu.make_async_copy(
            gone.at[lax.rem(parts - 1, 2), h],
            out.at[:, pl.ds(h * part, part)],
            ol.at[h],
        )

    def pass_on(s):
        slot = lax.rem(s, 2)
        for h in range(streams):
            local_copy(h, s).wait()

            @pl.when(s >= 2)
            def _():
                ring_copy(h, s - 2).wait_send()

            @pl.when(s == 0)
            def _():
                gone[slot, h] = loc[slot, h]

            @pl.when(s > 0)
            def _():
                ring_copy(h, s - 1).wait_recv()
                gone[slot, h] = (
                    loc[slot, h].astype(F32) + got[h, s - 1].astype(F32)
                ).astype(BF)

            @pl.when(s < parts - 1)
            def _():
                ring_copy(h, s).start()

            @pl.when(s == parts - 1)
            def _():
                out_copy(h).start()

            @pl.when(s < parts - 2)
            def _():
                local_copy(h, s + 2).start()

    def cols(k):
        return pl.ds(pl.multiple_of(k * cut, cut), cut)

    def rows_of(dx, c):
        group = wrap(x + dx, rows_x) * 2 + (core if c == 0 else 1 - core)
        return pl.ds(pl.multiple_of(group * count, count), count)

    rows_in, totals = (act, dhid), (ysum, dsum)

    def sum_sib(which, k):
        return remote(
            psib.at[:, :, cols(k)], sibr.at[which, :, :, cols(k)],
            gss.at[which, k], gsr.at[which, k], sib, f,
        )

    def sum_x(which, dx, k):
        to = wrap(x + dx, rows_x) * 2 + core
        return remote(
            xb.at[dx - 1, :, cols(k)], xrb.at[which, dx - 1, :, cols(k)],
            gns.at[which, dx, k], gnr.at[which, dx, k], to, f,
        )

    def take_rows(which, c):
        copies = [
            pltpu.make_async_copy(
                rows_in[which].at[rows_of(dx, c)], some.at[pl.ds(dx * count, count)], sl.at[dx]
            )
            for dx in range(rows_x)
        ]
        for copy in copies:
            copy.start()
        for copy in copies:
            copy.wait()

    def other_side(which, low, high):
        if low == 0:
            take_rows(which, 1)

        def one(k):
            psib[:, :, cols(k)] = (
                jnp.dot(some[...], wv[:, cols(k)], preferred_element_type=F32)
                .astype(BF)
                .reshape(rows_x, count, cut)
            )
            sum_sib(which, k).start()

        loop(low, high, one)

    def own_side(which, low, high):
        if low == 0:
            take_rows(which, 0)

        def one(k):
            here = jnp.dot(some[...], wv[:, cols(k)], preferred_element_type=F32)
            sum_sib(which, k).wait_recv()
            here = here.reshape(rows_x, count, cut) + sibr[which, :, :, cols(k)].astype(F32)
            for dx in far:
                xb[dx - 1, :, cols(k)] = here[dx].astype(BF)
                sum_x(which, dx, k).start()
            totals[which][:, cols(k)] = here[0]

        loop(low, high, one)

    def collect(which):
        def one(k):
            for dx in far:
                sum_x(which, dx, k).wait_recv()
                totals[which][:, cols(k)] += xrb[which, dx - 1, :, cols(k)].astype(F32)

        loop(0, chunks, one)

    def back_copy(d, came=False):
        return deal_copy(parts, dp, f, leaving, back, bs, br, d, came)

    def own_back():
        return pltpu.make_async_copy(leaving.at[f], back.at[f], bl)

    def send_back():
        piece = count // parts

        def one(j):
            rows = pl.ds(pl.multiple_of(j * piece, piece), piece)
            leaving[j] = (base[rows, :] + ysum[rows, :]).astype(BF)

        loop(0, parts, one)
        own_back().start()
        loop(1, parts, lambda d: back_copy(d).start())

    def sent_sib(which):
        loop(0, chunks, lambda k: sum_sib(which, k).wait_send())

    def sent_x(which):
        for dx in far:
            loop(0, chunks, lambda k: sum_x(which, dx, k).wait_send())

    def step(s):
        pass_on(s)

        @pl.when(s == 0)
        def _():
            w_loads[0].wait()
            other_side(0, 0, mid)

        @pl.when(s == 1)
        def _():
            other_side(0, mid, chunks)

        @pl.when(s == 2)
        def _():
            own_side(0, 0, mid)

        @pl.when(s == 3)
        def _():
            own_side(0, mid, chunks)
            w_loads[1].start()
            sent_sib(0)

        @pl.when(s == 4)
        def _():
            w_loads[1].wait()
            other_side(1, 0, mid)

        @pl.when(s == 5)
        def _():
            other_side(1, mid, chunks)
            collect(0)
            send_back()
            sent_x(0)

        @pl.when(s == 6)
        def _():
            own_side(1, 0, mid)

        @pl.when(s == 7)
        def _():
            own_side(1, mid, chunks)

    loop(0, parts, step)
    collect(1)
    for h in range(streams):
        ring_copy(h, parts - 2).wait_send()
        out_copy(h).wait()
    sent_sib(1)
    sent_x(1)
    own_back().wait()

    def returned(d):
        back_copy(d, True).wait_recv()
        back_copy(d).wait_send()

    loop(1, parts, returned)


def ffn_back(parts, groups, grad, act, dhid, w1, w2, base):
    chunks, streams, rows_x = 4, 4, groups // 2
    units, width = w1.shape
    count = act.shape[0] // groups
    block, part, piece = units // parts, width // streams, count // parts
    dma = pltpu.SemaphoreType.DMA
    hbm = pl.BlockSpec(memory_space=pl.ANY)
    vmem = pl.BlockSpec(memory_space=pltpu.VMEM)
    return pl.pallas_call(
        functools.partial(ffn_back_kernel, parts, groups, chunks, streams),
        out_shape=(
            jax.ShapeDtypeStruct((block, width), BF),
            jax.ShapeDtypeStruct((count, width), F32),
            jax.ShapeDtypeStruct((parts, piece, width), BF),
        ),
        in_specs=[hbm] * 5 + [vmem],
        out_specs=(hbm, vmem, hbm),
        scratch_shapes=[
            pltpu.VMEM((count, width), F32),
            pltpu.VMEM((parts, piece, width), BF),
            pltpu.VMEM((2, streams, block, part), BF),
            pltpu.VMEM((streams, parts - 1, block, part), BF),
            pltpu.VMEM((2, streams, block, part), BF),
            pltpu.VMEM((units, width), BF),
            pltpu.VMEM((rows_x * count, units), BF),
            pltpu.VMEM((rows_x, count, width), BF),
            pltpu.VMEM((2, rows_x, count, width), BF),
            pltpu.VMEM((rows_x - 1, count, width), BF),
            pltpu.VMEM((2, rows_x - 1, count, width), BF),
            dma((2, streams)), dma((streams,)),
            dma((streams, parts)), dma((streams, parts)), dma((2,)), dma((rows_x,)),
            dma((2, chunks)), dma((2, chunks)),
            dma((2, rows_x, chunks)), dma((2, rows_x, chunks)),
            dma((parts,)), dma((parts,)), dma(()),
        ],
        compiler_params=pltpu.CompilerParams(
            collective_id=3, has_side_effects=True, vmem_limit_bytes=60 * 2**20
        ),
        cost_estimate=lasting(130),
    )(grad, act, dhid, w1, w2, base)


def finish_kernel(
    parts, groups,
    grad_a, grad_b, gx, upg, vec,
    total_a, total_b, gx_out, upg_out, vec_out,
    loc_a, loc_b, sibr_a, sibr_b, xb_a, xb_b, xrb_a, xrb_b, got_a, got_b, gone_a, gone_b,
    local, ls, ss, sr, ns, nr, rs, rr, bs, br, us, ur, vs, vr,
):
    dp, f = lax.axis_index("dp"), lax.axis_index("fsdp")
    owners, rows_x = groups * parts, groups // 2
    x, core = lax.div(dp, 2), lax.rem(dp, 2)
    sib = x * 2 + 1 - core
    me = dp * parts + f
    p = ring_place(f, parts)
    nxt, prv = ring_index(p + 1, parts), ring_index(p - 1, parts)
    grads, total = (grad_a, grad_b), (total_a, total_b)
    loc, sibr, xb, xrb = (loc_a, loc_b), (sibr_a, sibr_b), (xb_a, xb_b), (xrb_a, xrb_b)
    got, gone = (got_a, got_b), (gone_a, gone_b)
    mine = [
        pltpu.make_async_copy(gx.at[f], gx_out.at[f], local.at[0]),
        pltpu.make_async_copy(vec.at[me], vec_out.at[me], local.at[1]),
        pltpu.make_async_copy(upg.at[me], upg_out.at[me], local.at[2]),
    ]
    for copy in mine:
        copy.start()
    greet_all(me, parts, owners)

    def chunk(h, s):
        return ring_index(p - 1 - s if h == 0 else p + 1 + s, parts)

    def sib_copy(h, s):
        piece = grads[h].at[:, 1 - core, chunk(h, s)]
        return remote(piece, sibr[h].at[s], ss.at[h, s], sr.at[h, s], sib, f)

    def own_copy(h, s):
        piece = grads[h].at[:, core, chunk(h, s)]
        return pltpu.make_async_copy(piece, loc[h].at[s], ls.at[h, s])

    def x_copy(h, s, dx):
        to = wrap(x + dx, rows_x) * 2 + core
        return remote(
            xb[h].at[s, dx - 1], xrb[h].at[s, dx - 1], ns.at[h, s, dx], nr.at[h, s, dx], to, f
        )

    def ring_copy(h, s):
        return remote(
            gone[h].at[s], got[h].at[s], rs.at[h, s], rr.at[h, s], dp, nxt if h == 0 else prv
        )

    def gx_copies(d, came=False):
        return deal_copy(parts, dp, f, gx, gx_out, bs, br, d, came)

    def upg_copies(d, came=False):
        return owner_copy(me, parts, owners, upg, upg_out, us, ur, d, came)

    def vec_copies(d, came=False):
        return owner_copy(me, parts, owners, vec, vec_out, vs, vr, d, came)

    def begin(s):
        for h in range(2):
            sib_copy(h, s).start()
            own_copy(h, s).start()

    def others(d):
        upg_copies(d).start()
        vec_copies(d).start()

    def returns(d):
        gx_copies(d).start()

    def pair(s):
        for h in range(2):
            sib_copy(h, s).wait_recv()
            own_copy(h, s).wait()
            for dx in range(1, rows_x):
                to = wrap(x + dx, rows_x)
                xb[h][s, dx - 1] = (sibr[h][s, to].astype(F32) + loc[h][s, to].astype(F32)).astype(BF)
                x_copy(h, s, dx).start()

    def step(s):
        for h in range(2):
            for dx in range(1, rows_x):
                x_copy(h, s, dx).wait_recv()

            def value():
                here = sibr[h][s, x].astype(F32) + loc[h][s, x].astype(F32)
                for dx in range(1, rows_x):
                    here = here + xrb[h][s, dx - 1].astype(F32)
                return here

            @pl.when(s == 0)
            def _():
                gone[h][s] = value().astype(BF)
                ring_copy(h, s).start()

            @pl.when((s > 0) & (s < parts - 1))
            def _():
                ring_copy(h, s - 1).wait_recv()
                gone[h][s] = (value() + got[h][s - 1].astype(F32)).astype(BF)
                ring_copy(h, s).start()

            @pl.when(s == parts - 1)
            def _():
                ring_copy(h, s - 1).wait_recv()
                total[h][...] = value() + got[h][s - 1].astype(F32)

    loop(0, parts, begin)
    loop(1, parts, returns)
    loop(1, owners, others)
    loop(0, parts, pair)
    loop(0, parts, step)

    def finish(s):
        for h in range(2):
            sib_copy(h, s).wait_send()
            for dx in range(1, rows_x):
                x_copy(h, s, dx).wait_send()

            @pl.when(s < parts - 1)
            def _():
                ring_copy(h, s).wait_send()

        @pl.when(s > 0)
        def _():
            gx_copies(s, True).wait_recv()
            gx_copies(s).wait_send()

    loop(0, parts, finish)

    def owner_finish(d):
        for copies in (upg_copies, vec_copies):
            copies(d, True).wait_recv()
            copies(d).wait_send()

    loop(1, owners, owner_finish)
    for copy in mine:
        copy.wait()


def finish_sums(parts, groups, grad_a, grad_b, gx, upg, vec):
    owners, rows_x = groups * parts, groups // 2
    rows = grad_a.shape[3]
    widths = (grad_a.shape[4], grad_b.shape[4])
    dma = pltpu.SemaphoreType.DMA
    hbm = pl.BlockSpec(memory_space=pl.ANY)
    return pl.pallas_call(
        functools.partial(finish_kernel, parts, groups),
        out_shape=(
            jax.ShapeDtypeStruct((rows, widths[0]), F32),
            jax.ShapeDtypeStruct((rows, widths[1]), F32),
            jax.ShapeDtypeStruct(gx.shape, BF),
            jax.ShapeDtypeStruct(upg.shape, BF),
            jax.ShapeDtypeStruct(vec.shape, F32),
        ),
        in_specs=[hbm] * 5,
        out_specs=(pl.BlockSpec(memory_space=pltpu.VMEM),) * 2 + (hbm,) * 3,
        scratch_shapes=[
            *(
                pltpu.VMEM(lead + (rows, width), BF)
                for lead in (
                    (parts, rows_x), (parts, rows_x), (parts, rows_x - 1), (parts, rows_x - 1),
                    (parts,), (parts,),
                )
                for width in widths
            ),
            dma((3,)),
            dma((2, parts)), dma((2, parts)), dma((2, parts)),
            dma((2, parts, rows_x)), dma((2, parts, rows_x)),
            dma((2, parts)), dma((2, parts)),
            dma((parts,)), dma((parts,)),
            dma((owners,)), dma((owners,)), dma((owners,)), dma((owners,)),
        ],
        compiler_params=pltpu.CompilerParams(
            collective_id=4, has_side_effects=True, vmem_limit_bytes=60 * 2**20
        ),
        cost_estimate=lasting(1),
    )(grad_a, grad_b, gx, upg, vec)


def shards(
    tokens,
    cotangent,
    lengths,
    routing,
    in_weight,
    in_first,
    in_second,
    out_weight,
    out_first,
    out_second,
    up_weight,
    up_first,
    up_second,
    down_weight,
    down_first,
    down_second,
    vectors,
    vector_first,
    vector_second,
):
    bf = jnp.bfloat16
    heads = D // HD
    count = tokens.shape[0]
    parts = lax.axis_size("fsdp")
    groups = lax.axis_size("dp")
    both = ("dp", "fsdp")
    piece = count // parts
    width_in = D + 2 * HD
    slots = jnp.arange(parts, dtype=jnp.int32)
    order = routing[0]
    inverse = jnp.sum(jnp.where(order[:, None] == slots[None, :], slots[:, None], 0), axis=0)

    def deal(array):
        return jnp.take(array.reshape(parts, piece, D), inverse, axis=0)

    def undeal(array):
        return jnp.take(array, order, axis=0).reshape(count, D)

    rows = in_weight.shape[0]
    owners = groups * parts
    out_vec = jnp.concatenate(
        [out_weight.astype(bf), jnp.pad(vectors.astype(bf), ((0, 0), (0, 128 - NVEC)))], axis=1
    )
    up_pieces = up_weight.astype(bf).reshape(rows, owners, FF // owners).transpose(1, 0, 2)
    up_block, dealt, dealt_grad, out_vec = lax.optimization_barrier(
        (exchange(parts, groups, up_pieces), deal(tokens), deal(cotangent), out_vec)
    )
    x_dealt, grad_dealt, whole_in, whole_out = spread(
        parts, groups, dealt, dealt_grad, in_weight.astype(bf), out_vec
    )
    inputs_here = x_dealt.reshape(count, D)
    grad_all = grad_dealt.reshape(groups * count, D)
    grad_here = lax.dynamic_index_in_dim(
        grad_dealt, lax.axis_index("dp"), 0, keepdims=False
    ).reshape(count, D)
    whole_in = whole_in.reshape(D, width_in)
    whole_out = whole_out.reshape(D, D + 128)
    part_down = lax.all_gather(down_weight.astype(bf), "fsdp", axis=0, tiled=True)
    part_up = lax.all_gather(up_block.reshape(D, FF // owners).T, "fsdp", axis=0, tiled=True)

    table = whole_out[:, D : D + NVEC].astype(jnp.float32)
    whole_out = whole_out[:, :D]
    gain_one = table[:, 0]
    shift_one = table[:, 1]
    query_bias = table[:, 2]
    branch_bias = table[:, 3]
    gain_two = table[:, 4]
    shift_two = table[:, 5]
    output_bias = table[:, 6]
    hidden_bias = table[:, 7:].T.reshape(FF)
    ff_here = FF // groups
    ff_start = lax.axis_index("dp") * ff_here
    hidden_bias_here = lax.dynamic_slice(hidden_bias, (ff_start,), (ff_here,))
    allowed = segment_mask(lengths[0], count)
    scale = 1.0 / math.sqrt(HD)
    inputs = inputs_here.astype(jnp.float32)
    norm_one_b = layer_norm(inputs, gain_one, shift_one).astype(bf)
    mixed = jnp.dot(norm_one_b, whole_in, preferred_element_type=jnp.float32)
    query_b = (mixed[:, :D] + query_bias).astype(bf)
    keys_b = mixed[:, D : D + HD].astype(bf)
    values_b = mixed[:, D + HD :].astype(bf)
    query_heads = query_b.reshape(count, heads, HD)

    def score_table():
        raw = (
            jnp.einsum("thd,sd->hts", query_heads, keys_b, preferred_element_type=jnp.float32)
            * scale
        )
        return jnp.where(allowed[None], raw, -1e30)

    scores = score_table()
    top = jnp.max(scores, axis=-1, keepdims=True)
    expo = jnp.exp(scores - top)
    total = jnp.sum(expo, axis=-1, keepdims=True)
    logsum = top + jnp.log(total)
    probs_b = (expo / total).astype(bf)
    attended_b = (
        jnp.einsum("hts,sd->thd", probs_b, values_b, preferred_element_type=jnp.float32)
        .reshape(count, D)
        .astype(bf)
    )
    middle = inputs + (
        jnp.dot(attended_b, whole_out, preferred_element_type=jnp.float32) + branch_bias
    )
    norm_two_b = layer_norm(middle, gain_two, shift_two).astype(bf)

    fused = parts == 8 and groups == 4
    if fused:
        norm_all = group_gather(groups, norm_two_b).reshape(groups * count, D)
    else:
        norm_all = lax.all_gather(norm_two_b, "dp", axis=0, tiled=True)
    hidden = contract_cols(norm_all, part_up) + hidden_bias_here
    grad_active = contract_cols(grad_all, part_down)
    gelu_value, gelu_pull = jax.vjp(gelu_tanh, hidden)
    active_b = gelu_value.astype(bf)
    grad_hidden_b = gelu_pull(grad_active)[0].astype(bf)
    down_parts = contract_rows(active_b, grad_all).astype(bf)
    up_parts = contract_rows(grad_hidden_b, norm_all).astype(bf)
    down_parts, up_parts = lax.optimization_barrier((down_parts, up_parts))
    if fused:
        up_grad_block, grad_norm_two, back_result = ffn_back(
            parts, groups, up_parts, active_b, grad_hidden_b, part_up, part_down,
            middle + output_bias,
        )
    else:
        up_grad_block = lax.psum_scatter(up_parts, "fsdp", scatter_dimension=0, tiled=True)
        grad_norm_two = lax.psum_scatter(
            jnp.dot(grad_hidden_b, part_up, preferred_element_type=jnp.float32).astype(bf),
            "dp", scatter_dimension=0, tiled=True,
        ).astype(jnp.float32)
        branch_two = lax.psum_scatter(
            jnp.dot(active_b, part_down, preferred_element_type=jnp.float32).astype(bf),
            "dp", scatter_dimension=0, tiled=True,
        ).astype(jnp.float32)
        back_result = lax.all_to_all(
            (middle + (branch_two + output_bias)).astype(bf),
            "fsdp", split_axis=0, concat_axis=0, tiled=True,
        ).reshape(parts, piece, D)
    down_parts, up_grad_block = lax.optimization_barrier((down_parts, up_grad_block))
    down_grad = lax.psum_scatter(down_parts, "fsdp", scatter_dimension=0, tiled=True)

    grad_y = grad_here.astype(jnp.float32)
    norm_value_two, pull_two = jax.vjp(layer_norm, middle, gain_two, shift_two)
    grad_middle_norm, grad_gain_two, grad_shift_two = pull_two(grad_norm_two)
    grad_middle = grad_y + grad_middle_norm
    grad_branch_b = grad_middle.astype(bf)
    grad_attended_b = contract_cols(grad_branch_b, whole_out).astype(bf)
    grad_heads = grad_attended_b.reshape(count, heads, HD)
    probs = jnp.exp(score_table() - logsum)
    probs_again_b = probs.astype(bf)
    grad_probs = jnp.einsum("thd,sd->hts", grad_heads, values_b, preferred_element_type=jnp.float32)
    grad_values_b = jnp.einsum(
        "hts,thd->sd", probs_again_b, grad_heads, preferred_element_type=jnp.float32
    ).astype(bf)
    weighted = jnp.sum(probs * grad_probs, axis=-1, keepdims=True)
    grad_scores_b = (probs * (grad_probs - weighted)).astype(bf)
    grad_query_b = (
        (
            jnp.einsum("hts,sd->thd", grad_scores_b, keys_b, preferred_element_type=jnp.float32)
            * scale
        )
        .reshape(count, D)
        .astype(bf)
    )
    grad_keys_b = (
        jnp.einsum("hts,thd->sd", grad_scores_b, query_heads, preferred_element_type=jnp.float32)
        * scale
    ).astype(bf)
    grad_mixed_b = jnp.concatenate([grad_query_b, grad_keys_b, grad_values_b], axis=1)
    grad_norm_one = contract_cols(grad_mixed_b, whole_in)
    norm_value_one, pull_one = jax.vjp(layer_norm, inputs, gain_one, shift_one)
    grad_inputs_norm, grad_gain_one, grad_shift_one = pull_one(grad_norm_one)
    grad_inputs = grad_middle + grad_inputs_norm
    hidden_sums = jnp.sum(grad_hidden_b.astype(jnp.float32), axis=0)
    hidden_whole = lax.dynamic_update_slice(
        jnp.zeros((FF,), jnp.float32), hidden_sums, (ff_start,)
    )
    vector_grad = jnp.concatenate(
        [
            jnp.stack(
                [
                    grad_gain_one,
                    grad_shift_one,
                    jnp.sum(grad_query_b.astype(jnp.float32), axis=0),
                    jnp.sum(grad_branch_b.astype(jnp.float32), axis=0),
                    grad_gain_two,
                    grad_shift_two,
                    jnp.sum(grad_y, axis=0),
                ],
                axis=0,
            ),
            hidden_whole.reshape(FF // D, D),
        ],
        axis=0,
    )
    vector_grad = vector_grad.reshape(NVEC, owners, rows).transpose(1, 0, 2)
    vector_grad = jnp.pad(vector_grad, ((0, 0), (0, 16 - NVEC), (0, 128 - rows)))
    grad_in, grad_out, back_grad, grad_up, vector_sum = finish_sums(
        parts,
        groups,
        contract_rows(norm_one_b, grad_mixed_b)
        .astype(bf)
        .reshape(groups // 2, 2, parts, rows, width_in),
        contract_rows(attended_b, grad_branch_b).astype(bf).reshape(groups // 2, 2, parts, rows, D),
        grad_inputs.astype(bf).reshape(parts, piece, D),
        up_grad_block.T.astype(bf).reshape(owners, rows, FF // owners),
        vector_grad,
    )
    grad_up = grad_up.transpose(1, 0, 2).reshape(rows, FF)
    vector_sum = jnp.sum(vector_sum, axis=0)
    grad_vec = vector_sum[:NVEC, :rows].T
    in_new = adam_update(in_weight, in_first, in_second, grad_in, 1.0 / math.sqrt(D), decay_rate)
    out_new = adam_update(
        out_weight, out_first, out_second, grad_out, 1.0 / math.sqrt(D * 8 // TOK_DEV), decay_rate
    )
    up_new = adam_update(up_weight, up_first, up_second, grad_up, 1.0 / math.sqrt(D), decay_rate)
    down_new = adam_update(
        down_weight, down_first, down_second, down_grad, 1.0 / math.sqrt(FF), decay_rate
    )
    vec_new = adam_update(vectors, vector_first, vector_second, grad_vec, 0.1, 0.0)
    return (undeal(back_result), undeal(back_grad)) + in_new + out_new + up_new + down_new + vec_new


def solution(mesh):
    spec = P(("dp", "fsdp"), None)
    return jax.shard_map(
        shards,
        mesh=mesh,
        in_specs=(spec,) * 19,
        out_specs=(spec,) * 17,
        check_vma=False,
    )
```

```python
import functools
import math

import jax
import jax.numpy as jnp
from jax import lax
from jax.experimental import pallas as pl
from jax.experimental.pallas import tpu as pltpu
from jax.sharding import PartitionSpec as P

D = 2048
FF = 8192
HD = 128
TOK_DEV = 384
STEP = 5
NVEC = 11


eps_norm = 1e-05
beta_one = 0.5
beta_two = 0.5
adam_eps = 1e-08
decay_rate = 0.1


def layer_norm(values, gain, shift):
    centered = values - jnp.mean(values, axis=-1, keepdims=True)
    scaled = centered * lax.rsqrt(jnp.mean(centered * centered, axis=-1, keepdims=True) + eps_norm)
    return scaled * gain + shift


def gelu_tanh(values):
    return (
        0.5
        * values
        * (1.0 + jnp.tanh(0.7978845608028654 * (values + 0.044715 * values * values * values)))
    )


def segment_mask(sizes, count):
    ends = jnp.cumsum(sizes)
    places = jnp.arange(count, dtype=jnp.int32)
    labels = jnp.sum((places[:, None] >= ends[None, :]).astype(jnp.int32), axis=1)
    return (labels[:, None] == labels[None, :]) & (places[None, :] <= places[:, None])


def adam_update(weight, first, second, grad, rate, decay):
    grad = grad.astype(jnp.float32)
    first_new = beta_one * first + (1.0 - beta_one) * grad
    second_new = beta_two * second + (1.0 - beta_two) * grad * grad
    fix_one = 1.0 - beta_one**STEP
    fix_two = 1.0 - beta_two**STEP
    step_size = first_new / fix_one / (jnp.sqrt(second_new / fix_two) + adam_eps)
    weight_new = weight - rate * (step_size + decay * weight)
    return (weight_new, first_new, second_new)


def contract_rows(left, right):
    return lax.dot_general(
        left, right, (((0,), (0,)), ((), ())), preferred_element_type=jnp.float32
    )


def contract_cols(left, right):
    return lax.dot_general(
        left, right, (((1,), (1,)), ((), ())), preferred_element_type=jnp.float32
    )


MESH = pl.DeviceIdType.MESH
F32 = jnp.float32
BF = jnp.bfloat16


def wrap(value, count):
    return lax.rem(value + 2 * count, count)


def ring_place(index, parts):
    if parts != 8:
        return index
    z, y = lax.div(index, 2), lax.rem(index, 2)
    return z + y * (7 - 2 * z)


def ring_index(place, parts):
    place = wrap(place, parts)
    if parts != 8:
        return place
    back = lax.div(place, 4)
    return (1 - back) * 2 * place + back * (15 - 2 * place)


def remote(src, dst, send, recv, dp, fs):
    return pltpu.make_async_remote_copy(
        src_ref=src, dst_ref=dst, send_sem=send, recv_sem=recv, device_id=(dp, fs), device_id_type=MESH
    )


def lasting(micros):
    return pl.CostEstimate(
        flops=int(micros * 1.1e9), bytes_accessed=int(micros * 3.3e6), transcendentals=0
    )


def greet(targets):
    barrier = pltpu.get_barrier_semaphore()
    for dp, fs in targets:
        pl.semaphore_signal(barrier, inc=1, device_id=(dp, fs), device_id_type=MESH)
    pl.semaphore_wait(barrier, len(targets))


def greet_all(me, parts, owners):
    barrier = pltpu.get_barrier_semaphore()

    def one(i, carry):
        peer = wrap(me + i, owners)
        pl.semaphore_signal(
            barrier, inc=1, device_id=(lax.div(peer, parts), lax.rem(peer, parts)), device_id_type=MESH
        )
        return carry

    lax.fori_loop(1, owners, one, 0)
    pl.semaphore_wait(barrier, owners - 1)


def loop(low, high, body):
    def one(i, carry):
        body(i)
        return carry

    lax.fori_loop(low, high, one, 0)


def deal_copy(parts, dp, f, src, dst, send, recv, d, came=False):
    to = wrap(f + d, parts)
    place = wrap(f - d, parts) if came else f
    return remote(src.at[to], dst.at[place], send.at[d], recv.at[d], dp, to)


def owner_copy(me, parts, owners, src, dst, send, recv, d, came=False):
    to = wrap(me + d, owners)
    place = wrap(me - d, owners) if came else me
    return remote(
        src.at[to], dst.at[place], send.at[d], recv.at[d], lax.div(to, parts), lax.rem(to, parts)
    )


def spread_kernel(
    parts, groups,
    xd, gd, inb, ovb,
    xo, eall, win, wov,
    local, xs, xr, gs, gr, rs, rr, ns, nr, ss, sr, ens, enr, ess, esr,
):
    dp, f = lax.axis_index("dp"), lax.axis_index("fsdp")
    owners, rows_x = groups * parts, groups // 2
    x, core = lax.div(dp, 2), lax.rem(dp, 2)
    sib = x * 2 + 1 - core
    me = dp * parts + f
    p = ring_place(f, parts)
    nxt, prv = ring_index(p + 1, parts), ring_index(p - 1, parts)
    whole = (win, wov)
    mine = [
        pltpu.make_async_copy(inb, win.at[me], local.at[0]),
        pltpu.make_async_copy(ovb, wov.at[me], local.at[1]),
        pltpu.make_async_copy(xd.at[f], xo.at[f], local.at[2]),
        pltpu.make_async_copy(gd.at[f], eall.at[dp, f], local.at[3]),
    ]
    for copy in mine:
        copy.start()
    greet(
        [(dp, wrap(f + d, parts)) for d in range(1, parts)]
        + [(sib, f)]
        + [(wrap(x + dx, rows_x) * 2 + core, f) for dx in range(1, rows_x)]
    )
    for copy in mine:
        copy.wait()

    def x_copies(d, came=False):
        return deal_copy(parts, dp, f, xd, xo, xs, xr, d, came)

    def g_copies(d, came=False):
        return deal_copy(parts, dp, f, gd, eall.at[dp], gs, gr, d, came)

    def origin(h, s):
        return ring_index(p - s if h == 0 else p + s, parts)

    def ring_send(h, s):
        ref = whole[h].at[dp * parts + origin(h, s)]
        return remote(ref, ref, rs.at[h, s], rr.at[h, s], dp, nxt if h == 0 else prv)

    def ring_recv(h, s):
        ref = whole[h].at[dp * parts + origin(h, s)]
        return remote(ref, ref, rs.at[h, s - 1], rr.at[h, s - 1], dp, nxt if h == 0 else prv)

    def x_send(h, s, dx):
        ref = whole[h].at[dp * parts + origin(h, s)]
        to = wrap(x + dx, rows_x) * 2 + core
        return remote(ref, ref, ns.at[h, s, dx], nr.at[h, s, dx], to, f)

    def x_recv(h, s, dx):
        came = wrap(x - dx, rows_x) * 2 + core
        ref = whole[h].at[came * parts + origin(h, s)]
        return remote(ref, ref, ns.at[h, s, dx], nr.at[h, s, dx], came, f)

    def sib_send(h, s, dx):
        came = wrap(x - dx, rows_x) * 2 + core
        ref = whole[h].at[came * parts + origin(h, s)]
        return remote(ref, ref, ss.at[h, s, dx], sr.at[h, s, dx], sib, f)

    def sib_recv(h, s, dx):
        came = wrap(x - dx, rows_x) * 2 + 1 - core
        ref = whole[h].at[came * parts + origin(h, s)]
        return remote(ref, ref, ss.at[h, s, dx], sr.at[h, s, dx], sib, f)

    def e_x_send(d, dx):
        ref = eall.at[dp, wrap(f - d, parts)]
        to = wrap(x + dx, rows_x) * 2 + core
        return remote(ref, ref, ens.at[d, dx], enr.at[d, dx], to, f)

    def e_x_recv(d, dx):
        came = wrap(x - dx, rows_x) * 2 + core
        ref = eall.at[came, wrap(f - d, parts)]
        return remote(ref, ref, ens.at[d, dx], enr.at[d, dx], came, f)

    def e_sib_send(d, dx):
        came = wrap(x - dx, rows_x) * 2 + core
        ref = eall.at[came, wrap(f - d, parts)]
        return remote(ref, ref, ess.at[d, dx], esr.at[d, dx], sib, f)

    def e_sib_recv(d, dx):
        came = wrap(x - dx, rows_x) * 2 + 1 - core
        ref = eall.at[came, wrap(f - d, parts)]
        return remote(ref, ref, ess.at[d, dx], esr.at[d, dx], sib, f)

    def ring_step(s):
        for h in range(2):
            @pl.when(s > 0)
            def _():
                ring_recv(h, s).wait_recv()

            @pl.when(s < parts - 1)
            def _():
                ring_send(h, s).start()

            for dx in range(1, rows_x):
                x_send(h, s, dx).start()
            sib_send(h, s, 0).start()

    def e_step(d):
        @pl.when(d > 0)
        def _():
            g_copies(d, True).wait_recv()

        for dx in range(1, rows_x):
            e_x_send(d, dx).start()
        e_sib_send(d, 0).start()

    def relay(s):
        for h in range(2):
            for dx in range(1, rows_x):
                x_recv(h, s, dx).wait_recv()
                sib_send(h, s, dx).start()

    def e_relay(d):
        for dx in range(1, rows_x):
            e_x_recv(d, dx).wait_recv()
            e_sib_send(d, dx).start()

    def main(s):
        @pl.when(s < parts)
        def _():
            ring_step(s)

        @pl.when(s < parts - 1)
        def _():
            x_copies(s + 1).start()
            g_copies(s + 1).start()

        @pl.when((s >= 1) & (s <= parts))
        def _():
            e_step(s - 1)

        @pl.when((s >= 2) & (s < parts + 2))
        def _():
            relay(s - 2)

        @pl.when(s >= 3)
        def _():
            e_relay(s - 3)

    loop(0, parts + 3, main)

    def finish(s):
        for h in range(2):
            @pl.when(s < parts - 1)
            def _():
                ring_send(h, s).wait_send()

            for dx in range(1, rows_x):
                x_send(h, s, dx).wait_send()
            for dx in range(rows_x):
                sib_recv(h, s, dx).wait_recv()
                sib_send(h, s, dx).wait_send()
        for dx in range(1, rows_x):
            e_x_send(s, dx).wait_send()
        for dx in range(rows_x):
            e_sib_recv(s, dx).wait_recv()
            e_sib_send(s, dx).wait_send()

        @pl.when(s > 0)
        def _():
            x_copies(s, True).wait_recv()
            x_copies(s).wait_send()
            g_copies(s).wait_send()

    loop(0, parts, finish)


def exchange_kernel(parts, groups, src, dst, local, us, ur):
    dp, f = lax.axis_index("dp"), lax.axis_index("fsdp")
    owners = groups * parts
    me = dp * parts + f
    mine = pltpu.make_async_copy(src.at[me], dst.at[me], local)
    mine.start()
    greet_all(me, parts, owners)
    loop(1, owners, lambda d: owner_copy(me, parts, owners, src, dst, us, ur, d).start())
    mine.wait()

    def finish(d):
        owner_copy(me, parts, owners, src, dst, us, ur, d, True).wait_recv()
        owner_copy(me, parts, owners, src, dst, us, ur, d).wait_send()

    loop(1, owners, finish)


def exchange(parts, groups, src):
    owners = groups * parts
    dma = pltpu.SemaphoreType.DMA
    return pl.pallas_call(
        functools.partial(exchange_kernel, parts, groups),
        out_shape=jax.ShapeDtypeStruct(src.shape, BF),
        in_specs=[pl.BlockSpec(memory_space=pl.ANY)],
        out_specs=pl.BlockSpec(memory_space=pl.ANY),
        scratch_shapes=[dma(()), dma((owners,)), dma((owners,))],
        compiler_params=pltpu.CompilerParams(collective_id=5, has_side_effects=True),
        cost_estimate=lasting(25),
    )(src)


def spread(parts, groups, xd, gd, inb, ovb):
    owners, rows_x = groups * parts, groups // 2
    dma = pltpu.SemaphoreType.DMA
    return pl.pallas_call(
        functools.partial(spread_kernel, parts, groups),
        out_shape=(
            jax.ShapeDtypeStruct(xd.shape, BF),
            jax.ShapeDtypeStruct((groups,) + gd.shape, BF),
            jax.ShapeDtypeStruct((owners,) + inb.shape, BF),
            jax.ShapeDtypeStruct((owners,) + ovb.shape, BF),
        ),
        in_specs=[pl.BlockSpec(memory_space=pl.ANY)] * 4,
        out_specs=(pl.BlockSpec(memory_space=pl.ANY),) * 4,
        scratch_shapes=[
            dma((4,)),
            dma((parts,)), dma((parts,)), dma((parts,)), dma((parts,)),
            dma((2, parts)), dma((2, parts)),
            dma((2, parts, rows_x)), dma((2, parts, rows_x)),
            dma((2, parts, rows_x)), dma((2, parts, rows_x)),
            dma((parts, rows_x)), dma((parts, rows_x)),
            dma((parts, rows_x)), dma((parts, rows_x)),
        ],
        compiler_params=pltpu.CompilerParams(collective_id=0, has_side_effects=True),
        cost_estimate=lasting(200),
    )(xd, gd, inb, ovb)


def group_gather_kernel(groups, chunks, src, out, local, ns, nr, ss, sr):
    dp, f = lax.axis_index("dp"), lax.axis_index("fsdp")
    rows_x = groups // 2
    x, core = lax.div(dp, 2), lax.rem(dp, 2)
    sib = x * 2 + 1 - core
    size = src.shape[0] // chunks
    mine = pltpu.make_async_copy(src, out.at[dp], local)
    mine.start()
    greet([(sib, f)] + [(wrap(x + dx, rows_x) * 2 + core, f) for dx in range(1, rows_x)])

    def part(ref, k):
        return ref.at[pl.ds(k * size, size)]

    def x_send(k, dx):
        to = wrap(x + dx, rows_x) * 2 + core
        return remote(part(src, k), part(out.at[dp], k), ns.at[k, dx], nr.at[k, dx], to, f)

    def x_recv(k, dx):
        came = wrap(x - dx, rows_x) * 2 + core
        ref = part(out.at[came], k)
        return remote(ref, ref, ns.at[k, dx], nr.at[k, dx], came, f)

    def sib_send(k, dx):
        came = wrap(x - dx, rows_x) * 2 + core
        ref = part(out.at[came], k)
        return remote(part(src, k) if dx == 0 else ref, ref, ss.at[k, dx], sr.at[k, dx], sib, f)

    def sib_recv(k, dx):
        came = wrap(x - dx, rows_x) * 2 + 1 - core
        ref = part(out.at[came], k)
        return remote(ref, ref, ss.at[k, dx], sr.at[k, dx], sib, f)

    for k in range(chunks):
        for dx in range(1, rows_x):
            x_send(k, dx).start()
    for k in range(chunks):
        sib_send(k, 0).start()
    for k in range(chunks):
        for dx in range(1, rows_x):
            x_recv(k, dx).wait_recv()
            sib_send(k, dx).start()
    mine.wait()
    for k in range(chunks):
        for dx in range(rows_x):
            sib_recv(k, dx).wait_recv()
            sib_send(k, dx).wait_send()
        for dx in range(1, rows_x):
            x_send(k, dx).wait_send()


def group_gather(groups, src):
    chunks, rows_x = 4, groups // 2
    dma = pltpu.SemaphoreType.DMA
    return pl.pallas_call(
        functools.partial(group_gather_kernel, groups, chunks),
        out_shape=jax.ShapeDtypeStruct((groups,) + src.shape, BF),
        in_specs=[pl.BlockSpec(memory_space=pl.ANY)],
        out_specs=pl.BlockSpec(memory_space=pl.ANY),
        scratch_shapes=[dma(())] + [dma((chunks, rows_x))] * 4,
        compiler_params=pltpu.CompilerParams(collective_id=1, has_side_effects=True),
        cost_estimate=lasting(45),
    )(src)


def ffn_back_kernel(
    parts, groups, chunks, streams,
    grad, act, dhid, w1, w2, base,
    out, dsum, back,
    ysum, leaving, loc, got, gone, wv, some, psib, sibr, xb, xrb,
    ll, ol, rs, rr, wl, sl, gss, gsr, gns, gnr, bs, br, bl,
):
    dp, f = lax.axis_index("dp"), lax.axis_index("fsdp")
    rows_x = groups // 2
    x, core = lax.div(dp, 2), lax.rem(dp, 2)
    sib = x * 2 + 1 - core
    p = ring_place(f, parts)
    nxt, prv = ring_index(p + 1, parts), ring_index(p - 1, parts)
    block, width = out.shape
    part, cut = width // streams, width // chunks
    count = dsum.shape[0]
    far = range(1, rows_x)

    def local_copy(h, s):
        c = ring_index(p - 1 - s if h % 2 == 0 else p + 1 + s, parts)
        return pltpu.make_async_copy(
            grad.at[
                pl.ds(pl.multiple_of(c * block, block), block), pl.ds(h * part, part)
            ],
            loc.at[lax.rem(s, 2), h], ll.at[lax.rem(s, 2), h],
        )

    w_loads = (
        pltpu.make_async_copy(w2, wv, wl.at[0]),
        pltpu.make_async_copy(w1, wv, wl.at[1]),
    )
    for s in range(2):
        for h in range(streams):
            local_copy(h, s).start()
    w_loads[0].start()
    greet(
        [(dp, wrap(f + d, parts)) for d in range(1, parts)]
        + [(sib, f)]
        + [(wrap(x + dx, rows_x) * 2 + core, f) for dx in range(1, rows_x)]
    )

    def ring_copy(h, s):
        return remote(
            gone.at[lax.rem(s, 2), h], got.at[h, s], rs.at[h, s], rr.at[h, s],
            dp, nxt if h % 2 == 0 else prv,
        )

    def out_copy(h):
        return pltpu.make_async_copy(
            gone.at[lax.rem(parts - 1, 2), h],
            out.at[:, pl.ds(h * part, part)],
            ol.at[h],
        )

    def pass_on(s):
        slot = lax.rem(s, 2)
        for h in range(streams):
            local_copy(h, s).wait()

            @pl.when(s >= 2)
            def _():
                ring_copy(h, s - 2).wait_send()

            @pl.when(s == 0)
            def _():
                gone[slot, h] = loc[slot, h]

            @pl.when(s > 0)
            def _():
                ring_copy(h, s - 1).wait_recv()
                gone[slot, h] = (
                    loc[slot, h].astype(F32) + got[h, s - 1].astype(F32)
                ).astype(BF)

            @pl.when(s < parts - 1)
            def _():
                ring_copy(h, s).start()

            @pl.when(s == parts - 1)
            def _():
                out_copy(h).start()

            @pl.when(s < parts - 2)
            def _():
                local_copy(h, s + 2).start()

    def cols(k):
        return pl.ds(pl.multiple_of(k * cut, cut), cut)

    def rows_of(dx, c):
        group = wrap(x + dx, rows_x) * 2 + (core if c == 0 else 1 - core)
        return pl.ds(pl.multiple_of(group * count, count), count)

    rows_in, totals = (act, dhid), (ysum, dsum)

    def sum_sib(which, k):
        return remote(
            psib.at[:, :, cols(k)], sibr.at[which, :, :, cols(k)],
            gss.at[which, k], gsr.at[which, k], sib, f,
        )

    def sum_x(which, dx, k):
        to = wrap(x + dx, rows_x) * 2 + core
        return remote(
            xb.at[which, dx - 1, :, cols(k)], xrb.at[which, dx - 1, :, cols(k)],
            gns.at[which, dx, k], gnr.at[which, dx, k], to, f,
        )

    def take_rows(which, c):
        copies = [
            pltpu.make_async_copy(
                rows_in[which].at[rows_of(dx, c)], some.at[pl.ds(dx * count, count)], sl.at[dx]
            )
            for dx in range(rows_x)
        ]
        for copy in copies:
            copy.start()
        for copy in copies:
            copy.wait()

    def other_side(which):
        take_rows(which, 1)

        def one(k):
            psib[:, :, cols(k)] = (
                jnp.dot(some[...], wv[:, cols(k)], preferred_element_type=F32)
                .astype(BF)
                .reshape(rows_x, count, cut)
            )
            sum_sib(which, k).start()

        loop(0, chunks, one)

    def own_side(which):
        take_rows(which, 0)

        def one(k):
            here = jnp.dot(some[...], wv[:, cols(k)], preferred_element_type=F32)
            sum_sib(which, k).wait_recv()
            here = here.reshape(rows_x, count, cut) + sibr[which, :, :, cols(k)].astype(F32)
            for dx in far:
                xb[which, dx - 1, :, cols(k)] = here[dx].astype(BF)
                sum_x(which, dx, k).start()
            totals[which][:, cols(k)] = here[0]

        loop(0, chunks, one)

    def collect(which):
        def one(k):
            for dx in far:
                sum_x(which, dx, k).wait_recv()
                totals[which][:, cols(k)] += xrb[which, dx - 1, :, cols(k)].astype(F32)

        loop(0, chunks, one)

    def back_copy(d, came=False):
        return deal_copy(parts, dp, f, leaving, back, bs, br, d, came)

    def own_back():
        return pltpu.make_async_copy(leaving.at[f], back.at[f], bl)

    def send_back():
        piece = count // parts

        def one(j):
            rows = pl.ds(pl.multiple_of(j * piece, piece), piece)
            leaving[j] = (base[rows, :] + ysum[rows, :]).astype(BF)

        loop(0, parts, one)
        own_back().start()
        loop(1, parts, lambda d: back_copy(d).start())

    def sent_sib(which):
        loop(0, chunks, lambda k: sum_sib(which, k).wait_send())

    def sent_x(which):
        for dx in far:
            loop(0, chunks, lambda k: sum_x(which, dx, k).wait_send())

    def step(s):
        pass_on(s)

        @pl.when(s == 0)
        def _():
            w_loads[0].wait()
            other_side(0)

        @pl.when(s == 1)
        def _():
            own_side(0)
            w_loads[1].start()

        @pl.when(s == 2)
        def _():
            w_loads[1].wait()
            sent_sib(0)
            other_side(1)

        @pl.when(s == 3)
        def _():
            own_side(1)

        @pl.when(s == 4)
        def _():
            collect(0)
            send_back()

    loop(0, parts, step)
    collect(1)
    for h in range(streams):
        ring_copy(h, parts - 2).wait_send()
        out_copy(h).wait()
    sent_sib(1)
    sent_x(0)
    sent_x(1)
    own_back().wait()

    def returned(d):
        back_copy(d, True).wait_recv()
        back_copy(d).wait_send()

    loop(1, parts, returned)


def ffn_back(parts, groups, grad, act, dhid, w1, w2, base):
    chunks, streams, rows_x = 4, 4, groups // 2
    units, width = w1.shape
    count = act.shape[0] // groups
    block, part, piece = units // parts, width // streams, count // parts
    dma = pltpu.SemaphoreType.DMA
    hbm = pl.BlockSpec(memory_space=pl.ANY)
    vmem = pl.BlockSpec(memory_space=pltpu.VMEM)
    return pl.pallas_call(
        functools.partial(ffn_back_kernel, parts, groups, chunks, streams),
        out_shape=(
            jax.ShapeDtypeStruct((block, width), BF),
            jax.ShapeDtypeStruct((count, width), F32),
            jax.ShapeDtypeStruct((parts, piece, width), BF),
        ),
        in_specs=[hbm] * 5 + [vmem],
        out_specs=(hbm, vmem, hbm),
        scratch_shapes=[
            pltpu.VMEM((count, width), F32),
            pltpu.VMEM((parts, piece, width), BF),
            pltpu.VMEM((2, streams, block, part), BF),
            pltpu.VMEM((streams, parts - 1, block, part), BF),
            pltpu.VMEM((2, streams, block, part), BF),
            pltpu.VMEM((units, width), BF),
            pltpu.VMEM((rows_x * count, units), BF),
            pltpu.VMEM((rows_x, count, width), BF),
            pltpu.VMEM((2, rows_x, count, width), BF),
            pltpu.VMEM((2, rows_x - 1, count, width), BF),
            pltpu.VMEM((2, rows_x - 1, count, width), BF),
            dma((2, streams)), dma((streams,)),
            dma((streams, parts)), dma((streams, parts)), dma((2,)), dma((rows_x,)),
            dma((2, chunks)), dma((2, chunks)),
            dma((2, rows_x, chunks)), dma((2, rows_x, chunks)),
            dma((parts,)), dma((parts,)), dma(()),
        ],
        compiler_params=pltpu.CompilerParams(
            collective_id=3, has_side_effects=True, vmem_limit_bytes=60 * 2**20
        ),
        cost_estimate=lasting(130),
    )(grad, act, dhid, w1, w2, base)


def finish_kernel(
    parts, groups,
    grad_a, grad_b, gx, upg, vec,
    total_a, total_b, gx_out, upg_out, vec_out,
    loc_a, loc_b, sibr_a, sibr_b, xb_a, xb_b, xrb_a, xrb_b, got_a, got_b, gone_a, gone_b,
    local, ls, ss, sr, ns, nr, rs, rr, bs, br, us, ur, vs, vr,
):
    dp, f = lax.axis_index("dp"), lax.axis_index("fsdp")
    owners, rows_x = groups * parts, groups // 2
    x, core = lax.div(dp, 2), lax.rem(dp, 2)
    sib = x * 2 + 1 - core
    me = dp * parts + f
    p = ring_place(f, parts)
    nxt, prv = ring_index(p + 1, parts), ring_index(p - 1, parts)
    grads, total = (grad_a, grad_b), (total_a, total_b)
    loc, sibr, xb, xrb = (loc_a, loc_b), (sibr_a, sibr_b), (xb_a, xb_b), (xrb_a, xrb_b)
    got, gone = (got_a, got_b), (gone_a, gone_b)
    mine = [
        pltpu.make_async_copy(gx.at[f], gx_out.at[f], local.at[0]),
        pltpu.make_async_copy(vec.at[me], vec_out.at[me], local.at[1]),
        pltpu.make_async_copy(upg.at[me], upg_out.at[me], local.at[2]),
    ]
    for copy in mine:
        copy.start()
    greet_all(me, parts, owners)

    def chunk(h, s):
        return ring_index(p - 1 - s if h == 0 else p + 1 + s, parts)

    def sib_copy(h, s):
        piece = grads[h].at[:, 1 - core, chunk(h, s)]
        return remote(piece, sibr[h].at[s], ss.at[h, s], sr.at[h, s], sib, f)

    def own_copy(h, s):
        piece = grads[h].at[:, core, chunk(h, s)]
        return pltpu.make_async_copy(piece, loc[h].at[s], ls.at[h, s])

    def x_copy(h, s, dx):
        to = wrap(x + dx, rows_x) * 2 + core
        return remote(
            xb[h].at[s, dx - 1], xrb[h].at[s, dx - 1], ns.at[h, s, dx], nr.at[h, s, dx], to, f
        )

    def ring_copy(h, s):
        return remote(
            gone[h].at[s], got[h].at[s], rs.at[h, s], rr.at[h, s], dp, nxt if h == 0 else prv
        )

    def gx_copies(d, came=False):
        return deal_copy(parts, dp, f, gx, gx_out, bs, br, d, came)

    def upg_copies(d, came=False):
        return owner_copy(me, parts, owners, upg, upg_out, us, ur, d, came)

    def vec_copies(d, came=False):
        return owner_copy(me, parts, owners, vec, vec_out, vs, vr, d, came)

    def begin(s):
        for h in range(2):
            sib_copy(h, s).start()
            own_copy(h, s).start()

    def others(d):
        upg_copies(d).start()
        vec_copies(d).start()

    def returns(d):
        gx_copies(d).start()

    def pair(s):
        for h in range(2):
            sib_copy(h, s).wait_recv()
            own_copy(h, s).wait()
            for dx in range(1, rows_x):
                to = wrap(x + dx, rows_x)
                xb[h][s, dx - 1] = (sibr[h][s, to].astype(F32) + loc[h][s, to].astype(F32)).astype(BF)
                x_copy(h, s, dx).start()

    def step(s):
        for h in range(2):
            for dx in range(1, rows_x):
                x_copy(h, s, dx).wait_recv()

            def value():
                here = sibr[h][s, x].astype(F32) + loc[h][s, x].astype(F32)
                for dx in range(1, rows_x):
                    here = here + xrb[h][s, dx - 1].astype(F32)
                return here

            @pl.when(s == 0)
            def _():
                gone[h][s] = value().astype(BF)
                ring_copy(h, s).start()

            @pl.when((s > 0) & (s < parts - 1))
            def _():
                ring_copy(h, s - 1).wait_recv()
                gone[h][s] = (value() + got[h][s - 1].astype(F32)).astype(BF)
                ring_copy(h, s).start()

            @pl.when(s == parts - 1)
            def _():
                ring_copy(h, s - 1).wait_recv()
                total[h][...] = value() + got[h][s - 1].astype(F32)

    loop(0, parts, begin)
    loop(1, parts, returns)
    loop(1, owners, others)
    loop(0, parts, pair)
    loop(0, parts, step)

    def finish(s):
        for h in range(2):
            sib_copy(h, s).wait_send()
            for dx in range(1, rows_x):
                x_copy(h, s, dx).wait_send()

            @pl.when(s < parts - 1)
            def _():
                ring_copy(h, s).wait_send()

        @pl.when(s > 0)
        def _():
            gx_copies(s, True).wait_recv()
            gx_copies(s).wait_send()

    loop(0, parts, finish)

    def owner_finish(d):
        for copies in (upg_copies, vec_copies):
            copies(d, True).wait_recv()
            copies(d).wait_send()

    loop(1, owners, owner_finish)
    for copy in mine:
        copy.wait()


def finish_sums(parts, groups, grad_a, grad_b, gx, upg, vec):
    owners, rows_x = groups * parts, groups // 2
    rows = grad_a.shape[3]
    widths = (grad_a.shape[4], grad_b.shape[4])
    dma = pltpu.SemaphoreType.DMA
    hbm = pl.BlockSpec(memory_space=pl.ANY)
    return pl.pallas_call(
        functools.partial(finish_kernel, parts, groups),
        out_shape=(
            jax.ShapeDtypeStruct((rows, widths[0]), F32),
            jax.ShapeDtypeStruct((rows, widths[1]), F32),
            jax.ShapeDtypeStruct(gx.shape, BF),
            jax.ShapeDtypeStruct(upg.shape, BF),
            jax.ShapeDtypeStruct(vec.shape, F32),
        ),
        in_specs=[hbm] * 5,
        out_specs=(pl.BlockSpec(memory_space=pltpu.VMEM),) * 2 + (hbm,) * 3,
        scratch_shapes=[
            *(
                pltpu.VMEM(lead + (rows, width), BF)
                for lead in (
                    (parts, rows_x), (parts, rows_x), (parts, rows_x - 1), (parts, rows_x - 1),
                    (parts,), (parts,),
                )
                for width in widths
            ),
            dma((3,)),
            dma((2, parts)), dma((2, parts)), dma((2, parts)),
            dma((2, parts, rows_x)), dma((2, parts, rows_x)),
            dma((2, parts)), dma((2, parts)),
            dma((parts,)), dma((parts,)),
            dma((owners,)), dma((owners,)), dma((owners,)), dma((owners,)),
        ],
        compiler_params=pltpu.CompilerParams(
            collective_id=4, has_side_effects=True, vmem_limit_bytes=60 * 2**20
        ),
        cost_estimate=lasting(1),
    )(grad_a, grad_b, gx, upg, vec)


def shards(
    tokens,
    cotangent,
    lengths,
    routing,
    in_weight,
    in_first,
    in_second,
    out_weight,
    out_first,
    out_second,
    up_weight,
    up_first,
    up_second,
    down_weight,
    down_first,
    down_second,
    vectors,
    vector_first,
    vector_second,
):
    bf = jnp.bfloat16
    heads = D // HD
    count = tokens.shape[0]
    parts = lax.axis_size("fsdp")
    groups = lax.axis_size("dp")
    both = ("dp", "fsdp")
    piece = count // parts
    width_in = D + 2 * HD
    slots = jnp.arange(parts, dtype=jnp.int32)
    order = routing[0]
    inverse = jnp.sum(jnp.where(order[:, None] == slots[None, :], slots[:, None], 0), axis=0)

    def deal(array):
        return jnp.take(array.reshape(parts, piece, D), inverse, axis=0)

    def undeal(array):
        return jnp.take(array, order, axis=0).reshape(count, D)

    rows = in_weight.shape[0]
    owners = groups * parts
    out_vec = jnp.concatenate(
        [out_weight.astype(bf), jnp.pad(vectors.astype(bf), ((0, 0), (0, 128 - NVEC)))], axis=1
    )
    up_pieces = up_weight.astype(bf).reshape(rows, owners, FF // owners).transpose(1, 0, 2)
    up_block, dealt, dealt_grad, out_vec = lax.optimization_barrier(
        (exchange(parts, groups, up_pieces), deal(tokens), deal(cotangent), out_vec)
    )
    x_dealt, grad_dealt, whole_in, whole_out = spread(
        parts, groups, dealt, dealt_grad, in_weight.astype(bf), out_vec
    )
    inputs_here = x_dealt.reshape(count, D)
    grad_all = grad_dealt.reshape(groups * count, D)
    grad_here = lax.dynamic_index_in_dim(
        grad_dealt, lax.axis_index("dp"), 0, keepdims=False
    ).reshape(count, D)
    whole_in = whole_in.reshape(D, width_in)
    whole_out = whole_out.reshape(D, D + 128)
    part_down = lax.all_gather(down_weight.astype(bf), "fsdp", axis=0, tiled=True)
    part_up = lax.all_gather(up_block.reshape(D, FF // owners).T, "fsdp", axis=0, tiled=True)

    table = whole_out[:, D : D + NVEC].astype(jnp.float32)
    whole_out = whole_out[:, :D]
    gain_one = table[:, 0]
    shift_one = table[:, 1]
    query_bias = table[:, 2]
    branch_bias = table[:, 3]
    gain_two = table[:, 4]
    shift_two = table[:, 5]
    output_bias = table[:, 6]
    hidden_bias = table[:, 7:].T.reshape(FF)
    ff_here = FF // groups
    ff_start = lax.axis_index("dp") * ff_here
    hidden_bias_here = lax.dynamic_slice(hidden_bias, (ff_start,), (ff_here,))
    allowed = segment_mask(lengths[0], count)
    scale = 1.0 / math.sqrt(HD)
    inputs = inputs_here.astype(jnp.float32)
    norm_one_b = layer_norm(inputs, gain_one, shift_one).astype(bf)
    mixed = jnp.dot(norm_one_b, whole_in, preferred_element_type=jnp.float32)
    query_b = (mixed[:, :D] + query_bias).astype(bf)
    keys_b = mixed[:, D : D + HD].astype(bf)
    values_b = mixed[:, D + HD :].astype(bf)
    query_heads = query_b.reshape(count, heads, HD)

    def score_table():
        raw = (
            jnp.einsum("thd,sd->hts", query_heads, keys_b, preferred_element_type=jnp.float32)
            * scale
        )
        return jnp.where(allowed[None], raw, -1e30)

    scores = score_table()
    top = jnp.max(scores, axis=-1, keepdims=True)
    expo = jnp.exp(scores - top)
    total = jnp.sum(expo, axis=-1, keepdims=True)
    logsum = top + jnp.log(total)
    probs_b = (expo / total).astype(bf)
    attended_b = (
        jnp.einsum("hts,sd->thd", probs_b, values_b, preferred_element_type=jnp.float32)
        .reshape(count, D)
        .astype(bf)
    )
    middle = inputs + (
        jnp.dot(attended_b, whole_out, preferred_element_type=jnp.float32) + branch_bias
    )
    norm_two_b = layer_norm(middle, gain_two, shift_two).astype(bf)

    fused = parts == 8 and groups == 4
    if fused:
        norm_all = group_gather(groups, norm_two_b).reshape(groups * count, D)
    else:
        norm_all = lax.all_gather(norm_two_b, "dp", axis=0, tiled=True)
    hidden = contract_cols(norm_all, part_up) + hidden_bias_here
    grad_active = contract_cols(grad_all, part_down)
    gelu_value, gelu_pull = jax.vjp(gelu_tanh, hidden)
    active_b = gelu_value.astype(bf)
    grad_hidden_b = gelu_pull(grad_active)[0].astype(bf)
    down_parts = contract_rows(active_b, grad_all).astype(bf)
    up_parts = contract_rows(grad_hidden_b, norm_all).astype(bf)
    down_parts, up_parts = lax.optimization_barrier((down_parts, up_parts))
    if fused:
        up_grad_block, grad_norm_two, back_result = ffn_back(
            parts, groups, up_parts, active_b, grad_hidden_b, part_up, part_down,
            middle + output_bias,
        )
    else:
        up_grad_block = lax.psum_scatter(up_parts, "fsdp", scatter_dimension=0, tiled=True)
        grad_norm_two = lax.psum_scatter(
            jnp.dot(grad_hidden_b, part_up, preferred_element_type=jnp.float32).astype(bf),
            "dp", scatter_dimension=0, tiled=True,
        ).astype(jnp.float32)
        branch_two = lax.psum_scatter(
            jnp.dot(active_b, part_down, preferred_element_type=jnp.float32).astype(bf),
            "dp", scatter_dimension=0, tiled=True,
        ).astype(jnp.float32)
        back_result = lax.all_to_all(
            (middle + (branch_two + output_bias)).astype(bf),
            "fsdp", split_axis=0, concat_axis=0, tiled=True,
        ).reshape(parts, piece, D)
    down_parts, up_grad_block = lax.optimization_barrier((down_parts, up_grad_block))
    down_grad = lax.psum_scatter(down_parts, "fsdp", scatter_dimension=0, tiled=True)

    grad_y = grad_here.astype(jnp.float32)
    norm_value_two, pull_two = jax.vjp(layer_norm, middle, gain_two, shift_two)
    grad_middle_norm, grad_gain_two, grad_shift_two = pull_two(grad_norm_two)
    grad_middle = grad_y + grad_middle_norm
    grad_branch_b = grad_middle.astype(bf)
    grad_attended_b = contract_cols(grad_branch_b, whole_out).astype(bf)
    grad_heads = grad_attended_b.reshape(count, heads, HD)
    probs = jnp.exp(score_table() - logsum)
    probs_again_b = probs.astype(bf)
    grad_probs = jnp.einsum("thd,sd->hts", grad_heads, values_b, preferred_element_type=jnp.float32)
    grad_values_b = jnp.einsum(
        "hts,thd->sd", probs_again_b, grad_heads, preferred_element_type=jnp.float32
    ).astype(bf)
    weighted = jnp.sum(probs * grad_probs, axis=-1, keepdims=True)
    grad_scores_b = (probs * (grad_probs - weighted)).astype(bf)
    grad_query_b = (
        (
            jnp.einsum("hts,sd->thd", grad_scores_b, keys_b, preferred_element_type=jnp.float32)
            * scale
        )
        .reshape(count, D)
        .astype(bf)
    )
    grad_keys_b = (
        jnp.einsum("hts,thd->sd", grad_scores_b, query_heads, preferred_element_type=jnp.float32)
        * scale
    ).astype(bf)
    grad_mixed_b = jnp.concatenate([grad_query_b, grad_keys_b, grad_values_b], axis=1)
    grad_norm_one = contract_cols(grad_mixed_b, whole_in)
    norm_value_one, pull_one = jax.vjp(layer_norm, inputs, gain_one, shift_one)
    grad_inputs_norm, grad_gain_one, grad_shift_one = pull_one(grad_norm_one)
    grad_inputs = grad_middle + grad_inputs_norm
    hidden_sums = jnp.sum(grad_hidden_b.astype(jnp.float32), axis=0)
    hidden_whole = lax.dynamic_update_slice(
        jnp.zeros((FF,), jnp.float32), hidden_sums, (ff_start,)
    )
    vector_grad = jnp.concatenate(
        [
            jnp.stack(
                [
                    grad_gain_one,
                    grad_shift_one,
                    jnp.sum(grad_query_b.astype(jnp.float32), axis=0),
                    jnp.sum(grad_branch_b.astype(jnp.float32), axis=0),
                    grad_gain_two,
                    grad_shift_two,
                    jnp.sum(grad_y, axis=0),
                ],
                axis=0,
            ),
            hidden_whole.reshape(FF // D, D),
        ],
        axis=0,
    )
    vector_grad = vector_grad.reshape(NVEC, owners, rows).transpose(1, 0, 2)
    vector_grad = jnp.pad(vector_grad, ((0, 0), (0, 16 - NVEC), (0, 128 - rows)))
    grad_in, grad_out, back_grad, grad_up, vector_sum = finish_sums(
        parts,
        groups,
        contract_rows(norm_one_b, grad_mixed_b)
        .astype(bf)
        .reshape(groups // 2, 2, parts, rows, width_in),
        contract_rows(attended_b, grad_branch_b).astype(bf).reshape(groups // 2, 2, parts, rows, D),
        grad_inputs.astype(bf).reshape(parts, piece, D),
        up_grad_block.T.astype(bf).reshape(owners, rows, FF // owners),
        vector_grad,
    )
    grad_up = grad_up.transpose(1, 0, 2).reshape(rows, FF)
    vector_sum = jnp.sum(vector_sum, axis=0)
    grad_vec = vector_sum[:NVEC, :rows].T
    in_new = adam_update(in_weight, in_first, in_second, grad_in, 1.0 / math.sqrt(D), decay_rate)
    out_new = adam_update(
        out_weight, out_first, out_second, grad_out, 1.0 / math.sqrt(D * 8 // TOK_DEV), decay_rate
    )
    up_new = adam_update(up_weight, up_first, up_second, grad_up, 1.0 / math.sqrt(D), decay_rate)
    down_new = adam_update(
        down_weight, down_first, down_second, down_grad, 1.0 / math.sqrt(FF), decay_rate
    )
    vec_new = adam_update(vectors, vector_first, vector_second, grad_vec, 0.1, 0.0)
    return (undeal(back_result), undeal(back_grad)) + in_new + out_new + up_new + down_new + vec_new


def solution(mesh):
    spec = P(("dp", "fsdp"), None)
    return jax.shard_map(
        shards,
        mesh=mesh,
        in_specs=(spec,) * 19,
        out_specs=(spec,) * 17,
        check_vma=False,
    )
```

```python
import functools
import math

import jax
import jax.numpy as jnp
from jax import lax
from jax.experimental import pallas as pl
from jax.experimental.pallas import tpu as pltpu
from jax.sharding import PartitionSpec as P

D = 2048
FF = 8192
HD = 128
TOK_DEV = 384
STEP = 5
NVEC = 11


eps_norm = 1e-05
beta_one = 0.5
beta_two = 0.5
adam_eps = 1e-08
decay_rate = 0.1


def layer_norm(values, gain, shift):
    centered = values - jnp.mean(values, axis=-1, keepdims=True)
    scaled = centered * lax.rsqrt(jnp.mean(centered * centered, axis=-1, keepdims=True) + eps_norm)
    return scaled * gain + shift


def gelu_tanh(values):
    return (
        0.5
        * values
        * (1.0 + jnp.tanh(0.7978845608028654 * (values + 0.044715 * values * values * values)))
    )


def segment_mask(sizes, count):
    ends = jnp.cumsum(sizes)
    places = jnp.arange(count, dtype=jnp.int32)
    labels = jnp.sum((places[:, None] >= ends[None, :]).astype(jnp.int32), axis=1)
    return (labels[:, None] == labels[None, :]) & (places[None, :] <= places[:, None])


def adam_update(weight, first, second, grad, rate, decay):
    grad = grad.astype(jnp.float32)
    first_new = beta_one * first + (1.0 - beta_one) * grad
    second_new = beta_two * second + (1.0 - beta_two) * grad * grad
    fix_one = 1.0 - beta_one**STEP
    fix_two = 1.0 - beta_two**STEP
    step_size = first_new / fix_one / (jnp.sqrt(second_new / fix_two) + adam_eps)
    weight_new = weight - rate * (step_size + decay * weight)
    return (weight_new, first_new, second_new)


def contract_rows(left, right):
    return lax.dot_general(
        left, right, (((0,), (0,)), ((), ())), preferred_element_type=jnp.float32
    )


def contract_cols(left, right):
    return lax.dot_general(
        left, right, (((1,), (1,)), ((), ())), preferred_element_type=jnp.float32
    )


MESH = pl.DeviceIdType.MESH
F32 = jnp.float32
BF = jnp.bfloat16


def wrap(value, count):
    return lax.rem(value + 2 * count, count)


def ring_place(index, parts):
    if parts != 8:
        return index
    z, y = lax.div(index, 2), lax.rem(index, 2)
    return z + y * (7 - 2 * z)


def ring_index(place, parts):
    place = wrap(place, parts)
    if parts != 8:
        return place
    back = lax.div(place, 4)
    return (1 - back) * 2 * place + back * (15 - 2 * place)


def remote(src, dst, send, recv, dp, fs):
    return pltpu.make_async_remote_copy(
        src_ref=src, dst_ref=dst, send_sem=send, recv_sem=recv, device_id=(dp, fs), device_id_type=MESH
    )


def lasting(micros):
    return pl.CostEstimate(
        flops=int(micros * 1.1e9), bytes_accessed=int(micros * 3.3e6), transcendentals=0
    )


def greet(targets):
    barrier = pltpu.get_barrier_semaphore()
    for dp, fs in targets:
        pl.semaphore_signal(barrier, inc=1, device_id=(dp, fs), device_id_type=MESH)
    pl.semaphore_wait(barrier, len(targets))


def greet_all(me, parts, owners):
    barrier = pltpu.get_barrier_semaphore()

    def one(i, carry):
        peer = wrap(me + i, owners)
        pl.semaphore_signal(
            barrier, inc=1, device_id=(lax.div(peer, parts), lax.rem(peer, parts)), device_id_type=MESH
        )
        return carry

    lax.fori_loop(1, owners, one, 0)
    pl.semaphore_wait(barrier, owners - 1)


def loop(low, high, body):
    def one(i, carry):
        body(i)
        return carry

    lax.fori_loop(low, high, one, 0)


def deal_copy(parts, dp, f, src, dst, send, recv, d, came=False):
    to = wrap(f + d, parts)
    place = wrap(f - d, parts) if came else f
    return remote(src.at[to], dst.at[place], send.at[d], recv.at[d], dp, to)


def owner_copy(me, parts, owners, src, dst, send, recv, d, came=False):
    to = wrap(me + d, owners)
    place = wrap(me - d, owners) if came else me
    return remote(
        src.at[to], dst.at[place], send.at[d], recv.at[d], lax.div(to, parts), lax.rem(to, parts)
    )


def spread_kernel(
    parts, groups,
    xd, gd, inb, ovb,
    xo, eall, win, wov,
    local, xs, xr, gs, gr, rs, rr, ns, nr, ss, sr, ens, enr, ess, esr,
):
    dp, f = lax.axis_index("dp"), lax.axis_index("fsdp")
    owners, rows_x = groups * parts, groups // 2
    x, core = lax.div(dp, 2), lax.rem(dp, 2)
    sib = x * 2 + 1 - core
    me = dp * parts + f
    p = ring_place(f, parts)
    nxt, prv = ring_index(p + 1, parts), ring_index(p - 1, parts)
    whole = (win, wov)
    mine = [
        pltpu.make_async_copy(inb, win.at[me], local.at[0]),
        pltpu.make_async_copy(ovb, wov.at[me], local.at[1]),
        pltpu.make_async_copy(xd.at[f], xo.at[f], local.at[2]),
        pltpu.make_async_copy(gd.at[f], eall.at[dp, f], local.at[3]),
    ]
    for copy in mine:
        copy.start()
    greet(
        [(dp, wrap(f + d, parts)) for d in range(1, parts)]
        + [(sib, f)]
        + [(wrap(x + dx, rows_x) * 2 + core, f) for dx in range(1, rows_x)]
    )
    for copy in mine:
        copy.wait()

    def x_copies(d, came=False):
        return deal_copy(parts, dp, f, xd, xo, xs, xr, d, came)

    def g_copies(d, came=False):
        return deal_copy(parts, dp, f, gd, eall.at[dp], gs, gr, d, came)

    def origin(h, s):
        return ring_index(p - s if h == 0 else p + s, parts)

    def ring_send(h, s):
        ref = whole[h].at[dp * parts + origin(h, s)]
        return remote(ref, ref, rs.at[h, s], rr.at[h, s], dp, nxt if h == 0 else prv)

    def ring_recv(h, s):
        ref = whole[h].at[dp * parts + origin(h, s)]
        return remote(ref, ref, rs.at[h, s - 1], rr.at[h, s - 1], dp, nxt if h == 0 else prv)

    def x_send(h, s, dx):
        ref = whole[h].at[dp * parts + origin(h, s)]
        to = wrap(x + dx, rows_x) * 2 + core
        return remote(ref, ref, ns.at[h, s, dx], nr.at[h, s, dx], to, f)

    def x_recv(h, s, dx):
        came = wrap(x - dx, rows_x) * 2 + core
        ref = whole[h].at[came * parts + origin(h, s)]
        return remote(ref, ref, ns.at[h, s, dx], nr.at[h, s, dx], came, f)

    def sib_send(h, s, dx):
        came = wrap(x - dx, rows_x) * 2 + core
        ref = whole[h].at[came * parts + origin(h, s)]
        return remote(ref, ref, ss.at[h, s, dx], sr.at[h, s, dx], sib, f)

    def sib_recv(h, s, dx):
        came = wrap(x - dx, rows_x) * 2 + 1 - core
        ref = whole[h].at[came * parts + origin(h, s)]
        return remote(ref, ref, ss.at[h, s, dx], sr.at[h, s, dx], sib, f)

    def e_x_send(d, dx):
        ref = eall.at[dp, wrap(f - d, parts)]
        to = wrap(x + dx, rows_x) * 2 + core
        return remote(ref, ref, ens.at[d, dx], enr.at[d, dx], to, f)

    def e_x_recv(d, dx):
        came = wrap(x - dx, rows_x) * 2 + core
        ref = eall.at[came, wrap(f - d, parts)]
        return remote(ref, ref, ens.at[d, dx], enr.at[d, dx], came, f)

    def e_sib_send(d, dx):
        came = wrap(x - dx, rows_x) * 2 + core
        ref = eall.at[came, wrap(f - d, parts)]
        return remote(ref, ref, ess.at[d, dx], esr.at[d, dx], sib, f)

    def e_sib_recv(d, dx):
        came = wrap(x - dx, rows_x) * 2 + 1 - core
        ref = eall.at[came, wrap(f - d, parts)]
        return remote(ref, ref, ess.at[d, dx], esr.at[d, dx], sib, f)

    def ring_step(s):
        for h in range(2):
            @pl.when(s > 0)
            def _():
                ring_recv(h, s).wait_recv()

            @pl.when(s < parts - 1)
            def _():
                ring_send(h, s).start()

            for dx in range(1, rows_x):
                x_send(h, s, dx).start()
            sib_send(h, s, 0).start()

    def e_step(d):
        @pl.when(d > 0)
        def _():
            g_copies(d, True).wait_recv()

        for dx in range(1, rows_x):
            e_x_send(d, dx).start()
        e_sib_send(d, 0).start()

    def relay(s):
        for h in range(2):
            for dx in range(1, rows_x):
                x_recv(h, s, dx).wait_recv()
                sib_send(h, s, dx).start()

    def e_relay(d):
        for dx in range(1, rows_x):
            e_x_recv(d, dx).wait_recv()
            e_sib_send(d, dx).start()

    def main(s):
        @pl.when(s < parts)
        def _():
            ring_step(s)

        @pl.when(s < parts - 1)
        def _():
            x_copies(s + 1).start()
            g_copies(s + 1).start()

        @pl.when((s >= 1) & (s <= parts))
        def _():
            e_step(s - 1)

        @pl.when((s >= 2) & (s < parts + 2))
        def _():
            relay(s - 2)

        @pl.when(s >= 3)
        def _():
            e_relay(s - 3)

    loop(0, parts + 3, main)

    def finish(s):
        for h in range(2):
            @pl.when(s < parts - 1)
            def _():
                ring_send(h, s).wait_send()

            for dx in range(1, rows_x):
                x_send(h, s, dx).wait_send()
            for dx in range(rows_x):
                sib_recv(h, s, dx).wait_recv()
                sib_send(h, s, dx).wait_send()
        for dx in range(1, rows_x):
            e_x_send(s, dx).wait_send()
        for dx in range(rows_x):
            e_sib_recv(s, dx).wait_recv()
            e_sib_send(s, dx).wait_send()

        @pl.when(s > 0)
        def _():
            x_copies(s, True).wait_recv()
            x_copies(s).wait_send()
            g_copies(s).wait_send()

    loop(0, parts, finish)


def exchange_kernel(parts, groups, src, dst, local, us, ur):
    dp, f = lax.axis_index("dp"), lax.axis_index("fsdp")
    owners = groups * parts
    me = dp * parts + f
    mine = pltpu.make_async_copy(src.at[me], dst.at[me], local)
    mine.start()
    greet_all(me, parts, owners)
    loop(1, owners, lambda d: owner_copy(me, parts, owners, src, dst, us, ur, d).start())
    mine.wait()

    def finish(d):
        owner_copy(me, parts, owners, src, dst, us, ur, d, True).wait_recv()
        owner_copy(me, parts, owners, src, dst, us, ur, d).wait_send()

    loop(1, owners, finish)


def exchange(parts, groups, src):
    owners = groups * parts
    dma = pltpu.SemaphoreType.DMA
    return pl.pallas_call(
        functools.partial(exchange_kernel, parts, groups),
        out_shape=jax.ShapeDtypeStruct(src.shape, BF),
        in_specs=[pl.BlockSpec(memory_space=pl.ANY)],
        out_specs=pl.BlockSpec(memory_space=pl.ANY),
        scratch_shapes=[dma(()), dma((owners,)), dma((owners,))],
        compiler_params=pltpu.CompilerParams(collective_id=5, has_side_effects=True),
        cost_estimate=lasting(25),
    )(src)


def spread(parts, groups, xd, gd, inb, ovb):
    owners, rows_x = groups * parts, groups // 2
    dma = pltpu.SemaphoreType.DMA
    return pl.pallas_call(
        functools.partial(spread_kernel, parts, groups),
        out_shape=(
            jax.ShapeDtypeStruct(xd.shape, BF),
            jax.ShapeDtypeStruct((groups,) + gd.shape, BF),
            jax.ShapeDtypeStruct((owners,) + inb.shape, BF),
            jax.ShapeDtypeStruct((owners,) + ovb.shape, BF),
        ),
        in_specs=[pl.BlockSpec(memory_space=pl.ANY)] * 4,
        out_specs=(pl.BlockSpec(memory_space=pl.ANY),) * 4,
        scratch_shapes=[
            dma((4,)),
            dma((parts,)), dma((parts,)), dma((parts,)), dma((parts,)),
            dma((2, parts)), dma((2, parts)),
            dma((2, parts, rows_x)), dma((2, parts, rows_x)),
            dma((2, parts, rows_x)), dma((2, parts, rows_x)),
            dma((parts, rows_x)), dma((parts, rows_x)),
            dma((parts, rows_x)), dma((parts, rows_x)),
        ],
        compiler_params=pltpu.CompilerParams(collective_id=0, has_side_effects=True),
        cost_estimate=lasting(200),
    )(xd, gd, inb, ovb)


def group_gather_kernel(groups, chunks, src, out, local, ns, nr, ss, sr):
    dp, f = lax.axis_index("dp"), lax.axis_index("fsdp")
    rows_x = groups // 2
    x, core = lax.div(dp, 2), lax.rem(dp, 2)
    sib = x * 2 + 1 - core
    size = src.shape[0] // chunks
    mine = pltpu.make_async_copy(src, out.at[dp], local)
    mine.start()
    greet([(sib, f)] + [(wrap(x + dx, rows_x) * 2 + core, f) for dx in range(1, rows_x)])

    def part(ref, k):
        return ref.at[pl.ds(k * size, size)]

    def x_send(k, dx):
        to = wrap(x + dx, rows_x) * 2 + core
        return remote(part(src, k), part(out.at[dp], k), ns.at[k, dx], nr.at[k, dx], to, f)

    def x_recv(k, dx):
        came = wrap(x - dx, rows_x) * 2 + core
        ref = part(out.at[came], k)
        return remote(ref, ref, ns.at[k, dx], nr.at[k, dx], came, f)

    def sib_send(k, dx):
        came = wrap(x - dx, rows_x) * 2 + core
        ref = part(out.at[came], k)
        return remote(part(src, k) if dx == 0 else ref, ref, ss.at[k, dx], sr.at[k, dx], sib, f)

    def sib_recv(k, dx):
        came = wrap(x - dx, rows_x) * 2 + 1 - core
        ref = part(out.at[came], k)
        return remote(ref, ref, ss.at[k, dx], sr.at[k, dx], sib, f)

    for k in range(chunks):
        for dx in range(1, rows_x):
            x_send(k, dx).start()
    for k in range(chunks):
        sib_send(k, 0).start()
    for k in range(chunks):
        for dx in range(1, rows_x):
            x_recv(k, dx).wait_recv()
            sib_send(k, dx).start()
    mine.wait()
    for k in range(chunks):
        for dx in range(rows_x):
            sib_recv(k, dx).wait_recv()
            sib_send(k, dx).wait_send()
        for dx in range(1, rows_x):
            x_send(k, dx).wait_send()


def group_gather(groups, src):
    chunks, rows_x = 4, groups // 2
    dma = pltpu.SemaphoreType.DMA
    return pl.pallas_call(
        functools.partial(group_gather_kernel, groups, chunks),
        out_shape=jax.ShapeDtypeStruct((groups,) + src.shape, BF),
        in_specs=[pl.BlockSpec(memory_space=pl.ANY)],
        out_specs=pl.BlockSpec(memory_space=pl.ANY),
        scratch_shapes=[dma(())] + [dma((chunks, rows_x))] * 4,
        compiler_params=pltpu.CompilerParams(collective_id=1, has_side_effects=True),
        cost_estimate=lasting(45),
    )(src)


def ffn_back_kernel(
    parts, groups, chunks, streams,
    grad, act, dhid, w1, w2, base,
    out, dsum, back,
    ysum, leaving, loc, got, gone, wv, some, psib, sibr, xb, xrb,
    ll, ol, rs, rr, wl, sl, gss, gsr, gns, gnr, bs, br, bl,
):
    dp, f = lax.axis_index("dp"), lax.axis_index("fsdp")
    rows_x = groups // 2
    x, core = lax.div(dp, 2), lax.rem(dp, 2)
    sib = x * 2 + 1 - core
    p = ring_place(f, parts)
    nxt, prv = ring_index(p + 1, parts), ring_index(p - 1, parts)
    block, width = out.shape
    part, cut = width // streams, width // chunks
    count = dsum.shape[0]
    far, mid = range(1, rows_x), chunks // 2

    def local_copy(h, s):
        c = ring_index(p - 1 - s if h % 2 == 0 else p + 1 + s, parts)
        return pltpu.make_async_copy(
            grad.at[
                pl.ds(pl.multiple_of(c * block, block), block), pl.ds(h * part, part)
            ],
            loc.at[lax.rem(s, 2), h], ll.at[lax.rem(s, 2), h],
        )

    w_loads = (
        pltpu.make_async_copy(w2, wv, wl.at[0]),
        pltpu.make_async_copy(w1, wv, wl.at[1]),
    )
    for s in range(2):
        for h in range(streams):
            local_copy(h, s).start()
    w_loads[0].start()
    greet(
        [(dp, wrap(f + d, parts)) for d in range(1, parts)]
        + [(sib, f)]
        + [(wrap(x + dx, rows_x) * 2 + core, f) for dx in range(1, rows_x)]
    )

    def ring_copy(h, s):
        return remote(
            gone.at[lax.rem(s, 2), h], got.at[h, s], rs.at[h, s], rr.at[h, s],
            dp, nxt if h % 2 == 0 else prv,
        )

    def out_copy(h):
        return pltpu.make_async_copy(
            gone.at[lax.rem(parts - 1, 2), h],
            out.at[:, pl.ds(h * part, part)],
            ol.at[h],
        )

    def pass_on(s):
        slot = lax.rem(s, 2)
        for h in range(streams):
            local_copy(h, s).wait()

            @pl.when(s >= 2)
            def _():
                ring_copy(h, s - 2).wait_send()

            @pl.when(s == 0)
            def _():
                gone[slot, h] = loc[slot, h]

            @pl.when(s > 0)
            def _():
                ring_copy(h, s - 1).wait_recv()
                gone[slot, h] = (
                    loc[slot, h].astype(F32) + got[h, s - 1].astype(F32)
                ).astype(BF)

            @pl.when(s < parts - 1)
            def _():
                ring_copy(h, s).start()

            @pl.when(s == parts - 1)
            def _():
                out_copy(h).start()

            @pl.when(s < parts - 2)
            def _():
                local_copy(h, s + 2).start()

    def cols(k):
        return pl.ds(pl.multiple_of(k * cut, cut), cut)

    def rows_of(dx, c):
        group = wrap(x + dx, rows_x) * 2 + (core if c == 0 else 1 - core)
        return pl.ds(pl.multiple_of(group * count, count), count)

    rows_in, totals = (act, dhid), (ysum, dsum)

    def sum_sib(which, k):
        return remote(
            psib.at[:, :, cols(k)], sibr.at[which, :, :, cols(k)],
            gss.at[which, k], gsr.at[which, k], sib, f,
        )

    def sum_x(which, dx, k):
        to = wrap(x + dx, rows_x) * 2 + core
        return remote(
            xb.at[which, dx - 1, :, cols(k)], xrb.at[which, dx - 1, :, cols(k)],
            gns.at[which, dx, k], gnr.at[which, dx, k], to, f,
        )

    def take_rows(which, c):
        copies = [
            pltpu.make_async_copy(
                rows_in[which].at[rows_of(dx, c)], some.at[pl.ds(dx * count, count)], sl.at[dx]
            )
            for dx in range(rows_x)
        ]
        for copy in copies:
            copy.start()
        for copy in copies:
            copy.wait()

    def other_side(which, low, high):
        if low == 0:
            take_rows(which, 1)

        def one(k):
            psib[:, :, cols(k)] = (
                jnp.dot(some[...], wv[:, cols(k)], preferred_element_type=F32)
                .astype(BF)
                .reshape(rows_x, count, cut)
            )
            sum_sib(which, k).start()

        loop(low, high, one)

    def own_side(which, low, high):
        if low == 0:
            take_rows(which, 0)

        def one(k):
            here = jnp.dot(some[...], wv[:, cols(k)], preferred_element_type=F32)
            sum_sib(which, k).wait_recv()
            here = here.reshape(rows_x, count, cut) + sibr[which, :, :, cols(k)].astype(F32)
            for dx in far:
                xb[which, dx - 1, :, cols(k)] = here[dx].astype(BF)
                sum_x(which, dx, k).start()
            totals[which][:, cols(k)] = here[0]

        loop(low, high, one)

    def collect(which):
        def one(k):
            for dx in far:
                sum_x(which, dx, k).wait_recv()
                totals[which][:, cols(k)] += xrb[which, dx - 1, :, cols(k)].astype(F32)

        loop(0, chunks, one)

    def back_copy(d, came=False):
        return deal_copy(parts, dp, f, leaving, back, bs, br, d, came)

    def own_back():
        return pltpu.make_async_copy(leaving.at[f], back.at[f], bl)

    def send_back():
        piece = count // parts

        def one(j):
            rows = pl.ds(pl.multiple_of(j * piece, piece), piece)
            leaving[j] = (base[rows, :] + ysum[rows, :]).astype(BF)

        loop(0, parts, one)
        own_back().start()
        loop(1, parts, lambda d: back_copy(d).start())

    def sent_sib(which):
        loop(0, chunks, lambda k: sum_sib(which, k).wait_send())

    def sent_x(which):
        for dx in far:
            loop(0, chunks, lambda k: sum_x(which, dx, k).wait_send())

    def step(s):
        pass_on(s)

        @pl.when(s == 0)
        def _():
            w_loads[0].wait()
            other_side(0, 0, mid)

        @pl.when(s == 1)
        def _():
            other_side(0, mid, chunks)

        @pl.when(s == 2)
        def _():
            own_side(0, 0, mid)

        @pl.when(s == 3)
        def _():
            own_side(0, mid, chunks)
            w_loads[1].start()
            sent_sib(0)
            w_loads[1].wait()
            other_side(1, 0, mid)

        @pl.when(s == 4)
        def _():
            other_side(1, mid, chunks)
            own_side(1, 0, mid)

        @pl.when(s == 5)
        def _():
            own_side(1, mid, chunks)

        @pl.when(s == 6)
        def _():
            collect(0)
            send_back()

    loop(0, parts, step)
    collect(1)
    for h in range(streams):
        ring_copy(h, parts - 2).wait_send()
        out_copy(h).wait()
    sent_sib(1)
    sent_x(0)
    sent_x(1)
    own_back().wait()

    def returned(d):
        back_copy(d, True).wait_recv()
        back_copy(d).wait_send()

    loop(1, parts, returned)


def ffn_back(parts, groups, grad, act, dhid, w1, w2, base):
    chunks, streams, rows_x = 4, 4, groups // 2
    units, width = w1.shape
    count = act.shape[0] // groups
    block, part, piece = units // parts, width // streams, count // parts
    dma = pltpu.SemaphoreType.DMA
    hbm = pl.BlockSpec(memory_space=pl.ANY)
    vmem = pl.BlockSpec(memory_space=pltpu.VMEM)
    return pl.pallas_call(
        functools.partial(ffn_back_kernel, parts, groups, chunks, streams),
        out_shape=(
            jax.ShapeDtypeStruct((block, width), BF),
            jax.ShapeDtypeStruct((count, width), F32),
            jax.ShapeDtypeStruct((parts, piece, width), BF),
        ),
        in_specs=[hbm] * 5 + [vmem],
        out_specs=(hbm, vmem, hbm),
        scratch_shapes=[
            pltpu.VMEM((count, width), F32),
            pltpu.VMEM((parts, piece, width), BF),
            pltpu.VMEM((2, streams, block, part), BF),
            pltpu.VMEM((streams, parts - 1, block, part), BF),
            pltpu.VMEM((2, streams, block, part), BF),
            pltpu.VMEM((units, width), BF),
            pltpu.VMEM((rows_x * count, units), BF),
            pltpu.VMEM((rows_x, count, width), BF),
            pltpu.VMEM((2, rows_x, count, width), BF),
            pltpu.VMEM((2, rows_x - 1, count, width), BF),
            pltpu.VMEM((2, rows_x - 1, count, width), BF),
            dma((2, streams)), dma((streams,)),
            dma((streams, parts)), dma((streams, parts)), dma((2,)), dma((rows_x,)),
            dma((2, chunks)), dma((2, chunks)),
            dma((2, rows_x, chunks)), dma((2, rows_x, chunks)),
            dma((parts,)), dma((parts,)), dma(()),
        ],
        compiler_params=pltpu.CompilerParams(
            collective_id=3, has_side_effects=True, vmem_limit_bytes=60 * 2**20
        ),
        cost_estimate=lasting(130),
    )(grad, act, dhid, w1, w2, base)


def finish_kernel(
    parts, groups,
    grad_a, grad_b, gx, upg, vec,
    total_a, total_b, gx_out, upg_out, vec_out,
    loc_a, loc_b, sibr_a, sibr_b, xb_a, xb_b, xrb_a, xrb_b, got_a, got_b, gone_a, gone_b,
    local, ls, ss, sr, ns, nr, rs, rr, bs, br, us, ur, vs, vr,
):
    dp, f = lax.axis_index("dp"), lax.axis_index("fsdp")
    owners, rows_x = groups * parts, groups // 2
    x, core = lax.div(dp, 2), lax.rem(dp, 2)
    sib = x * 2 + 1 - core
    me = dp * parts + f
    p = ring_place(f, parts)
    nxt, prv = ring_index(p + 1, parts), ring_index(p - 1, parts)
    grads, total = (grad_a, grad_b), (total_a, total_b)
    loc, sibr, xb, xrb = (loc_a, loc_b), (sibr_a, sibr_b), (xb_a, xb_b), (xrb_a, xrb_b)
    got, gone = (got_a, got_b), (gone_a, gone_b)
    mine = [
        pltpu.make_async_copy(gx.at[f], gx_out.at[f], local.at[0]),
        pltpu.make_async_copy(vec.at[me], vec_out.at[me], local.at[1]),
        pltpu.make_async_copy(upg.at[me], upg_out.at[me], local.at[2]),
    ]
    for copy in mine:
        copy.start()
    greet_all(me, parts, owners)

    def chunk(h, s):
        return ring_index(p - 1 - s if h == 0 else p + 1 + s, parts)

    def sib_copy(h, s):
        piece = grads[h].at[:, 1 - core, chunk(h, s)]
        return remote(piece, sibr[h].at[s], ss.at[h, s], sr.at[h, s], sib, f)

    def own_copy(h, s):
        piece = grads[h].at[:, core, chunk(h, s)]
        return pltpu.make_async_copy(piece, loc[h].at[s], ls.at[h, s])

    def x_copy(h, s, dx):
        to = wrap(x + dx, rows_x) * 2 + core
        return remote(
            xb[h].at[s, dx - 1], xrb[h].at[s, dx - 1], ns.at[h, s, dx], nr.at[h, s, dx], to, f
        )

    def ring_copy(h, s):
        return remote(
            gone[h].at[s], got[h].at[s], rs.at[h, s], rr.at[h, s], dp, nxt if h == 0 else prv
        )

    def gx_copies(d, came=False):
        return deal_copy(parts, dp, f, gx, gx_out, bs, br, d, came)

    def upg_copies(d, came=False):
        return owner_copy(me, parts, owners, upg, upg_out, us, ur, d, came)

    def vec_copies(d, came=False):
        return owner_copy(me, parts, owners, vec, vec_out, vs, vr, d, came)

    def begin(s):
        for h in range(2):
            sib_copy(h, s).start()
            own_copy(h, s).start()

    def others(d):
        upg_copies(d).start()
        vec_copies(d).start()

    def returns(d):
        gx_copies(d).start()

    def pair(s):
        for h in range(2):
            sib_copy(h, s).wait_recv()
            own_copy(h, s).wait()
            for dx in range(1, rows_x):
                to = wrap(x + dx, rows_x)
                xb[h][s, dx - 1] = (sibr[h][s, to].astype(F32) + loc[h][s, to].astype(F32)).astype(BF)
                x_copy(h, s, dx).start()

    def step(s):
        for h in range(2):
            for dx in range(1, rows_x):
                x_copy(h, s, dx).wait_recv()

            def value():
                here = sibr[h][s, x].astype(F32) + loc[h][s, x].astype(F32)
                for dx in range(1, rows_x):
                    here = here + xrb[h][s, dx - 1].astype(F32)
                return here

            @pl.when(s == 0)
            def _():
                gone[h][s] = value().astype(BF)
                ring_copy(h, s).start()

            @pl.when((s > 0) & (s < parts - 1))
            def _():
                ring_copy(h, s - 1).wait_recv()
                gone[h][s] = (value() + got[h][s - 1].astype(F32)).astype(BF)
                ring_copy(h, s).start()

            @pl.when(s == parts - 1)
            def _():
                ring_copy(h, s - 1).wait_recv()
                total[h][...] = value() + got[h][s - 1].astype(F32)

    loop(0, parts, begin)
    loop(1, parts, returns)
    loop(1, owners, others)
    loop(0, parts, pair)
    loop(0, parts, step)

    def finish(s):
        for h in range(2):
            sib_copy(h, s).wait_send()
            for dx in range(1, rows_x):
                x_copy(h, s, dx).wait_send()

            @pl.when(s < parts - 1)
            def _():
                ring_copy(h, s).wait_send()

        @pl.when(s > 0)
        def _():
            gx_copies(s, True).wait_recv()
            gx_copies(s).wait_send()

    loop(0, parts, finish)

    def owner_finish(d):
        for copies in (upg_copies, vec_copies):
            copies(d, True).wait_recv()
            copies(d).wait_send()

    loop(1, owners, owner_finish)
    for copy in mine:
        copy.wait()


def finish_sums(parts, groups, grad_a, grad_b, gx, upg, vec):
    owners, rows_x = groups * parts, groups // 2
    rows = grad_a.shape[3]
    widths = (grad_a.shape[4], grad_b.shape[4])
    dma = pltpu.SemaphoreType.DMA
    hbm = pl.BlockSpec(memory_space=pl.ANY)
    return pl.pallas_call(
        functools.partial(finish_kernel, parts, groups),
        out_shape=(
            jax.ShapeDtypeStruct((rows, widths[0]), F32),
            jax.ShapeDtypeStruct((rows, widths[1]), F32),
            jax.ShapeDtypeStruct(gx.shape, BF),
            jax.ShapeDtypeStruct(upg.shape, BF),
            jax.ShapeDtypeStruct(vec.shape, F32),
        ),
        in_specs=[hbm] * 5,
        out_specs=(pl.BlockSpec(memory_space=pltpu.VMEM),) * 2 + (hbm,) * 3,
        scratch_shapes=[
            *(
                pltpu.VMEM(lead + (rows, width), BF)
                for lead in (
                    (parts, rows_x), (parts, rows_x), (parts, rows_x - 1), (parts, rows_x - 1),
                    (parts,), (parts,),
                )
                for width in widths
            ),
            dma((3,)),
            dma((2, parts)), dma((2, parts)), dma((2, parts)),
            dma((2, parts, rows_x)), dma((2, parts, rows_x)),
            dma((2, parts)), dma((2, parts)),
            dma((parts,)), dma((parts,)),
            dma((owners,)), dma((owners,)), dma((owners,)), dma((owners,)),
        ],
        compiler_params=pltpu.CompilerParams(
            collective_id=4, has_side_effects=True, vmem_limit_bytes=60 * 2**20
        ),
        cost_estimate=lasting(1),
    )(grad_a, grad_b, gx, upg, vec)


def shards(
    tokens,
    cotangent,
    lengths,
    routing,
    in_weight,
    in_first,
    in_second,
    out_weight,
    out_first,
    out_second,
    up_weight,
    up_first,
    up_second,
    down_weight,
    down_first,
    down_second,
    vectors,
    vector_first,
    vector_second,
):
    bf = jnp.bfloat16
    heads = D // HD
    count = tokens.shape[0]
    parts = lax.axis_size("fsdp")
    groups = lax.axis_size("dp")
    both = ("dp", "fsdp")
    piece = count // parts
    width_in = D + 2 * HD
    slots = jnp.arange(parts, dtype=jnp.int32)
    order = routing[0]
    inverse = jnp.sum(jnp.where(order[:, None] == slots[None, :], slots[:, None], 0), axis=0)

    def deal(array):
        return jnp.take(array.reshape(parts, piece, D), inverse, axis=0)

    def undeal(array):
        return jnp.take(array, order, axis=0).reshape(count, D)

    rows = in_weight.shape[0]
    owners = groups * parts
    out_vec = jnp.concatenate(
        [out_weight.astype(bf), jnp.pad(vectors.astype(bf), ((0, 0), (0, 128 - NVEC)))], axis=1
    )
    up_pieces = up_weight.astype(bf).reshape(rows, owners, FF // owners).transpose(1, 0, 2)
    up_block, dealt, dealt_grad, out_vec = lax.optimization_barrier(
        (exchange(parts, groups, up_pieces), deal(tokens), deal(cotangent), out_vec)
    )
    x_dealt, grad_dealt, whole_in, whole_out = spread(
        parts, groups, dealt, dealt_grad, in_weight.astype(bf), out_vec
    )
    inputs_here = x_dealt.reshape(count, D)
    grad_all = grad_dealt.reshape(groups * count, D)
    grad_here = lax.dynamic_index_in_dim(
        grad_dealt, lax.axis_index("dp"), 0, keepdims=False
    ).reshape(count, D)
    whole_in = whole_in.reshape(D, width_in)
    whole_out = whole_out.reshape(D, D + 128)
    part_down = lax.all_gather(down_weight.astype(bf), "fsdp", axis=0, tiled=True)
    part_up = lax.all_gather(up_block.reshape(D, FF // owners).T, "fsdp", axis=0, tiled=True)

    table = whole_out[:, D : D + NVEC].astype(jnp.float32)
    whole_out = whole_out[:, :D]
    gain_one = table[:, 0]
    shift_one = table[:, 1]
    query_bias = table[:, 2]
    branch_bias = table[:, 3]
    gain_two = table[:, 4]
    shift_two = table[:, 5]
    output_bias = table[:, 6]
    hidden_bias = table[:, 7:].T.reshape(FF)
    ff_here = FF // groups
    ff_start = lax.axis_index("dp") * ff_here
    hidden_bias_here = lax.dynamic_slice(hidden_bias, (ff_start,), (ff_here,))
    allowed = segment_mask(lengths[0], count)
    scale = 1.0 / math.sqrt(HD)
    inputs = inputs_here.astype(jnp.float32)
    norm_one_b = layer_norm(inputs, gain_one, shift_one).astype(bf)
    mixed = jnp.dot(norm_one_b, whole_in, preferred_element_type=jnp.float32)
    query_b = (mixed[:, :D] + query_bias).astype(bf)
    keys_b = mixed[:, D : D + HD].astype(bf)
    values_b = mixed[:, D + HD :].astype(bf)
    query_heads = query_b.reshape(count, heads, HD)

    def score_table():
        raw = (
            jnp.einsum("thd,sd->hts", query_heads, keys_b, preferred_element_type=jnp.float32)
            * scale
        )
        return jnp.where(allowed[None], raw, -1e30)

    scores = score_table()
    top = jnp.max(scores, axis=-1, keepdims=True)
    expo = jnp.exp(scores - top)
    total = jnp.sum(expo, axis=-1, keepdims=True)
    logsum = top + jnp.log(total)
    probs_b = (expo / total).astype(bf)
    attended_b = (
        jnp.einsum("hts,sd->thd", probs_b, values_b, preferred_element_type=jnp.float32)
        .reshape(count, D)
        .astype(bf)
    )
    middle = inputs + (
        jnp.dot(attended_b, whole_out, preferred_element_type=jnp.float32) + branch_bias
    )
    norm_two_b = layer_norm(middle, gain_two, shift_two).astype(bf)

    fused = parts == 8 and groups == 4
    if fused:
        norm_all = group_gather(groups, norm_two_b).reshape(groups * count, D)
    else:
        norm_all = lax.all_gather(norm_two_b, "dp", axis=0, tiled=True)
    hidden = contract_cols(norm_all, part_up) + hidden_bias_here
    grad_active = contract_cols(grad_all, part_down)
    gelu_value, gelu_pull = jax.vjp(gelu_tanh, hidden)
    active_b = gelu_value.astype(bf)
    grad_hidden_b = gelu_pull(grad_active)[0].astype(bf)
    down_parts = contract_rows(active_b, grad_all).astype(bf)
    up_parts = contract_rows(grad_hidden_b, norm_all).astype(bf)
    down_parts, up_parts = lax.optimization_barrier((down_parts, up_parts))
    if fused:
        up_grad_block, grad_norm_two, back_result = ffn_back(
            parts, groups, up_parts, active_b, grad_hidden_b, part_up, part_down,
            middle + output_bias,
        )
    else:
        up_grad_block = lax.psum_scatter(up_parts, "fsdp", scatter_dimension=0, tiled=True)
        grad_norm_two = lax.psum_scatter(
            jnp.dot(grad_hidden_b, part_up, preferred_element_type=jnp.float32).astype(bf),
            "dp", scatter_dimension=0, tiled=True,
        ).astype(jnp.float32)
        branch_two = lax.psum_scatter(
            jnp.dot(active_b, part_down, preferred_element_type=jnp.float32).astype(bf),
            "dp", scatter_dimension=0, tiled=True,
        ).astype(jnp.float32)
        back_result = lax.all_to_all(
            (middle + (branch_two + output_bias)).astype(bf),
            "fsdp", split_axis=0, concat_axis=0, tiled=True,
        ).reshape(parts, piece, D)
    down_parts, up_grad_block = lax.optimization_barrier((down_parts, up_grad_block))
    down_grad = lax.psum_scatter(down_parts, "fsdp", scatter_dimension=0, tiled=True)

    grad_y = grad_here.astype(jnp.float32)
    norm_value_two, pull_two = jax.vjp(layer_norm, middle, gain_two, shift_two)
    grad_middle_norm, grad_gain_two, grad_shift_two = pull_two(grad_norm_two)
    grad_middle = grad_y + grad_middle_norm
    grad_branch_b = grad_middle.astype(bf)
    grad_attended_b = contract_cols(grad_branch_b, whole_out).astype(bf)
    grad_heads = grad_attended_b.reshape(count, heads, HD)
    probs = jnp.exp(score_table() - logsum)
    probs_again_b = probs.astype(bf)
    grad_probs = jnp.einsum("thd,sd->hts", grad_heads, values_b, preferred_element_type=jnp.float32)
    grad_values_b = jnp.einsum(
        "hts,thd->sd", probs_again_b, grad_heads, preferred_element_type=jnp.float32
    ).astype(bf)
    weighted = jnp.sum(probs * grad_probs, axis=-1, keepdims=True)
    grad_scores_b = (probs * (grad_probs - weighted)).astype(bf)
    grad_query_b = (
        (
            jnp.einsum("hts,sd->thd", grad_scores_b, keys_b, preferred_element_type=jnp.float32)
            * scale
        )
        .reshape(count, D)
        .astype(bf)
    )
    grad_keys_b = (
        jnp.einsum("hts,thd->sd", grad_scores_b, query_heads, preferred_element_type=jnp.float32)
        * scale
    ).astype(bf)
    grad_mixed_b = jnp.concatenate([grad_query_b, grad_keys_b, grad_values_b], axis=1)
    grad_norm_one = contract_cols(grad_mixed_b, whole_in)
    norm_value_one, pull_one = jax.vjp(layer_norm, inputs, gain_one, shift_one)
    grad_inputs_norm, grad_gain_one, grad_shift_one = pull_one(grad_norm_one)
    grad_inputs = grad_middle + grad_inputs_norm
    hidden_sums = jnp.sum(grad_hidden_b.astype(jnp.float32), axis=0)
    hidden_whole = lax.dynamic_update_slice(
        jnp.zeros((FF,), jnp.float32), hidden_sums, (ff_start,)
    )
    vector_grad = jnp.concatenate(
        [
            jnp.stack(
                [
                    grad_gain_one,
                    grad_shift_one,
                    jnp.sum(grad_query_b.astype(jnp.float32), axis=0),
                    jnp.sum(grad_branch_b.astype(jnp.float32), axis=0),
                    grad_gain_two,
                    grad_shift_two,
                    jnp.sum(grad_y, axis=0),
                ],
                axis=0,
            ),
            hidden_whole.reshape(FF // D, D),
        ],
        axis=0,
    )
    vector_grad = vector_grad.reshape(NVEC, owners, rows).transpose(1, 0, 2)
    vector_grad = jnp.pad(vector_grad, ((0, 0), (0, 16 - NVEC), (0, 128 - rows)))
    grad_in, grad_out, back_grad, grad_up, vector_sum = finish_sums(
        parts,
        groups,
        contract_rows(norm_one_b, grad_mixed_b)
        .astype(bf)
        .reshape(groups // 2, 2, parts, rows, width_in),
        contract_rows(attended_b, grad_branch_b).astype(bf).reshape(groups // 2, 2, parts, rows, D),
        grad_inputs.astype(bf).reshape(parts, piece, D),
        up_grad_block.T.astype(bf).reshape(owners, rows, FF // owners),
        vector_grad,
    )
    grad_up = grad_up.transpose(1, 0, 2).reshape(rows, FF)
    vector_sum = jnp.sum(vector_sum, axis=0)
    grad_vec = vector_sum[:NVEC, :rows].T
    in_new = adam_update(in_weight, in_first, in_second, grad_in, 1.0 / math.sqrt(D), decay_rate)
    out_new = adam_update(
        out_weight, out_first, out_second, grad_out, 1.0 / math.sqrt(D * 8 // TOK_DEV), decay_rate
    )
    up_new = adam_update(up_weight, up_first, up_second, grad_up, 1.0 / math.sqrt(D), decay_rate)
    down_new = adam_update(
        down_weight, down_first, down_second, down_grad, 1.0 / math.sqrt(FF), decay_rate
    )
    vec_new = adam_update(vectors, vector_first, vector_second, grad_vec, 0.1, 0.0)
    return (undeal(back_result), undeal(back_grad)) + in_new + out_new + up_new + down_new + vec_new


def solution(mesh):
    spec = P(("dp", "fsdp"), None)
    return jax.shard_map(
        shards,
        mesh=mesh,
        in_specs=(spec,) * 19,
        out_specs=(spec,) * 17,
        check_vma=False,
    )
```
